256 devices in a mesh: gx: 16 (over z, core), gy: 16 (over x, y).
Axes of the slice: x: 4, y: 4, z: 8, core: 2. Of those that a mesh axis runs over, the one named last changes fastest.
Arguments:
- gradient: float32 [3, 128, 128, 256], P(None, 'gx', 'gy'), may hold values from -80 to 80
- potential: float32 [128, 128, 256], P('gx', 'gy'), may hold values from -6 to 6
- coupling: float32 [3, 3, 128, 128, 256], P(None, None, 'gx', 'gy'), may hold values from -1 to 1
- region: int32 [128, 128, 256], P('gx', 'gy'), may hold values from 0 to 3
- contact: int32 [128, 128, 256], P('gx', 'gy'), may hold values 0 or 1
- rates: float32 [4, 3], replicated, may hold values from 3.5 to 10
Outputs:
- adjoint: float32 [3, 128, 128, 256], P(None, 'gx', 'gy')
The draws below stay inside these ranges and needn't reach their ends.
All inputs are finite; a program needn't handle non-finite values. No bound on the sum of `contact` on one device may be relied on, other than what follows from the above.
Results may differ from the reference program's by a relative error of at most 0.0003.
Values sent between devices are 32-bit elements; how exact they have to be, the bound alone decides.
A program may use at most 192 MiB of HBM per device.

```python
import math
import jax
import jax.numpy as jnp
from jax import lax

NZ = 256
LEVELS = 4
CYCLES = 2
COARSE_SWEEPS = 6
REGIONS = 4
NX = 128
NY = 128


def spread_blocks(values, factor):
    widened = jnp.repeat(values, factor, axis=1)
    widened = jnp.repeat(widened, factor, axis=2)
    return jnp.repeat(widened, factor, axis=3)


def draw_gradient(key, part):
    key = jax.random.fold_in(key, 11)
    factor = 2 ** (LEVELS - 1)
    key_sign, key_size, key_noise = jax.random.split(key, 3)
    coarse_shape = (3, NX // factor, NY // factor, NZ // factor)
    flips = jax.random.bernoulli(key_sign, 0.5, coarse_shape)
    signs = jnp.where(flips, 1.0, -1.0).astype(jnp.float32)
    sizes = jax.random.uniform(key_size, coarse_shape, jnp.float32, 30.0, 60.0)
    noise = jnp.clip(10.0 * jax.random.normal(key_noise, (3, NX, NY, NZ), jnp.float32), -20.0, 20.0)
    smooth_part = spread_blocks(signs * sizes, factor)
    return (smooth_part + noise).astype(jnp.float32)


def plant(values, rng, least, largest):
    place = [jax.random.randint(jax.random.fold_in(rng, axis), (), 0, length) for axis, length in enumerate(values.shape)]
    widest = values.shape.index(max(values.shape))
    neighbour = place[:widest] + [(place[widest] + 1) % values.shape[widest]] + place[widest + 1:]
    return values.at[tuple(place)].set(least).at[tuple(neighbour)].set(largest)


def block_levels(key, extent, pieces, least, largest):
    def one(axis_at, shards_of):
        steps = jax.random.uniform(jax.random.fold_in(jax.random.fold_in(key, 6), axis_at), (shards_of,), jnp.float32, least / len(pieces), largest / len(pieces))
        return jnp.repeat(jnp.exp(steps), extent[axis_at] // shards_of).reshape((-1,) + (1,) * (len(extent) - axis_at - 1))

    loudness = one(*pieces[0])
    for cut in pieces[1:]:
        loudness = loudness * one(*cut)
    return loudness


def scatter_about(key, dims, scale, limit, pieces=(), kind=jnp.bfloat16):
    drawn = jax.random.normal(key, dims, jnp.float32) * scale
    if len(pieces) > 0:
        drawn = block_levels(key, dims, pieces, -0.22, 0.18) * drawn
    return jnp.clip(drawn, min=-limit, max=limit).astype(kind)


def setup_inputs(seed: int = 0) -> dict:
    splits = jax.random.split(jax.random.key(seed), 7)
    gradient = draw_gradient(jax.random.fold_in(splits[6], 71), 0)
    potential = scatter_about(splits[1], (NX, NY, NZ), 1.5, 6.0, ((0, 16), (1, 16)), jnp.float32)
    coupling = jnp.clip(jax.random.uniform(splits[2], (3, 3, NX, NY, NZ), jnp.float32, -1.0, 1.0) * block_levels(splits[2], (3, 3, NX, NY, NZ), ((2, 16), (3, 16)), -0.4, 0.0), -1.0, 1.0)
    region = plant(jax.random.randint(splits[3], (NX, NY, NZ), 0, REGIONS), jax.random.fold_in(splits[3], 1), 0, REGIONS - 1).astype(jnp.int32)
    contact = plant((jax.random.randint(splits[4], (NX, NY, NZ), 0, 8) < 1).astype(jnp.int32), jax.random.fold_in(splits[4], 1), 0, 1)
    rates = jnp.clip(jnp.exp(jax.random.uniform(splits[5], (REGIONS, 3), jnp.float32, math.log(3.5), math.log(10.0))), 3.5, 10.0)
    return dict(gradient=gradient, potential=potential, coupling=coupling, region=region, contact=contact, rates=rates)


OMEGA = 0.8
STRENGTH = 8.0


def bernoulli(value):
    is_small = jnp.abs(value) < 1e-4
    safe_arg = jnp.where(is_small, 1.0, value)
    return jnp.where(is_small, 1.0 - 0.5 * value, safe_arg / jnp.expm1(safe_arg))


def beside_cells(padded):
    return [padded[..., 2:, 1:-1, 1:-1], padded[..., :-2, 1:-1, 1:-1],
            padded[..., 1:-1, 2:, 1:-1], padded[..., 1:-1, :-2, 1:-1],
            padded[..., 1:-1, 1:-1, 2:], padded[..., 1:-1, 1:-1, :-2]]


def outgoing_weights(potential, padded):
    unity = jnp.ones_like(potential)
    stacked = []
    for beside in beside_cells(padded):
        difference = potential - beside
        stacked.append(jnp.stack([unity, bernoulli(difference), bernoulli(-difference)]))
    return jnp.stack(stacked)


def node_reaction(coupling, region, contact, rates):
    contact_value = contact.astype(coupling.dtype)
    rows_list = []
    for component in range(3):
        diagonal_extra = STRENGTH * contact_value
        for region_pick in range(REGIONS):
            diagonal_extra = diagonal_extra + jnp.where(region == region_pick, rates[region_pick, component], 0.0)
        rows_list.append(diagonal_extra)
    diagonal = jnp.stack(rows_list)
    identity = jnp.eye(3, dtype=coupling.dtype)[:, :, None, None, None]
    return coupling + identity * diagonal[:, None]


def cofactor_entry(entries, row_pick, col_pick):
    row_one, row_two = (row_pick + 1) % 3, (row_pick + 2) % 3
    col_one, col_two = (col_pick + 1) % 3, (col_pick + 2) % 3
    return entries[row_one][col_one] * entries[row_two][col_two] - entries[row_one][col_two] * entries[row_two][col_one]


def diag_inverse(weights, reaction):
    sums = jnp.sum(weights, axis=0)
    entries = [[reaction[col_pick, row_pick] + (sums[row_pick] if row_pick == col_pick else 0.0) for col_pick in range(3)] for row_pick in range(3)]
    cofactor = [[cofactor_entry(entries, row_pick, col_pick) for col_pick in range(3)] for row_pick in range(3)]
    determinant = entries[0][0] * cofactor[0][0] + entries[0][1] * cofactor[0][1] + entries[0][2] * cofactor[0][2]
    return jnp.stack([jnp.stack([cofactor[col_pick][row_pick] / determinant for col_pick in range(3)]) for row_pick in range(3)])


def apply_inverse(inverse, residual):
    return jnp.sum(inverse * residual[None], axis=1)


def apply_adjoint(field, padded, weights, reaction):
    total = jnp.sum(weights, axis=0) * field
    for direction, beside in enumerate(beside_cells(padded)):
        total = total - weights[direction] * beside
    return total + jnp.sum(reaction * field[:, None], axis=0)


def coarsen_level(weights, reaction):
    span_x, span_y, span_z = weights.shape[2], weights.shape[3], weights.shape[4]
    blocks = weights.reshape(6, 3, span_x // 2, 2, span_y // 2, 2, span_z // 2, 2)
    picks = [(2, 1), (2, 0), (4, 1), (4, 0), (6, 1), (6, 0)]
    coarse_weights = jnp.stack([
        jnp.sum(lax.index_in_dim(blocks[direction], face_side, sub_axis, keepdims=True), axis=(2, 4, 6))
        for direction, (sub_axis, face_side) in enumerate(picks)])
    coarse_reaction = jnp.sum(reaction.reshape(3, 3, span_x // 2, 2, span_y // 2, 2, span_z // 2, 2), axis=(3, 5, 7))
    return coarse_weights, coarse_reaction


def restrict_field(field):
    span_x, span_y, span_z = field.shape[1], field.shape[2], field.shape[3]
    return jnp.sum(field.reshape(3, span_x // 2, 2, span_y // 2, 2, span_z // 2, 2), axis=(2, 4, 6))


def prolong_field(field):
    span_x, span_y, span_z = field.shape[1], field.shape[2], field.shape[3]
    spread = jnp.broadcast_to(field[:, :, None, :, None, :, None], (3, span_x, 2, span_y, 2, span_z, 2))
    return spread.reshape(3, 2 * span_x, 2 * span_y, 2 * span_z)


def padded_field(field):
    return jnp.pad(field, ((0, 0), (1, 1), (1, 1), (1, 1)))


def smooth_sweep(source, current, weights, reaction, inverse):
    residual = source - apply_adjoint(current, padded_field(current), weights, reaction)
    return current + OMEGA * apply_inverse(inverse, residual)


def multigrid_cycle(level_index, source, current, from_zero, levels):
    weights, reaction, inverse = levels[level_index]
    if level_index == LEVELS - 1:
        current = OMEGA * apply_inverse(inverse, source)
        for sweep_index in range(COARSE_SWEEPS - 1):
            current = smooth_sweep(source, current, weights, reaction, inverse)
        return current
    if from_zero:
        current = OMEGA * apply_inverse(inverse, source)
    else:
        current = smooth_sweep(source, current, weights, reaction, inverse)
    residual = source - apply_adjoint(current, padded_field(current), weights, reaction)
    correction = multigrid_cycle(level_index + 1, restrict_field(residual), None, True, levels)
    current = current + prolong_field(correction)
    return smooth_sweep(source, current, weights, reaction, inverse)


def reference(gradient, potential, coupling, region, contact, rates):
    weights = outgoing_weights(potential, jnp.pad(potential, 1))
    reaction = node_reaction(coupling, region, contact, rates)
    levels = [(weights, reaction, diag_inverse(weights, reaction))]
    for level_index in range(1, LEVELS):
        coarse_weights, coarse_reaction = coarsen_level(levels[-1][0], levels[-1][1])
        levels.append((coarse_weights, coarse_reaction, diag_inverse(coarse_weights, coarse_reaction)))
    adjoint = multigrid_cycle(0, gradient, None, True, levels)
    for cycle_index in range(CYCLES - 1):
        adjoint = multigrid_cycle(0, gradient, adjoint, False, levels)
    return adjoint
```

```python
import functools

import jax
import jax.numpy as jnp
from jax import lax
from jax.experimental import pallas as pl
from jax.experimental.pallas import tpu as pltpu
from jax.sharding import PartitionSpec as P

MESH = pl.DeviceIdType.MESH
LEVELS = 4
COARSE_SWEEPS = 6
REGIONS = 4
OMEGA = 0.8
STRENGTH = 8.0
ROWS = 8
NX = (8, 4, 2, 1)


def each(count, body):
    if count == 1:
        body(0)
        return

    def step(i, carry):
        body(i)
        return carry

    lax.fori_loop(0, count, step, 0)


def face_weights(difference):
    size = jnp.abs(difference)
    small = size < 0.5
    series = 1.0 / 362880.0
    for k in (40320.0, 5040.0, 720.0, 120.0, 24.0, 6.0, 2.0, 1.0):
        series = series * size + 1.0 / k
    below = jnp.where(small, series, jnp.exp(size) - 1.0)
    low = jnp.where(small, 1.0, size) / below
    low = jnp.where(size < 1e-4, 1.0 - 0.5 * size, low)
    high = low + size
    positive = difference > 0.0
    return jnp.where(positive, low, high), jnp.where(positive, high, low)


def kernel(counts, grad_in, pot_in, coup_in, region_in, contact_in, rates_in, out, *scratch):
    grad, pot, coup, region, contact, rates, in_sem = scratch[-7:]
    scratch = scratch[:-7]
    loads = {}
    for i, (name, source, target) in enumerate(
        (
            ("pot", pot_in, pot.at[pl.ds(1, 8)]),
            ("rates", rates_in, rates),
            ("region", region_in, region),
            ("contact", contact_in, contact),
            ("coup", coup_in, coup),
            ("grad", grad_in, grad),
        )
    ):
        loads[name] = pltpu.make_async_copy(source, target, in_sem.at[i])
        loads[name].start()
    weights, reaction, diag, inverse = (scratch[4 * i : 4 * i + 4] for i in range(4))
    sources = (None,) + tuple(scratch[16:19])
    fields = scratch[19:23]
    rows_halo, pot_y, send_y, send_x, recv_x, send_sem, recv_sem = scratch[23:]
    n_x, n_y = counts
    lanes = out.shape[-1]
    gx, gy = lax.axis_index("gx"), lax.axis_index("gy")
    x_low, x_high = lax.rem(gx + n_x - 1, n_x), lax.rem(gx + 1, n_x)
    y_low, y_high = lax.rem(gy + n_y - 1, n_y), lax.rem(gy + 1, n_y)
    beside = ((x_high, gy), (x_low, gy), (gx, y_high), (gx, y_low))

    barrier = pltpu.get_barrier_semaphore()
    for device in beside:
        pl.semaphore_signal(barrier, inc=1, device_id=device, device_id_type=MESH)
    pl.semaphore_wait(barrier, 4)

    tile = (ROWS, lanes)
    row_at = lax.broadcasted_iota(jnp.int32, tile, 0)
    lane_at = lax.broadcasted_iota(jnp.int32, tile, 1)
    wide = lambda row: jnp.broadcast_to(row, tile)
    down = lambda v, by: pltpu.roll(v, by % ROWS, 0) if by % ROWS else v
    along = lambda v, by: pltpu.roll(v, by % lanes, 1)

    done = [0]

    def exchange(parts):
        slot = done[0] % 2
        done[0] += 1
        copies = []
        for i, (source, target) in enumerate(parts):
            copy = pltpu.make_async_remote_copy(
                src_ref=source,
                dst_ref=target,
                send_sem=send_sem.at[i],
                recv_sem=recv_sem.at[slot, i],
                device_id=beside[i],
                device_id_type=MESH,
            )
            copy.start()
            copies.append(copy)
        for copy in copies:
            copy.wait()

    loads["pot"].wait()
    for side, at in ((0, ROWS - 1), (1, 0)):
        packed = wide(pot[1, at : at + 1, :])
        for x in range(1, 8):
            packed = jnp.where(row_at == x, wide(pot[x + 1, at : at + 1, :]), packed)
        send_y[side, 0] = packed
    exchange(
        [
            (pot.at[8], pot.at[0]),
            (pot.at[1], pot.at[9]),
            (send_y.at[0, 0], pot_y.at[0]),
            (send_y.at[1, 0], pot_y.at[1]),
        ]
    )
    is_low_x, is_high_x = gx == 0, gx == n_x - 1
    is_low_y, is_high_y = gy == 0, gy == n_y - 1
    pot[0] = jnp.where(is_low_x, 0.0, pot[0])
    pot[9] = jnp.where(is_high_x, 0.0, pot[9])
    pot_y[0] = jnp.where(is_low_y, 0.0, pot_y[0])
    pot_y[1] = jnp.where(is_high_y, 0.0, pot_y[1])

    for name in ("rates", "region", "contact", "coup"):
        loads[name].wait()

    def set_up(x):
        here = pot[x + 1]
        near = (
            pot[x + 2],
            pot[x],
            jnp.where(row_at == ROWS - 1, wide(pot_y[1, pl.ds(x, 1), :]), down(here, -1)),
            jnp.where(row_at == 0, wide(pot_y[0, pl.ds(x, 1), :]), down(here, 1)),
            jnp.where(lane_at == lanes - 1, 0.0, along(here, -1)),
            jnp.where(lane_at == 0, 0.0, along(here, 1)),
        )
        for k in range(6):
            plus, minus = face_weights(here - near[k])
            weights[0][x, 3 * k] = jnp.ones(tile, jnp.float32)
            weights[0][x, 3 * k + 1] = plus
            weights[0][x, 3 * k + 2] = minus
        at_contact = STRENGTH * contact[x].astype(jnp.float32)
        regions = region[x]
        for c in range(3):
            extra = jnp.full(tile, rates[0, c])
            for pick in range(1, REGIONS):
                extra = jnp.where(regions == pick, rates[pick, c], extra)
            for d in range(3):
                value = coup[c, d, x]
                reaction[0][x, 3 * c + d] = value + (extra + at_contact) if c == d else value

    each(NX[0], set_up)

    def finish_level(level):
        w, r, span = weights[level], reaction[level], 1 << level

        def body(x):
            m = [[r[x, 3 * col + row] for col in range(3)] for row in range(3)]
            for c in range(3):
                total = w[x, c]
                for k in range(1, 6):
                    total = total + w[x, 3 * k + c]
                m[c][c] = m[c][c] + total
                diag[level][x, c] = m[c][c]

            def cofactor(i, j):
                i1, i2, j1, j2 = (i + 1) % 3, (i + 2) % 3, (j + 1) % 3, (j + 2) % 3
                return m[i1][j1] * m[i2][j2] - m[i1][j2] * m[i2][j1]

            cof = [[cofactor(i, j) for j in range(3)] for i in range(3)]
            det = m[0][0] * cof[0][0] + m[0][1] * cof[0][1] + m[0][2] * cof[0][2]
            scale = OMEGA / det
            for i in range(3):
                for j in range(3):
                    inverse[level][x, 3 * i + j] = cof[j][i] * scale

        each(NX[level], body)

    def mask_level(level):
        w, span, last = weights[level], 1 << level, NX[level] - 1
        for c in range(3):
            w[last, c] = jnp.where(is_high_x, 0.0, w[last, c])
            w[0, 3 + c] = jnp.where(is_low_x, 0.0, w[0, 3 + c])
        off_high = jnp.logical_and(row_at >= ROWS - span, is_high_y)
        off_low = jnp.logical_and(row_at < span, is_low_y)
        off_up, off_down = lane_at >= lanes - span, lane_at < span

        def body(x):
            for k, off in ((2, off_high), (3, off_low), (4, off_up), (5, off_down)):
                for c in range(3):
                    w[x, 3 * k + c] = jnp.where(off, 0.0, w[x, 3 * k + c])

        each(NX[level], body)

    def pair_tools(level):
        span = 1 << level
        odd_row = (row_at & span) != 0
        odd_lane = (lane_at & span) != 0

        def high_row(v):
            return jnp.where(odd_row, v, down(v, -span))

        def low_row(v):
            return jnp.where(odd_row, down(v, span), v)

        def high_lane(v):
            return jnp.where(odd_lane, v, along(v, -span))

        def low_lane(v):
            return jnp.where(odd_lane, along(v, span), v)

        def rows(v):
            return v + jnp.where(odd_row, down(v, span), down(v, -span))

        def lanes_(v):
            return v + jnp.where(odd_lane, along(v, span), along(v, -span))

        return high_row, low_row, high_lane, low_lane, rows, lanes_

    def coarsen(level):
        high_row, low_row, high_lane, low_lane, rows, lanes_ = pair_tools(level)
        w, r, w_next, r_next = weights[level], reaction[level], weights[level + 1], reaction[level + 1]

        def body(x):
            for c in range(3):
                w_next[x, c] = lanes_(rows(w[2 * x + 1, c]))
                w_next[x, 3 + c] = lanes_(rows(w[2 * x, 3 + c]))
                pair = lambda k: w[2 * x, 3 * k + c] + w[2 * x + 1, 3 * k + c]
                w_next[x, 6 + c] = lanes_(high_row(pair(2)))
                w_next[x, 9 + c] = lanes_(low_row(pair(3)))
                w_next[x, 12 + c] = high_lane(rows(pair(4)))
                w_next[x, 15 + c] = low_lane(rows(pair(5)))
            for i in range(9):
                r_next[x, i] = lanes_(rows(r[2 * x, i] + r[2 * x + 1, i]))

        each(NX[level + 1], body)

    for level in range(LEVELS):
        finish_level(level)
        if level < LEVELS - 1:
            coarsen(level)
        mask_level(level)

    def source(level, x):
        if level == 0:
            return [grad[c, x] for c in range(3)]
        return [sources[level][x, c] for c in range(3)]

    def solve(level, x, r):
        v = inverse[level]
        return [v[x, 3 * c] * r[0] + v[x, 3 * c + 1] * r[1] + v[x, 3 * c + 2] * r[2] for c in range(3)]

    def share(level, at):
        slot, f, count = done[0] % 2, fields[level], NX[level]
        if level < 2:
            for side, row in ((0, ROWS - 1), (1, 0)):
                for c in range(3):
                    packed = wide(f[at, 1, c, row : row + 1, :])
                    for x in range(1, count):
                        packed = jnp.where(row_at == x, wide(f[at, x + 1, c, row : row + 1, :]), packed)
                    send_y[side, c] = packed
            exchange(
                [
                    (f.at[at, count], f.at[at, 0]),
                    (f.at[at, 1], f.at[at, count + 1]),
                    (send_y.at[0], rows_halo.at[slot, 0]),
                    (send_y.at[1], rows_halo.at[slot, 1]),
                ]
            )
            return slot
        for side, row in ((0, ROWS - 1), (1, 0)):
            packed = wide(f[at, 1, 0, row : row + 1, :])
            for x in range(count):
                for c in range(3):
                    packed = jnp.where(row_at == 4 * x + c, wide(f[at, x + 1, c, row : row + 1, :]), packed)
            send_y[side, 0] = packed
        for side, x in ((0, count), (1, 1)):
            by_four = row_at & 3
            packed = jnp.where(by_four == 0, f[at, x, 0], jnp.where(by_four == 1, f[at, x, 1], f[at, x, 2]))
            send_x[side] = packed
        exchange(
            [
                (send_x.at[0], recv_x.at[slot, 0]),
                (send_x.at[1], recv_x.at[slot, 1]),
                (send_y.at[0, 0], rows_halo.at[slot, 0, 0]),
                (send_y.at[1, 0], rows_halo.at[slot, 1, 0]),
            ]
        )
        for side, x in ((0, 0), (1, count + 1)):
            for c in range(3):
                value = wide(recv_x[slot, side, c : c + 1, :])
                if level == 2:
                    value = jnp.where(row_at < 4, value, wide(recv_x[slot, side, 4 + c : 5 + c, :]))
                f[at, x, c] = value
        return slot

    def residual(level, at, slot, x):
        f, w, r, span = fields[level], weights[level], reaction[level], 1 << level
        u = [f[at, x + 1, c] for c in range(3)]
        b = source(level, x)
        left = []
        for c in range(3):
            if level < 2:
                row_high, row_low = (rows_halo[slot, side, c, pl.ds(x, 1), :] for side in (1, 0))
            else:
                row_high, row_low = (rows_halo[slot, side, 0, pl.ds(4 * x + c, 1), :] for side in (1, 0))
            near = (
                f[at, x + 2, c],
                f[at, x, c],
                jnp.where(row_at >= ROWS - span, wide(row_high), down(u[c], -span)),
                jnp.where(row_at < span, wide(row_low), down(u[c], span)),
                along(u[c], -span),
                along(u[c], span),
            )
            value = b[c] - diag[level][x, c] * u[c]
            for k in range(6):
                value = value + w[x, 3 * k + c] * near[k]
            for d in range(3):
                if d != c:
                    value = value - r[x, 3 * d + c] * u[d]
            left.append(value)
        return u, left

    def sweep(level, at, slot, last=False):
        def body(x):
            u, left = residual(level, at, slot, x)
            step = solve(level, x, left)
            for c in range(3):
                if last:
                    out[c, x] = u[c] + step[c]
                else:
                    fields[level][1 - at, x + 1, c] = u[c] + step[c]

        each(NX[level], body)
        return 1 - at

    def restrict(level, at, slot):
        rows, lanes_ = pair_tools(level)[4:]

        def body(x):
            left = [residual(level, at, slot, 2 * x + i)[1] for i in range(2)]
            total = [lanes_(rows(left[0][c] + left[1][c])) for c in range(3)]
            first = solve(level + 1, x, total)
            for c in range(3):
                sources[level + 1][x, c] = total[c]
                fields[level + 1][0, x + 1, c] = first[c]

        each(NX[level + 1], body)

    def cycle(level, at, last=False):
        if level == LEVELS - 1:
            for _ in range(COARSE_SWEEPS - 1):
                at = sweep(level, at, share(level, at))
            return at
        restrict(level, at, share(level, at))
        e = cycle(level + 1, 0)

        def add(x):
            for c in range(3):
                for i in range(2):
                    fields[level][at, 2 * x + 1 + i, c] += fields[level + 1][e, x + 1, c]

        each(NX[level + 1], add)
        return sweep(level, at, share(level, at), last)

    def start(x):
        for c, value in enumerate(solve(0, x, source(0, x))):
            fields[0][0, x + 1, c] = value

    loads["grad"].wait()
    each(NX[0], start)
    at = cycle(0, 0)
    at = sweep(0, at, share(0, at))
    cycle(0, at, last=True)


def local(counts, gradient, potential, coupling, region, contact, rates):
    nz = potential.shape[-1]
    tile = (ROWS, nz)
    f32 = jnp.float32
    scratch = []
    for parts in (18, 9, 3, 9):
        scratch += [pltpu.VMEM((n, parts) + tile, f32) for n in NX]
    scratch += [pltpu.VMEM((n, 3) + tile, f32) for n in NX[1:]]
    scratch += [pltpu.VMEM((2, n + 2, 3) + tile, f32) for n in NX]
    scratch += [
        pltpu.VMEM((2, 2, 3) + tile, f32),
        pltpu.VMEM((2,) + tile, f32),
        pltpu.VMEM((2, 3) + tile, f32),
        pltpu.VMEM((2,) + tile, f32),
        pltpu.VMEM((2, 2) + tile, f32),
        pltpu.SemaphoreType.DMA((4,)),
        pltpu.SemaphoreType.DMA((2, 4)),
        pltpu.VMEM(gradient.shape, f32),
        pltpu.VMEM((10,) + tile, f32),
        pltpu.VMEM(coupling.shape, f32),
        pltpu.VMEM(region.shape, jnp.int32),
        pltpu.VMEM(contact.shape, jnp.int32),
        pltpu.SMEM(rates.shape, f32),
        pltpu.SemaphoreType.DMA((6,)),
    ]
    vmem = pl.BlockSpec(memory_space=pltpu.VMEM)
    return pl.pallas_call(
        functools.partial(kernel, counts),
        out_shape=jax.ShapeDtypeStruct(gradient.shape, f32),
        in_specs=[pl.BlockSpec(memory_space=pltpu.HBM)] * 6,
        out_specs=vmem,
        scratch_shapes=scratch,
        compiler_params=pltpu.CompilerParams(
            collective_id=0, has_side_effects=True, vmem_limit_bytes=40 * 1024 * 1024
        ),
    )(gradient, potential, coupling, region, contact, rates)


def solution(mesh):
    placed = (
        P(None, "gx", "gy", None),
        P("gx", "gy", None),
        P(None, None, "gx", "gy", None),
        P("gx", "gy", None),
        P("gx", "gy", None),
        P(),
    )
    counts = (mesh.shape["gx"], mesh.shape["gy"])
    return jax.shard_map(
        functools.partial(local, counts),
        mesh=mesh,
        in_specs=placed,
        out_specs=P(None, "gx", "gy", None),
        check_vma=False,
    )
```

```python
import functools

import jax
import jax.numpy as jnp
from jax import lax
from jax.experimental import pallas as pl
from jax.experimental.pallas import tpu as pltpu
from jax.sharding import PartitionSpec as P

MESH = pl.DeviceIdType.MESH
LEVELS = 4
COARSE_SWEEPS = 6
REGIONS = 4
OMEGA = 0.8
STRENGTH = 8.0
ROWS = 8
NX = (8, 4, 2, 1)
RADIUS = 3
WINDOW = [
    (i, j)
    for i in range(-RADIUS, RADIUS + 1)
    for j in range(-RADIUS, RADIUS + 1)
    if 0 < abs(i) + abs(j) <= RADIUS
]
SLOTS = 8


def each(count, body):
    if count == 1:
        body(0)
        return

    def step(i, carry):
        body(i)
        return carry

    lax.fori_loop(0, count, step, 0, unroll=count)


def face_weights(difference):
    size = jnp.abs(difference)
    small = size < 0.5
    series = 1.0 / 362880.0
    for k in (40320.0, 5040.0, 720.0, 120.0, 24.0, 6.0, 2.0, 1.0):
        series = series * size + 1.0 / k
    below = jnp.where(small, series, jnp.exp(size) - 1.0)
    low = jnp.where(small, 1.0, size) / below
    low = jnp.where(size < 1e-4, 1.0 - 0.5 * size, low)
    high = low + size
    positive = difference > 0.0
    return jnp.where(positive, low, high), jnp.where(positive, high, low)


def kernel(counts, grad_in, pot_in, coup_in, region_in, contact_in, rates_in, out, *scratch):
    grad, pot, coup, region, contact, rates, in_sem = scratch[-7:]
    scratch = scratch[:-7]
    loads = {}
    for i, (name, source, target) in enumerate(
        (
            ("pot", pot_in, pot.at[pl.ds(1, 8)]),
            ("rates", rates_in, rates),
            ("region", region_in, region),
            ("contact", contact_in, contact),
            ("coup", coup_in, coup),
            ("grad", grad_in, grad),
        )
    ):
        loads[name] = pltpu.make_async_copy(source, target, in_sem.at[i])
        loads[name].start()
    weights, reaction, diag, inverse = (scratch[4 * i : 4 * i + 4] for i in range(4))
    sources = (None,) + tuple(scratch[16:19])
    fields = scratch[19:23]
    rows_halo, pot_y, send_y, send_x, recv_x, send_sem, recv_sem = scratch[23:30]
    w_own, r_own, coef_send, coef_recv, cell_send, cell_recv, e_rows = scratch[30:37]
    coef_send_sem, coef_recv_sem, cell_send_sem, cell_recv_sem = scratch[37:]
    n_x, n_y = counts
    lanes = out.shape[-1]
    gx, gy = lax.axis_index("gx"), lax.axis_index("gy")
    x_low, x_high = lax.rem(gx + n_x - 1, n_x), lax.rem(gx + 1, n_x)
    y_low, y_high = lax.rem(gy + n_y - 1, n_y), lax.rem(gy + 1, n_y)
    beside = ((x_high, gy), (x_low, gy), (gx, y_high), (gx, y_low))

    barrier = pltpu.get_barrier_semaphore()
    around = [(lax.rem(gx + n_x + i, n_x), lax.rem(gy + n_y + j, n_y)) for i, j in WINDOW]
    for device in around:
        pl.semaphore_signal(barrier, inc=1, device_id=device, device_id_type=MESH)
    pl.semaphore_wait(barrier, len(WINDOW))

    tile = (ROWS, lanes)
    row_at = lax.broadcasted_iota(jnp.int32, tile, 0)
    lane_at = lax.broadcasted_iota(jnp.int32, tile, 1)
    wide = lambda row: jnp.broadcast_to(row, tile)
    down = lambda v, by: pltpu.roll(v, by % ROWS, 0) if by % ROWS else v
    along = lambda v, by: pltpu.roll(v, by % lanes, 1)

    done = [0]

    def exchange(parts):
        slot = done[0] % 2
        done[0] += 1
        copies = []
        for i in (2, 3, 0, 1):
            source, target = parts[i]
            copy = pltpu.make_async_remote_copy(
                src_ref=source,
                dst_ref=target,
                send_sem=send_sem.at[i],
                recv_sem=recv_sem.at[slot, i],
                device_id=beside[i],
                device_id_type=MESH,
            )
            copy.start()
            copies.append(copy)

        def wait():
            for copy in copies:
                copy.wait()

        return wait

    def gather(source, target, send, recv):
        copies = []
        for n, device in enumerate(around):
            copy = pltpu.make_async_remote_copy(
                src_ref=source,
                dst_ref=target.at[n],
                send_sem=send.at[n],
                recv_sem=recv.at[n],
                device_id=device,
                device_id_type=MESH,
            )
            copy.start()
            copies.append(copy)

        def wait():
            for copy in copies:
                copy.wait()

        return wait

    loads["pot"].wait()
    for side, at in ((0, ROWS - 1), (1, 0)):
        packed = wide(pot[1, at : at + 1, :])
        for x in range(1, 8):
            packed = jnp.where(row_at == x, wide(pot[x + 1, at : at + 1, :]), packed)
        send_y[side, 0] = packed
    wait = exchange(
        [
            (pot.at[8], pot.at[0]),
            (pot.at[1], pot.at[9]),
            (send_y.at[0, 0], pot_y.at[0]),
            (send_y.at[1, 0], pot_y.at[1]),
        ]
    )
    for name in ("rates", "region", "contact", "coup"):
        loads[name].wait()

    def put_faces(x, first, near):
        here = pot[x + 1]
        for k, value in enumerate(near):
            plus, minus = face_weights(here - value)
            weights[0][x, 3 * (first + k)] = jnp.ones(tile, jnp.float32)
            weights[0][x, 3 * (first + k) + 1] = plus
            weights[0][x, 3 * (first + k) + 2] = minus

    def set_up(x):
        here = pot[x + 1]
        near = (
            jnp.where(lane_at == lanes - 1, 0.0, along(here, -1)),
            jnp.where(lane_at == 0, 0.0, along(here, 1)),
        )
        put_faces(x, 4, near)
        at_contact = STRENGTH * contact[x].astype(jnp.float32)
        regions = region[x]
        for c in range(3):
            extra = jnp.full(tile, rates[0, c])
            for pick in range(1, REGIONS):
                extra = jnp.where(regions == pick, rates[pick, c], extra)
            for d in range(3):
                value = coup[c, d, x]
                reaction[0][x, 3 * c + d] = value + (extra + at_contact) if c == d else value

    each(NX[0], set_up)
    wait()
    is_low_x, is_high_x = gx == 0, gx == n_x - 1
    is_low_y, is_high_y = gy == 0, gy == n_y - 1
    pot[0] = jnp.where(is_low_x, 0.0, pot[0])
    pot[9] = jnp.where(is_high_x, 0.0, pot[9])
    pot_y[0] = jnp.where(is_low_y, 0.0, pot_y[0])
    pot_y[1] = jnp.where(is_high_y, 0.0, pot_y[1])

    def cross_faces(x):
        here = pot[x + 1]
        near = (
            pot[x + 2],
            pot[x],
            jnp.where(row_at == ROWS - 1, wide(pot_y[1, pl.ds(x, 1), :]), down(here, -1)),
            jnp.where(row_at == 0, wide(pot_y[0, pl.ds(x, 1), :]), down(here, 1)),
        )
        put_faces(x, 0, near)

    each(NX[0], cross_faces)

    def finish_level(level):
        w, r, span = weights[level], reaction[level], 1 << level

        def body(x):
            m = [[r[x, 3 * col + row] for col in range(3)] for row in range(3)]
            for c in range(3):
                total = w[x, c]
                for k in range(1, 6):
                    total = total + w[x, 3 * k + c]
                m[c][c] = m[c][c] + total
                diag[level][x, c] = m[c][c]

            def cofactor(i, j):
                i1, i2, j1, j2 = (i + 1) % 3, (i + 2) % 3, (j + 1) % 3, (j + 2) % 3
                return m[i1][j1] * m[i2][j2] - m[i1][j2] * m[i2][j1]

            cof = [[cofactor(i, j) for j in range(3)] for i in range(3)]
            det = m[0][0] * cof[0][0] + m[0][1] * cof[0][1] + m[0][2] * cof[0][2]
            scale = OMEGA / det
            for i in range(3):
                for j in range(3):
                    inverse[level][x, 3 * i + j] = cof[j][i] * scale

        each(NX[level], body)

    def mask_level(level):
        w, span, last = weights[level], 1 << level, NX[level] - 1
        for c in range(3):
            w[last, c] = jnp.where(is_high_x, 0.0, w[last, c])
            w[0, 3 + c] = jnp.where(is_low_x, 0.0, w[0, 3 + c])
        off_high = jnp.logical_and(row_at >= ROWS - span, is_high_y)
        off_low = jnp.logical_and(row_at < span, is_low_y)
        off_up, off_down = lane_at >= lanes - span, lane_at < span

        def body(x):
            for k, off in ((2, off_high), (3, off_low), (4, off_up), (5, off_down)):
                for c in range(3):
                    w[x, 3 * k + c] = jnp.where(off, 0.0, w[x, 3 * k + c])

        each(NX[level], body)

    def pair_tools(level):
        span = 1 << level
        odd_row = (row_at & span) != 0
        odd_lane = (lane_at & span) != 0

        def high_row(v):
            return jnp.where(odd_row, v, down(v, -span))

        def low_row(v):
            return jnp.where(odd_row, down(v, span), v)

        def high_lane(v):
            return jnp.where(odd_lane, v, along(v, -span))

        def low_lane(v):
            return jnp.where(odd_lane, along(v, span), v)

        def rows(v):
            return v + jnp.where(odd_row, down(v, span), down(v, -span))

        def lanes_(v):
            return v + jnp.where(odd_lane, along(v, span), along(v, -span))

        return high_row, low_row, high_lane, low_lane, rows, lanes_

    def coarsen(level):
        high_row, low_row, high_lane, low_lane, rows, lanes_ = pair_tools(level)
        w, r = weights[level], reaction[level]
        w_next, r_next = (w_own, r_own) if level == LEVELS - 2 else (weights[level + 1], reaction[level + 1])

        def body(x):
            for c in range(3):
                w_next[x, c] = lanes_(rows(w[2 * x + 1, c]))
                w_next[x, 3 + c] = lanes_(rows(w[2 * x, 3 + c]))
                pair = lambda k: w[2 * x, 3 * k + c] + w[2 * x + 1, 3 * k + c]
                w_next[x, 6 + c] = lanes_(high_row(pair(2)))
                w_next[x, 9 + c] = lanes_(low_row(pair(3)))
                w_next[x, 12 + c] = high_lane(rows(pair(4)))
                w_next[x, 15 + c] = low_lane(rows(pair(5)))
            for i in range(9):
                r_next[x, i] = lanes_(rows(r[2 * x, i] + r[2 * x + 1, i]))

        each(NX[level + 1], body)

    slot_at = lane_at & (SLOTS - 1)
    cells = [(-i, -j) for i, j in WINDOW] + [(0, 0)]

    def columns(row_of):
        for t in range(2 * RADIUS + 1):
            packed = jnp.zeros(tile, jnp.float32)
            for n, (i, j) in enumerate(cells):
                if j + RADIUS == t:
                    packed = jnp.where(row_at == i + RADIUS, wide(row_of(n)), packed)
            yield t, packed

    def send_coefficients():
        fields_ = [w_own[0, i] for i in range(18)] + [r_own[0, i] for i in range(9)]
        for row in range(4):
            part = fields_[SLOTS * row : SLOTS * row + SLOTS]
            packed = part[0]
            for i in range(1, len(part)):
                packed = jnp.where(slot_at == i, part[i], packed)
            coef_send[row : row + 1, :] = packed[0:1, :]
        return gather(coef_send, coef_recv, coef_send_sem, coef_recv_sem)

    def take_coefficients():
        top = LEVELS - 1
        w, r = weights[top], reaction[top]
        for row in range(4):
            row_of = lambda n: coef_recv[n, row : row + 1, :] if n < len(WINDOW) else coef_send[row : row + 1, :]
            count = min(SLOTS, 27 - SLOTS * row)
            made = [jnp.full(tile, 1.0 if SLOTS * row + i in (18, 22, 26) else 0.0) for i in range(count)]
            for t, packed in columns(row_of):
                for i in range(count):
                    made[i] = jnp.where(slot_at == t, along(packed, t - i), made[i])
            for i in range(count):
                at = SLOTS * row + i
                if at < 18:
                    w[0, at] = made[i]
                else:
                    r[0, at - 18] = made[i]
        finish_level(top)
        x_at, y_at = row_at + (gx - RADIUS), slot_at + (gy - RADIUS)
        offs = (
            jnp.logical_or(x_at == n_x - 1, x_at == -1),
            jnp.logical_or(x_at == 0, x_at == n_x),
            jnp.logical_or(y_at == n_y - 1, y_at == -1),
            jnp.logical_or(y_at == 0, y_at == n_y),
            lane_at >= lanes - SLOTS,
            lane_at < SLOTS,
        )
        for k, off in enumerate(offs):
            for c in range(3):
                w[0, 3 * k + c] = jnp.where(off, 0.0, w[0, 3 * k + c])

    def share_cells(which, values):
        packed = jnp.where(slot_at == 0, values[0], jnp.where(slot_at == 1, values[1], values[2]))
        cell_send[which] = packed[0:1, :]
        gather(cell_send.at[which], cell_recv.at[which], cell_send_sem, cell_recv_sem.at[which])()
        made = [jnp.zeros(tile, jnp.float32) for _ in range(3)]
        row_of = lambda n: cell_recv[which, n] if n < len(WINDOW) else cell_send[which]
        for t, packed in columns(row_of):
            for c in range(3):
                made[c] = jnp.where(slot_at == t, along(packed, t - c), made[c])
        return made

    def spread(value, t):
        value = jnp.where(slot_at == t, value, 0.0)
        for bit in (1, 2, 4):
            value = value + along(value, -bit if t & bit else bit)
        return value

    def window_sweep(b, u):
        top = LEVELS - 1
        w, r = weights[top], reaction[top]
        left = []
        for c in range(3):
            value = b[c] - diag[top][0, c] * u[c]
            near = (down(u[c], -1), down(u[c], 1), along(u[c], -1), along(u[c], 1), along(u[c], -SLOTS), along(u[c], SLOTS))
            for k in range(6):
                value = value + w[0, 3 * k + c] * near[k]
            for d in range(3):
                if d != c:
                    value = value - r[0, 3 * d + c] * u[d]
            left.append(value)
        step = solve(top, 0, left)
        return [u[c] + step[c] for c in range(3)]

    def coarsest(own):
        b = share_cells(0, own)
        u = solve(LEVELS - 1, 0, b)
        for _ in range(RADIUS):
            u = window_sweep(b, u)
        u = [spread(value, RADIUS) for value in u]
        u = share_cells(1, [value[RADIUS : RADIUS + 1, :] for value in u])
        for _ in range(COARSE_SWEEPS - 1 - RADIUS):
            u = window_sweep(b, u)
        for c in range(3):
            for j in range(3):
                e_rows[c, j] = spread(u[c], RADIUS - 1 + j)

    def e_at(c, i, j):
        return wide(e_rows[c, 1 + j, RADIUS + i : RADIUS + i + 1, :])

    def source(level, x):
        if level == 0:
            return [grad[c, x] for c in range(3)]
        return [sources[level][x, c] for c in range(3)]

    def solve(level, x, r):
        v = inverse[level]
        return [v[x, 3 * c] * r[0] + v[x, 3 * c + 1] * r[1] + v[x, 3 * c + 2] * r[2] for c in range(3)]

    def share(level, at, beside_it=lambda: None):
        slot, f, count = done[0] % 2, fields[level], NX[level]
        if level < 2:
            for side, row in ((0, ROWS - 1), (1, 0)):
                for c in range(3):
                    packed = wide(f[at, 1, c, row : row + 1, :])
                    for x in range(1, count):
                        packed = jnp.where(row_at == x, wide(f[at, x + 1, c, row : row + 1, :]), packed)
                    send_y[side, c] = packed
            wait = exchange(
                [
                    (f.at[at, count], f.at[at, 0]),
                    (f.at[at, 1], f.at[at, count + 1]),
                    (send_y.at[0], rows_halo.at[slot, 0]),
                    (send_y.at[1], rows_halo.at[slot, 1]),
                ]
            )
            beside_it()
            wait()
            return slot
        for side, row in ((0, ROWS - 1), (1, 0)):
            packed = wide(f[at, 1, 0, row : row + 1, :])
            for x in range(count):
                for c in range(3):
                    packed = jnp.where(row_at == 4 * x + c, wide(f[at, x + 1, c, row : row + 1, :]), packed)
            send_y[side, 0] = packed
        for side, x in ((0, count), (1, 1)):
            by_four = row_at & 3
            packed = jnp.where(by_four == 0, f[at, x, 0], jnp.where(by_four == 1, f[at, x, 1], f[at, x, 2]))
            send_x[side] = packed
        wait = exchange(
            [
                (send_x.at[0], recv_x.at[slot, 0]),
                (send_x.at[1], recv_x.at[slot, 1]),
                (send_y.at[0, 0], rows_halo.at[slot, 0, 0]),
                (send_y.at[1, 0], rows_halo.at[slot, 1, 0]),
            ]
        )
        beside_it()
        wait()
        for side, x in ((0, 0), (1, count + 1)):
            for c in range(3):
                value = wide(recv_x[slot, side, c : c + 1, :])
                if level == 2:
                    value = jnp.where(row_at < 4, value, wide(recv_x[slot, side, 4 + c : 5 + c, :]))
                f[at, x, c] = value
        return slot

    def residual(level, at, slot, x):
        f, w, r, span = fields[level], weights[level], reaction[level], 1 << level
        u = [f[at, x + 1, c] for c in range(3)]
        b = source(level, x)
        left = []
        for c in range(3):
            if level < 2:
                row_high, row_low = (rows_halo[slot, side, c, pl.ds(x, 1), :] for side in (1, 0))
            else:
                row_high, row_low = (rows_halo[slot, side, 0, pl.ds(4 * x + c, 1), :] for side in (1, 0))
            near = (
                f[at, x + 2, c],
                f[at, x, c],
                jnp.where(row_at >= ROWS - span, wide(row_high), down(u[c], -span)),
                jnp.where(row_at < span, wide(row_low), down(u[c], span)),
                along(u[c], -span),
                along(u[c], span),
            )
            value = b[c] - diag[level][x, c] * u[c]
            for k in range(6):
                value = value + w[x, 3 * k + c] * near[k]
            for d in range(3):
                if d != c:
                    value = value - r[x, 3 * d + c] * u[d]
            left.append(value)
        return u, left

    def sweep(level, at, slot, last=False):
        def body(x):
            u, left = residual(level, at, slot, x)
            step = solve(level, x, left)
            for c in range(3):
                if last:
                    out[c, x] = u[c] + step[c]
                else:
                    fields[level][1 - at, x + 1, c] = u[c] + step[c]

        each(NX[level], body)
        return 1 - at

    def restrict(level, at, slot):
        rows, lanes_ = pair_tools(level)[4:]

        def body(x):
            left = [residual(level, at, slot, 2 * x + i)[1] for i in range(2)]
            total = [lanes_(rows(left[0][c] + left[1][c])) for c in range(3)]
            if level == LEVELS - 2:
                coarsest(total)
                return
            first = solve(level + 1, x, total)
            for c in range(3):
                sources[level + 1][x, c] = total[c]
                fields[level + 1][0, x + 1, c] = first[c]

        each(NX[level + 1], body)

    def cycle(level, at, besides, last=False):
        f = fields[level]
        slot = share(level, at, besides[level])
        restrict(level, at, slot)
        if level == LEVELS - 2:
            for c in range(3):
                own = e_at(c, 0, 0)
                f[at, 0, c] += e_at(c, -1, 0)
                f[at, 1, c] += own
                f[at, 2, c] += own
                f[at, 3, c] += e_at(c, 1, 0)
            for side in range(2):
                step = [e_at(c, 0, 2 * side - 1) for c in range(3)]
                by_four = row_at & 3
                rows_halo[slot, side, 0] += jnp.where(by_four == 0, step[0], jnp.where(by_four == 1, step[1], step[2]))
            return sweep(level, at, slot)
        e = cycle(level + 1, 0, besides)

        def add(x):
            for c in range(3):
                for i in range(2):
                    f[at, 2 * x + 1 + i, c] += fields[level + 1][e, x + 1, c]

        each(NX[level + 1], add)
        return sweep(level, at, share(level, at), last)

    def start(x):
        for c, value in enumerate(solve(0, x, source(0, x))):
            fields[0][0, x + 1, c] = value

    finish_level(0)
    loads["grad"].wait()
    each(NX[0], start)
    pending = []

    def make_levels():
        coarsen(0)
        mask_level(0)
        finish_level(1)
        coarsen(1)
        mask_level(1)
        finish_level(2)
        coarsen(2)
        mask_level(2)
        pending.append(send_coefficients())

    def take():
        pending[0]()
        take_coefficients()

    nothing = lambda: None
    at = cycle(0, 0, (make_levels, take, nothing))
    at = sweep(0, at, share(0, at))
    cycle(0, at, (nothing,) * 3, last=True)


def local(counts, gradient, potential, coupling, region, contact, rates):
    nz = potential.shape[-1]
    tile = (ROWS, nz)
    f32 = jnp.float32
    scratch = []
    for parts in (18, 9, 3, 9):
        scratch += [pltpu.VMEM((n, parts) + tile, f32) for n in NX]
    scratch += [pltpu.VMEM((n, 3) + tile, f32) for n in NX[1:]]
    scratch += [pltpu.VMEM((2, n + 2, 3) + tile, f32) for n in NX]
    wide_window = len(WINDOW)
    scratch += [
        pltpu.VMEM((2, 2, 3) + tile, f32),
        pltpu.VMEM((2,) + tile, f32),
        pltpu.VMEM((2, 3) + tile, f32),
        pltpu.VMEM((2,) + tile, f32),
        pltpu.VMEM((2, 2) + tile, f32),
        pltpu.SemaphoreType.DMA((4,)),
        pltpu.SemaphoreType.DMA((2, 4)),
        pltpu.VMEM((1, 18) + tile, f32),
        pltpu.VMEM((1, 9) + tile, f32),
        pltpu.VMEM((4, nz), f32),
        pltpu.VMEM((wide_window, 4, nz), f32),
        pltpu.VMEM((2, 1, nz), f32),
        pltpu.VMEM((2, wide_window, 1, nz), f32),
        pltpu.VMEM((3, 3) + tile, f32),
        pltpu.SemaphoreType.DMA((wide_window,)),
        pltpu.SemaphoreType.DMA((wide_window,)),
        pltpu.SemaphoreType.DMA((wide_window,)),
        pltpu.SemaphoreType.DMA((2, wide_window)),
        pltpu.VMEM(gradient.shape, f32),
        pltpu.VMEM((10,) + tile, f32),
        pltpu.VMEM(coupling.shape, f32),
        pltpu.VMEM(region.shape, jnp.int32),
        pltpu.VMEM(contact.shape, jnp.int32),
        pltpu.SMEM(rates.shape, f32),
        pltpu.SemaphoreType.DMA((6,)),
    ]
    vmem = pl.BlockSpec(memory_space=pltpu.VMEM)
    return pl.pallas_call(
        functools.partial(kernel, counts),
        out_shape=jax.ShapeDtypeStruct(gradient.shape, f32),
        in_specs=[pl.BlockSpec(memory_space=pltpu.HBM)] * 6,
        out_specs=vmem,
        scratch_shapes=scratch,
        compiler_params=pltpu.CompilerParams(
            collective_id=0, has_side_effects=True, vmem_limit_bytes=60 * 1024 * 1024
        ),
    )(gradient, potential, coupling, region, contact, rates)


def solution(mesh):
    placed = (
        P(None, "gx", "gy", None),
        P("gx", "gy", None),
        P(None, None, "gx", "gy", None),
        P("gx", "gy", None),
        P("gx", "gy", None),
        P(),
    )
    counts = (mesh.shape["gx"], mesh.shape["gy"])
    return jax.shard_map(
        functools.partial(local, counts),
        mesh=mesh,
        in_specs=placed,
        out_specs=P(None, "gx", "gy", None),
        check_vma=False,
    )
```

```python
import functools

import jax
import jax.numpy as jnp
from jax import lax
from jax.experimental import pallas as pl
from jax.experimental.pallas import tpu as pltpu
from jax.sharding import PartitionSpec as P

MESH = pl.DeviceIdType.MESH
LEVELS = 4
COARSE_SWEEPS = 6
REGIONS = 4
OMEGA = 0.8
STRENGTH = 8.0
ROWS = 8
NX = (8, 4, 2, 1)
RADIUS = 3
SLOTS = 8


def around(shape, far):
    reach = range(-6, 7)
    distance = lambda i, j: min(abs(i - a) + abs(j - b) for a, b in shape)
    found = [(i, j) for i in reach for j in reach if distance(i, j) <= far and (i, j) != (0, 0)]
    return sorted(found, key=lambda o: -abs(o[0]) - abs(o[1]))


OWN = [(0, 0)]
SQUARE = [(i, j) for i in (-1, 0, 1) for j in (-1, 0, 1)]
INNER = around(OWN, 2)
OUTER = [o for o in around(OWN, 3) if o not in INNER]
FOURTH = around(SQUARE, 2)
THIRD = around(SQUARE, 3)


def each(count, body):
    if count == 1:
        body(0)
        return

    def step(i, carry):
        body(i)
        return carry

    lax.fori_loop(0, count, step, 0, unroll=count)


def face_weights(difference):
    size = jnp.abs(difference)
    small = size < 0.5
    series = 1.0 / 362880.0
    for k in (40320.0, 5040.0, 720.0, 120.0, 24.0, 6.0, 2.0, 1.0):
        series = series * size + 1.0 / k
    below = jnp.where(small, series, jnp.exp(size) - 1.0)
    low = jnp.where(small, 1.0, size) / below
    low = jnp.where(size < 1e-4, 1.0 - 0.5 * size, low)
    high = low + size
    positive = difference > 0.0
    return jnp.where(positive, low, high), jnp.where(positive, high, low)


def kernel(counts, grad_in, pot_in, coup_in, region_in, contact_in, rates_in, out, *scratch):
    grad, pot, coup, region, contact, rates, in_sem = scratch[-7:]
    scratch = scratch[:-7]
    loads = {}
    for i, (name, source, target) in enumerate(
        (
            ("pot", pot_in, pot.at[pl.ds(1, 8)]),
            ("rates", rates_in, rates),
            ("region", region_in, region),
            ("contact", contact_in, contact),
            ("coup", coup_in, coup),
            ("grad", grad_in, grad),
        )
    ):
        loads[name] = pltpu.make_async_copy(source, target, in_sem.at[i])
        loads[name].start()
    weights, reaction, diag, inverse = (scratch[4 * i : 4 * i + 4] for i in range(4))
    sources = (None,) + tuple(scratch[16:19])
    fields = scratch[19:23]
    rows_halo, pot_y, send_y, send_sem, recv_sem = scratch[23:28]
    w_own, r_own, w_wide, r_wide, diag_wide, inverse_wide, u_wide, b_wide, e_rows = scratch[28:37]
    mid_send, mid_recv, low_send, low_recv, mid_cell, mid_cells, low_cell, low_cells = scratch[37:45]
    mid_send_sem, mid_recv_sem, low_send_sem, low_recv_sem, p_send, p_recv, q_send, q_recv = scratch[45:53]
    ring_u, ring_b, ring_w, ring_r, ring_diag, ring_inverse, ring_out = scratch[53:60]
    pair_own, pair_x, pair_y_send, pair_y, pair_corner_send, pair_corner, pair_send_sem, pair_recv_sem = scratch[60:68]
    coef_own, coef_x, coef_y_send, coef_y, coef_send_sem, coef_recv_sem = scratch[68:]
    n_x, n_y = counts
    lanes = out.shape[-1]
    gx, gy = lax.axis_index("gx"), lax.axis_index("gy")
    x_low, x_high = lax.rem(gx + n_x - 1, n_x), lax.rem(gx + 1, n_x)
    y_low, y_high = lax.rem(gy + n_y - 1, n_y), lax.rem(gy + 1, n_y)
    beside = ((x_high, gy), (x_low, gy), (gx, y_high), (gx, y_low))

    barrier = pltpu.get_barrier_semaphore()
    at_offset = lambda i, j: (lax.rem(gx + n_x + i, n_x), lax.rem(gy + n_y + j, n_y))
    devices = {o: at_offset(*o) for o in THIRD}
    for device in devices.values():
        pl.semaphore_signal(barrier, inc=1, device_id=device, device_id_type=MESH)
    pl.semaphore_wait(barrier, len(THIRD))

    tile = (ROWS, lanes)
    row_at = lax.broadcasted_iota(jnp.int32, tile, 0)
    lane_at = lax.broadcasted_iota(jnp.int32, tile, 1)
    wide = lambda row: jnp.broadcast_to(row, tile)
    down = lambda v, by: pltpu.roll(v, by % ROWS, 0) if by % ROWS else v
    along = lambda v, by: pltpu.roll(v, by % lanes, 1)

    done = [0]

    def exchange(parts):
        slot = done[0] % 3
        done[0] += 1
        copies = []
        for i in (2, 3, 0, 1):
            source, target = parts[i]
            copy = pltpu.make_async_remote_copy(
                src_ref=source,
                dst_ref=target,
                send_sem=send_sem.at[i],
                recv_sem=recv_sem.at[slot, i],
                device_id=beside[i],
                device_id_type=MESH,
            )
            copy.start()
            copies.append(copy)

        def wait():
            for copy in copies:
                copy.wait()

        return wait

    def remote(source, target, send, recv, offset):
        copy = pltpu.make_async_remote_copy(
            src_ref=source,
            dst_ref=target,
            send_sem=send,
            recv_sem=recv,
            device_id=devices[offset],
            device_id_type=MESH,
        )
        copy.start()
        return copy

    def gather(offsets, source_of, target, send, recv):
        copies = []
        for n, (i, j) in enumerate(offsets):
            copy = pltpu.make_async_remote_copy(
                src_ref=source_of((i, j)),
                dst_ref=target.at[n],
                send_sem=send.at[n],
                recv_sem=recv.at[n],
                device_id=devices[(-i, -j)],
                device_id_type=MESH,
            )
            copy.start()
            copies.append(copy)

        def wait():
            for copy in copies:
                copy.wait()

        return wait

    loads["pot"].wait()
    for side, at in ((0, ROWS - 1), (1, 0)):
        packed = wide(pot[1, at : at + 1, :])
        for x in range(1, 8):
            packed = jnp.where(row_at == x, wide(pot[x + 1, at : at + 1, :]), packed)
        send_y[side, 0] = packed
    wait = exchange(
        [
            (pot.at[8], pot.at[0]),
            (pot.at[1], pot.at[9]),
            (send_y.at[0, 0], pot_y.at[0]),
            (send_y.at[1, 0], pot_y.at[1]),
        ]
    )
    for name in ("rates", "region", "contact", "coup"):
        loads[name].wait()

    def put_faces(x, first, near):
        here = pot[x + 1]
        for k, value in enumerate(near):
            plus, minus = face_weights(here - value)
            weights[0][x, 3 * (first + k)] = jnp.ones(tile, jnp.float32)
            weights[0][x, 3 * (first + k) + 1] = plus
            weights[0][x, 3 * (first + k) + 2] = minus

    def set_up(x):
        here = pot[x + 1]
        near = (
            jnp.where(lane_at == lanes - 1, 0.0, along(here, -1)),
            jnp.where(lane_at == 0, 0.0, along(here, 1)),
        )
        put_faces(x, 4, near)
        at_contact = STRENGTH * contact[x].astype(jnp.float32)
        regions = region[x]
        for c in range(3):
            extra = jnp.full(tile, rates[0, c])
            for pick in range(1, REGIONS):
                extra = jnp.where(regions == pick, rates[pick, c], extra)
            for d in range(3):
                value = coup[c, d, x]
                reaction[0][x, 3 * c + d] = value + (extra + at_contact) if c == d else value

    each(NX[0], set_up)
    wait()
    is_low_x, is_high_x = gx == 0, gx == n_x - 1
    is_low_y, is_high_y = gy == 0, gy == n_y - 1
    pot[0] = jnp.where(is_low_x, 0.0, pot[0])
    pot[9] = jnp.where(is_high_x, 0.0, pot[9])
    pot_y[0] = jnp.where(is_low_y, 0.0, pot_y[0])
    pot_y[1] = jnp.where(is_high_y, 0.0, pot_y[1])

    def cross_faces(x):
        here = pot[x + 1]
        near = (
            pot[x + 2],
            pot[x],
            jnp.where(row_at == ROWS - 1, wide(pot_y[1, pl.ds(x, 1), :]), down(here, -1)),
            jnp.where(row_at == 0, wide(pot_y[0, pl.ds(x, 1), :]), down(here, 1)),
        )
        put_faces(x, 0, near)

    each(NX[0], cross_faces)

    def finish(w, r, diagonal, inv, count):
        def body(x):
            m = [[r[x, 3 * col + row] for col in range(3)] for row in range(3)]
            for c in range(3):
                total = w[x, c]
                for k in range(1, 6):
                    total = total + w[x, 3 * k + c]
                m[c][c] = m[c][c] + total
                diagonal[x, c] = m[c][c]

            def cofactor(i, j):
                i1, i2, j1, j2 = (i + 1) % 3, (i + 2) % 3, (j + 1) % 3, (j + 2) % 3
                return m[i1][j1] * m[i2][j2] - m[i1][j2] * m[i2][j1]

            cof = [[cofactor(i, j) for j in range(3)] for i in range(3)]
            det = m[0][0] * cof[0][0] + m[0][1] * cof[0][1] + m[0][2] * cof[0][2]
            scale = OMEGA / det
            for i in range(3):
                for j in range(3):
                    inv[x, 3 * i + j] = cof[j][i] * scale

        each(count, body)

    def finish_level(level):
        finish(weights[level], reaction[level], diag[level], inverse[level], NX[level])

    def mask_level(level):
        w, span, last = weights[level], 1 << level, NX[level] - 1
        for c in range(3):
            w[last, c] = jnp.where(is_high_x, 0.0, w[last, c])
            w[0, 3 + c] = jnp.where(is_low_x, 0.0, w[0, 3 + c])
        off_high = jnp.logical_and(row_at >= ROWS - span, is_high_y)
        off_low = jnp.logical_and(row_at < span, is_low_y)
        off_up, off_down = lane_at >= lanes - span, lane_at < span

        def body(x):
            for k, off in ((2, off_high), (3, off_low), (4, off_up), (5, off_down)):
                for c in range(3):
                    w[x, 3 * k + c] = jnp.where(off, 0.0, w[x, 3 * k + c])

        each(NX[level], body)

    def pair_tools(level):
        span = 1 << level
        odd_row = (row_at & span) != 0
        odd_lane = (lane_at & span) != 0

        def high_row(v):
            return jnp.where(odd_row, v, down(v, -span))

        def low_row(v):
            return jnp.where(odd_row, down(v, span), v)

        def high_lane(v):
            return jnp.where(odd_lane, v, along(v, -span))

        def low_lane(v):
            return jnp.where(odd_lane, along(v, span), v)

        def rows(v):
            return v + jnp.where(odd_row, down(v, span), down(v, -span))

        def lanes_(v):
            return v + jnp.where(odd_lane, along(v, span), along(v, -span))

        return high_row, low_row, high_lane, low_lane, rows, lanes_

    def coarsen(level):
        high_row, low_row, high_lane, low_lane, rows, lanes_ = pair_tools(level)
        w, r = weights[level], reaction[level]
        w_next, r_next = (w_own, r_own) if level == LEVELS - 2 else (weights[level + 1], reaction[level + 1])

        def body(x):
            for c in range(3):
                w_next[x, c] = lanes_(rows(w[2 * x + 1, c]))
                w_next[x, 3 + c] = lanes_(rows(w[2 * x, 3 + c]))
                pair = lambda k: w[2 * x, 3 * k + c] + w[2 * x + 1, 3 * k + c]
                w_next[x, 6 + c] = lanes_(high_row(pair(2)))
                w_next[x, 9 + c] = lanes_(low_row(pair(3)))
                w_next[x, 12 + c] = high_lane(rows(pair(4)))
                w_next[x, 15 + c] = low_lane(rows(pair(5)))
            for i in range(9):
                r_next[x, i] = lanes_(rows(r[2 * x, i] + r[2 * x + 1, i]))

        each(NX[level + 1], body)

    slot_at = lane_at & (SLOTS - 1)
    x_at, y_at = row_at + (gx - RADIUS), slot_at + (gy - RADIUS)
    x_last = jnp.logical_or(x_at == n_x - 1, x_at == -1)
    x_first = jnp.logical_or(x_at == 0, x_at == n_x)
    y_last = jnp.logical_or(y_at == n_y - 1, y_at == -1)
    y_first = jnp.logical_or(y_at == 0, y_at == n_y)
    z_last, z_first = lane_at >= lanes - SLOTS, lane_at < SLOTS
    offs = (x_last, x_first, y_last, y_first, z_last, z_first)
    bits = (2, 2, 1, 1, 4, 4)

    def transposed(tiles):
        tiles = list(tiles)
        for bit in (1, 2, 4):
            clear = (slot_at & bit) == 0
            for p in range(SLOTS):
                if not p & bit:
                    one, two = tiles[p], tiles[p | bit]
                    tiles[p] = jnp.where(clear, one, along(two, bit))
                    tiles[p | bit] = jnp.where(clear, along(one, -bit), two)
        return tiles

    def unpacked(offsets, row_of, own, fill=0.0):
        tiles = [jnp.full(tile, fill) for _ in range(SLOTS)]
        for n, (i, j) in enumerate(list(offsets) + OWN):
            if min(i, j) >= -RADIUS:
                row = row_of(n) if n < len(offsets) else own
                tiles[j + RADIUS] = jnp.where(row_at == i + RADIUS, wide(row), tiles[j + RADIUS])
        return transposed(tiles)

    def child_row(f, x0, c):
        which = slot_at & 3
        rows = [wide(f[x0 + p // 2, c, 4 * (p % 2) : 4 * (p % 2) + 1, :]) for p in range(4)]
        packed = jnp.where(which == 0, rows[0], jnp.where(which == 1, rows[1], jnp.where(which == 2, rows[2], rows[3])))
        return packed[0:1, :]

    def slot_row(values):
        packed = values[0]
        for i in range(1, len(values)):
            packed = jnp.where(slot_at == i, values[i], packed)
        return packed

    def send_coefficients():
        for i in range(27):
            mid_send[i] = child_row(weights[2] if i < 18 else reaction[2], 0, i if i < 18 else i - 18)
        fields_ = [w_own[0, i] for i in range(18)] + [r_own[0, i] for i in range(9)]
        for row in range(4):
            low_send[row : row + 1, :] = slot_row(fields_[SLOTS * row : SLOTS * row + SLOTS])[0:1, :]
        first = gather(INNER, lambda o: mid_send, mid_recv, mid_send_sem, mid_recv_sem)
        second = gather(FOURTH, lambda o: low_send, low_recv, low_send_sem, low_recv_sem)
        return first, second

    def take_coefficients(waits):
        for wait in waits:
            wait()
        for i in range(27):
            made = unpacked(INNER, lambda n: mid_recv[n, i], mid_send[i], 1.0 if i in (18, 22, 26) else 0.0)
            for p in range(SLOTS):
                if i < 18:
                    w_wide[p, i] = made[p]
                else:
                    r_wide[p, i - 18] = made[p]
        finish(w_wide, r_wide, diag_wide, inverse_wide, SLOTS)
        for k in range(6):
            for p in range(SLOTS):
                if ((p & bits[k]) != 0) == (k % 2 == 0):
                    for c in range(3):
                        w_wide[p, 3 * k + c] = jnp.where(offs[k], 0.0, w_wide[p, 3 * k + c])
        top = LEVELS - 1
        w, r = weights[top], reaction[top]
        for row in range(4):
            here = slice(row, row + 1)
            made = unpacked(FOURTH, lambda n: low_recv[n, here, :], low_send[here, :])
            for p in range(SLOTS):
                i = SLOTS * row + p
                if i < 18:
                    w[0, i] = made[p]
                elif i < 27:
                    r[0, i - 18] = made[p]
        finish_level(top)
        for k in range(6):
            for c in range(3):
                w[0, 3 * k + c] = jnp.where(offs[k], 0.0, w[0, 3 * k + c])

    def spread(value, t):
        value = jnp.where(slot_at == t, value, 0.0)
        for bit in (1, 2, 4):
            value = value + along(value, -bit if t & bit else bit)
        return value

    def wide_residual(p, u):
        left = []
        for c in range(3):
            value = b_wide[p, c] - diag_wide[p, c] * u[p][c]
            for k in range(6):
                bit, ahead = bits[k], k % 2 == 0
                near = u[p ^ bit][c]
                if ((p & bit) != 0) == ahead:
                    turn = -1 if ahead else 1
                    near = down(near, turn) if k < 2 else along(near, turn if k < 4 else turn * SLOTS)
                value = value + w_wide[p, 3 * k + c] * near
            for d in range(3):
                if d != c:
                    value = value - r_wide[p, 3 * d + c] * u[p][d]
            left.append(value)
        return left

    def apply_inverse(v, x, r):
        return [v[x, 3 * c] * r[0] + v[x, 3 * c + 1] * r[1] + v[x, 3 * c + 2] * r[2] for c in range(3)]

    def wide_fields():
        return [[u_wide[p, c] for c in range(3)] for p in range(SLOTS)]

    def window_sweep(b, u, patches=None):
        top = LEVELS - 1
        w, r = weights[top], reaction[top]
        left = []
        for c in range(3):
            value = b[c] - diag[top][0, c] * u[c]
            before_x, before_y = down(u[c], 1), along(u[c], 1)
            if patches is not None:
                before_x = jnp.where(row_at == 0, patches[0][c], before_x)
                before_y = jnp.where(slot_at == 0, patches[1][c], before_y)
            near = (down(u[c], -1), before_x, along(u[c], -1), before_y, along(u[c], -SLOTS), along(u[c], SLOTS))
            for k in range(6):
                value = value + w[0, 3 * k + c] * near[k]
            for d in range(3):
                if d != c:
                    value = value - r[0, 3 * d + c] * u[d]
            left.append(value)
        step = apply_inverse(inverse[top], 0, left)
        return [u[c] + step[c] for c in range(3)]

    def lower(turn, beside_p, beside_q):
        for c in range(3):
            mid_cell[0, c] = child_row(sources[2], 0, c)
            mid_cell[1, c] = child_row(fields[2].at[0], 1, c)
        near = INNER + OUTER
        wait = gather(
            near, lambda o: mid_cell.at[0 if o in INNER else 1], mid_cells.at[turn], p_send, p_recv.at[turn]
        )
        beside_p()
        wait()
        for c in range(3):
            made = unpacked(near, lambda n: mid_cells[turn, n, c], mid_cell[0, c])
            for p in range(SLOTS):
                b_wide[p, c] = made[p]
        inner = jnp.abs(row_at - RADIUS) + jnp.abs(slot_at - RADIUS) <= 2
        for p in range(SLOTS):
            b = [b_wide[p, c] for c in range(3)]
            first = apply_inverse(inverse_wide, p, b)
            for c in range(3):
                u_wide[p, c] = jnp.where(inner, first[c], b[c])
        u_mid = wide_fields()
        b = [jnp.zeros(tile, jnp.float32) for _ in range(3)]
        for p in range(SLOTS):
            left = wide_residual(p, u_mid)
            b = [b[c] + left[c] for c in range(3)]
        u = apply_inverse(inverse[LEVELS - 1], 0, b)
        for _ in range(2):
            u = window_sweep(b, u)
        row = slot_row([spread(value, RADIUS) for value in u + b])
        low_cell[0] = row[RADIUS : RADIUS + 1, :]
        wait = gather(THIRD, lambda o: low_cell.at[0], low_cells.at[turn], q_send, q_recv.at[turn])
        beside_q()
        wait()
        made = unpacked(THIRD, lambda n: low_cells[turn, n], low_cell[0])
        u, b = made[:3], made[3:6]
        before_x = [jnp.zeros(tile, jnp.float32) for _ in range(3)]
        last_y = jnp.zeros(tile, jnp.float32)
        for n, (i, j) in enumerate(THIRD):
            if i < -RADIUS:
                for c in range(3):
                    value = along(wide(low_cells[turn, n]), j + RADIUS - c)
                    before_x[c] = jnp.where(slot_at == j + RADIUS, value, before_x[c])
            if j < -RADIUS:
                last_y = jnp.where(row_at == i + RADIUS, wide(low_cells[turn, n]), last_y)
        before_y = [along(last_y, -c) for c in range(3)]
        u = window_sweep(b, u, (before_x, before_y))
        for _ in range(COARSE_SWEEPS - 4):
            u = window_sweep(b, u)
        u_mid = [[u_wide[p, c] + u[c] for c in range(3)] for p in range(SLOTS)]
        last = []
        for p in range(SLOTS):
            step = apply_inverse(inverse_wide, p, wide_residual(p, u_mid))
            last.append([u_mid[p][c] + step[c] for c in range(3)])
        for c in range(3):
            for x in range(2):
                for at, (t, y) in enumerate(((RADIUS - 1, 1), (RADIUS, 0), (RADIUS, 1), (RADIUS + 1, 0))):
                    low, high = last[2 * x + y][c], last[4 + 2 * x + y][c]
                    if t & 4:
                        value = jnp.where(slot_at == t, high, 0.0) + along(jnp.where(slot_at == t, low, 0.0), -4)
                    else:
                        value = jnp.where(slot_at == t, low, 0.0) + along(jnp.where(slot_at == t, high, 0.0), 4)
                    for bit in (1, 2):
                        value = value + along(value, -bit if t & bit else bit)
                    e_rows[x, at, c] = value

    def mid_at(c, x, y):
        row = RADIUS + (x // 2)
        return wide(e_rows[x % 2, y + 1, c, row : row + 1, :])

    odd = (lane_at & 1) != 0

    def even_part(v):
        return jnp.where(odd, along(v, 1), v)

    def odd_part(v):
        return jnp.where(odd, v, along(v, -1))

    def rows_tile(rows):
        made = jnp.zeros(tile, jnp.float32)
        for at, value in rows:
            made = jnp.where(row_at == at, wide(value), made)
        return made

    def pair_up():
        for x in range(4):
            for j in range(14):
                part = [weights[1][x, i] if i < 18 else reaction[1][x, i - 18] for i in (2 * j, 2 * j + 1) if i < 27]
                coef_own[x, j] = jnp.where(odd, part[-1], part[0])
        for side, y in ((0, 6), (1, 0)):
            for j in range(0, 14, 2):
                rows = [(4 * i + x, coef_own[x, j + i, y : y + 1, :]) for i in range(2) for x in range(4)]
                coef_y_send[side, j // 2] = rows_tile(rows)

    def send_ring_coefficients():
        copies = []
        for side, turn in ((0, 1), (1, -1)):
            sems = lambda n: (coef_send_sem.at[n], coef_recv_sem.at[n])
            copies.append(remote(coef_y_send.at[side], coef_y.at[side], *sems(side), (0, turn)))
            copies.append(remote(coef_own.at[3 - 3 * side], coef_x.at[side], *sems(2 + side), (turn, 0)))
        return copies

    def take_ring_coefficients(copies):
        for copy in copies:
            copy.wait()
        for p in range(6):
            edge = 2 if p in (0, 5) else 1
            filled = jnp.logical_and(row_at >= edge, row_at < ROWS - edge)
            for j in range(14):
                if p in (0, 5):
                    rows = [(2 + k, coef_x[p // 5, j, 2 * k : 2 * k + 1, :]) for k in range(4)]
                else:
                    x = p - 1
                    rows = [(2 + k, coef_own[x, j, 2 * k : 2 * k + 1, :]) for k in range(4)]
                    at = 4 * (j % 2) + x
                    rows += [(1, coef_y[0, j // 2, at : at + 1, :]), (6, coef_y[1, j // 2, at : at + 1, :])]
                both = rows_tile(rows)
                for i, value in ((2 * j, even_part(both)), (2 * j + 1, odd_part(both))):
                    if i < 18:
                        ring_w[p, i] = value
                    elif i < 27:
                        ring_r[p, i - 18] = jnp.where(filled, value, 1.0) if i in (18, 22, 26) else value
        finish(ring_w, ring_r, ring_diag, ring_inverse, 6)
        off_high = jnp.logical_and(row_at == 5, is_high_y)
        off_low = jnp.logical_and(row_at == 2, is_low_y)
        for c in range(3):
            ring_w[4, c] = jnp.where(is_high_x, 0.0, ring_w[4, c])
            ring_w[1, 3 + c] = jnp.where(is_low_x, 0.0, ring_w[1, 3 + c])

        def body(p):
            for k, off in ((2, off_high), (3, off_low), (4, lane_at >= lanes - 2), (5, lane_at < 2)):
                for c in range(3):
                    ring_w[p, 3 * k + c] = jnp.where(off, 0.0, ring_w[p, 3 * k + c])

        each(6, body)

    def send_pairs(turn):
        for x in range(4):
            for c in range(3):
                pair_own[x, c] = jnp.where(odd, sources[1][x, c], fields[1][0, x + 1, c])
        for side, y in ((0, 4), (1, 0)):
            for c in range(3):
                rows = [(2 * x + k, pair_own[x, c, y + 2 * k : y + 2 * k + 1, :]) for x in range(4) for k in range(2)]
                pair_y_send[side, c] = rows_tile(rows)
        for sx in range(2):
            for sy in range(2):
                x, y = 3 - 3 * sx, 6 - 6 * sy
                for c in range(3):
                    pair_corner_send[2 * sx + sy, c : c + 1, :] = pair_own[x, c, y : y + 1, :]
        copies = []
        sems = lambda n: (pair_send_sem.at[n], pair_recv_sem.at[turn, n])
        for side, to in ((0, 1), (1, -1)):
            copies.append(remote(pair_y_send.at[side], pair_y.at[turn, side], *sems(side), (0, to)))
            source = pair_own.at[pl.ds(2 - 2 * side, 2)]
            copies.append(remote(source, pair_x.at[turn, side], *sems(2 + side), (to, 0)))
        for sx in range(2):
            for sy in range(2):
                n = 2 * sx + sy
                to = (1 - 2 * sx, 1 - 2 * sy)
                copies.append(remote(pair_corner_send.at[n], pair_corner.at[turn, n], *sems(4 + n), to))
        return copies

    def take_pairs(turn, copies):
        for copy in copies:
            copy.wait()
        for p in range(8):
            for c in range(3):
                if 2 <= p < 6:
                    x = p - 2
                    rows = [(2 + k, pair_own[x, c, 2 * k : 2 * k + 1, :]) for k in range(4)]
                    for side in range(2):
                        for k in range(2):
                            at = 2 * x + k
                            rows.append((6 * side + k, pair_y[turn, side, c, at : at + 1, :]))
                else:
                    side = p // 4
                    rows = [(2 + k, pair_x[turn, side, p - 6 * side, c, 2 * k : 2 * k + 1, :]) for k in range(4)]
                    if p in (1, 6):
                        for sy in range(2):
                            rows.append((1 + 5 * sy, pair_corner[turn, 2 * side + sy, c : c + 1, :]))
                both = rows_tile(rows)
                ring_u[p, c] = even_part(both)
                if 1 <= p < 7:
                    ring_b[p - 1, c] = odd_part(both)

    def ring_sweep():
        def add(p):
            x = p // 2 - 1
            for c in range(3):
                e = jnp.where(row_at < 2, mid_at(c, x, -1), mid_at(c, x, 0))
                e = jnp.where(row_at < 4, e, jnp.where(row_at < 6, mid_at(c, x, 1), mid_at(c, x, 2)))
                ring_u[p, c] += e

        for p in range(8):
            add(p)
        for p in range(6):
            u = [ring_u[p + 1, c] for c in range(3)]
            left = []
            for c in range(3):
                value = ring_b[p, c] - ring_diag[p, c] * u[c]
                near = (ring_u[p + 2, c], ring_u[p, c], down(u[c], -1), down(u[c], 1), along(u[c], -2), along(u[c], 2))
                for k in range(6):
                    value = value + ring_w[p, 3 * k + c] * near[k]
                for d in range(3):
                    if d != c:
                        value = value - ring_r[p, 3 * d + c] * u[d]
                left.append(value)
            step = apply_inverse(ring_inverse, p, left)
            for c in range(3):
                ring_out[p, c] = u[c] + step[c]

    def add_to_finest(at, slot):
        f = fields[0]
        for c in range(3):
            for p in range(6):
                rows = [wide(ring_out[p, c, 2 + k : 3 + k, :]) for k in range(4)]
                e = jnp.where(row_at < 2, rows[0], rows[1])
                e = jnp.where(row_at < 4, e, jnp.where(row_at < 6, rows[2], rows[3]))
                for x in {0: (-1,), 5: (8,)}.get(p, (2 * p - 2, 2 * p - 1)):
                    f[at, x + 1, c] += e
            for side, row in ((0, 1), (1, 6)):
                rows = [wide(ring_out[1 + k, c, row : row + 1, :]) for k in range(4)]
                e = jnp.where(row_at < 2, rows[0], rows[1])
                e = jnp.where(row_at < 4, e, jnp.where(row_at < 6, rows[2], rows[3]))
                rows_halo[slot, side, c] += e

    def source(level, x):
        if level == 0:
            return [grad[c, x] for c in range(3)]
        return [sources[level][x, c] for c in range(3)]

    def solve(level, x, r):
        v = inverse[level]
        return [v[x, 3 * c] * r[0] + v[x, 3 * c + 1] * r[1] + v[x, 3 * c + 2] * r[2] for c in range(3)]

    def share(level, at, beside_it=lambda: None):
        slot, f, count = done[0] % 3, fields[level], NX[level]
        for side, row in ((0, ROWS - 1), (1, 0)):
            for c in range(3):
                packed = wide(f[at, 1, c, row : row + 1, :])
                for x in range(1, count):
                    packed = jnp.where(row_at == x, wide(f[at, x + 1, c, row : row + 1, :]), packed)
                send_y[side, c] = packed
        wait = exchange(
            [
                (f.at[at, count], f.at[at, 0]),
                (f.at[at, 1], f.at[at, count + 1]),
                (send_y.at[0], rows_halo.at[slot, 0]),
                (send_y.at[1], rows_halo.at[slot, 1]),
            ]
        )
        beside_it()
        wait()
        return slot

    def residual(level, at, slot, x):
        f, w, r, span = fields[level], weights[level], reaction[level], 1 << level
        u = [f[at, x + 1, c] for c in range(3)]
        b = source(level, x)
        left = []
        for c in range(3):
            row_high, row_low = (rows_halo[slot, side, c, pl.ds(x, 1), :] for side in (1, 0))
            near = (
                f[at, x + 2, c],
                f[at, x, c],
                jnp.where(row_at >= ROWS - span, wide(row_high), down(u[c], -span)),
                jnp.where(row_at < span, wide(row_low), down(u[c], span)),
                along(u[c], -span),
                along(u[c], span),
            )
            value = b[c] - diag[level][x, c] * u[c]
            for k in range(6):
                value = value + w[x, 3 * k + c] * near[k]
            for d in range(3):
                if d != c:
                    value = value - r[x, 3 * d + c] * u[d]
            left.append(value)
        return u, left

    def sweep(level, at, slot, last=False):
        def body(x):
            u, left = residual(level, at, slot, x)
            step = solve(level, x, left)
            for c in range(3):
                if last:
                    out[c, x] = u[c] + step[c]
                else:
                    fields[level][1 - at, x + 1, c] = u[c] + step[c]

        each(NX[level], body)
        return 1 - at

    def restrict(level, at, slot):
        rows, lanes_ = pair_tools(level)[4:]

        def body(x):
            left = [residual(level, at, slot, 2 * x + i)[1] for i in range(2)]
            total = [lanes_(rows(left[0][c] + left[1][c])) for c in range(3)]
            first = solve(level + 1, x, total)
            for c in range(3):
                sources[level + 1][x, c] = total[c]
                fields[level + 1][0, x + 1, c] = first[c]

        each(NX[level + 1], body)

    def cycle(at, turn, besides, last=False):
        slot = share(0, at, besides[0])
        restrict(0, at, slot)
        pairs = []

        def beside():
            pairs.extend(send_pairs(turn))
            besides[1]()

        restrict(1, 0, share(1, 0, beside))
        lower(turn, besides[2], lambda: take_pairs(turn, pairs))
        ring_sweep()
        add_to_finest(at, slot)
        return sweep(0, at, slot, last)

    def start(x):
        for c, value in enumerate(solve(0, x, source(0, x))):
            fields[0][0, x + 1, c] = value

    finish_level(0)
    loads["grad"].wait()
    each(NX[0], start)
    pending, ring_pending = [], []

    def make_levels():
        coarsen(0)
        mask_level(0)
        finish_level(1)
        coarsen(1)
        finish_level(2)
        coarsen(2)
        pending.extend(send_coefficients())
        pair_up()
        mask_level(1)

    def take_wide():
        ring_pending.extend(send_ring_coefficients())
        take_coefficients(pending)

    nothing = lambda: None
    at = cycle(0, 0, (make_levels, take_wide, lambda: take_ring_coefficients(ring_pending)))
    at = sweep(0, at, share(0, at))
    cycle(at, 1, (nothing,) * 3, last=True)


def local(counts, gradient, potential, coupling, region, contact, rates):
    nz = potential.shape[-1]
    tile = (ROWS, nz)
    f32 = jnp.float32
    scratch = []
    for parts in (18, 9, 3, 9):
        scratch += [pltpu.VMEM((n, parts) + tile, f32) for n in NX]
    scratch += [pltpu.VMEM((n, 3) + tile, f32) for n in NX[1:]]
    scratch += [pltpu.VMEM((2, n + 2, 3) + tile, f32) for n in NX]
    scratch += [
        pltpu.VMEM((3, 2, 3) + tile, f32),
        pltpu.VMEM((2,) + tile, f32),
        pltpu.VMEM((2, 3) + tile, f32),
        pltpu.SemaphoreType.DMA((4,)),
        pltpu.SemaphoreType.DMA((3, 4)),
        pltpu.VMEM((1, 18) + tile, f32),
        pltpu.VMEM((1, 9) + tile, f32),
        pltpu.VMEM((SLOTS, 18) + tile, f32),
        pltpu.VMEM((SLOTS, 9) + tile, f32),
        pltpu.VMEM((SLOTS, 3) + tile, f32),
        pltpu.VMEM((SLOTS, 9) + tile, f32),
        pltpu.VMEM((SLOTS, 3) + tile, f32),
        pltpu.VMEM((SLOTS, 3) + tile, f32),
        pltpu.VMEM((2, 4, 3) + tile, f32),
        pltpu.VMEM((27, 1, nz), f32),
        pltpu.VMEM((len(INNER), 27, 1, nz), f32),
        pltpu.VMEM((4, nz), f32),
        pltpu.VMEM((len(FOURTH), 4, nz), f32),
        pltpu.VMEM((2, 3, 1, nz), f32),
        pltpu.VMEM((2, len(INNER + OUTER), 3, 1, nz), f32),
        pltpu.VMEM((1, 1, nz), f32),
        pltpu.VMEM((2, len(THIRD), 1, nz), f32),
        pltpu.SemaphoreType.DMA((len(INNER),)),
        pltpu.SemaphoreType.DMA((len(INNER),)),
        pltpu.SemaphoreType.DMA((len(FOURTH),)),
        pltpu.SemaphoreType.DMA((len(FOURTH),)),
        pltpu.SemaphoreType.DMA((len(INNER + OUTER),)),
        pltpu.SemaphoreType.DMA((2, len(INNER + OUTER))),
        pltpu.SemaphoreType.DMA((len(THIRD),)),
        pltpu.SemaphoreType.DMA((2, len(THIRD))),
        pltpu.VMEM((8, 3) + tile, f32),
        pltpu.VMEM((6, 3) + tile, f32),
        pltpu.VMEM((6, 18) + tile, f32),
        pltpu.VMEM((6, 9) + tile, f32),
        pltpu.VMEM((6, 3) + tile, f32),
        pltpu.VMEM((6, 9) + tile, f32),
        pltpu.VMEM((6, 3) + tile, f32),
        pltpu.VMEM((4, 3) + tile, f32),
        pltpu.VMEM((2, 2, 2, 3) + tile, f32),
        pltpu.VMEM((2, 3) + tile, f32),
        pltpu.VMEM((2, 2, 3) + tile, f32),
        pltpu.VMEM((4, 4, nz), f32),
        pltpu.VMEM((2, 4, 4, nz), f32),
        pltpu.SemaphoreType.DMA((8,)),
        pltpu.SemaphoreType.DMA((2, 8)),
        pltpu.VMEM((4, 14) + tile, f32),
        pltpu.VMEM((2, 14) + tile, f32),
        pltpu.VMEM((2, 7) + tile, f32),
        pltpu.VMEM((2, 7) + tile, f32),
        pltpu.SemaphoreType.DMA((4,)),
        pltpu.SemaphoreType.DMA((4,)),
        pltpu.VMEM(gradient.shape, f32),
        pltpu.VMEM((10,) + tile, f32),
        pltpu.VMEM(coupling.shape, f32),
        pltpu.VMEM(region.shape, jnp.int32),
        pltpu.VMEM(contact.shape, jnp.int32),
        pltpu.SMEM(rates.shape, f32),
        pltpu.SemaphoreType.DMA((6,)),
    ]
    vmem = pl.BlockSpec(memory_space=pltpu.VMEM)
    return pl.pallas_call(
        functools.partial(kernel, counts),
        out_shape=jax.ShapeDtypeStruct(gradient.shape, f32),
        in_specs=[pl.BlockSpec(memory_space=pltpu.HBM)] * 6,
        out_specs=vmem,
        scratch_shapes=scratch,
        compiler_params=pltpu.CompilerParams(
            collective_id=0, has_side_effects=True, vmem_limit_bytes=60 * 1024 * 1024
        ),
    )(gradient, potential, coupling, region, contact, rates)


def solution(mesh):
    placed = (
        P(None, "gx", "gy", None),
        P("gx", "gy", None),
        P(None, None, "gx", "gy", None),
        P("gx", "gy", None),
        P("gx", "gy", None),
        P(),
    )
    counts = (mesh.shape["gx"], mesh.shape["gy"])
    return jax.shard_map(
        functools.partial(local, counts),
        mesh=mesh,
        in_specs=placed,
        out_specs=P(None, "gx", "gy", None),
        check_vma=False,
    )
```

```python
import functools

import jax
import jax.numpy as jnp
from jax import lax
from jax.experimental import pallas as pl
from jax.experimental.pallas import tpu as pltpu
from jax.sharding import PartitionSpec as P

MESH = pl.DeviceIdType.MESH
LEVELS = 4
COARSE_SWEEPS = 6
REGIONS = 4
OMEGA = 0.8
STRENGTH = 8.0
ROWS = 8
NX = (8, 4, 2, 1)
RADIUS = 3
SLOTS = 8


def around(shape, far):
    reach = range(-6, 7)
    distance = lambda i, j: min(abs(i - a) + abs(j - b) for a, b in shape)
    found = [(i, j) for i in reach for j in reach if distance(i, j) <= far and (i, j) != (0, 0)]
    return sorted(found, key=lambda o: -abs(o[0]) - abs(o[1]))


OWN = [(0, 0)]
SQUARE = [(i, j) for i in (-1, 0, 1) for j in (-1, 0, 1)]
INNER = around(OWN, 2)
OUTER = [o for o in around(OWN, 3) if o not in INNER]
FOURTH = around(SQUARE, 2)
THIRD = around(SQUARE, 3)


def each(count, body):
    if count == 1:
        body(0)
        return

    def step(i, carry):
        body(i)
        return carry

    lax.fori_loop(0, count, step, 0, unroll=count)


def face_weights(difference):
    size = jnp.abs(difference)
    small = size < 0.5
    series = 1.0 / 362880.0
    for k in (40320.0, 5040.0, 720.0, 120.0, 24.0, 6.0, 2.0, 1.0):
        series = series * size + 1.0 / k
    below = jnp.where(small, series, jnp.exp(size) - 1.0)
    low = jnp.where(small, 1.0, size) / below
    low = jnp.where(size < 1e-4, 1.0 - 0.5 * size, low)
    high = low + size
    positive = difference > 0.0
    return jnp.where(positive, low, high), jnp.where(positive, high, low)


def kernel(counts, grad_in, pot_in, coup_in, region_in, contact_in, rates_in, out, *scratch):
    grad, pot, coup, region, contact, rates, in_sem = scratch[-7:]
    scratch = scratch[:-7]
    loads = {}
    for i, (name, source, target) in enumerate(
        (
            ("pot", pot_in, pot.at[pl.ds(1, 8)]),
            ("rates", rates_in, rates),
            ("region", region_in, region),
            ("contact", contact_in, contact),
            ("coup", coup_in, coup),
            ("grad", grad_in, grad),
        )
    ):
        loads[name] = pltpu.make_async_copy(source, target, in_sem.at[i])
        loads[name].start()
    weights, reaction, diag, inverse = (scratch[4 * i : 4 * i + 4] for i in range(4))
    sources = (None,) + tuple(scratch[16:19])
    fields = scratch[19:23]
    rows_halo, pot_y, send_y, send_sem, recv_sem = scratch[23:28]
    w_own, r_own, w_wide, r_wide, diag_wide, inverse_wide, u_wide, b_wide, e_rows = scratch[28:37]
    mid_send, mid_recv, low_send, low_recv, mid_cell, mid_cells, low_cell, low_cells = scratch[37:45]
    mid_send_sem, mid_recv_sem, low_send_sem, low_recv_sem, p_send, p_recv, q_send, q_recv = scratch[45:53]
    ring_u, ring_b, ring_w, ring_r, ring_diag, ring_inverse, ring_out = scratch[53:60]
    pair_own, pair_x, pair_y_send, pair_y, pair_corner_send, pair_corner, pair_send_sem, pair_recv_sem = scratch[60:68]
    coef_own, coef_x, coef_y_send, coef_y, coef_send_sem, coef_recv_sem = scratch[68:]
    n_x, n_y = counts
    lanes = out.shape[-1]
    gx, gy = lax.axis_index("gx"), lax.axis_index("gy")
    x_low, x_high = lax.rem(gx + n_x - 1, n_x), lax.rem(gx + 1, n_x)
    y_low, y_high = lax.rem(gy + n_y - 1, n_y), lax.rem(gy + 1, n_y)
    beside = ((x_high, gy), (x_low, gy), (gx, y_high), (gx, y_low))

    barrier = pltpu.get_barrier_semaphore()
    at_offset = lambda i, j: (lax.rem(gx + n_x + i, n_x), lax.rem(gy + n_y + j, n_y))
    devices = {o: at_offset(*o) for o in THIRD}
    for offset in INNER:
        pl.semaphore_signal(barrier, inc=1, device_id=devices[offset], device_id_type=MESH)
    pl.semaphore_wait(barrier, len(INNER))

    tile = (ROWS, lanes)
    row_at = lax.broadcasted_iota(jnp.int32, tile, 0)
    lane_at = lax.broadcasted_iota(jnp.int32, tile, 1)
    wide = lambda row: jnp.broadcast_to(row, tile)
    down = lambda v, by: pltpu.roll(v, by % ROWS, 0) if by % ROWS else v
    along = lambda v, by: pltpu.roll(v, by % lanes, 1)

    done = [0]

    def exchange(parts):
        slot = done[0] % 3
        done[0] += 1
        copies = []
        for i in (2, 3, 0, 1):
            source, target = parts[i]
            copy = pltpu.make_async_remote_copy(
                src_ref=source,
                dst_ref=target,
                send_sem=send_sem.at[i],
                recv_sem=recv_sem.at[slot, i],
                device_id=beside[i],
                device_id_type=MESH,
            )
            copy.start()
            copies.append(copy)

        def wait():
            for copy in copies:
                copy.wait()

        return wait

    def remote(source, target, send, recv, offset):
        copy = pltpu.make_async_remote_copy(
            src_ref=source,
            dst_ref=target,
            send_sem=send,
            recv_sem=recv,
            device_id=devices[offset],
            device_id_type=MESH,
        )
        copy.start()
        return copy

    def gather(offsets, source_of, target, send, recv):
        for n, (i, j) in enumerate(offsets):
            remote(source_of((i, j)), target.at[n], send, recv, (-i, -j))

        def wait():
            pltpu.make_async_copy(target, target, send).wait()
            pltpu.make_async_copy(target, target, recv).wait()

        return wait

    loads["pot"].wait()
    for side, at in ((0, ROWS - 1), (1, 0)):
        packed = wide(pot[1, at : at + 1, :])
        for x in range(1, 8):
            packed = jnp.where(row_at == x, wide(pot[x + 1, at : at + 1, :]), packed)
        send_y[side, 0] = packed
    wait = exchange(
        [
            (pot.at[8], pot.at[0]),
            (pot.at[1], pot.at[9]),
            (send_y.at[0, 0], pot_y.at[0]),
            (send_y.at[1, 0], pot_y.at[1]),
        ]
    )
    for name in ("rates", "region", "contact", "coup"):
        loads[name].wait()

    def put_faces(x, first, near):
        here = pot[x + 1]
        for k, value in enumerate(near):
            plus, minus = face_weights(here - value)
            weights[0][x, 3 * (first + k)] = jnp.ones(tile, jnp.float32)
            weights[0][x, 3 * (first + k) + 1] = plus
            weights[0][x, 3 * (first + k) + 2] = minus

    def set_up(x):
        here = pot[x + 1]
        near = (
            jnp.where(lane_at == lanes - 1, 0.0, along(here, -1)),
            jnp.where(lane_at == 0, 0.0, along(here, 1)),
        )
        put_faces(x, 4, near)
        at_contact = STRENGTH * contact[x].astype(jnp.float32)
        regions = region[x]
        for c in range(3):
            extra = jnp.full(tile, rates[0, c])
            for pick in range(1, REGIONS):
                extra = jnp.where(regions == pick, rates[pick, c], extra)
            for d in range(3):
                value = coup[c, d, x]
                reaction[0][x, 3 * c + d] = value + (extra + at_contact) if c == d else value

    each(NX[0], set_up)
    wait()
    is_low_x, is_high_x = gx == 0, gx == n_x - 1
    is_low_y, is_high_y = gy == 0, gy == n_y - 1
    pot[0] = jnp.where(is_low_x, 0.0, pot[0])
    pot[9] = jnp.where(is_high_x, 0.0, pot[9])
    pot_y[0] = jnp.where(is_low_y, 0.0, pot_y[0])
    pot_y[1] = jnp.where(is_high_y, 0.0, pot_y[1])

    def cross_faces(x):
        here = pot[x + 1]
        near = (
            pot[x + 2],
            pot[x],
            jnp.where(row_at == ROWS - 1, wide(pot_y[1, pl.ds(x, 1), :]), down(here, -1)),
            jnp.where(row_at == 0, wide(pot_y[0, pl.ds(x, 1), :]), down(here, 1)),
        )
        put_faces(x, 0, near)

    each(NX[0], cross_faces)

    def finish(w, r, diagonal, inv, count):
        def body(x):
            m = [[r[x, 3 * col + row] for col in range(3)] for row in range(3)]
            for c in range(3):
                total = w[x, c]
                for k in range(1, 6):
                    total = total + w[x, 3 * k + c]
                m[c][c] = m[c][c] + total
                diagonal[x, c] = m[c][c]

            def cofactor(i, j):
                i1, i2, j1, j2 = (i + 1) % 3, (i + 2) % 3, (j + 1) % 3, (j + 2) % 3
                return m[i1][j1] * m[i2][j2] - m[i1][j2] * m[i2][j1]

            cof = [[cofactor(i, j) for j in range(3)] for i in range(3)]
            det = m[0][0] * cof[0][0] + m[0][1] * cof[0][1] + m[0][2] * cof[0][2]
            scale = OMEGA / det
            for i in range(3):
                for j in range(3):
                    inv[x, 3 * i + j] = cof[j][i] * scale

        each(count, body)

    def finish_level(level):
        finish(weights[level], reaction[level], diag[level], inverse[level], NX[level])

    def mask_level(level):
        w, span, last = weights[level], 1 << level, NX[level] - 1
        for c in range(3):
            w[last, c] = jnp.where(is_high_x, 0.0, w[last, c])
            w[0, 3 + c] = jnp.where(is_low_x, 0.0, w[0, 3 + c])
        off_high = jnp.logical_and(row_at >= ROWS - span, is_high_y)
        off_low = jnp.logical_and(row_at < span, is_low_y)
        off_up, off_down = lane_at >= lanes - span, lane_at < span

        def body(x):
            for k, off in ((2, off_high), (3, off_low), (4, off_up), (5, off_down)):
                for c in range(3):
                    w[x, 3 * k + c] = jnp.where(off, 0.0, w[x, 3 * k + c])

        each(NX[level], body)

    def pair_tools(level):
        span = 1 << level
        odd_row = (row_at & span) != 0
        odd_lane = (lane_at & span) != 0

        def high_row(v):
            return jnp.where(odd_row, v, down(v, -span))

        def low_row(v):
            return jnp.where(odd_row, down(v, span), v)

        def high_lane(v):
            return jnp.where(odd_lane, v, along(v, -span))

        def low_lane(v):
            return jnp.where(odd_lane, along(v, span), v)

        def rows(v):
            return v + jnp.where(odd_row, down(v, span), down(v, -span))

        def lanes_(v):
            return v + jnp.where(odd_lane, along(v, span), along(v, -span))

        return high_row, low_row, high_lane, low_lane, rows, lanes_

    def coarsen(level):
        high_row, low_row, high_lane, low_lane, rows, lanes_ = pair_tools(level)
        w, r = weights[level], reaction[level]
        w_next, r_next = (w_own, r_own) if level == LEVELS - 2 else (weights[level + 1], reaction[level + 1])

        def body(x):
            for c in range(3):
                w_next[x, c] = lanes_(rows(w[2 * x + 1, c]))
                w_next[x, 3 + c] = lanes_(rows(w[2 * x, 3 + c]))
                pair = lambda k: w[2 * x, 3 * k + c] + w[2 * x + 1, 3 * k + c]
                w_next[x, 6 + c] = lanes_(high_row(pair(2)))
                w_next[x, 9 + c] = lanes_(low_row(pair(3)))
                w_next[x, 12 + c] = high_lane(rows(pair(4)))
                w_next[x, 15 + c] = low_lane(rows(pair(5)))
            for i in range(9):
                r_next[x, i] = lanes_(rows(r[2 * x, i] + r[2 * x + 1, i]))

        each(NX[level + 1], body)

    slot_at = lane_at & (SLOTS - 1)
    x_at, y_at = row_at + (gx - RADIUS), slot_at + (gy - RADIUS)
    x_last = jnp.logical_or(x_at == n_x - 1, x_at == -1)
    x_first = jnp.logical_or(x_at == 0, x_at == n_x)
    y_last = jnp.logical_or(y_at == n_y - 1, y_at == -1)
    y_first = jnp.logical_or(y_at == 0, y_at == n_y)
    z_last, z_first = lane_at >= lanes - SLOTS, lane_at < SLOTS
    offs = (x_last, x_first, y_last, y_first, z_last, z_first)
    bits = (2, 2, 1, 1, 4, 4)

    def transposed(tiles):
        tiles = list(tiles)
        for bit in (1, 2, 4):
            clear = (slot_at & bit) == 0
            for p in range(SLOTS):
                if not p & bit:
                    one, two = tiles[p], tiles[p | bit]
                    tiles[p] = jnp.where(clear, one, along(two, bit))
                    tiles[p | bit] = jnp.where(clear, along(one, -bit), two)
        return tiles

    def unpacked(offsets, row_of, own, fill=0.0):
        tiles = [jnp.full(tile, fill) for _ in range(SLOTS)]
        for n, (i, j) in enumerate(list(offsets) + OWN):
            if min(i, j) >= -RADIUS:
                row = row_of(n) if n < len(offsets) else own
                tiles[j + RADIUS] = jnp.where(row_at == i + RADIUS, wide(row), tiles[j + RADIUS])
        return transposed(tiles)

    def child_row(f, x0, c):
        which = slot_at & 3
        rows = [wide(f[x0 + p // 2, c, 4 * (p % 2) : 4 * (p % 2) + 1, :]) for p in range(4)]
        packed = jnp.where(which == 0, rows[0], jnp.where(which == 1, rows[1], jnp.where(which == 2, rows[2], rows[3])))
        return packed[0:1, :]

    def slot_row(values):
        packed = values[0]
        for i in range(1, len(values)):
            packed = jnp.where(slot_at == i, values[i], packed)
        return packed

    def send_coefficients():
        for i in range(27):
            mid_send[i] = child_row(weights[2] if i < 18 else reaction[2], 0, i if i < 18 else i - 18)
        fields_ = [w_own[0, i] for i in range(18)] + [r_own[0, i] for i in range(9)]
        for row in range(4):
            low_send[row : row + 1, :] = slot_row(fields_[SLOTS * row : SLOTS * row + SLOTS])[0:1, :]
        return gather(INNER, lambda o: mid_send, mid_recv, mid_send_sem, mid_recv_sem)

    def send_low_coefficients():
        return gather(FOURTH, lambda o: low_send, low_recv, low_send_sem, low_recv_sem)

    def take_coefficients(waits):
        for wait in waits:
            wait()
        for i in range(27):
            made = unpacked(INNER, lambda n: mid_recv[n, i], mid_send[i], 1.0 if i in (18, 22, 26) else 0.0)
            for p in range(SLOTS):
                if i < 18:
                    w_wide[p, i] = made[p]
                else:
                    r_wide[p, i - 18] = made[p]
        finish(w_wide, r_wide, diag_wide, inverse_wide, SLOTS)
        for k in range(6):
            for p in range(SLOTS):
                if ((p & bits[k]) != 0) == (k % 2 == 0):
                    for c in range(3):
                        w_wide[p, 3 * k + c] = jnp.where(offs[k], 0.0, w_wide[p, 3 * k + c])
        top = LEVELS - 1
        w, r = weights[top], reaction[top]
        for row in range(4):
            here = slice(row, row + 1)
            made = unpacked(FOURTH, lambda n: low_recv[n, here, :], low_send[here, :])
            for p in range(SLOTS):
                i = SLOTS * row + p
                if i < 18:
                    w[0, i] = made[p]
                elif i < 27:
                    r[0, i - 18] = made[p]
        finish_level(top)
        for k in range(6):
            for c in range(3):
                w[0, 3 * k + c] = jnp.where(offs[k], 0.0, w[0, 3 * k + c])

    def spread(value, t):
        value = jnp.where(slot_at == t, value, 0.0)
        for bit in (1, 2, 4):
            value = value + along(value, -bit if t & bit else bit)
        return value

    def wide_residual(p, u):
        left = []
        for c in range(3):
            value = b_wide[p, c] - diag_wide[p, c] * u[p][c]
            for k in range(6):
                bit, ahead = bits[k], k % 2 == 0
                near = u[p ^ bit][c]
                if ((p & bit) != 0) == ahead:
                    turn = -1 if ahead else 1
                    near = down(near, turn) if k < 2 else along(near, turn if k < 4 else turn * SLOTS)
                value = value + w_wide[p, 3 * k + c] * near
            for d in range(3):
                if d != c:
                    value = value - r_wide[p, 3 * d + c] * u[p][d]
            left.append(value)
        return left

    def apply_inverse(v, x, r):
        return [v[x, 3 * c] * r[0] + v[x, 3 * c + 1] * r[1] + v[x, 3 * c + 2] * r[2] for c in range(3)]

    def wide_fields():
        return [[u_wide[p, c] for c in range(3)] for p in range(SLOTS)]

    def window_sweep(b, u, patches=None):
        top = LEVELS - 1
        w, r = weights[top], reaction[top]
        left = []
        for c in range(3):
            value = b[c] - diag[top][0, c] * u[c]
            before_x, before_y = down(u[c], 1), along(u[c], 1)
            if patches is not None:
                before_x = jnp.where(row_at == 0, patches[0][c], before_x)
                before_y = jnp.where(slot_at == 0, patches[1][c], before_y)
            near = (down(u[c], -1), before_x, along(u[c], -1), before_y, along(u[c], -SLOTS), along(u[c], SLOTS))
            for k in range(6):
                value = value + w[0, 3 * k + c] * near[k]
            for d in range(3):
                if d != c:
                    value = value - r[0, 3 * d + c] * u[d]
            left.append(value)
        step = apply_inverse(inverse[top], 0, left)
        return [u[c] + step[c] for c in range(3)]

    def lower(turn, beside_p, beside_q):
        for c in range(3):
            mid_cell[0, c] = child_row(sources[2], 0, c)
            mid_cell[1, c] = child_row(fields[2].at[0], 1, c)
        near = INNER + OUTER
        wait = gather(
            near, lambda o: mid_cell.at[0 if o in INNER else 1], mid_cells.at[turn], p_send, p_recv.at[turn]
        )
        beside_p()
        wait()
        for c in range(3):
            made = unpacked(near, lambda n: mid_cells[turn, n, c], mid_cell[0, c])
            for p in range(SLOTS):
                b_wide[p, c] = made[p]
        inner = jnp.abs(row_at - RADIUS) + jnp.abs(slot_at - RADIUS) <= 2
        for p in range(SLOTS):
            b = [b_wide[p, c] for c in range(3)]
            first = apply_inverse(inverse_wide, p, b)
            for c in range(3):
                u_wide[p, c] = jnp.where(inner, first[c], b[c])
        u_mid = wide_fields()
        b = [jnp.zeros(tile, jnp.float32) for _ in range(3)]
        for p in range(SLOTS):
            left = wide_residual(p, u_mid)
            b = [b[c] + left[c] for c in range(3)]
        u = apply_inverse(inverse[LEVELS - 1], 0, b)
        for _ in range(2):
            u = window_sweep(b, u)
        row = slot_row([spread(value, RADIUS) for value in u + b])
        low_cell[0] = row[RADIUS : RADIUS + 1, :]
        wait = gather(THIRD, lambda o: low_cell.at[0], low_cells.at[turn], q_send, q_recv.at[turn])
        beside_q()
        wait()
        made = unpacked(THIRD, lambda n: low_cells[turn, n], low_cell[0])
        u, b = made[:3], made[3:6]
        before_x = [jnp.zeros(tile, jnp.float32) for _ in range(3)]
        last_y = jnp.zeros(tile, jnp.float32)
        for n, (i, j) in enumerate(THIRD):
            if i < -RADIUS:
                for c in range(3):
                    value = along(wide(low_cells[turn, n]), j + RADIUS - c)
                    before_x[c] = jnp.where(slot_at == j + RADIUS, value, before_x[c])
            if j < -RADIUS:
                last_y = jnp.where(row_at == i + RADIUS, wide(low_cells[turn, n]), last_y)
        before_y = [along(last_y, -c) for c in range(3)]
        u = window_sweep(b, u, (before_x, before_y))
        for _ in range(COARSE_SWEEPS - 4):
            u = window_sweep(b, u)
        u_mid = [[u_wide[p, c] + u[c] for c in range(3)] for p in range(SLOTS)]
        last = []
        for p in range(SLOTS):
            step = apply_inverse(inverse_wide, p, wide_residual(p, u_mid))
            last.append([u_mid[p][c] + step[c] for c in range(3)])
        for c in range(3):
            for x in range(2):
                for at, (t, y) in enumerate(((RADIUS - 1, 1), (RADIUS, 0), (RADIUS, 1), (RADIUS + 1, 0))):
                    low, high = last[2 * x + y][c], last[4 + 2 * x + y][c]
                    if t & 4:
                        value = jnp.where(slot_at == t, high, 0.0) + along(jnp.where(slot_at == t, low, 0.0), -4)
                    else:
                        value = jnp.where(slot_at == t, low, 0.0) + along(jnp.where(slot_at == t, high, 0.0), 4)
                    for bit in (1, 2):
                        value = value + along(value, -bit if t & bit else bit)
                    e_rows[x, at, c] = value

    def mid_at(c, x, y):
        row = RADIUS + (x // 2)
        return wide(e_rows[x % 2, y + 1, c, row : row + 1, :])

    odd = (lane_at & 1) != 0

    def even_part(v):
        return jnp.where(odd, along(v, 1), v)

    def odd_part(v):
        return jnp.where(odd, v, along(v, -1))

    def rows_tile(rows):
        made = jnp.zeros(tile, jnp.float32)
        for at, value in rows:
            made = jnp.where(row_at == at, wide(value), made)
        return made

    def pair_up():
        for x in range(4):
            for j in range(14):
                part = [weights[1][x, i] if i < 18 else reaction[1][x, i - 18] for i in (2 * j, 2 * j + 1) if i < 27]
                coef_own[x, j] = jnp.where(odd, part[-1], part[0])
        for side, y in ((0, 6), (1, 0)):
            for j in range(0, 14, 2):
                rows = [(4 * i + x, coef_own[x, j + i, y : y + 1, :]) for i in range(2) for x in range(4)]
                coef_y_send[side, j // 2] = rows_tile(rows)

    def send_ring_coefficients():
        copies = []
        for side, turn in ((0, 1), (1, -1)):
            sems = lambda n: (coef_send_sem.at[n], coef_recv_sem.at[n])
            copies.append(remote(coef_y_send.at[side], coef_y.at[side], *sems(side), (0, turn)))
            copies.append(remote(coef_own.at[3 - 3 * side], coef_x.at[side], *sems(2 + side), (turn, 0)))
        return copies

    def take_ring_coefficients(copies):
        for copy in copies:
            copy.wait()
        for p in range(6):
            edge = 2 if p in (0, 5) else 1
            filled = jnp.logical_and(row_at >= edge, row_at < ROWS - edge)
            for j in range(14):
                if p in (0, 5):
                    rows = [(2 + k, coef_x[p // 5, j, 2 * k : 2 * k + 1, :]) for k in range(4)]
                else:
                    x = p - 1
                    rows = [(2 + k, coef_own[x, j, 2 * k : 2 * k + 1, :]) for k in range(4)]
                    at = 4 * (j % 2) + x
                    rows += [(1, coef_y[0, j // 2, at : at + 1, :]), (6, coef_y[1, j // 2, at : at + 1, :])]
                both = rows_tile(rows)
                for i, value in ((2 * j, even_part(both)), (2 * j + 1, odd_part(both))):
                    if i < 18:
                        ring_w[p, i] = value
                    elif i < 27:
                        ring_r[p, i - 18] = jnp.where(filled, value, 1.0) if i in (18, 22, 26) else value
        finish(ring_w, ring_r, ring_diag, ring_inverse, 6)
        off_high = jnp.logical_and(row_at == 5, is_high_y)
        off_low = jnp.logical_and(row_at == 2, is_low_y)
        for c in range(3):
            ring_w[4, c] = jnp.where(is_high_x, 0.0, ring_w[4, c])
            ring_w[1, 3 + c] = jnp.where(is_low_x, 0.0, ring_w[1, 3 + c])

        def body(p):
            for k, off in ((2, off_high), (3, off_low), (4, lane_at >= lanes - 2), (5, lane_at < 2)):
                for c in range(3):
                    ring_w[p, 3 * k + c] = jnp.where(off, 0.0, ring_w[p, 3 * k + c])

        each(6, body)

    def send_pairs(turn):
        for x in range(4):
            for c in range(3):
                pair_own[x, c] = jnp.where(odd, sources[1][x, c], fields[1][0, x + 1, c])
        for side, y in ((0, 4), (1, 0)):
            for c in range(3):
                rows = [(2 * x + k, pair_own[x, c, y + 2 * k : y + 2 * k + 1, :]) for x in range(4) for k in range(2)]
                pair_y_send[side, c] = rows_tile(rows)
        for sx in range(2):
            for sy in range(2):
                x, y = 3 - 3 * sx, 6 - 6 * sy
                for c in range(3):
                    pair_corner_send[2 * sx + sy, c : c + 1, :] = pair_own[x, c, y : y + 1, :]
        copies = []
        sems = lambda n: (pair_send_sem.at[n], pair_recv_sem.at[turn, n])
        for side, to in ((0, 1), (1, -1)):
            copies.append(remote(pair_y_send.at[side], pair_y.at[turn, side], *sems(side), (0, to)))
            source = pair_own.at[pl.ds(2 - 2 * side, 2)]
            copies.append(remote(source, pair_x.at[turn, side], *sems(2 + side), (to, 0)))
        for sx in range(2):
            for sy in range(2):
                n = 2 * sx + sy
                to = (1 - 2 * sx, 1 - 2 * sy)
                copies.append(remote(pair_corner_send.at[n], pair_corner.at[turn, n], *sems(4 + n), to))
        return copies

    def take_pairs(turn, copies):
        for copy in copies:
            copy.wait()
        for p in range(8):
            for c in range(3):
                if 2 <= p < 6:
                    x = p - 2
                    rows = [(2 + k, pair_own[x, c, 2 * k : 2 * k + 1, :]) for k in range(4)]
                    for side in range(2):
                        for k in range(2):
                            at = 2 * x + k
                            rows.append((6 * side + k, pair_y[turn, side, c, at : at + 1, :]))
                else:
                    side = p // 4
                    rows = [(2 + k, pair_x[turn, side, p - 6 * side, c, 2 * k : 2 * k + 1, :]) for k in range(4)]
                    if p in (1, 6):
                        for sy in range(2):
                            rows.append((1 + 5 * sy, pair_corner[turn, 2 * side + sy, c : c + 1, :]))
                both = rows_tile(rows)
                ring_u[p, c] = even_part(both)
                if 1 <= p < 7:
                    ring_b[p - 1, c] = odd_part(both)

    def ring_sweep():
        def add(p):
            x = p // 2 - 1
            for c in range(3):
                e = jnp.where(row_at < 2, mid_at(c, x, -1), mid_at(c, x, 0))
                e = jnp.where(row_at < 4, e, jnp.where(row_at < 6, mid_at(c, x, 1), mid_at(c, x, 2)))
                ring_u[p, c] += e

        for p in range(8):
            add(p)
        for p in range(6):
            u = [ring_u[p + 1, c] for c in range(3)]
            left = []
            for c in range(3):
                value = ring_b[p, c] - ring_diag[p, c] * u[c]
                near = (ring_u[p + 2, c], ring_u[p, c], down(u[c], -1), down(u[c], 1), along(u[c], -2), along(u[c], 2))
                for k in range(6):
                    value = value + ring_w[p, 3 * k + c] * near[k]
                for d in range(3):
                    if d != c:
                        value = value - ring_r[p, 3 * d + c] * u[d]
                left.append(value)
            step = apply_inverse(ring_inverse, p, left)
            for c in range(3):
                ring_out[p, c] = u[c] + step[c]

    def add_to_finest(at, slot):
        f = fields[0]
        for c in range(3):
            for p in range(6):
                rows = [wide(ring_out[p, c, 2 + k : 3 + k, :]) for k in range(4)]
                e = jnp.where(row_at < 2, rows[0], rows[1])
                e = jnp.where(row_at < 4, e, jnp.where(row_at < 6, rows[2], rows[3]))
                for x in {0: (-1,), 5: (8,)}.get(p, (2 * p - 2, 2 * p - 1)):
                    f[at, x + 1, c] += e
            for side, row in ((0, 1), (1, 6)):
                rows = [wide(ring_out[1 + k, c, row : row + 1, :]) for k in range(4)]
                e = jnp.where(row_at < 2, rows[0], rows[1])
                e = jnp.where(row_at < 4, e, jnp.where(row_at < 6, rows[2], rows[3]))
                rows_halo[slot, side, c] += e

    def source(level, x):
        if level == 0:
            return [grad[c, x] for c in range(3)]
        return [sources[level][x, c] for c in range(3)]

    def solve(level, x, r):
        v = inverse[level]
        return [v[x, 3 * c] * r[0] + v[x, 3 * c + 1] * r[1] + v[x, 3 * c + 2] * r[2] for c in range(3)]

    def share(level, at, beside_it=lambda: None):
        slot, f, count = done[0] % 3, fields[level], NX[level]
        for side, row in ((0, ROWS - 1), (1, 0)):
            for c in range(3):
                packed = wide(f[at, 1, c, row : row + 1, :])
                for x in range(1, count):
                    packed = jnp.where(row_at == x, wide(f[at, x + 1, c, row : row + 1, :]), packed)
                send_y[side, c] = packed
        wait = exchange(
            [
                (f.at[at, count], f.at[at, 0]),
                (f.at[at, 1], f.at[at, count + 1]),
                (send_y.at[0], rows_halo.at[slot, 0]),
                (send_y.at[1], rows_halo.at[slot, 1]),
            ]
        )
        beside_it()
        wait()
        return slot

    def residual(level, at, slot, x):
        f, w, r, span = fields[level], weights[level], reaction[level], 1 << level
        u = [f[at, x + 1, c] for c in range(3)]
        b = source(level, x)
        left = []
        for c in range(3):
            row_high, row_low = (rows_halo[slot, side, c, pl.ds(x, 1), :] for side in (1, 0))
            near = (
                f[at, x + 2, c],
                f[at, x, c],
                jnp.where(row_at >= ROWS - span, wide(row_high), down(u[c], -span)),
                jnp.where(row_at < span, wide(row_low), down(u[c], span)),
                along(u[c], -span),
                along(u[c], span),
            )
            value = b[c] - diag[level][x, c] * u[c]
            for k in range(6):
                value = value + w[x, 3 * k + c] * near[k]
            for d in range(3):
                if d != c:
                    value = value - r[x, 3 * d + c] * u[d]
            left.append(value)
        return u, left

    def sweep(level, at, slot, last=False):
        def body(x):
            u, left = residual(level, at, slot, x)
            step = solve(level, x, left)
            for c in range(3):
                if last:
                    out[c, x] = u[c] + step[c]
                else:
                    fields[level][1 - at, x + 1, c] = u[c] + step[c]

        each(NX[level], body)
        return 1 - at

    def restrict(level, at, slot):
        rows, lanes_ = pair_tools(level)[4:]

        def body(x):
            left = [residual(level, at, slot, 2 * x + i)[1] for i in range(2)]
            total = [lanes_(rows(left[0][c] + left[1][c])) for c in range(3)]
            first = solve(level + 1, x, total)
            for c in range(3):
                sources[level + 1][x, c] = total[c]
                fields[level + 1][0, x + 1, c] = first[c]

        each(NX[level + 1], body)

    def cycle(at, turn, besides, last=False):
        slot = share(0, at, besides[0])
        restrict(0, at, slot)
        pairs = []

        def beside():
            pairs.extend(send_pairs(turn))
            besides[1]()

        restrict(1, 0, share(1, 0, beside))
        lower(turn, besides[2], lambda: take_pairs(turn, pairs))
        ring_sweep()
        add_to_finest(at, slot)
        return sweep(0, at, slot, last)

    def start(x):
        for c, value in enumerate(solve(0, x, source(0, x))):
            fields[0][0, x + 1, c] = value

    finish_level(0)
    loads["grad"].wait()
    each(NX[0], start)
    pending, ring_pending = [], []

    def make_levels():
        coarsen(0)
        mask_level(0)
        finish_level(1)
        coarsen(1)
        finish_level(2)
        coarsen(2)
        pending.append(send_coefficients())
        pair_up()
        mask_level(1)

    def take_wide():
        pending.append(send_low_coefficients())
        ring_pending.extend(send_ring_coefficients())
        take_coefficients(pending)

    nothing = lambda: None
    at = cycle(0, 0, (make_levels, take_wide, lambda: take_ring_coefficients(ring_pending)))
    at = sweep(0, at, share(0, at))
    cycle(at, 1, (nothing,) * 3, last=True)


def local(counts, gradient, potential, coupling, region, contact, rates):
    nz = potential.shape[-1]
    tile = (ROWS, nz)
    f32 = jnp.float32
    scratch = []
    for parts in (18, 9, 3, 9):
        scratch += [pltpu.VMEM((n, parts) + tile, f32) for n in NX]
    scratch += [pltpu.VMEM((n, 3) + tile, f32) for n in NX[1:]]
    scratch += [pltpu.VMEM((2, n + 2, 3) + tile, f32) for n in NX]
    scratch += [
        pltpu.VMEM((3, 2, 3) + tile, f32),
        pltpu.VMEM((2,) + tile, f32),
        pltpu.VMEM((2, 3) + tile, f32),
        pltpu.SemaphoreType.DMA((4,)),
        pltpu.SemaphoreType.DMA((3, 4)),
        pltpu.VMEM((1, 18) + tile, f32),
        pltpu.VMEM((1, 9) + tile, f32),
        pltpu.VMEM((SLOTS, 18) + tile, f32),
        pltpu.VMEM((SLOTS, 9) + tile, f32),
        pltpu.VMEM((SLOTS, 3) + tile, f32),
        pltpu.VMEM((SLOTS, 9) + tile, f32),
        pltpu.VMEM((SLOTS, 3) + tile, f32),
        pltpu.VMEM((SLOTS, 3) + tile, f32),
        pltpu.VMEM((2, 4, 3) + tile, f32),
        pltpu.VMEM((27, 1, nz), f32),
        pltpu.VMEM((len(INNER), 27, 1, nz), f32),
        pltpu.VMEM((4, nz), f32),
        pltpu.VMEM((len(FOURTH), 4, nz), f32),
        pltpu.VMEM((2, 3, 1, nz), f32),
        pltpu.VMEM((2, len(INNER + OUTER), 3, 1, nz), f32),
        pltpu.VMEM((1, 1, nz), f32),
        pltpu.VMEM((2, len(THIRD), 1, nz), f32),
        pltpu.SemaphoreType.DMA,
        pltpu.SemaphoreType.DMA,
        pltpu.SemaphoreType.DMA,
        pltpu.SemaphoreType.DMA,
        pltpu.SemaphoreType.DMA,
        pltpu.SemaphoreType.DMA((2,)),
        pltpu.SemaphoreType.DMA,
        pltpu.SemaphoreType.DMA((2,)),
        pltpu.VMEM((8, 3) + tile, f32),
        pltpu.VMEM((6, 3) + tile, f32),
        pltpu.VMEM((6, 18) + tile, f32),
        pltpu.VMEM((6, 9) + tile, f32),
        pltpu.VMEM((6, 3) + tile, f32),
        pltpu.VMEM((6, 9) + tile, f32),
        pltpu.VMEM((6, 3) + tile, f32),
        pltpu.VMEM((4, 3) + tile, f32),
        pltpu.VMEM((2, 2, 2, 3) + tile, f32),
        pltpu.VMEM((2, 3) + tile, f32),
        pltpu.VMEM((2, 2, 3) + tile, f32),
        pltpu.VMEM((4, 4, nz), f32),
        pltpu.VMEM((2, 4, 4, nz), f32),
        pltpu.SemaphoreType.DMA((8,)),
        pltpu.SemaphoreType.DMA((2, 8)),
        pltpu.VMEM((4, 14) + tile, f32),
        pltpu.VMEM((2, 14) + tile, f32),
        pltpu.VMEM((2, 7) + tile, f32),
        pltpu.VMEM((2, 7) + tile, f32),
        pltpu.SemaphoreType.DMA((4,)),
        pltpu.SemaphoreType.DMA((4,)),
        pltpu.VMEM(gradient.shape, f32),
        pltpu.VMEM((10,) + tile, f32),
        pltpu.VMEM(coupling.shape, f32),
        pltpu.VMEM(region.shape, jnp.int32),
        pltpu.VMEM(contact.shape, jnp.int32),
        pltpu.SMEM(rates.shape, f32),
        pltpu.SemaphoreType.DMA((6,)),
    ]
    vmem = pl.BlockSpec(memory_space=pltpu.VMEM)
    return pl.pallas_call(
        functools.partial(kernel, counts),
        out_shape=jax.ShapeDtypeStruct(gradient.shape, f32),
        in_specs=[pl.BlockSpec(memory_space=pltpu.HBM)] * 6,
        out_specs=vmem,
        scratch_shapes=scratch,
        compiler_params=pltpu.CompilerParams(
            collective_id=0, has_side_effects=True, vmem_limit_bytes=60 * 1024 * 1024
        ),
    )(gradient, potential, coupling, region, contact, rates)


def solution(mesh):
    placed = (
        P(None, "gx", "gy", None),
        P("gx", "gy", None),
        P(None, None, "gx", "gy", None),
        P("gx", "gy", None),
        P("gx", "gy", None),
        P(),
    )
    counts = (mesh.shape["gx"], mesh.shape["gy"])
    return jax.shard_map(
        functools.partial(local, counts),
        mesh=mesh,
        in_specs=placed,
        out_specs=P(None, "gx", "gy", None),
        check_vma=False,
    )
```

```python
import functools

import jax
import jax.numpy as jnp
from jax import lax
from jax.experimental import pallas as pl
from jax.experimental.pallas import tpu as pltpu
from jax.sharding import PartitionSpec as P

MESH = pl.DeviceIdType.MESH
LEVELS = 4
COARSE_SWEEPS = 6
REGIONS = 4
OMEGA = 0.8
STRENGTH = 8.0
ROWS = 8
NX = (8, 4, 2, 1)
RADIUS = 3
SLOTS = 8


def around(shape, far):
    reach = range(-6, 7)
    distance = lambda i, j: min(abs(i - a) + abs(j - b) for a, b in shape)
    found = [(i, j) for i in reach for j in reach if distance(i, j) <= far and (i, j) != (0, 0)]
    return sorted(found, key=lambda o: -abs(o[0]) - abs(o[1]))


OWN = [(0, 0)]
SQUARE = [(i, j) for i in (-1, 0, 1) for j in (-1, 0, 1)]
INNER = around(OWN, 2)
OUTER = [o for o in around(OWN, 3) if o not in INNER]
FOURTH = around(SQUARE, 2)
THIRD = around(SQUARE, 3)


def each(count, body):
    if count == 1:
        body(0)
        return

    def step(i, carry):
        body(i)
        return carry

    lax.fori_loop(0, count, step, 0, unroll=count)


def face_weights(difference):
    size = jnp.abs(difference)
    small = size < 0.5
    series = 1.0 / 362880.0
    for k in (40320.0, 5040.0, 720.0, 120.0, 24.0, 6.0, 2.0, 1.0):
        series = series * size + 1.0 / k
    below = jnp.where(small, series, jnp.exp(size) - 1.0)
    low = jnp.where(small, 1.0, size) / below
    low = jnp.where(size < 1e-4, 1.0 - 0.5 * size, low)
    high = low + size
    positive = difference > 0.0
    return jnp.where(positive, low, high), jnp.where(positive, high, low)


def kernel(counts, grad_in, pot_in, coup_in, region_in, contact_in, rates_in, out, *scratch):
    grad, pot, coup, region, contact, rates, in_sem = scratch[-7:]
    scratch = scratch[:-7]
    loads = {}
    for i, (name, source, target) in enumerate(
        (
            ("pot", pot_in, pot.at[pl.ds(1, 8)]),
            ("rates", rates_in, rates),
            ("region", region_in, region),
            ("contact", contact_in, contact),
            ("coup", coup_in, coup),
            ("grad", grad_in, grad),
        )
    ):
        loads[name] = pltpu.make_async_copy(source, target, in_sem.at[i])
        loads[name].start()
    weights, reaction, diag, inverse = (scratch[4 * i : 4 * i + 4] for i in range(4))
    sources = (None,) + tuple(scratch[16:19])
    fields = scratch[19:23]
    rows_halo, pot_y, send_y, send_sem, recv_sem = scratch[23:28]
    w_own, r_own, w_wide, r_wide, diag_wide, inverse_wide, u_wide, b_wide, e_rows = scratch[28:37]
    mid_send, mid_recv, low_send, low_recv, mid_cell, mid_cells, low_cell, low_cells = scratch[37:45]
    mid_send_sem, mid_recv_sem, low_send_sem, low_recv_sem, p_send, p_recv, q_send, q_recv = scratch[45:53]
    ring_u, ring_b, ring_w, ring_r, ring_diag, ring_inverse, ring_out = scratch[53:60]
    pair_own, pair_x, pair_y_send, pair_y, pair_corner_send, pair_corner, pair_send_sem, pair_recv_sem = scratch[60:68]
    coef_own, coef_x, coef_y_send, coef_y, coef_send_sem, coef_recv_sem, part = scratch[68:]
    n_x, n_y = counts
    lanes = out.shape[-1]
    gx, gy = lax.axis_index("gx"), lax.axis_index("gy")
    x_low, x_high = lax.rem(gx + n_x - 1, n_x), lax.rem(gx + 1, n_x)
    y_low, y_high = lax.rem(gy + n_y - 1, n_y), lax.rem(gy + 1, n_y)
    beside = ((x_high, gy), (x_low, gy), (gx, y_high), (gx, y_low))

    barrier = pltpu.get_barrier_semaphore()
    at_offset = lambda i, j: (lax.rem(gx + n_x + i, n_x), lax.rem(gy + n_y + j, n_y))
    devices = {o: at_offset(*o) for o in THIRD}
    for offset in INNER:
        pl.semaphore_signal(barrier, inc=1, device_id=devices[offset], device_id_type=MESH)
    pl.semaphore_wait(barrier, len(INNER))

    tile = (ROWS, lanes)
    row_at = lax.broadcasted_iota(jnp.int32, tile, 0)
    lane_at = lax.broadcasted_iota(jnp.int32, tile, 1)
    wide = lambda row: jnp.broadcast_to(row, tile)
    down = lambda v, by: pltpu.roll(v, by % ROWS, 0) if by % ROWS else v
    along = lambda v, by: pltpu.roll(v, by % lanes, 1)

    done = [0]

    def exchange(parts):
        slot = done[0] % 3
        done[0] += 1
        copies = []
        for i in (2, 3, 0, 1):
            source, target = parts[i]
            copy = pltpu.make_async_remote_copy(
                src_ref=source,
                dst_ref=target,
                send_sem=send_sem.at[i],
                recv_sem=recv_sem.at[slot, i],
                device_id=beside[i],
                device_id_type=MESH,
            )
            copy.start()
            copies.append(copy)

        def wait():
            for copy in copies:
                copy.wait()

        return wait

    def remote(source, target, send, recv, offset):
        copy = pltpu.make_async_remote_copy(
            src_ref=source,
            dst_ref=target,
            send_sem=send,
            recv_sem=recv,
            device_id=devices[offset],
            device_id_type=MESH,
        )
        copy.start()
        return copy

    def gather(offsets, source_of, target, send, recv):
        for n, (i, j) in enumerate(offsets):
            remote(source_of((i, j)), target.at[n], send, recv, (-i, -j))

        def wait():
            pltpu.make_async_copy(target, target, send).wait()
            pltpu.make_async_copy(target, target, recv).wait()

        return wait

    loads["pot"].wait()
    for side, at in ((0, ROWS - 1), (1, 0)):
        packed = wide(pot[1, at : at + 1, :])
        for x in range(1, 8):
            packed = jnp.where(row_at == x, wide(pot[x + 1, at : at + 1, :]), packed)
        send_y[side, 0] = packed
    wait = exchange(
        [
            (pot.at[8], pot.at[0]),
            (pot.at[1], pot.at[9]),
            (send_y.at[0, 0], pot_y.at[0]),
            (send_y.at[1, 0], pot_y.at[1]),
        ]
    )
    for name in ("rates", "region", "contact", "coup"):
        loads[name].wait()

    def put_faces(x, first, near):
        here = pot[x + 1]
        for k, value in enumerate(near):
            plus, minus = face_weights(here - value)
            weights[0][x, 3 * (first + k)] = jnp.ones(tile, jnp.float32)
            weights[0][x, 3 * (first + k) + 1] = plus
            weights[0][x, 3 * (first + k) + 2] = minus

    def set_up(x):
        here = pot[x + 1]
        near = (
            jnp.where(lane_at == lanes - 1, 0.0, along(here, -1)),
            jnp.where(lane_at == 0, 0.0, along(here, 1)),
        )
        put_faces(x, 4, near)
        at_contact = STRENGTH * contact[x].astype(jnp.float32)
        regions = region[x]
        for c in range(3):
            extra = jnp.full(tile, rates[0, c])
            for pick in range(1, REGIONS):
                extra = jnp.where(regions == pick, rates[pick, c], extra)
            for d in range(3):
                value = coup[c, d, x]
                reaction[0][x, 3 * c + d] = value + (extra + at_contact) if c == d else value

    each(NX[0], set_up)
    wait()
    is_low_x, is_high_x = gx == 0, gx == n_x - 1
    is_low_y, is_high_y = gy == 0, gy == n_y - 1
    pot[0] = jnp.where(is_low_x, 0.0, pot[0])
    pot[9] = jnp.where(is_high_x, 0.0, pot[9])
    pot_y[0] = jnp.where(is_low_y, 0.0, pot_y[0])
    pot_y[1] = jnp.where(is_high_y, 0.0, pot_y[1])

    def cross_faces(x):
        here = pot[x + 1]
        near = (
            pot[x + 2],
            pot[x],
            jnp.where(row_at == ROWS - 1, wide(pot_y[1, pl.ds(x, 1), :]), down(here, -1)),
            jnp.where(row_at == 0, wide(pot_y[0, pl.ds(x, 1), :]), down(here, 1)),
        )
        put_faces(x, 0, near)

    each(NX[0], cross_faces)

    def finish(w, r, diagonal, inv, count):
        def body(x):
            m = [[r[x, 3 * col + row] for col in range(3)] for row in range(3)]
            for c in range(3):
                total = w[x, c]
                for k in range(1, 6):
                    total = total + w[x, 3 * k + c]
                m[c][c] = m[c][c] + total
                diagonal[x, c] = m[c][c]

            def cofactor(i, j):
                i1, i2, j1, j2 = (i + 1) % 3, (i + 2) % 3, (j + 1) % 3, (j + 2) % 3
                return m[i1][j1] * m[i2][j2] - m[i1][j2] * m[i2][j1]

            cof = [[cofactor(i, j) for j in range(3)] for i in range(3)]
            det = m[0][0] * cof[0][0] + m[0][1] * cof[0][1] + m[0][2] * cof[0][2]
            scale = OMEGA / det
            for i in range(3):
                for j in range(3):
                    inv[x, 3 * i + j] = cof[j][i] * scale

        each(count, body)

    def finish_level(level):
        finish(weights[level], reaction[level], diag[level], inverse[level], NX[level])

    def mask_level(level):
        w, span, last = weights[level], 1 << level, NX[level] - 1
        for c in range(3):
            w[last, c] = jnp.where(is_high_x, 0.0, w[last, c])
            w[0, 3 + c] = jnp.where(is_low_x, 0.0, w[0, 3 + c])
        off_high = jnp.logical_and(row_at >= ROWS - span, is_high_y)
        off_low = jnp.logical_and(row_at < span, is_low_y)
        off_up, off_down = lane_at >= lanes - span, lane_at < span

        def body(x):
            for k, off in ((2, off_high), (3, off_low), (4, off_up), (5, off_down)):
                for c in range(3):
                    w[x, 3 * k + c] = jnp.where(off, 0.0, w[x, 3 * k + c])

        each(NX[level], body)

    def pair_tools(level):
        span = 1 << level
        odd_row = (row_at & span) != 0
        odd_lane = (lane_at & span) != 0

        def high_row(v):
            return jnp.where(odd_row, v, down(v, -span))

        def low_row(v):
            return jnp.where(odd_row, down(v, span), v)

        def high_lane(v):
            return jnp.where(odd_lane, v, along(v, -span))

        def low_lane(v):
            return jnp.where(odd_lane, along(v, span), v)

        def rows(v):
            return v + jnp.where(odd_row, down(v, span), down(v, -span))

        def lanes_(v):
            return v + jnp.where(odd_lane, along(v, span), along(v, -span))

        return high_row, low_row, high_lane, low_lane, rows, lanes_

    def coarsen(level):
        high_row, low_row, high_lane, low_lane, rows, lanes_ = pair_tools(level)
        w, r = weights[level], reaction[level]
        w_next, r_next = (w_own, r_own) if level == LEVELS - 2 else (weights[level + 1], reaction[level + 1])

        def body(x):
            for c in range(3):
                w_next[x, c] = lanes_(rows(w[2 * x + 1, c]))
                w_next[x, 3 + c] = lanes_(rows(w[2 * x, 3 + c]))
                pair = lambda k: w[2 * x, 3 * k + c] + w[2 * x + 1, 3 * k + c]
                w_next[x, 6 + c] = lanes_(high_row(pair(2)))
                w_next[x, 9 + c] = lanes_(low_row(pair(3)))
                w_next[x, 12 + c] = high_lane(rows(pair(4)))
                w_next[x, 15 + c] = low_lane(rows(pair(5)))
            for i in range(9):
                r_next[x, i] = lanes_(rows(r[2 * x, i] + r[2 * x + 1, i]))

        each(NX[level + 1], body)

    slot_at = lane_at & (SLOTS - 1)
    x_at, y_at = row_at + (gx - RADIUS), slot_at + (gy - RADIUS)
    x_last = jnp.logical_or(x_at == n_x - 1, x_at == -1)
    x_first = jnp.logical_or(x_at == 0, x_at == n_x)
    y_last = jnp.logical_or(y_at == n_y - 1, y_at == -1)
    y_first = jnp.logical_or(y_at == 0, y_at == n_y)
    z_last, z_first = lane_at >= lanes - SLOTS, lane_at < SLOTS
    offs = (x_last, x_first, y_last, y_first, z_last, z_first)
    bits = (2, 2, 1, 1, 4, 4)

    def transposed(tiles):
        tiles = list(tiles)
        for bit in (1, 2, 4):
            clear = (slot_at & bit) == 0
            for p in range(SLOTS):
                if not p & bit:
                    one, two = tiles[p], tiles[p | bit]
                    tiles[p] = jnp.where(clear, one, along(two, bit))
                    tiles[p | bit] = jnp.where(clear, along(one, -bit), two)
        return tiles

    def unpacked(offsets, row_of, own, fill=0.0):
        tiles = [jnp.full(tile, fill) for _ in range(SLOTS)]
        for n, (i, j) in enumerate(list(offsets) + OWN):
            if min(i, j) >= -RADIUS:
                row = row_of(n) if n < len(offsets) else own
                tiles[j + RADIUS] = jnp.where(row_at == i + RADIUS, wide(row), tiles[j + RADIUS])
        return transposed(tiles)

    def child_row(f, x0, c):
        which = slot_at & 3
        rows = [wide(f[x0 + p // 2, c, 4 * (p % 2) : 4 * (p % 2) + 1, :]) for p in range(4)]
        packed = jnp.where(which == 0, rows[0], jnp.where(which == 1, rows[1], jnp.where(which == 2, rows[2], rows[3])))
        return packed[0:1, :]

    def slot_row(values):
        packed = values[0]
        for i in range(1, len(values)):
            packed = jnp.where(slot_at == i, values[i], packed)
        return packed

    def send_coefficients():
        for i in range(27):
            mid_send[i] = child_row(weights[2] if i < 18 else reaction[2], 0, i if i < 18 else i - 18)
        return gather(INNER, lambda o: mid_send, mid_recv, mid_send_sem, mid_recv_sem)

    def send_low_coefficients():
        fields_ = [w_own[0, i] for i in range(18)] + [r_own[0, i] for i in range(9)]
        for row in range(4):
            low_send[row : row + 1, :] = slot_row(fields_[SLOTS * row : SLOTS * row + SLOTS])[0:1, :]
        return gather(FOURTH, lambda o: low_send, low_recv, low_send_sem, low_recv_sem)

    def take_coefficients(waits):
        for wait in waits:
            wait()
        for i in range(27):
            made = unpacked(INNER, lambda n: mid_recv[n, i], mid_send[i], 1.0 if i in (18, 22, 26) else 0.0)
            for p in range(SLOTS):
                if i < 18:
                    w_wide[p, i] = made[p]
                else:
                    r_wide[p, i - 18] = made[p]
        finish(w_wide, r_wide, diag_wide, inverse_wide, SLOTS)
        for k in range(6):
            for p in range(SLOTS):
                if ((p & bits[k]) != 0) == (k % 2 == 0):
                    for c in range(3):
                        w_wide[p, 3 * k + c] = jnp.where(offs[k], 0.0, w_wide[p, 3 * k + c])
        top = LEVELS - 1
        w, r = weights[top], reaction[top]
        for row in range(4):
            here = slice(row, row + 1)
            made = unpacked(FOURTH, lambda n: low_recv[n, here, :], low_send[here, :])
            for p in range(SLOTS):
                i = SLOTS * row + p
                if i < 18:
                    w[0, i] = made[p]
                elif i < 27:
                    r[0, i - 18] = made[p]
        finish_level(top)
        for k in range(6):
            for c in range(3):
                w[0, 3 * k + c] = jnp.where(offs[k], 0.0, w[0, 3 * k + c])

    def spread(value, t):
        value = jnp.where(slot_at == t, value, 0.0)
        for bit in (1, 2, 4):
            value = value + along(value, -bit if t & bit else bit)
        return value

    def wide_residual(p, u):
        left = []
        for c in range(3):
            value = b_wide[p, c] - diag_wide[p, c] * u[p][c]
            for k in range(6):
                bit, ahead = bits[k], k % 2 == 0
                near = u[p ^ bit][c]
                if ((p & bit) != 0) == ahead:
                    turn = -1 if ahead else 1
                    near = down(near, turn) if k < 2 else along(near, turn if k < 4 else turn * SLOTS)
                value = value + w_wide[p, 3 * k + c] * near
            for d in range(3):
                if d != c:
                    value = value - r_wide[p, 3 * d + c] * u[p][d]
            left.append(value)
        return left

    def apply_inverse(v, x, r):
        return [v[x, 3 * c] * r[0] + v[x, 3 * c + 1] * r[1] + v[x, 3 * c + 2] * r[2] for c in range(3)]

    def wide_fields():
        return [[u_wide[p, c] for c in range(3)] for p in range(SLOTS)]

    def window_sweep(b, u, patches=None):
        top = LEVELS - 1
        w, r = weights[top], reaction[top]
        left = []
        for c in range(3):
            value = b[c] - diag[top][0, c] * u[c]
            before_x, before_y = down(u[c], 1), along(u[c], 1)
            if patches is not None:
                before_x = jnp.where(row_at == 0, patches[0][c], before_x)
                before_y = jnp.where(slot_at == 0, patches[1][c], before_y)
            near = (down(u[c], -1), before_x, along(u[c], -1), before_y, along(u[c], -SLOTS), along(u[c], SLOTS))
            for k in range(6):
                value = value + w[0, 3 * k + c] * near[k]
            for d in range(3):
                if d != c:
                    value = value - r[0, 3 * d + c] * u[d]
            left.append(value)
        step = apply_inverse(inverse[top], 0, left)
        return [u[c] + step[c] for c in range(3)]

    def lower(turn, beside_p, beside_q):
        for c in range(3):
            mid_cell[0, c] = child_row(sources[2], 0, c)
            mid_cell[1, c] = child_row(fields[2].at[0], 1, c)
        near = INNER + OUTER
        wait = gather(
            near, lambda o: mid_cell.at[0 if o in INNER else 1], mid_cells.at[turn], p_send, p_recv.at[turn]
        )
        beside_p()
        wait()
        for c in range(3):
            made = unpacked(near, lambda n: mid_cells[turn, n, c], mid_cell[0, c])
            for p in range(SLOTS):
                b_wide[p, c] = made[p]
        inner = jnp.abs(row_at - RADIUS) + jnp.abs(slot_at - RADIUS) <= 2
        for p in range(SLOTS):
            b = [b_wide[p, c] for c in range(3)]
            first = apply_inverse(inverse_wide, p, b)
            for c in range(3):
                u_wide[p, c] = jnp.where(inner, first[c], b[c])
        u_mid = wide_fields()
        b = [jnp.zeros(tile, jnp.float32) for _ in range(3)]
        for p in range(SLOTS):
            left = wide_residual(p, u_mid)
            b = [b[c] + left[c] for c in range(3)]
        u = apply_inverse(inverse[LEVELS - 1], 0, b)
        for _ in range(2):
            u = window_sweep(b, u)
        row = slot_row([spread(value, RADIUS) for value in u + b])
        low_cell[0] = row[RADIUS : RADIUS + 1, :]
        wait = gather(THIRD, lambda o: low_cell.at[0], low_cells.at[turn], q_send, q_recv.at[turn])
        beside_q()
        wait()
        made = unpacked(THIRD, lambda n: low_cells[turn, n], low_cell[0])
        u, b = made[:3], made[3:6]
        before_x = [jnp.zeros(tile, jnp.float32) for _ in range(3)]
        last_y = jnp.zeros(tile, jnp.float32)
        for n, (i, j) in enumerate(THIRD):
            if i < -RADIUS:
                for c in range(3):
                    value = along(wide(low_cells[turn, n]), j + RADIUS - c)
                    before_x[c] = jnp.where(slot_at == j + RADIUS, value, before_x[c])
            if j < -RADIUS:
                last_y = jnp.where(row_at == i + RADIUS, wide(low_cells[turn, n]), last_y)
        before_y = [along(last_y, -c) for c in range(3)]
        u = window_sweep(b, u, (before_x, before_y))
        for _ in range(COARSE_SWEEPS - 4):
            u = window_sweep(b, u)
        u_mid = [[u_wide[p, c] + u[c] for c in range(3)] for p in range(SLOTS)]
        last = []
        for p in range(SLOTS):
            step = apply_inverse(inverse_wide, p, wide_residual(p, u_mid))
            last.append([u_mid[p][c] + step[c] for c in range(3)])
        for c in range(3):
            for x in range(2):
                for at, (t, y) in enumerate(((RADIUS - 1, 1), (RADIUS, 0), (RADIUS, 1), (RADIUS + 1, 0))):
                    low, high = last[2 * x + y][c], last[4 + 2 * x + y][c]
                    if t & 4:
                        value = jnp.where(slot_at == t, high, 0.0) + along(jnp.where(slot_at == t, low, 0.0), -4)
                    else:
                        value = jnp.where(slot_at == t, low, 0.0) + along(jnp.where(slot_at == t, high, 0.0), 4)
                    for bit in (1, 2):
                        value = value + along(value, -bit if t & bit else bit)
                    e_rows[x, at, c] = value

    def mid_at(c, x, y):
        row = RADIUS + (x // 2)
        return wide(e_rows[x % 2, y + 1, c, row : row + 1, :])

    odd = (lane_at & 1) != 0

    def even_part(v):
        return jnp.where(odd, along(v, 1), v)

    def odd_part(v):
        return jnp.where(odd, v, along(v, -1))

    def rows_tile(rows):
        made = jnp.zeros(tile, jnp.float32)
        for at, value in rows:
            made = jnp.where(row_at == at, wide(value), made)
        return made

    def pair_up():
        for x in range(4):
            for j in range(14):
                part = [weights[1][x, i] if i < 18 else reaction[1][x, i - 18] for i in (2 * j, 2 * j + 1) if i < 27]
                coef_own[x, j] = jnp.where(odd, part[-1], part[0])
        for side, y in ((0, 6), (1, 0)):
            for j in range(0, 14, 2):
                rows = [(4 * i + x, coef_own[x, j + i, y : y + 1, :]) for i in range(2) for x in range(4)]
                coef_y_send[side, j // 2] = rows_tile(rows)

    def send_ring_coefficients():
        copies = []
        for side, turn in ((0, 1), (1, -1)):
            sems = lambda n: (coef_send_sem.at[n], coef_recv_sem.at[n])
            copies.append(remote(coef_y_send.at[side], coef_y.at[side], *sems(side), (0, turn)))
            copies.append(remote(coef_own.at[3 - 3 * side], coef_x.at[side], *sems(2 + side), (turn, 0)))
        return copies

    def take_ring_coefficients(copies):
        for copy in copies:
            copy.wait()
        for p in range(6):
            edge = 2 if p in (0, 5) else 1
            filled = jnp.logical_and(row_at >= edge, row_at < ROWS - edge)
            for j in range(14):
                if p in (0, 5):
                    rows = [(2 + k, coef_x[p // 5, j, 2 * k : 2 * k + 1, :]) for k in range(4)]
                else:
                    x = p - 1
                    rows = [(2 + k, coef_own[x, j, 2 * k : 2 * k + 1, :]) for k in range(4)]
                    at = 4 * (j % 2) + x
                    rows += [(1, coef_y[0, j // 2, at : at + 1, :]), (6, coef_y[1, j // 2, at : at + 1, :])]
                both = rows_tile(rows)
                for i, value in ((2 * j, even_part(both)), (2 * j + 1, odd_part(both))):
                    if i < 18:
                        ring_w[p, i] = value
                    elif i < 27:
                        ring_r[p, i - 18] = jnp.where(filled, value, 1.0) if i in (18, 22, 26) else value
        finish(ring_w, ring_r, ring_diag, ring_inverse, 6)
        off_high = jnp.logical_and(row_at == 5, is_high_y)
        off_low = jnp.logical_and(row_at == 2, is_low_y)
        for c in range(3):
            ring_w[4, c] = jnp.where(is_high_x, 0.0, ring_w[4, c])
            ring_w[1, 3 + c] = jnp.where(is_low_x, 0.0, ring_w[1, 3 + c])

        def body(p):
            for k, off in ((2, off_high), (3, off_low), (4, lane_at >= lanes - 2), (5, lane_at < 2)):
                for c in range(3):
                    ring_w[p, 3 * k + c] = jnp.where(off, 0.0, ring_w[p, 3 * k + c])

        each(6, body)

    def send_pairs(turn):
        for x in range(4):
            for c in range(3):
                pair_own[x, c] = jnp.where(odd, sources[1][x, c], fields[1][0, x + 1, c])
        for side, y in ((0, 4), (1, 0)):
            for c in range(3):
                rows = [(2 * x + k, pair_own[x, c, y + 2 * k : y + 2 * k + 1, :]) for x in range(4) for k in range(2)]
                pair_y_send[side, c] = rows_tile(rows)
        for sx in range(2):
            for sy in range(2):
                x, y = 3 - 3 * sx, 6 - 6 * sy
                for c in range(3):
                    pair_corner_send[2 * sx + sy, c : c + 1, :] = pair_own[x, c, y : y + 1, :]
        copies = []
        sems = lambda n: (pair_send_sem.at[n], pair_recv_sem.at[turn, n])
        for side, to in ((0, 1), (1, -1)):
            copies.append(remote(pair_y_send.at[side], pair_y.at[turn, side], *sems(side), (0, to)))
            source = pair_own.at[pl.ds(2 - 2 * side, 2)]
            copies.append(remote(source, pair_x.at[turn, side], *sems(2 + side), (to, 0)))
        for sx in range(2):
            for sy in range(2):
                n = 2 * sx + sy
                to = (1 - 2 * sx, 1 - 2 * sy)
                copies.append(remote(pair_corner_send.at[n], pair_corner.at[turn, n], *sems(4 + n), to))
        return copies

    def take_pairs(turn, copies):
        for copy in copies:
            copy.wait()
        for p in range(8):
            for c in range(3):
                if 2 <= p < 6:
                    x = p - 2
                    rows = [(2 + k, pair_own[x, c, 2 * k : 2 * k + 1, :]) for k in range(4)]
                    for side in range(2):
                        for k in range(2):
                            at = 2 * x + k
                            rows.append((6 * side + k, pair_y[turn, side, c, at : at + 1, :]))
                else:
                    side = p // 4
                    rows = [(2 + k, pair_x[turn, side, p - 6 * side, c, 2 * k : 2 * k + 1, :]) for k in range(4)]
                    if p in (1, 6):
                        for sy in range(2):
                            rows.append((1 + 5 * sy, pair_corner[turn, 2 * side + sy, c : c + 1, :]))
                both = rows_tile(rows)
                ring_u[p, c] = even_part(both)
                if 1 <= p < 7:
                    ring_b[p - 1, c] = odd_part(both)

    def ring_sweep():
        def add(p):
            x = p // 2 - 1
            for c in range(3):
                e = jnp.where(row_at < 2, mid_at(c, x, -1), mid_at(c, x, 0))
                e = jnp.where(row_at < 4, e, jnp.where(row_at < 6, mid_at(c, x, 1), mid_at(c, x, 2)))
                ring_u[p, c] += e

        for p in range(8):
            add(p)
        for p in range(6):
            u = [ring_u[p + 1, c] for c in range(3)]
            left = []
            for c in range(3):
                value = ring_b[p, c] - ring_diag[p, c] * u[c]
                near = (ring_u[p + 2, c], ring_u[p, c], down(u[c], -1), down(u[c], 1), along(u[c], -2), along(u[c], 2))
                for k in range(6):
                    value = value + ring_w[p, 3 * k + c] * near[k]
                for d in range(3):
                    if d != c:
                        value = value - ring_r[p, 3 * d + c] * u[d]
                left.append(value)
            step = apply_inverse(ring_inverse, p, left)
            for c in range(3):
                ring_out[p, c] = u[c] + step[c]

    def add_to_finest(at, slot):
        f = fields[0]
        for c in range(3):
            for p in range(6):
                rows = [wide(ring_out[p, c, 2 + k : 3 + k, :]) for k in range(4)]
                e = jnp.where(row_at < 2, rows[0], rows[1])
                e = jnp.where(row_at < 4, e, jnp.where(row_at < 6, rows[2], rows[3]))
                for x in {0: (-1,), 5: (8,)}.get(p, (2 * p - 2, 2 * p - 1)):
                    f[at, x + 1, c] += e
            for side, row in ((0, 1), (1, 6)):
                rows = [wide(ring_out[1 + k, c, row : row + 1, :]) for k in range(4)]
                e = jnp.where(row_at < 2, rows[0], rows[1])
                e = jnp.where(row_at < 4, e, jnp.where(row_at < 6, rows[2], rows[3]))
                rows_halo[slot, side, c] += e

    def source(level, x):
        if level == 0:
            return [grad[c, x] for c in range(3)]
        return [sources[level][x, c] for c in range(3)]

    def solve(level, x, r):
        v = inverse[level]
        return [v[x, 3 * c] * r[0] + v[x, 3 * c + 1] * r[1] + v[x, 3 * c + 2] * r[2] for c in range(3)]

    def share(level, at, beside_it=lambda: None):
        slot, f, count = done[0] % 3, fields[level], NX[level]
        for side, row in ((0, ROWS - 1), (1, 0)):
            for c in range(3):
                packed = wide(f[at, 1, c, row : row + 1, :])
                for x in range(1, count):
                    packed = jnp.where(row_at == x, wide(f[at, x + 1, c, row : row + 1, :]), packed)
                send_y[side, c] = packed
        wait = exchange(
            [
                (f.at[at, count], f.at[at, 0]),
                (f.at[at, 1], f.at[at, count + 1]),
                (send_y.at[0], rows_halo.at[slot, 0]),
                (send_y.at[1], rows_halo.at[slot, 1]),
            ]
        )
        beside_it()
        inner(level, at)
        wait()
        return slot

    def inner(level, at):
        f, w, r, span, count = fields[level], weights[level], reaction[level], 1 << level, NX[level]
        for x in range(count):
            u = [f[at, x + 1, c] for c in range(3)]
            b = source(level, x)
            for c in range(3):
                value = b[c] - diag[level][x, c] * u[c]
                value = value + w[x, 6 + c] * jnp.where(row_at >= ROWS - span, 0.0, down(u[c], -span))
                value = value + w[x, 9 + c] * jnp.where(row_at < span, 0.0, down(u[c], span))
                value = value + w[x, 12 + c] * along(u[c], -span) + w[x, 15 + c] * along(u[c], span)
                if x < count - 1:
                    value = value + w[x, c] * f[at, x + 2, c]
                if x > 0:
                    value = value + w[x, 3 + c] * f[at, x, c]
                for d in range(3):
                    if d != c:
                        value = value - r[x, 3 * d + c] * u[d]
                part[x, c] = value

    def rest(level, at, slot, x):
        f, w, span, count = fields[level], weights[level], 1 << level, NX[level]
        left = []
        for c in range(3):
            row_high, row_low = (rows_halo[slot, side, c, x : x + 1, :] for side in (1, 0))
            value = jnp.where(row_at >= ROWS - span, w[x, 6 + c] * wide(row_high), 0.0)
            value = part[x, c] + jnp.where(row_at < span, w[x, 9 + c] * wide(row_low), value)
            if x == 0:
                value = value + w[x, 3 + c] * f[at, 0, c]
            if x == count - 1:
                value = value + w[x, c] * f[at, count + 1, c]
            left.append(value)
        return [f[at, x + 1, c] for c in range(3)], left

    def residual(level, at, slot, x):
        f, w, r, span = fields[level], weights[level], reaction[level], 1 << level
        u = [f[at, x + 1, c] for c in range(3)]
        b = source(level, x)
        left = []
        for c in range(3):
            near = (
                f[at, x + 2, c],
                f[at, x, c],
                jnp.where(row_at >= ROWS - span, wide(rows_halo[slot, 1, c, x : x + 1, :]), down(u[c], -span)),
                jnp.where(row_at < span, wide(rows_halo[slot, 0, c, x : x + 1, :]), down(u[c], span)),
                along(u[c], -span),
                along(u[c], span),
            )
            value = b[c] - diag[level][x, c] * u[c]
            for k in range(6):
                value = value + w[x, 3 * k + c] * near[k]
            for d in range(3):
                if d != c:
                    value = value - r[x, 3 * d + c] * u[d]
            left.append(value)
        return u, left

    def sweep(at, slot, left_of, last=False):
        for x in range(NX[0]):
            u, left = left_of(0, at, slot, x)
            step = solve(0, x, left)
            for c in range(3):
                if last:
                    out[c, x] = u[c] + step[c]
                else:
                    fields[0][1 - at, x + 1, c] = u[c] + step[c]
        return 1 - at

    def restrict(level, at, slot):
        rows, lanes_ = pair_tools(level)[4:]
        for x in range(NX[level + 1]):
            left = [rest(level, at, slot, 2 * x + i)[1] for i in range(2)]
            total = [lanes_(rows(left[0][c] + left[1][c])) for c in range(3)]
            first = solve(level + 1, x, total)
            for c in range(3):
                sources[level + 1][x, c] = total[c]
                fields[level + 1][0, x + 1, c] = first[c]

    def cycle(at, turn, besides, last=False):
        slot = share(0, at, besides[0])
        restrict(0, at, slot)
        pairs = []

        def beside():
            pairs.extend(send_pairs(turn))
            besides[1]()

        restrict(1, 0, share(1, 0, beside))

        def beside_q():
            take_pairs(turn, pairs)
            besides[3]()

        lower(turn, besides[2], beside_q)
        ring_sweep()
        add_to_finest(at, slot)
        return sweep(at, slot, residual, last)

    def start(x):
        for c, value in enumerate(solve(0, x, source(0, x))):
            fields[0][0, x + 1, c] = value

    finish_level(0)
    loads["grad"].wait()
    each(NX[0], start)
    pending, ring_pending = [], []

    def beside_first():
        coarsen(0)
        mask_level(0)
        finish_level(1)
        coarsen(1)
        pending.append(send_coefficients())

    def beside_second():
        pair_up()
        ring_pending.extend(send_ring_coefficients())
        mask_level(1)
        finish_level(2)
        coarsen(2)
        pending.append(send_low_coefficients())

    nothing = lambda: None
    at = cycle(
        0,
        0,
        (
            beside_first,
            beside_second,
            lambda: take_coefficients(pending),
            lambda: take_ring_coefficients(ring_pending),
        ),
    )
    at = sweep(at, share(0, at), rest)
    cycle(at, 1, (nothing,) * 4, last=True)


def local(counts, gradient, potential, coupling, region, contact, rates):
    nz = potential.shape[-1]
    tile = (ROWS, nz)
    f32 = jnp.float32
    scratch = []
    for parts in (18, 9, 3, 9):
        scratch += [pltpu.VMEM((n, parts) + tile, f32) for n in NX]
    scratch += [pltpu.VMEM((n, 3) + tile, f32) for n in NX[1:]]
    scratch += [pltpu.VMEM((2, n + 2, 3) + tile, f32) for n in NX]
    scratch += [
        pltpu.VMEM((3, 2, 3) + tile, f32),
        pltpu.VMEM((2,) + tile, f32),
        pltpu.VMEM((2, 3) + tile, f32),
        pltpu.SemaphoreType.DMA((4,)),
        pltpu.SemaphoreType.DMA((3, 4)),
        pltpu.VMEM((1, 18) + tile, f32),
        pltpu.VMEM((1, 9) + tile, f32),
        pltpu.VMEM((SLOTS, 18) + tile, f32),
        pltpu.VMEM((SLOTS, 9) + tile, f32),
        pltpu.VMEM((SLOTS, 3) + tile, f32),
        pltpu.VMEM((SLOTS, 9) + tile, f32),
        pltpu.VMEM((SLOTS, 3) + tile, f32),
        pltpu.VMEM((SLOTS, 3) + tile, f32),
        pltpu.VMEM((2, 4, 3) + tile, f32),
        pltpu.VMEM((27, 1, nz), f32),
        pltpu.VMEM((len(INNER), 27, 1, nz), f32),
        pltpu.VMEM((4, nz), f32),
        pltpu.VMEM((len(FOURTH), 4, nz), f32),
        pltpu.VMEM((2, 3, 1, nz), f32),
        pltpu.VMEM((2, len(INNER + OUTER), 3, 1, nz), f32),
        pltpu.VMEM((1, 1, nz), f32),
        pltpu.VMEM((2, len(THIRD), 1, nz), f32),
        pltpu.SemaphoreType.DMA,
        pltpu.SemaphoreType.DMA,
        pltpu.SemaphoreType.DMA,
        pltpu.SemaphoreType.DMA,
        pltpu.SemaphoreType.DMA,
        pltpu.SemaphoreType.DMA((2,)),
        pltpu.SemaphoreType.DMA,
        pltpu.SemaphoreType.DMA((2,)),
        pltpu.VMEM((8, 3) + tile, f32),
        pltpu.VMEM((6, 3) + tile, f32),
        pltpu.VMEM((6, 18) + tile, f32),
        pltpu.VMEM((6, 9) + tile, f32),
        pltpu.VMEM((6, 3) + tile, f32),
        pltpu.VMEM((6, 9) + tile, f32),
        pltpu.VMEM((6, 3) + tile, f32),
        pltpu.VMEM((4, 3) + tile, f32),
        pltpu.VMEM((2, 2, 2, 3) + tile, f32),
        pltpu.VMEM((2, 3) + tile, f32),
        pltpu.VMEM((2, 2, 3) + tile, f32),
        pltpu.VMEM((4, 4, nz), f32),
        pltpu.VMEM((2, 4, 4, nz), f32),
        pltpu.SemaphoreType.DMA((8,)),
        pltpu.SemaphoreType.DMA((2, 8)),
        pltpu.VMEM((4, 14) + tile, f32),
        pltpu.VMEM((2, 14) + tile, f32),
        pltpu.VMEM((2, 7) + tile, f32),
        pltpu.VMEM((2, 7) + tile, f32),
        pltpu.SemaphoreType.DMA((4,)),
        pltpu.SemaphoreType.DMA((4,)),
        pltpu.VMEM((NX[0], 3) + tile, f32),
        pltpu.VMEM(gradient.shape, f32),
        pltpu.VMEM((10,) + tile, f32),
        pltpu.VMEM(coupling.shape, f32),
        pltpu.VMEM(region.shape, jnp.int32),
        pltpu.VMEM(contact.shape, jnp.int32),
        pltpu.SMEM(rates.shape, f32),
        pltpu.SemaphoreType.DMA((6,)),
    ]
    vmem = pl.BlockSpec(memory_space=pltpu.VMEM)
    return pl.pallas_call(
        functools.partial(kernel, counts),
        out_shape=jax.ShapeDtypeStruct(gradient.shape, f32),
        in_specs=[pl.BlockSpec(memory_space=pltpu.HBM)] * 6,
        out_specs=vmem,
        scratch_shapes=scratch,
        compiler_params=pltpu.CompilerParams(
            collective_id=0, has_side_effects=True, vmem_limit_bytes=60 * 1024 * 1024
        ),
    )(gradient, potential, coupling, region, contact, rates)


def solution(mesh):
    placed = (
        P(None, "gx", "gy", None),
        P("gx", "gy", None),
        P(None, None, "gx", "gy", None),
        P("gx", "gy", None),
        P("gx", "gy", None),
        P(),
    )
    counts = (mesh.shape["gx"], mesh.shape["gy"])
    return jax.shard_map(
        functools.partial(local, counts),
        mesh=mesh,
        in_specs=placed,
        out_specs=P(None, "gx", "gy", None),
        check_vma=False,
    )
```

```python
import functools

import jax
import jax.numpy as jnp
from jax import lax
from jax.experimental import pallas as pl
from jax.experimental.pallas import tpu as pltpu
from jax.sharding import PartitionSpec as P

MESH = pl.DeviceIdType.MESH
LEVELS = 4
COARSE_SWEEPS = 6
REGIONS = 4
OMEGA = 0.8
STRENGTH = 8.0
ROWS = 8
NX = (8, 4, 2, 1)
RADIUS = 3
SLOTS = 8


def around(shape, far):
    reach = range(-6, 7)
    distance = lambda i, j: min(abs(i - a) + abs(j - b) for a, b in shape)
    found = [(i, j) for i in reach for j in reach if distance(i, j) <= far and (i, j) != (0, 0)]
    return sorted(found, key=lambda o: -abs(o[0]) - abs(o[1]))


OWN = [(0, 0)]
SQUARE = [(i, j) for i in (-1, 0, 1) for j in (-1, 0, 1)]
INNER = around(OWN, 2)
OUTER = [o for o in around(OWN, 3) if o not in INNER]
FOURTH = around(SQUARE, 2)
THIRD = around(SQUARE, 3)


def each(count, body):
    if count == 1:
        body(0)
        return

    def step(i, carry):
        body(i)
        return carry

    lax.fori_loop(0, count, step, 0, unroll=count)


def face_weights(difference):
    size = jnp.abs(difference)
    small = size < 0.5
    series = 1.0 / 362880.0
    for k in (40320.0, 5040.0, 720.0, 120.0, 24.0, 6.0, 2.0, 1.0):
        series = series * size + 1.0 / k
    below = jnp.where(small, series, jnp.exp(size) - 1.0)
    low = jnp.where(small, 1.0, size) / below
    low = jnp.where(size < 1e-4, 1.0 - 0.5 * size, low)
    high = low + size
    positive = difference > 0.0
    return jnp.where(positive, low, high), jnp.where(positive, high, low)


def kernel(counts, grad_in, pot_in, coup_in, region_in, contact_in, rates_in, out, *scratch):
    grad, pot, coup, region, contact, rates, in_sem = scratch[-7:]
    scratch = scratch[:-7]
    loads = {}
    for i, (name, source, target) in enumerate(
        (
            ("pot", pot_in, pot.at[pl.ds(1, 8)]),
            ("rates", rates_in, rates),
            ("region", region_in, region),
            ("contact", contact_in, contact),
            ("coup", coup_in, coup),
            ("grad", grad_in, grad),
        )
    ):
        loads[name] = pltpu.make_async_copy(source, target, in_sem.at[i])
        loads[name].start()
    weights, reaction, diag, inverse = (scratch[4 * i : 4 * i + 4] for i in range(4))
    sources = (None,) + tuple(scratch[16:19])
    fields = scratch[19:23]
    rows_halo, pot_y, send_y, send_sem, recv_sem = scratch[23:28]
    w_own, r_own, w_wide, r_wide, diag_wide, inverse_wide, u_wide, b_wide, e_rows = scratch[28:37]
    mid_send, mid_recv, low_send, low_recv, mid_cell, mid_cells, low_cell, low_cells = scratch[37:45]
    mid_send_sem, mid_recv_sem, low_send_sem, low_recv_sem, p_send, p_recv, q_send, q_recv = scratch[45:53]
    ring_u, ring_b, ring_w, ring_r, ring_diag, ring_inverse, ring_out = scratch[53:60]
    pair_own, pair_x, pair_y_send, pair_y, pair_corner_send, pair_corner, pair_send_sem, pair_recv_sem = scratch[60:68]
    coef_own, coef_x, coef_y_send, coef_y, coef_send_sem, coef_recv_sem, part, coef_corner_send, coef_corner = scratch[68:77]
    rim_w, rim_r, rim_diag, rim_inverse, rim_base, rim_pot, rim_pot_corner_send, rim_pot_corner = scratch[77:85]
    base, rim_y_send, rim_y, rim_send_sem, rim_recv_sem = scratch[85:]
    n_x, n_y = counts
    lanes = out.shape[-1]
    gx, gy = lax.axis_index("gx"), lax.axis_index("gy")
    x_low, x_high = lax.rem(gx + n_x - 1, n_x), lax.rem(gx + 1, n_x)
    y_low, y_high = lax.rem(gy + n_y - 1, n_y), lax.rem(gy + 1, n_y)
    beside = ((x_high, gy), (x_low, gy), (gx, y_high), (gx, y_low))

    barrier = pltpu.get_barrier_semaphore()
    at_offset = lambda i, j: (lax.rem(gx + n_x + i, n_x), lax.rem(gy + n_y + j, n_y))
    devices = {o: at_offset(*o) for o in THIRD}
    for offset in INNER:
        pl.semaphore_signal(barrier, inc=1, device_id=devices[offset], device_id_type=MESH)
    pl.semaphore_wait(barrier, len(INNER))

    tile = (ROWS, lanes)
    row_at = lax.broadcasted_iota(jnp.int32, tile, 0)
    lane_at = lax.broadcasted_iota(jnp.int32, tile, 1)
    wide = lambda row: jnp.broadcast_to(row, tile)
    down = lambda v, by: pltpu.roll(v, by % ROWS, 0) if by % ROWS else v
    along = lambda v, by: pltpu.roll(v, by % lanes, 1)

    done = [0]

    def exchange(parts):
        slot = done[0] % 3
        done[0] += 1
        copies = []
        for i in (2, 3, 0, 1):
            source, target = parts[i]
            copy = pltpu.make_async_remote_copy(
                src_ref=source,
                dst_ref=target,
                send_sem=send_sem.at[i],
                recv_sem=recv_sem.at[slot, i],
                device_id=beside[i],
                device_id_type=MESH,
            )
            copy.start()
            copies.append(copy)

        def wait():
            for copy in copies:
                copy.wait()

        return wait

    def remote(source, target, send, recv, offset):
        copy = pltpu.make_async_remote_copy(
            src_ref=source,
            dst_ref=target,
            send_sem=send,
            recv_sem=recv,
            device_id=devices[offset],
            device_id_type=MESH,
        )
        copy.start()
        return copy

    def gather(offsets, source_of, target, send, recv):
        for n, (i, j) in enumerate(offsets):
            remote(source_of((i, j)), target.at[n], send, recv, (-i, -j))

        def wait():
            pltpu.make_async_copy(target, target, send).wait()
            pltpu.make_async_copy(target, target, recv).wait()

        return wait

    loads["pot"].wait()
    for side, at in ((0, ROWS - 1), (1, 0)):
        packed = wide(pot[1, at : at + 1, :])
        for x in range(1, 8):
            packed = jnp.where(row_at == x, wide(pot[x + 1, at : at + 1, :]), packed)
        send_y[side, 0] = packed
    wait = exchange(
        [
            (pot.at[8], pot.at[0]),
            (pot.at[1], pot.at[9]),
            (send_y.at[0, 0], pot_y.at[0]),
            (send_y.at[1, 0], pot_y.at[1]),
        ]
    )
    for name in ("rates", "region", "contact", "coup"):
        loads[name].wait()

    def put_faces(x, first, near):
        here = pot[x + 1]
        for k, value in enumerate(near):
            plus, minus = face_weights(here - value)
            weights[0][x, 3 * (first + k)] = jnp.ones(tile, jnp.float32)
            weights[0][x, 3 * (first + k) + 1] = plus
            weights[0][x, 3 * (first + k) + 2] = minus

    def set_up(x):
        here = pot[x + 1]
        near = (
            jnp.where(lane_at == lanes - 1, 0.0, along(here, -1)),
            jnp.where(lane_at == 0, 0.0, along(here, 1)),
        )
        put_faces(x, 4, near)
        at_contact = STRENGTH * contact[x].astype(jnp.float32)
        regions = region[x]
        for c in range(3):
            extra = jnp.full(tile, rates[0, c])
            for pick in range(1, REGIONS):
                extra = jnp.where(regions == pick, rates[pick, c], extra)
            for d in range(3):
                value = coup[c, d, x]
                reaction[0][x, 3 * c + d] = value + (extra + at_contact) if c == d else value

    each(NX[0], set_up)
    wait()
    is_low_x, is_high_x = gx == 0, gx == n_x - 1
    is_low_y, is_high_y = gy == 0, gy == n_y - 1
    pot[0] = jnp.where(is_low_x, 0.0, pot[0])
    pot[9] = jnp.where(is_high_x, 0.0, pot[9])
    pot_y[0] = jnp.where(is_low_y, 0.0, pot_y[0])
    pot_y[1] = jnp.where(is_high_y, 0.0, pot_y[1])

    def cross_faces(x):
        here = pot[x + 1]
        near = (
            pot[x + 2],
            pot[x],
            jnp.where(row_at == ROWS - 1, wide(pot_y[1, pl.ds(x, 1), :]), down(here, -1)),
            jnp.where(row_at == 0, wide(pot_y[0, pl.ds(x, 1), :]), down(here, 1)),
        )
        put_faces(x, 0, near)

    each(NX[0], cross_faces)

    def finish(w, r, diagonal, inv, count):
        def body(x):
            m = [[r[x, 3 * col + row] for col in range(3)] for row in range(3)]
            for c in range(3):
                total = w[x, c]
                for k in range(1, 6):
                    total = total + w[x, 3 * k + c]
                m[c][c] = m[c][c] + total
                diagonal[x, c] = m[c][c]

            def cofactor(i, j):
                i1, i2, j1, j2 = (i + 1) % 3, (i + 2) % 3, (j + 1) % 3, (j + 2) % 3
                return m[i1][j1] * m[i2][j2] - m[i1][j2] * m[i2][j1]

            cof = [[cofactor(i, j) for j in range(3)] for i in range(3)]
            det = m[0][0] * cof[0][0] + m[0][1] * cof[0][1] + m[0][2] * cof[0][2]
            scale = OMEGA / det
            for i in range(3):
                for j in range(3):
                    inv[x, 3 * i + j] = cof[j][i] * scale

        each(count, body)

    def finish_level(level):
        finish(weights[level], reaction[level], diag[level], inverse[level], NX[level])

    def mask_level(level):
        w, span, last = weights[level], 1 << level, NX[level] - 1
        for c in range(3):
            w[last, c] = jnp.where(is_high_x, 0.0, w[last, c])
            w[0, 3 + c] = jnp.where(is_low_x, 0.0, w[0, 3 + c])
        off_high = jnp.logical_and(row_at >= ROWS - span, is_high_y)
        off_low = jnp.logical_and(row_at < span, is_low_y)
        off_up, off_down = lane_at >= lanes - span, lane_at < span

        def body(x):
            for k, off in ((2, off_high), (3, off_low), (4, off_up), (5, off_down)):
                for c in range(3):
                    w[x, 3 * k + c] = jnp.where(off, 0.0, w[x, 3 * k + c])

        each(NX[level], body)

    def pair_tools(level):
        span = 1 << level
        odd_row = (row_at & span) != 0
        odd_lane = (lane_at & span) != 0

        def high_row(v):
            return jnp.where(odd_row, v, down(v, -span))

        def low_row(v):
            return jnp.where(odd_row, down(v, span), v)

        def high_lane(v):
            return jnp.where(odd_lane, v, along(v, -span))

        def low_lane(v):
            return jnp.where(odd_lane, along(v, span), v)

        def rows(v):
            return v + jnp.where(odd_row, down(v, span), down(v, -span))

        def lanes_(v):
            return v + jnp.where(odd_lane, along(v, span), along(v, -span))

        return high_row, low_row, high_lane, low_lane, rows, lanes_

    def coarsen(level):
        high_row, low_row, high_lane, low_lane, rows, lanes_ = pair_tools(level)
        w, r = weights[level], reaction[level]
        w_next, r_next = (w_own, r_own) if level == LEVELS - 2 else (weights[level + 1], reaction[level + 1])

        def body(x):
            for c in range(3):
                w_next[x, c] = lanes_(rows(w[2 * x + 1, c]))
                w_next[x, 3 + c] = lanes_(rows(w[2 * x, 3 + c]))
                pair = lambda k: w[2 * x, 3 * k + c] + w[2 * x + 1, 3 * k + c]
                w_next[x, 6 + c] = lanes_(high_row(pair(2)))
                w_next[x, 9 + c] = lanes_(low_row(pair(3)))
                w_next[x, 12 + c] = high_lane(rows(pair(4)))
                w_next[x, 15 + c] = low_lane(rows(pair(5)))
            for i in range(9):
                r_next[x, i] = lanes_(rows(r[2 * x, i] + r[2 * x + 1, i]))

        each(NX[level + 1], body)

    slot_at = lane_at & (SLOTS - 1)
    x_at, y_at = row_at + (gx - RADIUS), slot_at + (gy - RADIUS)
    x_last = jnp.logical_or(x_at == n_x - 1, x_at == -1)
    x_first = jnp.logical_or(x_at == 0, x_at == n_x)
    y_last = jnp.logical_or(y_at == n_y - 1, y_at == -1)
    y_first = jnp.logical_or(y_at == 0, y_at == n_y)
    z_last, z_first = lane_at >= lanes - SLOTS, lane_at < SLOTS
    offs = (x_last, x_first, y_last, y_first, z_last, z_first)
    bits = (2, 2, 1, 1, 4, 4)

    def transposed(tiles):
        tiles = list(tiles)
        for bit in (1, 2, 4):
            clear = (slot_at & bit) == 0
            for p in range(SLOTS):
                if not p & bit:
                    one, two = tiles[p], tiles[p | bit]
                    tiles[p] = jnp.where(clear, one, along(two, bit))
                    tiles[p | bit] = jnp.where(clear, along(one, -bit), two)
        return tiles

    def unpacked(offsets, row_of, own, fill=0.0):
        tiles = [jnp.full(tile, fill) for _ in range(SLOTS)]
        for n, (i, j) in enumerate(list(offsets) + OWN):
            if min(i, j) >= -RADIUS:
                row = row_of(n) if n < len(offsets) else own
                tiles[j + RADIUS] = jnp.where(row_at == i + RADIUS, wide(row), tiles[j + RADIUS])
        return transposed(tiles)

    def child_row(f, x0, c):
        which = slot_at & 3
        rows = [wide(f[x0 + p // 2, c, 4 * (p % 2) : 4 * (p % 2) + 1, :]) for p in range(4)]
        packed = jnp.where(which == 0, rows[0], jnp.where(which == 1, rows[1], jnp.where(which == 2, rows[2], rows[3])))
        return packed[0:1, :]

    def slot_row(values):
        packed = values[0]
        for i in range(1, len(values)):
            packed = jnp.where(slot_at == i, values[i], packed)
        return packed

    def send_coefficients():
        for i in range(27):
            mid_send[i] = child_row(weights[2] if i < 18 else reaction[2], 0, i if i < 18 else i - 18)
        return gather(INNER, lambda o: mid_send, mid_recv, mid_send_sem, mid_recv_sem)

    def send_low_coefficients():
        fields_ = [w_own[0, i] for i in range(18)] + [r_own[0, i] for i in range(9)]
        for row in range(4):
            low_send[row : row + 1, :] = slot_row(fields_[SLOTS * row : SLOTS * row + SLOTS])[0:1, :]
        return gather(FOURTH, lambda o: low_send, low_recv, low_send_sem, low_recv_sem)

    def take_coefficients(waits):
        for wait in waits:
            wait()
        for i in range(27):
            made = unpacked(INNER, lambda n: mid_recv[n, i], mid_send[i], 1.0 if i in (18, 22, 26) else 0.0)
            for p in range(SLOTS):
                if i < 18:
                    w_wide[p, i] = made[p]
                else:
                    r_wide[p, i - 18] = made[p]
        finish(w_wide, r_wide, diag_wide, inverse_wide, SLOTS)
        for k in range(6):
            for p in range(SLOTS):
                if ((p & bits[k]) != 0) == (k % 2 == 0):
                    for c in range(3):
                        w_wide[p, 3 * k + c] = jnp.where(offs[k], 0.0, w_wide[p, 3 * k + c])
        top = LEVELS - 1
        w, r = weights[top], reaction[top]
        for row in range(4):
            here = slice(row, row + 1)
            made = unpacked(FOURTH, lambda n: low_recv[n, here, :], low_send[here, :])
            for p in range(SLOTS):
                i = SLOTS * row + p
                if i < 18:
                    w[0, i] = made[p]
                elif i < 27:
                    r[0, i - 18] = made[p]
        finish_level(top)
        for k in range(6):
            for c in range(3):
                w[0, 3 * k + c] = jnp.where(offs[k], 0.0, w[0, 3 * k + c])

    def spread(value, t):
        value = jnp.where(slot_at == t, value, 0.0)
        for bit in (1, 2, 4):
            value = value + along(value, -bit if t & bit else bit)
        return value

    def wide_residual(p, u):
        left = []
        for c in range(3):
            value = b_wide[p, c] - diag_wide[p, c] * u[p][c]
            for k in range(6):
                bit, ahead = bits[k], k % 2 == 0
                near = u[p ^ bit][c]
                if ((p & bit) != 0) == ahead:
                    turn = -1 if ahead else 1
                    near = down(near, turn) if k < 2 else along(near, turn if k < 4 else turn * SLOTS)
                value = value + w_wide[p, 3 * k + c] * near
            for d in range(3):
                if d != c:
                    value = value - r_wide[p, 3 * d + c] * u[p][d]
            left.append(value)
        return left

    def apply_inverse(v, x, r):
        return [v[x, 3 * c] * r[0] + v[x, 3 * c + 1] * r[1] + v[x, 3 * c + 2] * r[2] for c in range(3)]

    def wide_fields():
        return [[u_wide[p, c] for c in range(3)] for p in range(SLOTS)]

    def window_sweep(b, u, patches=None):
        top = LEVELS - 1
        w, r = weights[top], reaction[top]
        left = []
        for c in range(3):
            value = b[c] - diag[top][0, c] * u[c]
            before_x, before_y = down(u[c], 1), along(u[c], 1)
            if patches is not None:
                before_x = jnp.where(row_at == 0, patches[0][c], before_x)
                before_y = jnp.where(slot_at == 0, patches[1][c], before_y)
            near = (down(u[c], -1), before_x, along(u[c], -1), before_y, along(u[c], -SLOTS), along(u[c], SLOTS))
            for k in range(6):
                value = value + w[0, 3 * k + c] * near[k]
            for d in range(3):
                if d != c:
                    value = value - r[0, 3 * d + c] * u[d]
            left.append(value)
        step = apply_inverse(inverse[top], 0, left)
        return [u[c] + step[c] for c in range(3)]

    def lower(turn, beside_p, beside_q):
        for c in range(3):
            mid_cell[0, c] = child_row(sources[2], 0, c)
            mid_cell[1, c] = child_row(fields[2].at[0], 1, c)
        near = INNER + OUTER
        wait = gather(
            near, lambda o: mid_cell.at[0 if o in INNER else 1], mid_cells.at[turn], p_send, p_recv.at[turn]
        )
        beside_p()
        wait()
        for c in range(3):
            made = unpacked(near, lambda n: mid_cells[turn, n, c], mid_cell[0, c])
            for p in range(SLOTS):
                b_wide[p, c] = made[p]
        inner = jnp.abs(row_at - RADIUS) + jnp.abs(slot_at - RADIUS) <= 2
        for p in range(SLOTS):
            b = [b_wide[p, c] for c in range(3)]
            first = apply_inverse(inverse_wide, p, b)
            for c in range(3):
                u_wide[p, c] = jnp.where(inner, first[c], b[c])
        u_mid = wide_fields()
        b = [jnp.zeros(tile, jnp.float32) for _ in range(3)]
        for p in range(SLOTS):
            left = wide_residual(p, u_mid)
            b = [b[c] + left[c] for c in range(3)]
        u = apply_inverse(inverse[LEVELS - 1], 0, b)
        for _ in range(2):
            u = window_sweep(b, u)
        row = slot_row([spread(value, RADIUS) for value in u + b])
        low_cell[0] = row[RADIUS : RADIUS + 1, :]
        wait = gather(THIRD, lambda o: low_cell.at[0], low_cells.at[turn], q_send, q_recv.at[turn])
        beside_q()
        wait()
        made = unpacked(THIRD, lambda n: low_cells[turn, n], low_cell[0])
        u, b = made[:3], made[3:6]
        before_x = [jnp.zeros(tile, jnp.float32) for _ in range(3)]
        last_y = jnp.zeros(tile, jnp.float32)
        for n, (i, j) in enumerate(THIRD):
            if i < -RADIUS:
                for c in range(3):
                    value = along(wide(low_cells[turn, n]), j + RADIUS - c)
                    before_x[c] = jnp.where(slot_at == j + RADIUS, value, before_x[c])
            if j < -RADIUS:
                last_y = jnp.where(row_at == i + RADIUS, wide(low_cells[turn, n]), last_y)
        before_y = [along(last_y, -c) for c in range(3)]
        u = window_sweep(b, u, (before_x, before_y))
        for _ in range(COARSE_SWEEPS - 4):
            u = window_sweep(b, u)
        u_mid = [[u_wide[p, c] + u[c] for c in range(3)] for p in range(SLOTS)]
        last = []
        for p in range(SLOTS):
            step = apply_inverse(inverse_wide, p, wide_residual(p, u_mid))
            last.append([u_mid[p][c] + step[c] for c in range(3)])
        for c in range(3):
            for x in range(2):
                for at, (t, y) in enumerate(((RADIUS - 1, 1), (RADIUS, 0), (RADIUS, 1), (RADIUS + 1, 0))):
                    low, high = last[2 * x + y][c], last[4 + 2 * x + y][c]
                    if t & 4:
                        value = jnp.where(slot_at == t, high, 0.0) + along(jnp.where(slot_at == t, low, 0.0), -4)
                    else:
                        value = jnp.where(slot_at == t, low, 0.0) + along(jnp.where(slot_at == t, high, 0.0), 4)
                    for bit in (1, 2):
                        value = value + along(value, -bit if t & bit else bit)
                    e_rows[x, at, c] = value

    def mid_at(c, x, y):
        row = RADIUS + (x // 2)
        return wide(e_rows[x % 2, y + 1, c, row : row + 1, :])

    odd = (lane_at & 1) != 0

    def even_part(v):
        return jnp.where(odd, along(v, 1), v)

    def odd_part(v):
        return jnp.where(odd, v, along(v, -1))

    def rows_tile(rows):
        made = jnp.zeros(tile, jnp.float32)
        for at, value in rows:
            made = jnp.where(row_at == at, wide(value), made)
        return made

    def pair_up():
        for x in range(4):
            for j in range(14):
                part = [weights[1][x, i] if i < 18 else reaction[1][x, i - 18] for i in (2 * j, 2 * j + 1) if i < 27]
                coef_own[x, j] = jnp.where(odd, part[-1], part[0])
        for side, y in ((0, 6), (1, 0)):
            for j in range(0, 14, 2):
                rows = [(4 * i + x, coef_own[x, j + i, y : y + 1, :]) for i in range(2) for x in range(4)]
                coef_y_send[side, j // 2] = rows_tile(rows)

    def send_ring_coefficients():
        copies = []
        for side, turn in ((0, 1), (1, -1)):
            sems = lambda n: (coef_send_sem.at[n], coef_recv_sem.at[n])
            copies.append(remote(coef_y_send.at[side], coef_y.at[side], *sems(side), (0, turn)))
            copies.append(remote(coef_own.at[3 - 3 * side], coef_x.at[side], *sems(2 + side), (turn, 0)))
        for n in range(4):
            x, y = 3 - 3 * (n // 2), 6 - 6 * (n % 2)
            for j in range(14):
                coef_corner_send[n, j : j + 1, :] = coef_own[x, j, y : y + 1, :]
            to = (1 - 2 * (n // 2), 1 - 2 * (n % 2))
            copies.append(
                remote(coef_corner_send.at[n], coef_corner.at[n], coef_send_sem.at[4 + n], coef_recv_sem.at[4 + n], to)
            )
        return copies

    def take_ring_coefficients(copies):
        for copy in copies:
            copy.wait()
        for p in range(6):
            filled = jnp.logical_and(row_at >= 1, row_at < ROWS - 1)
            for j in range(14):
                if p in (0, 5):
                    rows = [(2 + k, coef_x[p // 5, j, 2 * k : 2 * k + 1, :]) for k in range(4)]
                    rows += [(1 + 5 * sy, coef_corner[2 * (p // 5) + sy, j : j + 1, :]) for sy in range(2)]
                else:
                    x = p - 1
                    rows = [(2 + k, coef_own[x, j, 2 * k : 2 * k + 1, :]) for k in range(4)]
                    at = 4 * (j % 2) + x
                    rows += [(1, coef_y[0, j // 2, at : at + 1, :]), (6, coef_y[1, j // 2, at : at + 1, :])]
                both = rows_tile(rows)
                for i, value in ((2 * j, even_part(both)), (2 * j + 1, odd_part(both))):
                    if i < 18:
                        ring_w[p, i] = value
                    elif i < 27:
                        ring_r[p, i - 18] = jnp.where(filled, value, 1.0) if i in (18, 22, 26) else value
        finish(ring_w, ring_r, ring_diag, ring_inverse, 6)
        off_high = jnp.logical_and(row_at == 5, is_high_y)
        off_low = jnp.logical_and(row_at == 2, is_low_y)
        for c in range(3):
            ring_w[4, c] = jnp.where(is_high_x, 0.0, ring_w[4, c])
            ring_w[1, 3 + c] = jnp.where(is_low_x, 0.0, ring_w[1, 3 + c])

        def body(p):
            for k, off in ((2, off_high), (3, off_low), (4, lane_at >= lanes - 2), (5, lane_at < 2)):
                for c in range(3):
                    ring_w[p, 3 * k + c] = jnp.where(off, 0.0, ring_w[p, 3 * k + c])

        each(6, body)

    def send_pairs(turn):
        for x in range(4):
            for c in range(3):
                pair_own[x, c] = jnp.where(odd, sources[1][x, c], fields[1][0, x + 1, c])
        for side, y in ((0, 4), (1, 0)):
            for c in range(3):
                rows = [(2 * x + k, pair_own[x, c, y + 2 * k : y + 2 * k + 1, :]) for x in range(4) for k in range(2)]
                pair_y_send[side, c] = rows_tile(rows)
        for sx in range(2):
            for sy in range(2):
                x, y = 3 - 3 * sx, 6 - 6 * sy
                for i, (at_x, at_y) in enumerate(((x, y), (2 - sx, y), (x, 4 - 2 * sy))):
                    for c in range(3):
                        n = 3 * i + c
                        pair_corner_send[2 * sx + sy, n : n + 1, :] = pair_own[at_x, c, at_y : at_y + 1, :]
        copies = []
        sems = lambda n: (pair_send_sem.at[n], pair_recv_sem.at[turn, n])
        for side, to in ((0, 1), (1, -1)):
            copies.append(remote(pair_y_send.at[side], pair_y.at[turn, side], *sems(side), (0, to)))
            source = pair_own.at[pl.ds(2 - 2 * side, 2)]
            copies.append(remote(source, pair_x.at[turn, side], *sems(2 + side), (to, 0)))
        for sx in range(2):
            for sy in range(2):
                n = 2 * sx + sy
                to = (1 - 2 * sx, 1 - 2 * sy)
                copies.append(remote(pair_corner_send.at[n], pair_corner.at[turn, n], *sems(4 + n), to))
        return copies

    def take_pairs(turn, copies):
        for copy in copies:
            copy.wait()
        for p in range(8):
            for c in range(3):
                if 2 <= p < 6:
                    x = p - 2
                    rows = [(2 + k, pair_own[x, c, 2 * k : 2 * k + 1, :]) for k in range(4)]
                    for side in range(2):
                        for k in range(2):
                            at = 2 * x + k
                            rows.append((6 * side + k, pair_y[turn, side, c, at : at + 1, :]))
                else:
                    side = p // 4
                    rows = [(2 + k, pair_x[turn, side, p - 6 * side, c, 2 * k : 2 * k + 1, :]) for k in range(4)]
                    for sy in range(2):
                        cells = ((0, 1 + 5 * sy), (2, 7 * sy)) if p in (1, 6) else ((1, 1 + 5 * sy),)
                        for i, row in cells:
                            n = 3 * i + c
                            rows.append((row, pair_corner[turn, 2 * side + sy, n : n + 1, :]))
                both = rows_tile(rows)
                ring_u[p, c] = even_part(both)
                if 1 <= p < 7:
                    ring_b[p - 1, c] = odd_part(both)

    def ring_sweep():
        def add(p):
            x = p // 2 - 1
            for c in range(3):
                e = jnp.where(row_at < 2, mid_at(c, x, -1), mid_at(c, x, 0))
                e = jnp.where(row_at < 4, e, jnp.where(row_at < 6, mid_at(c, x, 1), mid_at(c, x, 2)))
                ring_u[p, c] += e

        for p in range(8):
            add(p)
        for p in range(6):
            u = [ring_u[p + 1, c] for c in range(3)]
            left = []
            for c in range(3):
                value = ring_b[p, c] - ring_diag[p, c] * u[c]
                near = (ring_u[p + 2, c], ring_u[p, c], down(u[c], -1), down(u[c], 1), along(u[c], -2), along(u[c], 2))
                for k in range(6):
                    value = value + ring_w[p, 3 * k + c] * near[k]
                for d in range(3):
                    if d != c:
                        value = value - ring_r[p, 3 * d + c] * u[d]
                left.append(value)
            step = apply_inverse(ring_inverse, p, left)
            for c in range(3):
                ring_out[p, c] = u[c] + step[c]

    def add_to_finest(at, slot):
        f = fields[0]
        for c in range(3):
            for p in range(6):
                rows = [wide(ring_out[p, c, 2 + k : 3 + k, :]) for k in range(4)]
                e = jnp.where(row_at < 2, rows[0], rows[1])
                e = jnp.where(row_at < 4, e, jnp.where(row_at < 6, rows[2], rows[3]))
                for x in {0: (-1,), 5: (8,)}.get(p, (2 * p - 2, 2 * p - 1)):
                    f[at, x + 1, c] += e
            for side, row in ((0, 1), (1, 6)):
                rows = [wide(ring_out[1 + k, c, row : row + 1, :]) for k in range(4)]
                e = jnp.where(row_at < 2, rows[0], rows[1])
                e = jnp.where(row_at < 4, e, jnp.where(row_at < 6, rows[2], rows[3]))
                rows_halo[slot, side, c] += e

    def packed_y(f, at):
        return rows_tile([(x, f(x)[at : at + 1, :]) for x in range(8)])

    def send_rim():
        copies = []
        sems = lambda n: (rim_send_sem.at[n], rim_recv_sem.at[n])
        for side, to in ((0, 1), (1, -1)):
            row, second = 7 - 7 * side, 6 - 5 * side
            for i in range(9):
                rim_y_send[side, i] = rows_tile([(x, reaction[0][x, i, row : row + 1, :]) for x in range(8)])
            rim_y_send[side, 9] = rows_tile([(x, pot[x + 1, second : second + 1, :]) for x in range(8)])
            for c in range(3):
                rim_y_send[side, 10 + c] = rows_tile([(x, base[x, c, row : row + 1, :]) for x in range(8)])
            copies.append(remote(rim_y_send.at[side], rim_y.at[side], *sems(side), (0, to)))
            copies.append(remote(reaction[0].at[row], rim_r.at[side], *sems(2 + side), (to, 0)))
            copies.append(remote(pot.at[second + 1], rim_pot.at[side], *sems(4 + side), (to, 0)))
            copies.append(remote(base.at[row], rim_base.at[side], *sems(6 + side), (to, 0)))
        for n in range(4):
            x, y = 7 - 7 * (n // 2), 7 - 7 * (n % 2)
            rim_pot_corner_send[n] = pot[x + 1, y : y + 1, :]
            to = (1 - 2 * (n // 2), 1 - 2 * (n % 2))
            copies.append(remote(rim_pot_corner_send.at[n], rim_pot_corner.at[n], *sems(8 + n), to))
        return copies

    def ordered(t, out_side, in_side, ahead, behind, above, below):
        across = (in_side, out_side) if t % 2 == 0 else (out_side, in_side)
        return (across + (ahead, behind) if t < 2 else (ahead, behind) + across) + (above, below)

    def take_rim(copies):
        for copy in copies:
            copy.wait()
        for side in range(2):
            for i in range(9):
                rim_r[2 + side, i] = rim_y[side, i]
            for c in range(3):
                rim_base[2 + side, c] = rim_y[side, 10 + c]
        for t in range(4):
            side = t % 2
            if t < 2:
                here, beyond, inside = pot[9 * side], rim_pot[side], pot[1 + 7 * side]
                first, last = 2 * side, 2 * side + 1
                edges = (is_low_y, is_high_y)
            else:
                here, beyond = pot_y[side], rim_y[side, 9]
                row = 7 * side
                inside = rows_tile([(x, pot[x + 1, row : row + 1, :]) for x in range(8)])
                first, last = side, 2 + side
                edges = (is_low_x, is_high_x)
            corner = lambda n, off: jnp.where(off, 0.0, wide(rim_pot_corner[n]))
            near = ordered(
                t,
                beyond,
                inside,
                jnp.where(row_at == ROWS - 1, corner(last, edges[1]), down(here, -1)),
                jnp.where(row_at == 0, corner(first, edges[0]), down(here, 1)),
                jnp.where(lane_at == lanes - 1, 0.0, along(here, -1)),
                jnp.where(lane_at == 0, 0.0, along(here, 1)),
            )
            for k in range(6):
                plus, minus = face_weights(here - near[k])
                rim_w[t, 3 * k] = jnp.ones(tile, jnp.float32)
                rim_w[t, 3 * k + 1] = plus
                rim_w[t, 3 * k + 2] = minus
        finish(rim_w, rim_r, rim_diag, rim_inverse, 4)
        for t in range(4):
            ahead, off_high, off_low = (2, is_high_y, is_low_y) if t < 2 else (0, is_high_x, is_low_x)
            masks = (
                (ahead, jnp.logical_and(row_at == ROWS - 1, off_high)),
                (ahead + 1, jnp.logical_and(row_at == 0, off_low)),
                (4, lane_at == lanes - 1),
                (5, lane_at == 0),
            )
            for k, off in masks:
                for c in range(3):
                    rim_w[t, 3 * k + c] = jnp.where(off, 0.0, rim_w[t, 3 * k + c])

    def doubled(rows):
        e = jnp.where(row_at < 2, wide(rows[0]), wide(rows[1]))
        return jnp.where(row_at < 4, e, jnp.where(row_at < 6, wide(rows[2]), wide(rows[3])))

    def rim_sweep(at):
        for t in range(4):
            side = t % 2
            e, near = [], []
            for c in range(3):
                cell = lambda p, row: ring_out[p, c, row : row + 1, :]
                if t < 2:
                    p, p_in = 5 * side, 1 + 3 * side
                    here = doubled([cell(p, 2 + k) for k in range(4)])
                    inside = doubled([cell(p_in, 2 + k) for k in range(4)])
                    first, last = cell(p, 1), cell(p, 6)
                else:
                    row, row_in = 1 + 5 * side, 2 + 3 * side
                    here = doubled([cell(1 + k, row) for k in range(4)])
                    inside = doubled([cell(1 + k, row_in) for k in range(4)])
                    first, last = cell(0, row), cell(5, row)
                e.append(here)
                near.append(
                    ordered(
                        t,
                        here,
                        inside,
                        jnp.where(row_at == ROWS - 1, wide(last), down(here, -1)),
                        jnp.where(row_at == 0, wide(first), down(here, 1)),
                        along(here, -1),
                        along(here, 1),
                    )
                )
            left = []
            for c in range(3):
                value = -rim_diag[t, c] * e[c]
                for k in range(6):
                    value = value + rim_w[t, 3 * k + c] * near[c][k]
                for d in range(3):
                    if d != c:
                        value = value - rim_r[t, 3 * d + c] * e[d]
                left.append(value)
            step = apply_inverse(rim_inverse, t, left)
            for c in range(3):
                value = rim_base[t, c] + e[c] + step[c]
                if t < 2:
                    fields[0][at, 9 * side, c] = value
                else:
                    rows_halo[3, side, c] = value

    def source(level, x):
        if level == 0:
            return [grad[c, x] for c in range(3)]
        return [sources[level][x, c] for c in range(3)]

    def solve(level, x, r):
        v = inverse[level]
        return [v[x, 3 * c] * r[0] + v[x, 3 * c + 1] * r[1] + v[x, 3 * c + 2] * r[2] for c in range(3)]

    def share(level, at, beside_it=lambda: None):
        slot, f, count = done[0] % 3, fields[level], NX[level]
        for side, row in ((0, ROWS - 1), (1, 0)):
            for c in range(3):
                packed = wide(f[at, 1, c, row : row + 1, :])
                for x in range(1, count):
                    packed = jnp.where(row_at == x, wide(f[at, x + 1, c, row : row + 1, :]), packed)
                send_y[side, c] = packed
        wait = exchange(
            [
                (f.at[at, count], f.at[at, 0]),
                (f.at[at, 1], f.at[at, count + 1]),
                (send_y.at[0], rows_halo.at[slot, 0]),
                (send_y.at[1], rows_halo.at[slot, 1]),
            ]
        )
        beside_it()
        inner(level, at)
        wait()
        return slot

    def inner(level, at):
        f, w, r, span, count = fields[level], weights[level], reaction[level], 1 << level, NX[level]
        for x in range(count):
            u = [f[at, x + 1, c] for c in range(3)]
            b = source(level, x)
            for c in range(3):
                value = b[c] - diag[level][x, c] * u[c]
                value = value + w[x, 6 + c] * jnp.where(row_at >= ROWS - span, 0.0, down(u[c], -span))
                value = value + w[x, 9 + c] * jnp.where(row_at < span, 0.0, down(u[c], span))
                value = value + w[x, 12 + c] * along(u[c], -span) + w[x, 15 + c] * along(u[c], span)
                if x < count - 1:
                    value = value + w[x, c] * f[at, x + 2, c]
                if x > 0:
                    value = value + w[x, 3 + c] * f[at, x, c]
                for d in range(3):
                    if d != c:
                        value = value - r[x, 3 * d + c] * u[d]
                part[x, c] = value

    def rest(level, at, slot, x):
        f, w, span, count = fields[level], weights[level], 1 << level, NX[level]
        left = []
        for c in range(3):
            row_high, row_low = (rows_halo[slot, side, c, x : x + 1, :] for side in (1, 0))
            value = jnp.where(row_at >= ROWS - span, w[x, 6 + c] * wide(row_high), 0.0)
            value = part[x, c] + jnp.where(row_at < span, w[x, 9 + c] * wide(row_low), value)
            if x == 0:
                value = value + w[x, 3 + c] * f[at, 0, c]
            if x == count - 1:
                value = value + w[x, c] * f[at, count + 1, c]
            left.append(value)
        return [f[at, x + 1, c] for c in range(3)], left

    def residual(level, at, slot, x):
        f, w, r, span = fields[level], weights[level], reaction[level], 1 << level
        u = [f[at, x + 1, c] for c in range(3)]
        b = source(level, x)
        left = []
        for c in range(3):
            near = (
                f[at, x + 2, c],
                f[at, x, c],
                jnp.where(row_at >= ROWS - span, wide(rows_halo[slot, 1, c, x : x + 1, :]), down(u[c], -span)),
                jnp.where(row_at < span, wide(rows_halo[slot, 0, c, x : x + 1, :]), down(u[c], span)),
                along(u[c], -span),
                along(u[c], span),
            )
            value = b[c] - diag[level][x, c] * u[c]
            for k in range(6):
                value = value + w[x, 3 * k + c] * near[k]
            for d in range(3):
                if d != c:
                    value = value - r[x, 3 * d + c] * u[d]
            left.append(value)
        return u, left

    def sweep(at, slot, left_of, last=False):
        for x in range(NX[0]):
            u, left = left_of(0, at, slot, x)
            step = solve(0, x, left)
            for c in range(3):
                if last:
                    out[c, x] = u[c] + step[c]
                else:
                    fields[0][at + 1, x + 1, c] = u[c] + step[c]
        return at + 1

    def restrict(level, at, slot, keep=False):
        rows, lanes_ = pair_tools(level)[4:]
        for x in range(NX[level + 1]):
            left = []
            for i in range(2):
                u, r = rest(level, at, slot, 2 * x + i)
                left.append(r)
                if keep:
                    step = solve(level, 2 * x + i, r)
                    for c in range(3):
                        base[2 * x + i, c] = u[c] + step[c]
            total = [lanes_(rows(left[0][c] + left[1][c])) for c in range(3)]
            first = solve(level + 1, x, total)
            for c in range(3):
                sources[level + 1][x, c] = total[c]
                fields[level + 1][0, x + 1, c] = first[c]

    def cycle(at, turn, besides, last=False):
        slot = share(0, at, besides[0])
        restrict(0, at, slot, keep=not last)
        pairs = []

        def beside():
            pairs.extend(send_pairs(turn))
            besides[1]()

        restrict(1, 0, share(1, 0, beside))

        def beside_q():
            take_pairs(turn, pairs)
            besides[3]()

        lower(turn, besides[2], beside_q)
        ring_sweep()
        if not last:
            rim_sweep(at + 1)
        add_to_finest(at, slot)
        return sweep(at, slot, residual, last)

    def start(x):
        for c, value in enumerate(solve(0, x, source(0, x))):
            fields[0][0, x + 1, c] = value

    finish_level(0)
    loads["grad"].wait()
    each(NX[0], start)
    pending, ring_pending, rim_pending = [], [], []

    def beside_first():
        coarsen(0)
        mask_level(0)
        finish_level(1)
        coarsen(1)
        pending.append(send_coefficients())

    def beside_second():
        pair_up()
        ring_pending.extend(send_ring_coefficients())
        mask_level(1)
        finish_level(2)
        coarsen(2)
        pending.append(send_low_coefficients())
        rim_pending.extend(send_rim())

    def beside_fourth():
        take_ring_coefficients(ring_pending)
        take_rim(rim_pending)

    nothing = lambda: None
    at = cycle(
        0,
        0,
        (
            beside_first,
            beside_second,
            lambda: take_coefficients(pending),
            beside_fourth,
        ),
    )
    at = sweep(at, 3, residual)
    cycle(at, 1, (nothing,) * 4, last=True)


def local(counts, gradient, potential, coupling, region, contact, rates):
    nz = potential.shape[-1]
    tile = (ROWS, nz)
    f32 = jnp.float32
    scratch = []
    for parts in (18, 9, 3, 9):
        scratch += [pltpu.VMEM((n, parts) + tile, f32) for n in NX]
    scratch += [pltpu.VMEM((n, 3) + tile, f32) for n in NX[1:]]
    scratch += [pltpu.VMEM((3, n + 2, 3) + tile, f32) for n in NX]
    scratch += [
        pltpu.VMEM((4, 2, 3) + tile, f32),
        pltpu.VMEM((2,) + tile, f32),
        pltpu.VMEM((2, 3) + tile, f32),
        pltpu.SemaphoreType.DMA((4,)),
        pltpu.SemaphoreType.DMA((3, 4)),
        pltpu.VMEM((1, 18) + tile, f32),
        pltpu.VMEM((1, 9) + tile, f32),
        pltpu.VMEM((SLOTS, 18) + tile, f32),
        pltpu.VMEM((SLOTS, 9) + tile, f32),
        pltpu.VMEM((SLOTS, 3) + tile, f32),
        pltpu.VMEM((SLOTS, 9) + tile, f32),
        pltpu.VMEM((SLOTS, 3) + tile, f32),
        pltpu.VMEM((SLOTS, 3) + tile, f32),
        pltpu.VMEM((2, 4, 3) + tile, f32),
        pltpu.VMEM((27, 1, nz), f32),
        pltpu.VMEM((len(INNER), 27, 1, nz), f32),
        pltpu.VMEM((4, nz), f32),
        pltpu.VMEM((len(FOURTH), 4, nz), f32),
        pltpu.VMEM((2, 3, 1, nz), f32),
        pltpu.VMEM((2, len(INNER + OUTER), 3, 1, nz), f32),
        pltpu.VMEM((1, 1, nz), f32),
        pltpu.VMEM((2, len(THIRD), 1, nz), f32),
        pltpu.SemaphoreType.DMA,
        pltpu.SemaphoreType.DMA,
        pltpu.SemaphoreType.DMA,
        pltpu.SemaphoreType.DMA,
        pltpu.SemaphoreType.DMA,
        pltpu.SemaphoreType.DMA((2,)),
        pltpu.SemaphoreType.DMA,
        pltpu.SemaphoreType.DMA((2,)),
        pltpu.VMEM((8, 3) + tile, f32),
        pltpu.VMEM((6, 3) + tile, f32),
        pltpu.VMEM((6, 18) + tile, f32),
        pltpu.VMEM((6, 9) + tile, f32),
        pltpu.VMEM((6, 3) + tile, f32),
        pltpu.VMEM((6, 9) + tile, f32),
        pltpu.VMEM((6, 3) + tile, f32),
        pltpu.VMEM((4, 3) + tile, f32),
        pltpu.VMEM((2, 2, 2, 3) + tile, f32),
        pltpu.VMEM((2, 3) + tile, f32),
        pltpu.VMEM((2, 2, 3) + tile, f32),
        pltpu.VMEM((4, 2 * ROWS, nz), f32),
        pltpu.VMEM((2, 4, 2 * ROWS, nz), f32),
        pltpu.SemaphoreType.DMA((8,)),
        pltpu.SemaphoreType.DMA((2, 8)),
        pltpu.VMEM((4, 14) + tile, f32),
        pltpu.VMEM((2, 14) + tile, f32),
        pltpu.VMEM((2, 7) + tile, f32),
        pltpu.VMEM((2, 7) + tile, f32),
        pltpu.SemaphoreType.DMA((8,)),
        pltpu.SemaphoreType.DMA((8,)),
        pltpu.VMEM((NX[0], 3) + tile, f32),
        pltpu.VMEM((4, 2 * ROWS, nz), f32),
        pltpu.VMEM((4, 2 * ROWS, nz), f32),
        pltpu.VMEM((4, 18) + tile, f32),
        pltpu.VMEM((4, 9) + tile, f32),
        pltpu.VMEM((4, 3) + tile, f32),
        pltpu.VMEM((4, 9) + tile, f32),
        pltpu.VMEM((4, 3) + tile, f32),
        pltpu.VMEM((2,) + tile, f32),
        pltpu.VMEM((4, 1, nz), f32),
        pltpu.VMEM((4, 1, nz), f32),
        pltpu.VMEM((NX[0], 3) + tile, f32),
        pltpu.VMEM((2, 13) + tile, f32),
        pltpu.VMEM((2, 13) + tile, f32),
        pltpu.SemaphoreType.DMA((12,)),
        pltpu.SemaphoreType.DMA((12,)),
        pltpu.VMEM(gradient.shape, f32),
        pltpu.VMEM((10,) + tile, f32),
        pltpu.VMEM(coupling.shape, f32),
        pltpu.VMEM(region.shape, jnp.int32),
        pltpu.VMEM(contact.shape, jnp.int32),
        pltpu.SMEM(rates.shape, f32),
        pltpu.SemaphoreType.DMA((6,)),
    ]
    vmem = pl.BlockSpec(memory_space=pltpu.VMEM)
    return pl.pallas_call(
        functools.partial(kernel, counts),
        out_shape=jax.ShapeDtypeStruct(gradient.shape, f32),
        in_specs=[pl.BlockSpec(memory_space=pltpu.HBM)] * 6,
        out_specs=vmem,
        scratch_shapes=scratch,
        compiler_params=pltpu.CompilerParams(
            collective_id=0, has_side_effects=True, vmem_limit_bytes=60 * 1024 * 1024
        ),
    )(gradient, potential, coupling, region, contact, rates)


def solution(mesh):
    placed = (
        P(None, "gx", "gy", None),
        P("gx", "gy", None),
        P(None, None, "gx", "gy", None),
        P("gx", "gy", None),
        P("gx", "gy", None),
        P(),
    )
    counts = (mesh.shape["gx"], mesh.shape["gy"])
    return jax.shard_map(
        functools.partial(local, counts),
        mesh=mesh,
        in_specs=placed,
        out_specs=P(None, "gx", "gy", None),
        check_vma=False,
    )
```

```python
import functools

import jax
import jax.numpy as jnp
from jax import lax
from jax.experimental import pallas as pl
from jax.experimental.pallas import tpu as pltpu
from jax.sharding import PartitionSpec as P

MESH = pl.DeviceIdType.MESH
LEVELS = 4
COARSE_SWEEPS = 6
REGIONS = 4
OMEGA = 0.8
STRENGTH = 8.0
ROWS = 8
NX = (8, 4, 2, 1)
RADIUS = 3
SLOTS = 8


def around(shape, far):
    reach = range(-6, 7)
    distance = lambda i, j: min(abs(i - a) + abs(j - b) for a, b in shape)
    found = [(i, j) for i in reach for j in reach if distance(i, j) <= far and (i, j) != (0, 0)]
    return sorted(found, key=lambda o: -abs(o[0]) - abs(o[1]))


OWN = [(0, 0)]
SQUARE = [(i, j) for i in (-1, 0, 1) for j in (-1, 0, 1)]
INNER = around(OWN, 2)
OUTER = [o for o in around(OWN, 3) if o not in INNER]
FOURTH = around(SQUARE, 2)
THIRD = around(SQUARE, 3)


def each(count, body):
    if count == 1:
        body(0)
        return

    def step(i, carry):
        body(i)
        return carry

    lax.fori_loop(0, count, step, 0, unroll=count)


def face_weights(difference):
    size = jnp.abs(difference)
    small = size < 0.5
    series = 1.0 / 362880.0
    for k in (40320.0, 5040.0, 720.0, 120.0, 24.0, 6.0, 2.0, 1.0):
        series = series * size + 1.0 / k
    below = jnp.where(small, series, jnp.exp(size) - 1.0)
    low = jnp.where(small, 1.0, size) / below
    low = jnp.where(size < 1e-4, 1.0 - 0.5 * size, low)
    high = low + size
    positive = difference > 0.0
    return jnp.where(positive, low, high), jnp.where(positive, high, low)


def kernel(counts, grad_in, pot_in, coup_in, region_in, contact_in, rates_in, out, *scratch):
    grad, pot, coup, region, contact, rates, in_sem = scratch[-7:]
    scratch = scratch[:-7]
    loads = {}
    for i, (name, source, target) in enumerate(
        (
            ("pot", pot_in, pot.at[pl.ds(1, 8)]),
            ("rates", rates_in, rates),
            ("region", region_in, region),
            ("contact", contact_in, contact),
            ("coup", coup_in, coup),
            ("grad", grad_in, grad),
        )
    ):
        loads[name] = pltpu.make_async_copy(source, target, in_sem.at[i])
        loads[name].start()
    weights, reaction, diag, inverse = (scratch[4 * i : 4 * i + 4] for i in range(4))
    sources = (None,) + tuple(scratch[16:19])
    fields = scratch[19:23]
    rows_halo, pot_y, send_y, send_sem, recv_sem = scratch[23:28]
    w_own, r_own, w_wide, r_wide, diag_wide, inverse_wide, u_wide, b_wide, e_rows = scratch[28:37]
    mid_send, mid_recv, low_send, low_recv, mid_cell, mid_cells, low_cell, low_cells = scratch[37:45]
    mid_send_sem, mid_recv_sem, low_send_sem, low_recv_sem, p_send, p_recv, q_send, q_recv = scratch[45:53]
    ring_u, ring_b, ring_w, ring_r, ring_diag, ring_inverse, ring_out = scratch[53:60]
    pair_own, pair_x, pair_y_send, pair_y, pair_corner_send, pair_corner, pair_send_sem, pair_recv_sem = scratch[60:68]
    coef_own, coef_x, coef_y_send, coef_y, coef_send_sem, coef_recv_sem, part, coef_corner_send, coef_corner = scratch[68:77]
    rim_w, rim_r, rim_diag, rim_inverse, rim_base, rim_pot, rim_pot_corner_send, rim_pot_corner = scratch[77:85]
    base, rim_y_send, rim_y, rim_send_sem, rim_recv_sem, result, out_sem = scratch[85:]
    n_x, n_y = counts
    lanes = out.shape[-1]
    gx, gy = lax.axis_index("gx"), lax.axis_index("gy")
    x_low, x_high = lax.rem(gx + n_x - 1, n_x), lax.rem(gx + 1, n_x)
    y_low, y_high = lax.rem(gy + n_y - 1, n_y), lax.rem(gy + 1, n_y)
    beside = ((x_high, gy), (x_low, gy), (gx, y_high), (gx, y_low))

    barrier = pltpu.get_barrier_semaphore()
    at_offset = lambda i, j: (lax.rem(gx + n_x + i, n_x), lax.rem(gy + n_y + j, n_y))
    devices = {o: at_offset(*o) for o in THIRD}
    for offset in INNER:
        pl.semaphore_signal(barrier, inc=1, device_id=devices[offset], device_id_type=MESH)
    pl.semaphore_wait(barrier, len(INNER))

    tile = (ROWS, lanes)
    row_at = lax.broadcasted_iota(jnp.int32, tile, 0)
    lane_at = lax.broadcasted_iota(jnp.int32, tile, 1)
    wide = lambda row: jnp.broadcast_to(row, tile)
    down = lambda v, by: pltpu.roll(v, by % ROWS, 0) if by % ROWS else v
    along = lambda v, by: pltpu.roll(v, by % lanes, 1)

    done = [0]

    def exchange(parts):
        slot = done[0] % 3
        done[0] += 1
        copies = []
        for i in (2, 3, 0, 1):
            source, target = parts[i]
            copy = pltpu.make_async_remote_copy(
                src_ref=source,
                dst_ref=target,
                send_sem=send_sem.at[i],
                recv_sem=recv_sem.at[slot, i],
                device_id=beside[i],
                device_id_type=MESH,
            )
            copy.start()
            copies.append(copy)

        def wait():
            for copy in copies:
                copy.wait()

        return wait

    def remote(source, target, send, recv, offset):
        copy = pltpu.make_async_remote_copy(
            src_ref=source,
            dst_ref=target,
            send_sem=send,
            recv_sem=recv,
            device_id=devices[offset],
            device_id_type=MESH,
        )
        copy.start()
        return copy

    def gather(offsets, source_of, target, send, recv):
        for n, (i, j) in enumerate(offsets):
            remote(source_of((i, j)), target.at[n], send, recv, (-i, -j))

        def wait():
            pltpu.make_async_copy(target, target, send).wait()
            pltpu.make_async_copy(target, target, recv).wait()

        return wait

    loads["pot"].wait()
    for side, at in ((0, ROWS - 1), (1, 0)):
        packed = wide(pot[1, at : at + 1, :])
        for x in range(1, 8):
            packed = jnp.where(row_at == x, wide(pot[x + 1, at : at + 1, :]), packed)
        send_y[side, 0] = packed
    wait = exchange(
        [
            (pot.at[8], pot.at[0]),
            (pot.at[1], pot.at[9]),
            (send_y.at[0, 0], pot_y.at[0]),
            (send_y.at[1, 0], pot_y.at[1]),
        ]
    )
    for name in ("rates", "region", "contact", "coup"):
        loads[name].wait()

    def put_faces(x, k, plus, minus):
        weights[0][x, 3 * k] = jnp.ones(tile, jnp.float32)
        weights[0][x, 3 * k + 1] = plus
        weights[0][x, 3 * k + 2] = minus

    def set_up(x):
        here = pot[x + 1]
        put_faces(x, 4, *face_weights(here - jnp.where(lane_at == lanes - 1, 0.0, along(here, -1))))
        put_faces(x, 5, *face_weights(here - jnp.where(lane_at == 0, 0.0, along(here, 1))))
        plus, minus = face_weights(here - down(here, -1))
        put_faces(x, 2, plus, minus)
        put_faces(x, 3, down(minus, 1), down(plus, 1))
        at_contact = STRENGTH * contact[x].astype(jnp.float32)
        regions = region[x]
        for c in range(3):
            extra = jnp.full(tile, rates[0, c])
            for pick in range(1, REGIONS):
                extra = jnp.where(regions == pick, rates[pick, c], extra)
            for d in range(3):
                value = coup[c, d, x]
                reaction[0][x, 3 * c + d] = value + (extra + at_contact) if c == d else value

    each(NX[0], set_up)
    for x in range(7):
        plus, minus = face_weights(pot[x + 1] - pot[x + 2])
        put_faces(x, 0, plus, minus)
        put_faces(x + 1, 1, minus, plus)
    wait()
    is_low_x, is_high_x = gx == 0, gx == n_x - 1
    is_low_y, is_high_y = gy == 0, gy == n_y - 1
    pot[0] = jnp.where(is_low_x, 0.0, pot[0])
    pot[9] = jnp.where(is_high_x, 0.0, pot[9])
    pot_y[0] = jnp.where(is_low_y, 0.0, pot_y[0])
    pot_y[1] = jnp.where(is_high_y, 0.0, pot_y[1])

    put_faces(0, 1, *face_weights(pot[1] - pot[0]))
    put_faces(7, 0, *face_weights(pot[8] - pot[9]))
    for side, k, row in ((0, 2, ROWS - 1), (1, 3, 0)):
        part[side, 0], part[side, 1] = face_weights(send_y[side, 0] - pot_y[1 - side])
        for x in range(8):
            for c in (1, 2):
                value = wide(part[side, c - 1, x : x + 1, :])
                weights[0][x, 3 * k + c] = jnp.where(row_at == row, value, weights[0][x, 3 * k + c])

    def finish(w, r, diagonal, inv, count):
        def body(x):
            m = [[r[x, 3 * col + row] for col in range(3)] for row in range(3)]
            for c in range(3):
                total = w[x, c]
                for k in range(1, 6):
                    total = total + w[x, 3 * k + c]
                m[c][c] = m[c][c] + total
                diagonal[x, c] = m[c][c]

            def cofactor(i, j):
                i1, i2, j1, j2 = (i + 1) % 3, (i + 2) % 3, (j + 1) % 3, (j + 2) % 3
                return m[i1][j1] * m[i2][j2] - m[i1][j2] * m[i2][j1]

            cof = [[cofactor(i, j) for j in range(3)] for i in range(3)]
            det = m[0][0] * cof[0][0] + m[0][1] * cof[0][1] + m[0][2] * cof[0][2]
            scale = OMEGA / det
            for i in range(3):
                for j in range(3):
                    inv[x, 3 * i + j] = cof[j][i] * scale

        each(count, body)

    def finish_level(level):
        finish(weights[level], reaction[level], diag[level], inverse[level], NX[level])

    def mask_level(level):
        w, span, last = weights[level], 1 << level, NX[level] - 1
        for c in range(3):
            w[last, c] = jnp.where(is_high_x, 0.0, w[last, c])
            w[0, 3 + c] = jnp.where(is_low_x, 0.0, w[0, 3 + c])
        off_high = jnp.logical_and(row_at >= ROWS - span, is_high_y)
        off_low = jnp.logical_and(row_at < span, is_low_y)
        off_up, off_down = lane_at >= lanes - span, lane_at < span

        def body(x):
            for k, off in ((2, off_high), (3, off_low), (4, off_up), (5, off_down)):
                for c in range(3):
                    w[x, 3 * k + c] = jnp.where(off, 0.0, w[x, 3 * k + c])

        each(NX[level], body)

    def pair_tools(level):
        span = 1 << level
        odd_row = (row_at & span) != 0
        odd_lane = (lane_at & span) != 0

        def high_row(v):
            return jnp.where(odd_row, v, down(v, -span))

        def low_row(v):
            return jnp.where(odd_row, down(v, span), v)

        def high_lane(v):
            return jnp.where(odd_lane, v, along(v, -span))

        def low_lane(v):
            return jnp.where(odd_lane, along(v, span), v)

        def rows(v):
            return v + jnp.where(odd_row, down(v, span), down(v, -span))

        def lanes_(v):
            return v + jnp.where(odd_lane, along(v, span), along(v, -span))

        return high_row, low_row, high_lane, low_lane, rows, lanes_

    def coarsen(level):
        high_row, low_row, high_lane, low_lane, rows, lanes_ = pair_tools(level)
        w, r = weights[level], reaction[level]
        w_next, r_next = (w_own, r_own) if level == LEVELS - 2 else (weights[level + 1], reaction[level + 1])

        def body(x):
            for c in range(3):
                w_next[x, c] = lanes_(rows(w[2 * x + 1, c]))
                w_next[x, 3 + c] = lanes_(rows(w[2 * x, 3 + c]))
                pair = lambda k: w[2 * x, 3 * k + c] + w[2 * x + 1, 3 * k + c]
                w_next[x, 6 + c] = lanes_(high_row(pair(2)))
                w_next[x, 9 + c] = lanes_(low_row(pair(3)))
                w_next[x, 12 + c] = high_lane(rows(pair(4)))
                w_next[x, 15 + c] = low_lane(rows(pair(5)))
            for i in range(9):
                r_next[x, i] = lanes_(rows(r[2 * x, i] + r[2 * x + 1, i]))

        each(NX[level + 1], body)

    slot_at = lane_at & (SLOTS - 1)
    x_at, y_at = row_at + (gx - RADIUS), slot_at + (gy - RADIUS)
    x_last = jnp.logical_or(x_at == n_x - 1, x_at == -1)
    x_first = jnp.logical_or(x_at == 0, x_at == n_x)
    y_last = jnp.logical_or(y_at == n_y - 1, y_at == -1)
    y_first = jnp.logical_or(y_at == 0, y_at == n_y)
    z_last, z_first = lane_at >= lanes - SLOTS, lane_at < SLOTS
    offs = (x_last, x_first, y_last, y_first, z_last, z_first)
    bits = (2, 2, 1, 1, 4, 4)

    def transposed(tiles):
        tiles = list(tiles)
        for bit in (1, 2, 4):
            clear = (slot_at & bit) == 0
            for p in range(SLOTS):
                if not p & bit:
                    one, two = tiles[p], tiles[p | bit]
                    tiles[p] = jnp.where(clear, one, along(two, bit))
                    tiles[p | bit] = jnp.where(clear, along(one, -bit), two)
        return tiles

    def unpacked(offsets, row_of, own, fill=0.0):
        tiles = [jnp.full(tile, fill) for _ in range(SLOTS)]
        for n, (i, j) in enumerate(list(offsets) + OWN):
            if min(i, j) >= -RADIUS:
                row = row_of(n) if n < len(offsets) else own
                tiles[j + RADIUS] = jnp.where(row_at == i + RADIUS, wide(row), tiles[j + RADIUS])
        return transposed(tiles)

    def child_row(f, x0, c):
        which = slot_at & 3
        rows = [wide(f[x0 + p // 2, c, 4 * (p % 2) : 4 * (p % 2) + 1, :]) for p in range(4)]
        packed = jnp.where(which == 0, rows[0], jnp.where(which == 1, rows[1], jnp.where(which == 2, rows[2], rows[3])))
        return packed[0:1, :]

    def slot_row(values):
        packed = values[0]
        for i in range(1, len(values)):
            packed = jnp.where(slot_at == i, values[i], packed)
        return packed

    def send_coefficients():
        for i in range(27):
            mid_send[i] = child_row(weights[2] if i < 18 else reaction[2], 0, i if i < 18 else i - 18)
        return gather(INNER, lambda o: mid_send, mid_recv, mid_send_sem, mid_recv_sem)

    def send_low_coefficients():
        fields_ = [w_own[0, i] for i in range(18)] + [r_own[0, i] for i in range(9)]
        for row in range(4):
            low_send[row : row + 1, :] = slot_row(fields_[SLOTS * row : SLOTS * row + SLOTS])[0:1, :]
        return gather(FOURTH, lambda o: low_send, low_recv, low_send_sem, low_recv_sem)

    def take_coefficients(waits):
        for wait in waits:
            wait()
        for i in range(27):
            made = unpacked(INNER, lambda n: mid_recv[n, i], mid_send[i], 1.0 if i in (18, 22, 26) else 0.0)
            for p in range(SLOTS):
                if i < 18:
                    w_wide[p, i] = made[p]
                else:
                    r_wide[p, i - 18] = made[p]
        finish(w_wide, r_wide, diag_wide, inverse_wide, SLOTS)
        for k in range(6):
            for p in range(SLOTS):
                if ((p & bits[k]) != 0) == (k % 2 == 0):
                    for c in range(3):
                        w_wide[p, 3 * k + c] = jnp.where(offs[k], 0.0, w_wide[p, 3 * k + c])
        top = LEVELS - 1
        w, r = weights[top], reaction[top]
        for row in range(4):
            here = slice(row, row + 1)
            made = unpacked(FOURTH, lambda n: low_recv[n, here, :], low_send[here, :])
            for p in range(SLOTS):
                i = SLOTS * row + p
                if i < 18:
                    w[0, i] = made[p]
                elif i < 27:
                    r[0, i - 18] = made[p]
        finish_level(top)
        for k in range(6):
            for c in range(3):
                w[0, 3 * k + c] = jnp.where(offs[k], 0.0, w[0, 3 * k + c])

    def wide_residual(p, u):
        left = []
        for c in range(3):
            value = b_wide[p, c] - diag_wide[p, c] * u[p][c]
            for k in range(6):
                bit, ahead = bits[k], k % 2 == 0
                near = u[p ^ bit][c]
                if ((p & bit) != 0) == ahead:
                    turn = -1 if ahead else 1
                    near = down(near, turn) if k < 2 else along(near, turn if k < 4 else turn * SLOTS)
                value = value + w_wide[p, 3 * k + c] * near
            for d in range(3):
                if d != c:
                    value = value - r_wide[p, 3 * d + c] * u[p][d]
            left.append(value)
        return left

    def apply_inverse(v, x, r):
        return [v[x, 3 * c] * r[0] + v[x, 3 * c + 1] * r[1] + v[x, 3 * c + 2] * r[2] for c in range(3)]

    def wide_fields():
        return [[u_wide[p, c] for c in range(3)] for p in range(SLOTS)]

    def window_sweep(b, u, patches=None):
        top = LEVELS - 1
        w, r = weights[top], reaction[top]
        left = []
        for c in range(3):
            value = b[c] - diag[top][0, c] * u[c]
            before_x, before_y = down(u[c], 1), along(u[c], 1)
            if patches is not None:
                before_x = jnp.where(row_at == 0, patches[0][c], before_x)
                before_y = jnp.where(slot_at == 0, patches[1][c], before_y)
            near = (down(u[c], -1), before_x, along(u[c], -1), before_y, along(u[c], -SLOTS), along(u[c], SLOTS))
            for k in range(6):
                value = value + w[0, 3 * k + c] * near[k]
            for d in range(3):
                if d != c:
                    value = value - r[0, 3 * d + c] * u[d]
            left.append(value)
        step = apply_inverse(inverse[top], 0, left)
        return [u[c] + step[c] for c in range(3)]

    def lower(turn, beside_p, beside_q):
        for c in range(3):
            mid_cell[0, c] = child_row(sources[2], 0, c)
            mid_cell[1, c] = child_row(fields[2].at[0], 1, c)
        near = INNER + OUTER
        wait = gather(
            near, lambda o: mid_cell.at[0 if o in INNER else 1], mid_cells.at[turn], p_send, p_recv.at[turn]
        )
        beside_p()
        wait()
        for c in range(3):
            made = unpacked(near, lambda n: mid_cells[turn, n, c], mid_cell[0, c])
            for p in range(SLOTS):
                b_wide[p, c] = made[p]
        inner = jnp.abs(row_at - RADIUS) + jnp.abs(slot_at - RADIUS) <= 2
        for p in range(SLOTS):
            b = [b_wide[p, c] for c in range(3)]
            first = apply_inverse(inverse_wide, p, b)
            for c in range(3):
                u_wide[p, c] = jnp.where(inner, first[c], b[c])
        u_mid = wide_fields()
        b = [jnp.zeros(tile, jnp.float32) for _ in range(3)]
        for p in range(SLOTS):
            left = wide_residual(p, u_mid)
            b = [b[c] + left[c] for c in range(3)]
        u = apply_inverse(inverse[LEVELS - 1], 0, b)
        for _ in range(2):
            u = window_sweep(b, u)
        row = slot_row([along(value, i - RADIUS) for i, value in enumerate(u + b)])
        low_cell[0] = row[RADIUS : RADIUS + 1, :]
        wait = gather(THIRD, lambda o: low_cell.at[0], low_cells.at[turn], q_send, q_recv.at[turn])
        beside_q()
        wait()
        made = unpacked(THIRD, lambda n: low_cells[turn, n], low_cell[0])
        u, b = made[:3], made[3:6]
        before_x = [jnp.zeros(tile, jnp.float32) for _ in range(3)]
        last_y = jnp.zeros(tile, jnp.float32)
        for n, (i, j) in enumerate(THIRD):
            if i < -RADIUS:
                for c in range(3):
                    value = along(wide(low_cells[turn, n]), j + RADIUS - c)
                    before_x[c] = jnp.where(slot_at == j + RADIUS, value, before_x[c])
            if j < -RADIUS:
                last_y = jnp.where(row_at == i + RADIUS, wide(low_cells[turn, n]), last_y)
        before_y = [along(last_y, -c) for c in range(3)]
        u = window_sweep(b, u, (before_x, before_y))
        for _ in range(COARSE_SWEEPS - 4):
            u = window_sweep(b, u)
        u_mid = [[u_wide[p, c] + u[c] for c in range(3)] for p in range(SLOTS)]
        last = []
        for p in range(SLOTS):
            step = apply_inverse(inverse_wide, p, wide_residual(p, u_mid))
            last.append([u_mid[p][c] + step[c] for c in range(3)])
        for c in range(3):
            for x in range(2):
                for at, (t, y) in enumerate(((RADIUS - 1, 1), (RADIUS, 0), (RADIUS, 1), (RADIUS + 1, 0))):
                    low, high = last[2 * x + y][c], last[4 + 2 * x + y][c]
                    if t & 4:
                        value = jnp.where(slot_at == t, high, 0.0) + along(jnp.where(slot_at == t, low, 0.0), -4)
                    else:
                        value = jnp.where(slot_at == t, low, 0.0) + along(jnp.where(slot_at == t, high, 0.0), 4)
                    for bit in (1, 2):
                        value = value + along(value, -bit if t & bit else bit)
                    e_rows[x, at, c] = value

    def mid_at(c, x, y):
        row = RADIUS + (x // 2)
        return wide(e_rows[x % 2, y + 1, c, row : row + 1, :])

    odd = (lane_at & 1) != 0

    def even_part(v):
        return jnp.where(odd, along(v, 1), v)

    def odd_part(v):
        return jnp.where(odd, v, along(v, -1))

    def rows_tile(rows):
        made = jnp.zeros(tile, jnp.float32)
        for at, value in rows:
            made = jnp.where(row_at == at, wide(value), made)
        return made

    def pair_up():
        for x in range(4):
            for j in range(14):
                part = [weights[1][x, i] if i < 18 else reaction[1][x, i - 18] for i in (2 * j, 2 * j + 1) if i < 27]
                coef_own[x, j] = jnp.where(odd, part[-1], part[0])
        for side, y in ((0, 6), (1, 0)):
            for j in range(0, 14, 2):
                rows = [(4 * i + x, coef_own[x, j + i, y : y + 1, :]) for i in range(2) for x in range(4)]
                coef_y_send[side, j // 2] = rows_tile(rows)

    def send_ring_coefficients():
        copies = []
        for side, turn in ((0, 1), (1, -1)):
            sems = lambda n: (coef_send_sem.at[n], coef_recv_sem.at[n])
            copies.append(remote(coef_y_send.at[side], coef_y.at[side], *sems(side), (0, turn)))
            copies.append(remote(coef_own.at[3 - 3 * side], coef_x.at[side], *sems(2 + side), (turn, 0)))
        for n in range(4):
            x, y = 3 - 3 * (n // 2), 6 - 6 * (n % 2)
            for j in range(14):
                coef_corner_send[n, j : j + 1, :] = coef_own[x, j, y : y + 1, :]
            to = (1 - 2 * (n // 2), 1 - 2 * (n % 2))
            copies.append(
                remote(coef_corner_send.at[n], coef_corner.at[n], coef_send_sem.at[4 + n], coef_recv_sem.at[4 + n], to)
            )
        return copies

    def take_ring_coefficients(copies):
        for copy in copies:
            copy.wait()
        for p in range(6):
            filled = jnp.logical_and(row_at >= 1, row_at < ROWS - 1)
            for j in range(14):
                if p in (0, 5):
                    rows = [(2 + k, coef_x[p // 5, j, 2 * k : 2 * k + 1, :]) for k in range(4)]
                    rows += [(1 + 5 * sy, coef_corner[2 * (p // 5) + sy, j : j + 1, :]) for sy in range(2)]
                else:
                    x = p - 1
                    rows = [(2 + k, coef_own[x, j, 2 * k : 2 * k + 1, :]) for k in range(4)]
                    at = 4 * (j % 2) + x
                    rows += [(1, coef_y[0, j // 2, at : at + 1, :]), (6, coef_y[1, j // 2, at : at + 1, :])]
                both = rows_tile(rows)
                for i, value in ((2 * j, even_part(both)), (2 * j + 1, odd_part(both))):
                    if i < 18:
                        ring_w[p, i] = value
                    elif i < 27:
                        ring_r[p, i - 18] = jnp.where(filled, value, 1.0) if i in (18, 22, 26) else value
        finish(ring_w, ring_r, ring_diag, ring_inverse, 6)
        off_high = jnp.logical_and(row_at == 5, is_high_y)
        off_low = jnp.logical_and(row_at == 2, is_low_y)
        for c in range(3):
            ring_w[4, c] = jnp.where(is_high_x, 0.0, ring_w[4, c])
            ring_w[1, 3 + c] = jnp.where(is_low_x, 0.0, ring_w[1, 3 + c])

        def body(p):
            for k, off in ((2, off_high), (3, off_low), (4, lane_at >= lanes - 2), (5, lane_at < 2)):
                for c in range(3):
                    ring_w[p, 3 * k + c] = jnp.where(off, 0.0, ring_w[p, 3 * k + c])

        each(6, body)

    def send_pairs(turn):
        for x in range(4):
            for c in range(3):
                pair_own[x, c] = jnp.where(odd, sources[1][x, c], fields[1][0, x + 1, c])
        for side, y in ((0, 4), (1, 0)):
            for c in range(3):
                rows = [(2 * x + k, pair_own[x, c, y + 2 * k : y + 2 * k + 1, :]) for x in range(4) for k in range(2)]
                pair_y_send[side, c] = rows_tile(rows)
        for sx in range(2):
            for sy in range(2):
                x, y = 3 - 3 * sx, 6 - 6 * sy
                for i, (at_x, at_y) in enumerate(((x, y), (2 - sx, y), (x, 4 - 2 * sy))):
                    for c in range(3):
                        n = 3 * i + c
                        pair_corner_send[2 * sx + sy, n : n + 1, :] = pair_own[at_x, c, at_y : at_y + 1, :]
        copies = []
        sems = lambda n: (pair_send_sem.at[n], pair_recv_sem.at[turn, n])
        for side, to in ((0, 1), (1, -1)):
            copies.append(remote(pair_y_send.at[side], pair_y.at[turn, side], *sems(side), (0, to)))
            source = pair_own.at[pl.ds(2 - 2 * side, 2)]
            copies.append(remote(source, pair_x.at[turn, side], *sems(2 + side), (to, 0)))
        for sx in range(2):
            for sy in range(2):
                n = 2 * sx + sy
                to = (1 - 2 * sx, 1 - 2 * sy)
                copies.append(remote(pair_corner_send.at[n], pair_corner.at[turn, n], *sems(4 + n), to))
        return copies

    def take_pairs(turn, copies):
        for copy in copies:
            copy.wait()
        for p in range(8):
            for c in range(3):
                if 2 <= p < 6:
                    x = p - 2
                    rows = [(2 + k, pair_own[x, c, 2 * k : 2 * k + 1, :]) for k in range(4)]
                    for side in range(2):
                        for k in range(2):
                            at = 2 * x + k
                            rows.append((6 * side + k, pair_y[turn, side, c, at : at + 1, :]))
                else:
                    side = p // 4
                    rows = [(2 + k, pair_x[turn, side, p - 6 * side, c, 2 * k : 2 * k + 1, :]) for k in range(4)]
                    for sy in range(2):
                        cells = ((0, 1 + 5 * sy), (2, 7 * sy)) if p in (1, 6) else ((1, 1 + 5 * sy),)
                        for i, row in cells:
                            n = 3 * i + c
                            rows.append((row, pair_corner[turn, 2 * side + sy, n : n + 1, :]))
                both = rows_tile(rows)
                ring_u[p, c] = even_part(both)
                if 1 <= p < 7:
                    ring_b[p - 1, c] = odd_part(both)

    def ring_sweep():
        def add(p):
            x = p // 2 - 1
            for c in range(3):
                e = jnp.where(row_at < 2, mid_at(c, x, -1), mid_at(c, x, 0))
                e = jnp.where(row_at < 4, e, jnp.where(row_at < 6, mid_at(c, x, 1), mid_at(c, x, 2)))
                ring_u[p, c] += e

        for p in range(8):
            add(p)
        for p in range(6):
            u = [ring_u[p + 1, c] for c in range(3)]
            left = []
            for c in range(3):
                value = ring_b[p, c] - ring_diag[p, c] * u[c]
                near = (ring_u[p + 2, c], ring_u[p, c], down(u[c], -1), down(u[c], 1), along(u[c], -2), along(u[c], 2))
                for k in range(6):
                    value = value + ring_w[p, 3 * k + c] * near[k]
                for d in range(3):
                    if d != c:
                        value = value - ring_r[p, 3 * d + c] * u[d]
                left.append(value)
            step = apply_inverse(ring_inverse, p, left)
            for c in range(3):
                ring_out[p, c] = u[c] + step[c]

    def add_to_finest(at, slot):
        f = fields[0]
        for c in range(3):
            for p in range(6):
                rows = [wide(ring_out[p, c, 2 + k : 3 + k, :]) for k in range(4)]
                e = jnp.where(row_at < 2, rows[0], rows[1])
                e = jnp.where(row_at < 4, e, jnp.where(row_at < 6, rows[2], rows[3]))
                for x in {0: (-1,), 5: (8,)}.get(p, (2 * p - 2, 2 * p - 1)):
                    f[at, x + 1, c] += e
            for side, row in ((0, 1), (1, 6)):
                rows = [wide(ring_out[1 + k, c, row : row + 1, :]) for k in range(4)]
                e = jnp.where(row_at < 2, rows[0], rows[1])
                e = jnp.where(row_at < 4, e, jnp.where(row_at < 6, rows[2], rows[3]))
                rows_halo[slot, side, c] += e

    def packed_y(f, at):
        return rows_tile([(x, f(x)[at : at + 1, :]) for x in range(8)])

    def send_rim():
        copies = []
        sems = lambda n: (rim_send_sem.at[n], rim_recv_sem.at[n])
        for side, to in ((0, 1), (1, -1)):
            row, second = 7 - 7 * side, 6 - 5 * side
            for i in range(9):
                rim_y_send[side, i] = rows_tile([(x, reaction[0][x, i, row : row + 1, :]) for x in range(8)])
            rim_y_send[side, 9] = rows_tile([(x, pot[x + 1, second : second + 1, :]) for x in range(8)])
            for c in range(3):
                rim_y_send[side, 10 + c] = rows_tile([(x, base[x, c, row : row + 1, :]) for x in range(8)])
            copies.append(remote(rim_y_send.at[side], rim_y.at[side], *sems(side), (0, to)))
            copies.append(remote(reaction[0].at[row], rim_r.at[side], *sems(2 + side), (to, 0)))
            copies.append(remote(pot.at[second + 1], rim_pot.at[side], *sems(4 + side), (to, 0)))
            copies.append(remote(base.at[row], rim_base.at[side], *sems(6 + side), (to, 0)))
        for n in range(4):
            x, y = 7 - 7 * (n // 2), 7 - 7 * (n % 2)
            rim_pot_corner_send[n] = pot[x + 1, y : y + 1, :]
            to = (1 - 2 * (n // 2), 1 - 2 * (n % 2))
            copies.append(remote(rim_pot_corner_send.at[n], rim_pot_corner.at[n], *sems(8 + n), to))
        return copies

    def ordered(t, out_side, in_side, ahead, behind, above, below):
        across = (in_side, out_side) if t % 2 == 0 else (out_side, in_side)
        return (across + (ahead, behind) if t < 2 else (ahead, behind) + across) + (above, below)

    def take_rim(copies):
        for copy in copies:
            copy.wait()
        for side in range(2):
            for i in range(9):
                rim_r[2 + side, i] = rim_y[side, i]
            for c in range(3):
                rim_base[2 + side, c] = rim_y[side, 10 + c]
        for t in range(4):
            side = t % 2
            if t < 2:
                here, beyond, inside = pot[9 * side], rim_pot[side], pot[1 + 7 * side]
                first, last = 2 * side, 2 * side + 1
                edges = (is_low_y, is_high_y)
            else:
                here, beyond = pot_y[side], rim_y[side, 9]
                row = 7 * side
                inside = rows_tile([(x, pot[x + 1, row : row + 1, :]) for x in range(8)])
                first, last = side, 2 + side
                edges = (is_low_x, is_high_x)
            corner = lambda n, off: jnp.where(off, 0.0, wide(rim_pot_corner[n]))
            near = ordered(
                t,
                beyond,
                inside,
                jnp.where(row_at == ROWS - 1, corner(last, edges[1]), down(here, -1)),
                jnp.where(row_at == 0, corner(first, edges[0]), down(here, 1)),
                jnp.where(lane_at == lanes - 1, 0.0, along(here, -1)),
                jnp.where(lane_at == 0, 0.0, along(here, 1)),
            )
            for k in range(6):
                plus, minus = face_weights(here - near[k])
                rim_w[t, 3 * k] = jnp.ones(tile, jnp.float32)
                rim_w[t, 3 * k + 1] = plus
                rim_w[t, 3 * k + 2] = minus
        finish(rim_w, rim_r, rim_diag, rim_inverse, 4)
        for t in range(4):
            ahead, off_high, off_low = (2, is_high_y, is_low_y) if t < 2 else (0, is_high_x, is_low_x)
            masks = (
                (ahead, jnp.logical_and(row_at == ROWS - 1, off_high)),
                (ahead + 1, jnp.logical_and(row_at == 0, off_low)),
                (4, lane_at == lanes - 1),
                (5, lane_at == 0),
            )
            for k, off in masks:
                for c in range(3):
                    rim_w[t, 3 * k + c] = jnp.where(off, 0.0, rim_w[t, 3 * k + c])

    def doubled(rows):
        e = jnp.where(row_at < 2, wide(rows[0]), wide(rows[1]))
        return jnp.where(row_at < 4, e, jnp.where(row_at < 6, wide(rows[2]), wide(rows[3])))

    def rim_sweep(at):
        for t in range(4):
            side = t % 2
            e, near = [], []
            for c in range(3):
                cell = lambda p, row: ring_out[p, c, row : row + 1, :]
                if t < 2:
                    p, p_in = 5 * side, 1 + 3 * side
                    here = doubled([cell(p, 2 + k) for k in range(4)])
                    inside = doubled([cell(p_in, 2 + k) for k in range(4)])
                    first, last = cell(p, 1), cell(p, 6)
                else:
                    row, row_in = 1 + 5 * side, 2 + 3 * side
                    here = doubled([cell(1 + k, row) for k in range(4)])
                    inside = doubled([cell(1 + k, row_in) for k in range(4)])
                    first, last = cell(0, row), cell(5, row)
                e.append(here)
                near.append(
                    ordered(
                        t,
                        here,
                        inside,
                        jnp.where(row_at == ROWS - 1, wide(last), down(here, -1)),
                        jnp.where(row_at == 0, wide(first), down(here, 1)),
                        along(here, -1),
                        along(here, 1),
                    )
                )
            left = []
            for c in range(3):
                value = -rim_diag[t, c] * e[c]
                for k in range(6):
                    value = value + rim_w[t, 3 * k + c] * near[c][k]
                for d in range(3):
                    if d != c:
                        value = value - rim_r[t, 3 * d + c] * e[d]
                left.append(value)
            step = apply_inverse(rim_inverse, t, left)
            for c in range(3):
                value = rim_base[t, c] + e[c] + step[c]
                if t < 2:
                    fields[0][at, 9 * side, c] = value
                else:
                    rows_halo[3, side, c] = value

    def source(level, x):
        if level == 0:
            return [grad[c, x] for c in range(3)]
        return [sources[level][x, c] for c in range(3)]

    def solve(level, x, r):
        v = inverse[level]
        return [v[x, 3 * c] * r[0] + v[x, 3 * c + 1] * r[1] + v[x, 3 * c + 2] * r[2] for c in range(3)]

    def share(level, at, beside_it=lambda: None):
        slot, f, count = done[0] % 3, fields[level], NX[level]
        for side, row in ((0, ROWS - 1), (1, 0)):
            for c in range(3):
                packed = wide(f[at, 1, c, row : row + 1, :])
                for x in range(1, count):
                    packed = jnp.where(row_at == x, wide(f[at, x + 1, c, row : row + 1, :]), packed)
                send_y[side, c] = packed
        wait = exchange(
            [
                (f.at[at, count], f.at[at, 0]),
                (f.at[at, 1], f.at[at, count + 1]),
                (send_y.at[0], rows_halo.at[slot, 0]),
                (send_y.at[1], rows_halo.at[slot, 1]),
            ]
        )
        beside_it()
        inner(level, at)
        wait()
        return slot

    def inner(level, at):
        f, w, r, span, count = fields[level], weights[level], reaction[level], 1 << level, NX[level]
        for x in range(count):
            u = [f[at, x + 1, c] for c in range(3)]
            b = source(level, x)
            for c in range(3):
                value = b[c] - diag[level][x, c] * u[c]
                value = value + w[x, 6 + c] * jnp.where(row_at >= ROWS - span, 0.0, down(u[c], -span))
                value = value + w[x, 9 + c] * jnp.where(row_at < span, 0.0, down(u[c], span))
                value = value + w[x, 12 + c] * along(u[c], -span) + w[x, 15 + c] * along(u[c], span)
                if x < count - 1:
                    value = value + w[x, c] * f[at, x + 2, c]
                if x > 0:
                    value = value + w[x, 3 + c] * f[at, x, c]
                for d in range(3):
                    if d != c:
                        value = value - r[x, 3 * d + c] * u[d]
                part[x, c] = value

    def rest(level, at, slot, x):
        f, w, span, count = fields[level], weights[level], 1 << level, NX[level]
        left = []
        for c in range(3):
            row_high, row_low = (rows_halo[slot, side, c, x : x + 1, :] for side in (1, 0))
            value = jnp.where(row_at >= ROWS - span, w[x, 6 + c] * wide(row_high), 0.0)
            value = part[x, c] + jnp.where(row_at < span, w[x, 9 + c] * wide(row_low), value)
            if x == 0:
                value = value + w[x, 3 + c] * f[at, 0, c]
            if x == count - 1:
                value = value + w[x, c] * f[at, count + 1, c]
            left.append(value)
        return [f[at, x + 1, c] for c in range(3)], left

    def residual(level, at, slot, x):
        f, w, r, span = fields[level], weights[level], reaction[level], 1 << level
        u = [f[at, x + 1, c] for c in range(3)]
        b = source(level, x)
        left = []
        for c in range(3):
            near = (
                f[at, x + 2, c],
                f[at, x, c],
                jnp.where(row_at >= ROWS - span, wide(rows_halo[slot, 1, c, x : x + 1, :]), down(u[c], -span)),
                jnp.where(row_at < span, wide(rows_halo[slot, 0, c, x : x + 1, :]), down(u[c], span)),
                along(u[c], -span),
                along(u[c], span),
            )
            value = b[c] - diag[level][x, c] * u[c]
            for k in range(6):
                value = value + w[x, 3 * k + c] * near[k]
            for d in range(3):
                if d != c:
                    value = value - r[x, 3 * d + c] * u[d]
            left.append(value)
        return u, left

    def sweep(at, slot, left_of, last=False):
        copies = []
        for x in range(NX[0]):
            u, left = left_of(0, at, slot, x)
            step = solve(0, x, left)
            for c in range(3):
                if last:
                    result[c, x] = u[c] + step[c]
                else:
                    fields[0][at + 1, x + 1, c] = u[c] + step[c]
            if last:
                copies.append(pltpu.make_async_copy(result.at[:, x], out.at[:, x], out_sem.at[x]))
                copies[-1].start()
        for copy in copies:
            copy.wait()
        return at + 1

    def restrict(level, at, slot, keep=False):
        rows, lanes_ = pair_tools(level)[4:]
        for x in range(NX[level + 1]):
            left = []
            for i in range(2):
                u, r = rest(level, at, slot, 2 * x + i)
                left.append(r)
                if keep:
                    step = solve(level, 2 * x + i, r)
                    for c in range(3):
                        base[2 * x + i, c] = u[c] + step[c]
            total = [lanes_(rows(left[0][c] + left[1][c])) for c in range(3)]
            first = solve(level + 1, x, total)
            for c in range(3):
                sources[level + 1][x, c] = total[c]
                fields[level + 1][0, x + 1, c] = first[c]

    def cycle(at, turn, besides, last=False):
        slot = share(0, at, besides[0])
        restrict(0, at, slot, keep=not last)
        pairs = []

        def beside():
            pairs.extend(send_pairs(turn))
            besides[1]()

        restrict(1, 0, share(1, 0, beside))

        def beside_q():
            take_pairs(turn, pairs)
            besides[3]()

        lower(turn, besides[2], beside_q)
        ring_sweep()
        if not last:
            rim_sweep(at + 1)
        add_to_finest(at, slot)
        return sweep(at, slot, residual, last)

    def start(x):
        for c, value in enumerate(solve(0, x, source(0, x))):
            fields[0][0, x + 1, c] = value

    finish_level(0)
    loads["grad"].wait()
    each(NX[0], start)
    pending, ring_pending, rim_pending = [], [], []

    def beside_first():
        coarsen(0)
        mask_level(0)
        finish_level(1)
        coarsen(1)
        pending.append(send_coefficients())

    def beside_second():
        pair_up()
        mask_level(1)
        finish_level(2)
        coarsen(2)
        pending.append(send_low_coefficients())

    def beside_third():
        ring_pending.extend(send_ring_coefficients())
        rim_pending.extend(send_rim())
        take_coefficients(pending)

    def beside_fourth():
        take_ring_coefficients(ring_pending)
        take_rim(rim_pending)

    nothing = lambda: None
    at = cycle(
        0,
        0,
        (
            beside_first,
            beside_second,
            beside_third,
            beside_fourth,
        ),
    )
    at = sweep(at, 3, residual)
    cycle(at, 1, (nothing,) * 4, last=True)


def local(counts, gradient, potential, coupling, region, contact, rates):
    nz = potential.shape[-1]
    tile = (ROWS, nz)
    f32 = jnp.float32
    scratch = []
    for parts in (18, 9, 3, 9):
        scratch += [pltpu.VMEM((n, parts) + tile, f32) for n in NX]
    scratch += [pltpu.VMEM((n, 3) + tile, f32) for n in NX[1:]]
    scratch += [pltpu.VMEM((3, n + 2, 3) + tile, f32) for n in NX]
    scratch += [
        pltpu.VMEM((4, 2, 3) + tile, f32),
        pltpu.VMEM((2,) + tile, f32),
        pltpu.VMEM((2, 3) + tile, f32),
        pltpu.SemaphoreType.DMA((4,)),
        pltpu.SemaphoreType.DMA((3, 4)),
        pltpu.VMEM((1, 18) + tile, f32),
        pltpu.VMEM((1, 9) + tile, f32),
        pltpu.VMEM((SLOTS, 18) + tile, f32),
        pltpu.VMEM((SLOTS, 9) + tile, f32),
        pltpu.VMEM((SLOTS, 3) + tile, f32),
        pltpu.VMEM((SLOTS, 9) + tile, f32),
        pltpu.VMEM((SLOTS, 3) + tile, f32),
        pltpu.VMEM((SLOTS, 3) + tile, f32),
        pltpu.VMEM((2, 4, 3) + tile, f32),
        pltpu.VMEM((27, 1, nz), f32),
        pltpu.VMEM((len(INNER), 27, 1, nz), f32),
        pltpu.VMEM((4, nz), f32),
        pltpu.VMEM((len(FOURTH), 4, nz), f32),
        pltpu.VMEM((2, 3, 1, nz), f32),
        pltpu.VMEM((2, len(INNER + OUTER), 3, 1, nz), f32),
        pltpu.VMEM((1, 1, nz), f32),
        pltpu.VMEM((2, len(THIRD), 1, nz), f32),
        pltpu.SemaphoreType.DMA,
        pltpu.SemaphoreType.DMA,
        pltpu.SemaphoreType.DMA,
        pltpu.SemaphoreType.DMA,
        pltpu.SemaphoreType.DMA,
        pltpu.SemaphoreType.DMA((2,)),
        pltpu.SemaphoreType.DMA,
        pltpu.SemaphoreType.DMA((2,)),
        pltpu.VMEM((8, 3) + tile, f32),
        pltpu.VMEM((6, 3) + tile, f32),
        pltpu.VMEM((6, 18) + tile, f32),
        pltpu.VMEM((6, 9) + tile, f32),
        pltpu.VMEM((6, 3) + tile, f32),
        pltpu.VMEM((6, 9) + tile, f32),
        pltpu.VMEM((6, 3) + tile, f32),
        pltpu.VMEM((4, 3) + tile, f32),
        pltpu.VMEM((2, 2, 2, 3) + tile, f32),
        pltpu.VMEM((2, 3) + tile, f32),
        pltpu.VMEM((2, 2, 3) + tile, f32),
        pltpu.VMEM((4, 2 * ROWS, nz), f32),
        pltpu.VMEM((2, 4, 2 * ROWS, nz), f32),
        pltpu.SemaphoreType.DMA((8,)),
        pltpu.SemaphoreType.DMA((2, 8)),
        pltpu.VMEM((4, 14) + tile, f32),
        pltpu.VMEM((2, 14) + tile, f32),
        pltpu.VMEM((2, 7) + tile, f32),
        pltpu.VMEM((2, 7) + tile, f32),
        pltpu.SemaphoreType.DMA((8,)),
        pltpu.SemaphoreType.DMA((8,)),
        pltpu.VMEM((NX[0], 3) + tile, f32),
        pltpu.VMEM((4, 2 * ROWS, nz), f32),
        pltpu.VMEM((4, 2 * ROWS, nz), f32),
        pltpu.VMEM((4, 18) + tile, f32),
        pltpu.VMEM((4, 9) + tile, f32),
        pltpu.VMEM((4, 3) + tile, f32),
        pltpu.VMEM((4, 9) + tile, f32),
        pltpu.VMEM((4, 3) + tile, f32),
        pltpu.VMEM((2,) + tile, f32),
        pltpu.VMEM((4, 1, nz), f32),
        pltpu.VMEM((4, 1, nz), f32),
        pltpu.VMEM((NX[0], 3) + tile, f32),
        pltpu.VMEM((2, 13) + tile, f32),
        pltpu.VMEM((2, 13) + tile, f32),
        pltpu.SemaphoreType.DMA((12,)),
        pltpu.SemaphoreType.DMA((12,)),
        pltpu.VMEM(gradient.shape, f32),
        pltpu.SemaphoreType.DMA((NX[0],)),
        pltpu.VMEM(gradient.shape, f32),
        pltpu.VMEM((10,) + tile, f32),
        pltpu.VMEM(coupling.shape, f32),
        pltpu.VMEM(region.shape, jnp.int32),
        pltpu.VMEM(contact.shape, jnp.int32),
        pltpu.SMEM(rates.shape, f32),
        pltpu.SemaphoreType.DMA((6,)),
    ]
    return pl.pallas_call(
        functools.partial(kernel, counts),
        out_shape=jax.ShapeDtypeStruct(gradient.shape, f32),
        in_specs=[pl.BlockSpec(memory_space=pltpu.HBM)] * 6,
        out_specs=pl.BlockSpec(memory_space=pltpu.HBM),
        scratch_shapes=scratch,
        compiler_params=pltpu.CompilerParams(
            collective_id=0, has_side_effects=True, vmem_limit_bytes=60 * 1024 * 1024
        ),
    )(gradient, potential, coupling, region, contact, rates)


def solution(mesh):
    placed = (
        P(None, "gx", "gy", None),
        P("gx", "gy", None),
        P(None, None, "gx", "gy", None),
        P("gx", "gy", None),
        P("gx", "gy", None),
        P(),
    )
    counts = (mesh.shape["gx"], mesh.shape["gy"])
    return jax.shard_map(
        functools.partial(local, counts),
        mesh=mesh,
        in_specs=placed,
        out_specs=P(None, "gx", "gy", None),
        check_vma=False,
    )
```

```python
import functools

import jax
import jax.numpy as jnp
from jax import lax
from jax.experimental import pallas as pl
from jax.experimental.pallas import tpu as pltpu
from jax.sharding import PartitionSpec as P

MESH = pl.DeviceIdType.MESH
LEVELS = 4
COARSE_SWEEPS = 6
REGIONS = 4
OMEGA = 0.8
STRENGTH = 8.0
ROWS = 8
NX = (8, 4, 2, 1)
RADIUS = 3
SLOTS = 8


def around(shape, far):
    reach = range(-6, 7)
    distance = lambda i, j: min(abs(i - a) + abs(j - b) for a, b in shape)
    found = [(i, j) for i in reach for j in reach if distance(i, j) <= far and (i, j) != (0, 0)]
    return sorted(found, key=lambda o: -abs(o[0]) - abs(o[1]))


OWN = [(0, 0)]
SQUARE = [(i, j) for i in (-1, 0, 1) for j in (-1, 0, 1)]
INNER = around(OWN, 2)
OUTER = [o for o in around(OWN, 3) if o not in INNER]
FOURTH = around(SQUARE, 2)
THIRD = around(SQUARE, 3)


def each(count, body):
    if count == 1:
        body(0)
        return

    def step(i, carry):
        body(i)
        return carry

    lax.fori_loop(0, count, step, 0, unroll=count)


def face_weights(difference):
    size = jnp.abs(difference)
    small = size < 0.5
    series = 1.0 / 362880.0
    for k in (40320.0, 5040.0, 720.0, 120.0, 24.0, 6.0, 2.0, 1.0):
        series = series * size + 1.0 / k
    below = jnp.where(small, series, jnp.exp(size) - 1.0)
    low = jnp.where(small, 1.0, size) / below
    low = jnp.where(size < 1e-4, 1.0 - 0.5 * size, low)
    high = low + size
    positive = difference > 0.0
    return jnp.where(positive, low, high), jnp.where(positive, high, low)


def kernel(counts, grad_in, pot_in, coup_in, region_in, contact_in, rates_in, out, *scratch):
    grad, pot, coup, region, contact, rates, in_sem = scratch[-7:]
    scratch = scratch[:-7]
    loads = {}
    for i, (name, source, target) in enumerate(
        (
            ("pot", pot_in, pot.at[pl.ds(1, 8)]),
            ("rates", rates_in, rates),
            ("region", region_in, region),
            ("contact", contact_in, contact),
            ("coup", coup_in, coup),
            ("grad", grad_in, grad),
        )
    ):
        loads[name] = pltpu.make_async_copy(source, target, in_sem.at[i])
        loads[name].start()
    weights, reaction, diag, inverse = (scratch[4 * i : 4 * i + 4] for i in range(4))
    sources = (None,) + tuple(scratch[16:19])
    fields = scratch[19:23]
    rows_halo, pot_y, send_y, send_sem, recv_sem = scratch[23:28]
    w_own, r_own, w_wide, r_wide, diag_wide, inverse_wide, u_wide, b_wide, e_rows = scratch[28:37]
    mid_send, mid_recv, low_send, low_recv, mid_cell, mid_cells, low_cell, low_cells = scratch[37:45]
    mid_send_sem, mid_recv_sem, low_send_sem, low_recv_sem, p_send, p_recv, q_send, q_recv = scratch[45:53]
    ring_u, ring_b, ring_w, ring_r, ring_diag, ring_inverse, ring_out = scratch[53:60]
    pair_own, pair_x, pair_y_send, pair_y, pair_corner_send, pair_corner, pair_send_sem, pair_recv_sem = scratch[60:68]
    coef_own, coef_x, coef_y_send, coef_y, coef_send_sem, coef_recv_sem, part, coef_corner_send, coef_corner = scratch[68:77]
    rim_w, rim_r, rim_diag, rim_inverse, rim_base, rim_pot, rim_pot_corner_send, rim_pot_corner = scratch[77:85]
    base, rim_y_send, rim_y, rim_send_sem, rim_recv_sem, result, out_sem = scratch[85:92]
    halo_inverse, cross, cross_send, cross_recv, lean, lean_x, lean_y_send, lean_y = scratch[92:100]
    lean_send_sem, lean_recv_sem = scratch[100:]
    n_x, n_y = counts
    lanes = out.shape[-1]
    gx, gy = lax.axis_index("gx"), lax.axis_index("gy")
    x_low, x_high = lax.rem(gx + n_x - 1, n_x), lax.rem(gx + 1, n_x)
    y_low, y_high = lax.rem(gy + n_y - 1, n_y), lax.rem(gy + 1, n_y)
    beside = ((x_high, gy), (x_low, gy), (gx, y_high), (gx, y_low))

    barrier = pltpu.get_barrier_semaphore()
    at_offset = lambda i, j: (lax.rem(gx + n_x + i, n_x), lax.rem(gy + n_y + j, n_y))
    devices = {o: at_offset(*o) for o in THIRD}
    for offset in INNER:
        pl.semaphore_signal(barrier, inc=1, device_id=devices[offset], device_id_type=MESH)
    pl.semaphore_wait(barrier, len(INNER))

    tile = (ROWS, lanes)
    row_at = lax.broadcasted_iota(jnp.int32, tile, 0)
    lane_at = lax.broadcasted_iota(jnp.int32, tile, 1)
    wide = lambda row: jnp.broadcast_to(row, tile)
    down = lambda v, by: pltpu.roll(v, by % ROWS, 0) if by % ROWS else v
    along = lambda v, by: pltpu.roll(v, by % lanes, 1)

    done = [0]

    def exchange(parts):
        slot = done[0] % 3
        done[0] += 1
        copies = []
        for i in (2, 3, 0, 1):
            source, target = parts[i]
            copy = pltpu.make_async_remote_copy(
                src_ref=source,
                dst_ref=target,
                send_sem=send_sem.at[i],
                recv_sem=recv_sem.at[slot, i],
                device_id=beside[i],
                device_id_type=MESH,
            )
            copy.start()
            copies.append(copy)

        def wait():
            for copy in copies:
                copy.wait()

        return wait

    def remote(source, target, send, recv, offset):
        copy = pltpu.make_async_remote_copy(
            src_ref=source,
            dst_ref=target,
            send_sem=send,
            recv_sem=recv,
            device_id=devices[offset],
            device_id_type=MESH,
        )
        copy.start()
        return copy

    def gather(offsets, source_of, target, send, recv):
        for n, (i, j) in enumerate(offsets):
            remote(source_of((i, j)), target.at[n], send, recv, (-i, -j))

        def wait():
            pltpu.make_async_copy(target, target, send).wait()
            pltpu.make_async_copy(target, target, recv).wait()

        return wait

    loads["pot"].wait()
    for side, at in ((0, ROWS - 1), (1, 0)):
        packed = wide(pot[1, at : at + 1, :])
        for x in range(1, 8):
            packed = jnp.where(row_at == x, wide(pot[x + 1, at : at + 1, :]), packed)
        send_y[side, 0] = packed
    wait = exchange(
        [
            (pot.at[8], pot.at[0]),
            (pot.at[1], pot.at[9]),
            (send_y.at[0, 0], pot_y.at[0]),
            (send_y.at[1, 0], pot_y.at[1]),
        ]
    )
    for name in ("rates", "region", "contact", "coup"):
        loads[name].wait()

    def put_faces(x, k, plus, minus):
        weights[0][x, 3 * k] = jnp.ones(tile, jnp.float32)
        weights[0][x, 3 * k + 1] = plus
        weights[0][x, 3 * k + 2] = minus

    def set_up(x):
        here = pot[x + 1]
        put_faces(x, 4, *face_weights(here - jnp.where(lane_at == lanes - 1, 0.0, along(here, -1))))
        put_faces(x, 5, *face_weights(here - jnp.where(lane_at == 0, 0.0, along(here, 1))))
        plus, minus = face_weights(here - down(here, -1))
        put_faces(x, 2, plus, minus)
        put_faces(x, 3, down(minus, 1), down(plus, 1))
        at_contact = STRENGTH * contact[x].astype(jnp.float32)
        regions = region[x]
        for c in range(3):
            extra = jnp.full(tile, rates[0, c])
            for pick in range(1, REGIONS):
                extra = jnp.where(regions == pick, rates[pick, c], extra)
            for d in range(3):
                value = coup[c, d, x]
                reaction[0][x, 3 * c + d] = value + (extra + at_contact) if c == d else value

    each(NX[0], set_up)
    for x in range(7):
        plus, minus = face_weights(pot[x + 1] - pot[x + 2])
        put_faces(x, 0, plus, minus)
        put_faces(x + 1, 1, minus, plus)
    wait()
    is_low_x, is_high_x = gx == 0, gx == n_x - 1
    is_low_y, is_high_y = gy == 0, gy == n_y - 1
    pot[0] = jnp.where(is_low_x, 0.0, pot[0])
    pot[9] = jnp.where(is_high_x, 0.0, pot[9])
    pot_y[0] = jnp.where(is_low_y, 0.0, pot_y[0])
    pot_y[1] = jnp.where(is_high_y, 0.0, pot_y[1])

    put_faces(0, 1, *face_weights(pot[1] - pot[0]))
    put_faces(7, 0, *face_weights(pot[8] - pot[9]))
    for side, k, row in ((0, 2, ROWS - 1), (1, 3, 0)):
        part[side, 0], part[side, 1] = face_weights(send_y[side, 0] - pot_y[1 - side])
        for x in range(8):
            for c in (1, 2):
                value = wide(part[side, c - 1, x : x + 1, :])
                weights[0][x, 3 * k + c] = jnp.where(row_at == row, value, weights[0][x, 3 * k + c])

    def finish(w, r, diagonal, inv, count):
        def body(x):
            m = [[r[x, 3 * col + row] for col in range(3)] for row in range(3)]
            for c in range(3):
                total = w[x, c]
                for k in range(1, 6):
                    total = total + w[x, 3 * k + c]
                m[c][c] = m[c][c] + total
                diagonal[x, c] = m[c][c]

            def cofactor(i, j):
                i1, i2, j1, j2 = (i + 1) % 3, (i + 2) % 3, (j + 1) % 3, (j + 2) % 3
                return m[i1][j1] * m[i2][j2] - m[i1][j2] * m[i2][j1]

            cof = [[cofactor(i, j) for j in range(3)] for i in range(3)]
            det = m[0][0] * cof[0][0] + m[0][1] * cof[0][1] + m[0][2] * cof[0][2]
            scale = OMEGA / det
            for i in range(3):
                for j in range(3):
                    inv[x, 3 * i + j] = cof[j][i] * scale

        each(count, body)

    def finish_level(level):
        finish(weights[level], reaction[level], diag[level], inverse[level], NX[level])

    def mask_level(level):
        w, span, last = weights[level], 1 << level, NX[level] - 1
        for c in range(3):
            w[last, c] = jnp.where(is_high_x, 0.0, w[last, c])
            w[0, 3 + c] = jnp.where(is_low_x, 0.0, w[0, 3 + c])
        off_high = jnp.logical_and(row_at >= ROWS - span, is_high_y)
        off_low = jnp.logical_and(row_at < span, is_low_y)
        off_up, off_down = lane_at >= lanes - span, lane_at < span

        def body(x):
            for k, off in ((2, off_high), (3, off_low), (4, off_up), (5, off_down)):
                for c in range(3):
                    w[x, 3 * k + c] = jnp.where(off, 0.0, w[x, 3 * k + c])

        each(NX[level], body)

    def pair_tools(level):
        span = 1 << level
        odd_row = (row_at & span) != 0
        odd_lane = (lane_at & span) != 0

        def high_row(v):
            return jnp.where(odd_row, v, down(v, -span))

        def low_row(v):
            return jnp.where(odd_row, down(v, span), v)

        def high_lane(v):
            return jnp.where(odd_lane, v, along(v, -span))

        def low_lane(v):
            return jnp.where(odd_lane, along(v, span), v)

        def rows(v):
            return v + jnp.where(odd_row, down(v, span), down(v, -span))

        def lanes_(v):
            return v + jnp.where(odd_lane, along(v, span), along(v, -span))

        return high_row, low_row, high_lane, low_lane, rows, lanes_

    def coarsen(level):
        high_row, low_row, high_lane, low_lane, rows, lanes_ = pair_tools(level)
        w, r = weights[level], reaction[level]
        w_next, r_next = (w_own, r_own) if level == LEVELS - 2 else (weights[level + 1], reaction[level + 1])

        def body(x):
            for c in range(3):
                w_next[x, c] = lanes_(rows(w[2 * x + 1, c]))
                w_next[x, 3 + c] = lanes_(rows(w[2 * x, 3 + c]))
                pair = lambda k: w[2 * x, 3 * k + c] + w[2 * x + 1, 3 * k + c]
                w_next[x, 6 + c] = lanes_(high_row(pair(2)))
                w_next[x, 9 + c] = lanes_(low_row(pair(3)))
                w_next[x, 12 + c] = high_lane(rows(pair(4)))
                w_next[x, 15 + c] = low_lane(rows(pair(5)))
            for i in range(9):
                r_next[x, i] = lanes_(rows(r[2 * x, i] + r[2 * x + 1, i]))

        each(NX[level + 1], body)

    slot_at = lane_at & (SLOTS - 1)
    x_at, y_at = row_at + (gx - RADIUS), slot_at + (gy - RADIUS)
    x_last = jnp.logical_or(x_at == n_x - 1, x_at == -1)
    x_first = jnp.logical_or(x_at == 0, x_at == n_x)
    y_last = jnp.logical_or(y_at == n_y - 1, y_at == -1)
    y_first = jnp.logical_or(y_at == 0, y_at == n_y)
    z_last, z_first = lane_at >= lanes - SLOTS, lane_at < SLOTS
    offs = (x_last, x_first, y_last, y_first, z_last, z_first)
    bits = (2, 2, 1, 1, 4, 4)

    def transposed(tiles):
        tiles = list(tiles)
        for bit in (1, 2, 4):
            clear = (slot_at & bit) == 0
            for p in range(SLOTS):
                if not p & bit:
                    one, two = tiles[p], tiles[p | bit]
                    tiles[p] = jnp.where(clear, one, along(two, bit))
                    tiles[p | bit] = jnp.where(clear, along(one, -bit), two)
        return tiles

    def unpacked(offsets, row_of, own, fill=0.0):
        tiles = [jnp.full(tile, fill) for _ in range(SLOTS)]
        for n, (i, j) in enumerate(list(offsets) + OWN):
            if min(i, j) >= -RADIUS:
                row = row_of(n) if n < len(offsets) else own
                tiles[j + RADIUS] = jnp.where(row_at == i + RADIUS, wide(row), tiles[j + RADIUS])
        return transposed(tiles)

    def child_row(f, x0, c):
        which = slot_at & 3
        rows = [wide(f[x0 + p // 2, c, 4 * (p % 2) : 4 * (p % 2) + 1, :]) for p in range(4)]
        packed = jnp.where(which == 0, rows[0], jnp.where(which == 1, rows[1], jnp.where(which == 2, rows[2], rows[3])))
        return packed[0:1, :]

    def slot_row(values):
        packed = values[0]
        for i in range(1, len(values)):
            packed = jnp.where(slot_at == i, values[i], packed)
        return packed

    def send_coefficients():
        for i in range(27):
            mid_send[i] = child_row(weights[2] if i < 18 else reaction[2], 0, i if i < 18 else i - 18)
        return gather(INNER, lambda o: mid_send, mid_recv, mid_send_sem, mid_recv_sem)

    def send_low_coefficients():
        fields_ = [w_own[0, i] for i in range(18)] + [r_own[0, i] for i in range(9)]
        for row in range(4):
            low_send[row : row + 1, :] = slot_row(fields_[SLOTS * row : SLOTS * row + SLOTS])[0:1, :]
        return gather(FOURTH, lambda o: low_send, low_recv, low_send_sem, low_recv_sem)

    def take_coefficients(waits):
        for wait in waits:
            wait()
        for i in range(27):
            made = unpacked(INNER, lambda n: mid_recv[n, i], mid_send[i], 1.0 if i in (18, 22, 26) else 0.0)
            for p in range(SLOTS):
                if i < 18:
                    w_wide[p, i] = made[p]
                else:
                    r_wide[p, i - 18] = made[p]
        finish(w_wide, r_wide, diag_wide, inverse_wide, SLOTS)
        for k in range(6):
            for p in range(SLOTS):
                if ((p & bits[k]) != 0) == (k % 2 == 0):
                    for c in range(3):
                        w_wide[p, 3 * k + c] = jnp.where(offs[k], 0.0, w_wide[p, 3 * k + c])
        top = LEVELS - 1
        w, r = weights[top], reaction[top]
        for row in range(4):
            here = slice(row, row + 1)
            made = unpacked(FOURTH, lambda n: low_recv[n, here, :], low_send[here, :])
            for p in range(SLOTS):
                i = SLOTS * row + p
                if i < 18:
                    w[0, i] = made[p]
                elif i < 27:
                    r[0, i - 18] = made[p]
        finish_level(top)
        for k in range(6):
            for c in range(3):
                w[0, 3 * k + c] = jnp.where(offs[k], 0.0, w[0, 3 * k + c])

    def wide_residual(p, u):
        left = []
        for c in range(3):
            value = b_wide[p, c] - diag_wide[p, c] * u[p][c]
            for k in range(6):
                bit, ahead = bits[k], k % 2 == 0
                near = u[p ^ bit][c]
                if ((p & bit) != 0) == ahead:
                    turn = -1 if ahead else 1
                    near = down(near, turn) if k < 2 else along(near, turn if k < 4 else turn * SLOTS)
                value = value + w_wide[p, 3 * k + c] * near
            for d in range(3):
                if d != c:
                    value = value - r_wide[p, 3 * d + c] * u[p][d]
            left.append(value)
        return left

    def apply_inverse(v, x, r):
        return [v[x, 3 * c] * r[0] + v[x, 3 * c + 1] * r[1] + v[x, 3 * c + 2] * r[2] for c in range(3)]

    def wide_fields():
        return [[u_wide[p, c] for c in range(3)] for p in range(SLOTS)]

    def window_sweep(b, u, patches=None):
        top = LEVELS - 1
        w, r = weights[top], reaction[top]
        left = []
        for c in range(3):
            value = b[c] - diag[top][0, c] * u[c]
            before_x, before_y = down(u[c], 1), along(u[c], 1)
            if patches is not None:
                before_x = jnp.where(row_at == 0, patches[0][c], before_x)
                before_y = jnp.where(slot_at == 0, patches[1][c], before_y)
            near = (down(u[c], -1), before_x, along(u[c], -1), before_y, along(u[c], -SLOTS), along(u[c], SLOTS))
            for k in range(6):
                value = value + w[0, 3 * k + c] * near[k]
            for d in range(3):
                if d != c:
                    value = value - r[0, 3 * d + c] * u[d]
            left.append(value)
        step = apply_inverse(inverse[top], 0, left)
        return [u[c] + step[c] for c in range(3)]

    def lower(turn, beside_p, beside_q):
        for c in range(3):
            mid_cell[0, c] = child_row(sources[2], 0, c)
            mid_cell[1, c] = child_row(fields[2].at[0], 1, c)
        near = INNER + OUTER
        wait = gather(
            near, lambda o: mid_cell.at[0 if o in INNER else 1], mid_cells.at[turn], p_send, p_recv.at[turn]
        )
        beside_p()
        wait()
        for c in range(3):
            made = unpacked(near, lambda n: mid_cells[turn, n, c], mid_cell[0, c])
            for p in range(SLOTS):
                b_wide[p, c] = made[p]
        inner = jnp.abs(row_at - RADIUS) + jnp.abs(slot_at - RADIUS) <= 2
        for p in range(SLOTS):
            b = [b_wide[p, c] for c in range(3)]
            first = apply_inverse(inverse_wide, p, b)
            for c in range(3):
                u_wide[p, c] = jnp.where(inner, first[c], b[c])
        u_mid = wide_fields()
        b = [jnp.zeros(tile, jnp.float32) for _ in range(3)]
        for p in range(SLOTS):
            left = wide_residual(p, u_mid)
            b = [b[c] + left[c] for c in range(3)]
        u = apply_inverse(inverse[LEVELS - 1], 0, b)
        for _ in range(2):
            u = window_sweep(b, u)
        row = slot_row([along(value, i - RADIUS) for i, value in enumerate(u + b)])
        low_cell[0] = row[RADIUS : RADIUS + 1, :]
        wait = gather(THIRD, lambda o: low_cell.at[0], low_cells.at[turn], q_send, q_recv.at[turn])
        beside_q()
        wait()
        made = unpacked(THIRD, lambda n: low_cells[turn, n], low_cell[0])
        u, b = made[:3], made[3:6]
        before_x = [jnp.zeros(tile, jnp.float32) for _ in range(3)]
        last_y = jnp.zeros(tile, jnp.float32)
        for n, (i, j) in enumerate(THIRD):
            if i < -RADIUS:
                for c in range(3):
                    value = along(wide(low_cells[turn, n]), j + RADIUS - c)
                    before_x[c] = jnp.where(slot_at == j + RADIUS, value, before_x[c])
            if j < -RADIUS:
                last_y = jnp.where(row_at == i + RADIUS, wide(low_cells[turn, n]), last_y)
        before_y = [along(last_y, -c) for c in range(3)]
        u = window_sweep(b, u, (before_x, before_y))
        for _ in range(COARSE_SWEEPS - 4):
            u = window_sweep(b, u)
        u_mid = [[u_wide[p, c] + u[c] for c in range(3)] for p in range(SLOTS)]
        last = []
        for p in range(SLOTS):
            step = apply_inverse(inverse_wide, p, wide_residual(p, u_mid))
            last.append([u_mid[p][c] + step[c] for c in range(3)])
        for c in range(3):
            for x in range(2):
                for at, (t, y) in enumerate(((RADIUS - 1, 1), (RADIUS, 0), (RADIUS, 1), (RADIUS + 1, 0))):
                    low, high = last[2 * x + y][c], last[4 + 2 * x + y][c]
                    if t & 4:
                        value = jnp.where(slot_at == t, high, 0.0) + along(jnp.where(slot_at == t, low, 0.0), -4)
                    else:
                        value = jnp.where(slot_at == t, low, 0.0) + along(jnp.where(slot_at == t, high, 0.0), 4)
                    for bit in (1, 2):
                        value = value + along(value, -bit if t & bit else bit)
                    e_rows[x, at, c] = value

    def mid_at(c, x, y):
        row = RADIUS + (x // 2)
        return wide(e_rows[x % 2, y + 1, c, row : row + 1, :])

    odd = (lane_at & 1) != 0

    def even_part(v):
        return jnp.where(odd, along(v, 1), v)

    def odd_part(v):
        return jnp.where(odd, v, along(v, -1))

    def rows_tile(rows):
        made = jnp.zeros(tile, jnp.float32)
        for at, value in rows:
            made = jnp.where(row_at == at, wide(value), made)
        return made

    def pair_up():
        for x in range(4):
            for j in range(14):
                part = [weights[1][x, i] if i < 18 else reaction[1][x, i - 18] for i in (2 * j, 2 * j + 1) if i < 27]
                coef_own[x, j] = jnp.where(odd, part[-1], part[0])
        for side, y in ((0, 6), (1, 0)):
            for j in range(0, 14, 2):
                rows = [(4 * i + x, coef_own[x, j + i, y : y + 1, :]) for i in range(2) for x in range(4)]
                coef_y_send[side, j // 2] = rows_tile(rows)

    def send_ring_coefficients():
        copies = []
        for side, turn in ((0, 1), (1, -1)):
            sems = lambda n: (coef_send_sem.at[n], coef_recv_sem.at[n])
            copies.append(remote(coef_y_send.at[side], coef_y.at[side], *sems(side), (0, turn)))
            copies.append(remote(coef_own.at[3 - 3 * side], coef_x.at[side], *sems(2 + side), (turn, 0)))
        for n in range(4):
            x, y = 3 - 3 * (n // 2), 6 - 6 * (n % 2)
            for j in range(14):
                coef_corner_send[n, j : j + 1, :] = coef_own[x, j, y : y + 1, :]
            to = (1 - 2 * (n // 2), 1 - 2 * (n % 2))
            copies.append(
                remote(coef_corner_send.at[n], coef_corner.at[n], coef_send_sem.at[4 + n], coef_recv_sem.at[4 + n], to)
            )
        return copies

    def take_ring_coefficients(copies):
        for copy in copies:
            copy.wait()
        for p in range(6):
            filled = jnp.logical_and(row_at >= 1, row_at < ROWS - 1)
            for j in range(14):
                if p in (0, 5):
                    rows = [(2 + k, coef_x[p // 5, j, 2 * k : 2 * k + 1, :]) for k in range(4)]
                    rows += [(1 + 5 * sy, coef_corner[2 * (p // 5) + sy, j : j + 1, :]) for sy in range(2)]
                else:
                    x = p - 1
                    rows = [(2 + k, coef_own[x, j, 2 * k : 2 * k + 1, :]) for k in range(4)]
                    at = 4 * (j % 2) + x
                    rows += [(1, coef_y[0, j // 2, at : at + 1, :]), (6, coef_y[1, j // 2, at : at + 1, :])]
                both = rows_tile(rows)
                for i, value in ((2 * j, even_part(both)), (2 * j + 1, odd_part(both))):
                    if i < 18:
                        ring_w[p, i] = value
                    elif i < 27:
                        ring_r[p, i - 18] = jnp.where(filled, value, 1.0) if i in (18, 22, 26) else value
        finish(ring_w, ring_r, ring_diag, ring_inverse, 6)
        off_high = jnp.logical_and(row_at == 5, is_high_y)
        off_low = jnp.logical_and(row_at == 2, is_low_y)
        for c in range(3):
            ring_w[4, c] = jnp.where(is_high_x, 0.0, ring_w[4, c])
            ring_w[1, 3 + c] = jnp.where(is_low_x, 0.0, ring_w[1, 3 + c])

        def body(p):
            for k, off in ((2, off_high), (3, off_low), (4, lane_at >= lanes - 2), (5, lane_at < 2)):
                for c in range(3):
                    ring_w[p, 3 * k + c] = jnp.where(off, 0.0, ring_w[p, 3 * k + c])

        each(6, body)

    def send_pairs(turn):
        for x in range(4):
            for c in range(3):
                pair_own[x, c] = jnp.where(odd, sources[1][x, c], fields[1][0, x + 1, c])
        for side, y in ((0, 4), (1, 0)):
            for c in range(3):
                rows = [(2 * x + k, pair_own[x, c, y + 2 * k : y + 2 * k + 1, :]) for x in range(4) for k in range(2)]
                pair_y_send[side, c] = rows_tile(rows)
        for sx in range(2):
            for sy in range(2):
                x, y = 3 - 3 * sx, 6 - 6 * sy
                for i, (at_x, at_y) in enumerate(((x, y), (2 - sx, y), (x, 4 - 2 * sy))):
                    for c in range(3):
                        n = 3 * i + c
                        pair_corner_send[2 * sx + sy, n : n + 1, :] = pair_own[at_x, c, at_y : at_y + 1, :]
        copies = []
        sems = lambda n: (pair_send_sem.at[n], pair_recv_sem.at[turn, n])
        for side, to in ((0, 1), (1, -1)):
            copies.append(remote(pair_y_send.at[side], pair_y.at[turn, side], *sems(side), (0, to)))
            source = pair_own.at[pl.ds(2 - 2 * side, 2)]
            copies.append(remote(source, pair_x.at[turn, side], *sems(2 + side), (to, 0)))
        for sx in range(2):
            for sy in range(2):
                n = 2 * sx + sy
                to = (1 - 2 * sx, 1 - 2 * sy)
                copies.append(remote(pair_corner_send.at[n], pair_corner.at[turn, n], *sems(4 + n), to))
        return copies

    def take_pairs(turn, copies):
        for copy in copies:
            copy.wait()
        for p in range(8):
            for c in range(3):
                if 2 <= p < 6:
                    x = p - 2
                    rows = [(2 + k, pair_own[x, c, 2 * k : 2 * k + 1, :]) for k in range(4)]
                    for side in range(2):
                        for k in range(2):
                            at = 2 * x + k
                            rows.append((6 * side + k, pair_y[turn, side, c, at : at + 1, :]))
                else:
                    side = p // 4
                    rows = [(2 + k, pair_x[turn, side, p - 6 * side, c, 2 * k : 2 * k + 1, :]) for k in range(4)]
                    for sy in range(2):
                        cells = ((0, 1 + 5 * sy), (2, 7 * sy)) if p in (1, 6) else ((1, 1 + 5 * sy),)
                        for i, row in cells:
                            n = 3 * i + c
                            rows.append((row, pair_corner[turn, 2 * side + sy, n : n + 1, :]))
                both = rows_tile(rows)
                ring_u[p, c] = even_part(both)
                if 1 <= p < 7:
                    ring_b[p - 1, c] = odd_part(both)

    def ring_sweep():
        def add(p):
            x = p // 2 - 1
            for c in range(3):
                e = jnp.where(row_at < 2, mid_at(c, x, -1), mid_at(c, x, 0))
                e = jnp.where(row_at < 4, e, jnp.where(row_at < 6, mid_at(c, x, 1), mid_at(c, x, 2)))
                ring_u[p, c] += e

        for p in range(8):
            add(p)
        for p in range(6):
            u = [ring_u[p + 1, c] for c in range(3)]
            left = []
            for c in range(3):
                value = ring_b[p, c] - ring_diag[p, c] * u[c]
                near = (ring_u[p + 2, c], ring_u[p, c], down(u[c], -1), down(u[c], 1), along(u[c], -2), along(u[c], 2))
                for k in range(6):
                    value = value + ring_w[p, 3 * k + c] * near[k]
                for d in range(3):
                    if d != c:
                        value = value - ring_r[p, 3 * d + c] * u[d]
                left.append(value)
            step = apply_inverse(ring_inverse, p, left)
            for c in range(3):
                ring_out[p, c] = u[c] + step[c]

    def add_to_finest(at, slot):
        f = fields[0]
        for c in range(3):
            for p in range(6):
                rows = [wide(ring_out[p, c, 2 + k : 3 + k, :]) for k in range(4)]
                e = jnp.where(row_at < 2, rows[0], rows[1])
                e = jnp.where(row_at < 4, e, jnp.where(row_at < 6, rows[2], rows[3]))
                for x in {0: (-1,), 5: (8,)}.get(p, (2 * p - 2, 2 * p - 1)):
                    f[at, x + 1, c] += e
            for side, row in ((0, 1), (1, 6)):
                rows = [wide(ring_out[1 + k, c, row : row + 1, :]) for k in range(4)]
                e = jnp.where(row_at < 2, rows[0], rows[1])
                e = jnp.where(row_at < 4, e, jnp.where(row_at < 6, rows[2], rows[3]))
                rows_halo[slot, side, c] += e

    def packed_y(f, at):
        return rows_tile([(x, f(x)[at : at + 1, :]) for x in range(8)])

    def send_rim():
        copies = []
        sems = lambda n: (rim_send_sem.at[n], rim_recv_sem.at[n])
        for side, to in ((0, 1), (1, -1)):
            row, second = 7 - 7 * side, 6 - 5 * side
            for i in range(9):
                rim_y_send[side, i] = rows_tile([(x, reaction[0][x, i, row : row + 1, :]) for x in range(8)])
            rim_y_send[side, 9] = rows_tile([(x, pot[x + 1, second : second + 1, :]) for x in range(8)])
            for c in range(3):
                rim_y_send[side, 10 + c] = rows_tile([(x, base[x, c, row : row + 1, :]) for x in range(8)])
            copies.append(remote(rim_y_send.at[side], rim_y.at[side], *sems(side), (0, to)))
            copies.append(remote(reaction[0].at[row], rim_r.at[side], *sems(2 + side), (to, 0)))
            copies.append(remote(pot.at[second + 1], rim_pot.at[side], *sems(4 + side), (to, 0)))
            copies.append(remote(base.at[row], rim_base.at[side], *sems(6 + side), (to, 0)))
        for n in range(4):
            x, y = 7 - 7 * (n // 2), 7 - 7 * (n % 2)
            rim_pot_corner_send[n] = pot[x + 1, y : y + 1, :]
            to = (1 - 2 * (n // 2), 1 - 2 * (n % 2))
            copies.append(remote(rim_pot_corner_send.at[n], rim_pot_corner.at[n], *sems(8 + n), to))
        return copies

    def ordered(t, out_side, in_side, ahead, behind, above, below):
        across = (in_side, out_side) if t % 2 == 0 else (out_side, in_side)
        return (across + (ahead, behind) if t < 2 else (ahead, behind) + across) + (above, below)

    def take_rim(copies):
        for copy in copies:
            copy.wait()
        for side in range(2):
            for i in range(9):
                rim_r[2 + side, i] = rim_y[side, i]
            for c in range(3):
                rim_base[2 + side, c] = rim_y[side, 10 + c]
        for t in range(4):
            side = t % 2
            if t < 2:
                here, beyond, inside = pot[9 * side], rim_pot[side], pot[1 + 7 * side]
                first, last = 2 * side, 2 * side + 1
                edges = (is_low_y, is_high_y)
            else:
                here, beyond = pot_y[side], rim_y[side, 9]
                row = 7 * side
                inside = rows_tile([(x, pot[x + 1, row : row + 1, :]) for x in range(8)])
                first, last = side, 2 + side
                edges = (is_low_x, is_high_x)
            corner = lambda n, off: jnp.where(off, 0.0, wide(rim_pot_corner[n]))
            near = ordered(
                t,
                beyond,
                inside,
                jnp.where(row_at == ROWS - 1, corner(last, edges[1]), down(here, -1)),
                jnp.where(row_at == 0, corner(first, edges[0]), down(here, 1)),
                jnp.where(lane_at == lanes - 1, 0.0, along(here, -1)),
                jnp.where(lane_at == 0, 0.0, along(here, 1)),
            )
            for k in range(6):
                plus, minus = face_weights(here - near[k])
                rim_w[t, 3 * k] = jnp.ones(tile, jnp.float32)
                rim_w[t, 3 * k + 1] = plus
                rim_w[t, 3 * k + 2] = minus
        finish(rim_w, rim_r, rim_diag, rim_inverse, 4)
        for t in range(4):
            ahead, off_high, off_low = (2, is_high_y, is_low_y) if t < 2 else (0, is_high_x, is_low_x)
            masks = (
                (ahead, jnp.logical_and(row_at == ROWS - 1, off_high)),
                (ahead + 1, jnp.logical_and(row_at == 0, off_low)),
                (4, lane_at == lanes - 1),
                (5, lane_at == 0),
            )
            for k, off in masks:
                for c in range(3):
                    rim_w[t, 3 * k + c] = jnp.where(off, 0.0, rim_w[t, 3 * k + c])

    def doubled(rows):
        e = jnp.where(row_at < 2, wide(rows[0]), wide(rows[1]))
        return jnp.where(row_at < 4, e, jnp.where(row_at < 6, wide(rows[2]), wide(rows[3])))

    def rim_sweep(at):
        for t in range(4):
            side = t % 2
            e, near = [], []
            for c in range(3):
                cell = lambda p, row: ring_out[p, c, row : row + 1, :]
                if t < 2:
                    p, p_in = 5 * side, 1 + 3 * side
                    here = doubled([cell(p, 2 + k) for k in range(4)])
                    inside = doubled([cell(p_in, 2 + k) for k in range(4)])
                    first, last = cell(p, 1), cell(p, 6)
                else:
                    row, row_in = 1 + 5 * side, 2 + 3 * side
                    here = doubled([cell(1 + k, row) for k in range(4)])
                    inside = doubled([cell(1 + k, row_in) for k in range(4)])
                    first, last = cell(0, row), cell(5, row)
                e.append(here)
                near.append(
                    ordered(
                        t,
                        here,
                        inside,
                        jnp.where(row_at == ROWS - 1, wide(last), down(here, -1)),
                        jnp.where(row_at == 0, wide(first), down(here, 1)),
                        along(here, -1),
                        along(here, 1),
                    )
                )
            left = []
            for c in range(3):
                value = -rim_diag[t, c] * e[c]
                for k in range(6):
                    value = value + rim_w[t, 3 * k + c] * near[c][k]
                for d in range(3):
                    if d != c:
                        value = value - rim_r[t, 3 * d + c] * e[d]
                left.append(value)
            step = apply_inverse(rim_inverse, t, left)
            for c in range(3):
                value = rim_base[t, c] + e[c] + step[c]
                if t < 2:
                    fields[0][at, 9 * side, c] = value
                else:
                    rows_halo[3, side, c] = value

    def source(level, x):
        if level == 0:
            return [grad[c, x] for c in range(3)]
        return [sources[level][x, c] for c in range(3)]

    def solve(level, x, r):
        v = inverse[level]
        return [v[x, 3 * c] * r[0] + v[x, 3 * c + 1] * r[1] + v[x, 3 * c + 2] * r[2] for c in range(3)]

    def post(level, at):
        slot, f, count = done[0] % 3, fields[level], NX[level]
        for side, row in ((0, ROWS - 1), (1, 0)):
            for c in range(3):
                packed = wide(f[at, 1, c, row : row + 1, :])
                for x in range(1, count):
                    packed = jnp.where(row_at == x, wide(f[at, x + 1, c, row : row + 1, :]), packed)
                send_y[side, c] = packed
        wait = exchange(
            [
                (f.at[at, count], f.at[at, 0]),
                (f.at[at, 1], f.at[at, count + 1]),
                (send_y.at[0], rows_halo.at[slot, 0]),
                (send_y.at[1], rows_halo.at[slot, 1]),
            ]
        )
        return slot, wait

    def share(level, at, beside_it):
        slot, wait = post(level, at)
        beside_it()
        inner(level, at)
        wait()
        return slot

    def inner(level, at):
        f, w, r, span, count = fields[level], weights[level], reaction[level], 1 << level, NX[level]
        for x in range(count):
            u = [f[at, x + 1, c] for c in range(3)]
            b = source(level, x)
            for c in range(3):
                value = b[c] - diag[level][x, c] * u[c]
                value = value + w[x, 6 + c] * jnp.where(row_at >= ROWS - span, 0.0, down(u[c], -span))
                value = value + w[x, 9 + c] * jnp.where(row_at < span, 0.0, down(u[c], span))
                value = value + w[x, 12 + c] * along(u[c], -span) + w[x, 15 + c] * along(u[c], span)
                if x < count - 1:
                    value = value + w[x, c] * f[at, x + 2, c]
                if x > 0:
                    value = value + w[x, 3 + c] * f[at, x, c]
                for d in range(3):
                    if d != c:
                        value = value - r[x, 3 * d + c] * u[d]
                part[x, c] = value

    def rest(level, at, slot, x, stride=1, whole=True):
        f, w, span, count = fields[level], weights[level], 1 << level, NX[level]
        left = []
        for c in range(3):
            row = x * stride
            row_high, row_low = (rows_halo[slot, side, c, row : row + 1, :] for side in (1, 0))
            value = jnp.where(row_at >= ROWS - span, w[x, 6 + c] * wide(row_high), 0.0)
            value = jnp.where(row_at < span, w[x, 9 + c] * wide(row_low), value)
            if whole:
                value = part[x, c] + value
            if x == 0:
                value = value + w[x, 3 + c] * f[at, 0, c]
            if x == count - 1:
                value = value + w[x, c] * f[at, count + 1, c]
            left.append(value)
        return [f[at, x + 1, c] for c in range(3)], left

    def residual(level, at, slot, x):
        f, w, r, span = fields[level], weights[level], reaction[level], 1 << level
        u = [f[at, x + 1, c] for c in range(3)]
        b = source(level, x)
        left = []
        for c in range(3):
            near = (
                f[at, x + 2, c],
                f[at, x, c],
                jnp.where(row_at >= ROWS - span, wide(rows_halo[slot, 1, c, x : x + 1, :]), down(u[c], -span)),
                jnp.where(row_at < span, wide(rows_halo[slot, 0, c, x : x + 1, :]), down(u[c], span)),
                along(u[c], -span),
                along(u[c], span),
            )
            value = b[c] - diag[level][x, c] * u[c]
            for k in range(6):
                value = value + w[x, 3 * k + c] * near[k]
            for d in range(3):
                if d != c:
                    value = value - r[x, 3 * d + c] * u[d]
            left.append(value)
        return u, left

    def sweep(at, slot, left_of, last=False):
        copies = []
        for x in range(NX[0]):
            u, left = left_of(0, at, slot, x)
            step = solve(0, x, left)
            for c in range(3):
                if last:
                    result[c, x] = u[c] + step[c]
                else:
                    fields[0][at + 1, x + 1, c] = u[c] + step[c]
            if last:
                copies.append(pltpu.make_async_copy(result.at[:, x], out.at[:, x], out_sem.at[x]))
                copies[-1].start()
        for copy in copies:
            copy.wait()
        return at + 1

    def make_halo_inverse():
        for i in range(9):
            for side in range(2):
                row = 1 + 5 * side
                halo_inverse[side, i] = doubled([ring_inverse[5 * side, i, 2 + k : 3 + k, :] for k in range(4)])
                halo_inverse[2 + side, i] = doubled([ring_inverse[1 + k, i, row : row + 1, :] for k in range(4)])

    def restrict_with_halo(at):
        slot, wait = post(0, at)
        rows, lanes_ = pair_tools(0)[4:]
        outside = (is_low_x, is_high_x, is_low_y, is_high_y)
        for t in range(4):
            for c in range(3):
                edge = fields[0][at, 1 + 7 * t, c] if t < 2 else send_y[3 - t, c]
                value = jnp.where(outside[t], 0.0, rim_w[t, 3 * t + c] * edge)
                cross[t, c] = lanes_(rows(value))
        copies = []
        sems = lambda n: (lean_send_sem.at[n], lean_recv_sem.at[n])
        for n in range(4):
            sx, sy = n // 2, n % 2
            for c in range(3):
                row = 6 - 6 * sx
                cross_send[n, c : c + 1, :] = cross[3 - sy, c, row : row + 1, :]
                row = 6 - 6 * sy
                cross_send[n, 3 + c : 4 + c, :] = cross[1 - sx, c, row : row + 1, :]
            copies.append(remote(cross_send.at[n], cross_recv.at[n], *sems(4 + n), (1 - 2 * sx, 1 - 2 * sy)))
        inner(0, at)
        for x in range(4):
            for c in range(3):
                lean[x, c] = lanes_(rows(part[2 * x, c] + part[2 * x + 1, c]))
        for side, to in ((0, 1), (1, -1)):
            row = 6 - 6 * side
            for c in range(3):
                lean_y_send[side, c] = doubled([lean[k, c, row : row + 1, :] for k in range(4)])
            copies.append(remote(lean_y_send.at[side], lean_y.at[side], *sems(side), (0, to)))
            copies.append(remote(lean.at[3 - 3 * side], lean_x.at[side], *sems(2 + side), (to, 0)))
        wait()
        for x in range(4):
            more = [rest(0, at, slot, 2 * x + i, whole=False)[1] for i in range(2)]
            total = [lean[x, c] + lanes_(rows(more[0][c] + more[1][c])) for c in range(3)]
            first = solve(1, x, total)
            for c in range(3):
                sources[1][x, c] = total[c]
                fields[1][0, x + 1, c] = first[c]
        for copy in copies:
            copy.wait()
        for t in range(4):
            side = t % 2
            total = []
            for c in range(3):
                if t < 2:
                    value, first, last, row = lean_x[side, c], 2 * side, 2 * side + 1, c
                else:
                    value, first, last, row = lean_y[side, c], side, 2 + side, 3 + c
                low, high = (wide(cross_recv[n, row : row + 1, :]) for n in (first, last))
                value = value + cross[t, c]
                total.append(value + jnp.where(row_at < 2, low, jnp.where(row_at >= 6, high, 0.0)))
            first = apply_inverse(halo_inverse, t, total)
            for c in range(3):
                if t < 2:
                    fields[1][0, 5 * side, c] = first[c]
                else:
                    rows_halo[3, side, c] = first[c]
        inner(1, 0)
        return slot

    def restrict(level, at, slot, keep=False, stride=1):
        rows, lanes_ = pair_tools(level)[4:]
        for x in range(NX[level + 1]):
            left = []
            for i in range(2):
                u, r = rest(level, at, slot, 2 * x + i, stride)
                left.append(r)
                if keep:
                    step = solve(level, 2 * x + i, r)
                    for c in range(3):
                        base[2 * x + i, c] = u[c] + step[c]
            total = [lanes_(rows(left[0][c] + left[1][c])) for c in range(3)]
            first = solve(level + 1, x, total)
            for c in range(3):
                sources[level + 1][x, c] = total[c]
                fields[level + 1][0, x + 1, c] = first[c]

    def cycle(at, turn, besides, last=False):
        pairs = []
        if last:
            slot = restrict_with_halo(at)
            restrict(1, 0, 3, stride=2)
        else:
            slot = share(0, at, besides[0])
            restrict(0, at, slot, keep=True)

            def beside():
                pairs.extend(send_pairs(turn))
                besides[1]()

            restrict(1, 0, share(1, 0, beside))

        def beside_p():
            if last:
                pairs.extend(send_pairs(turn))
            besides[2]()

        def beside_q():
            take_pairs(turn, pairs)
            besides[3]()

        lower(turn, beside_p, beside_q)
        ring_sweep()
        if not last:
            rim_sweep(at + 1)
        add_to_finest(at, slot)
        return sweep(at, slot, residual, last)

    def start(x):
        for c, value in enumerate(solve(0, x, source(0, x))):
            fields[0][0, x + 1, c] = value

    finish_level(0)
    loads["grad"].wait()
    each(NX[0], start)
    pending, ring_pending, rim_pending = [], [], []

    def beside_first():
        coarsen(0)
        mask_level(0)
        finish_level(1)
        coarsen(1)
        pending.append(send_coefficients())

    def beside_second():
        pair_up()
        mask_level(1)
        finish_level(2)
        coarsen(2)
        pending.append(send_low_coefficients())

    def beside_third():
        ring_pending.extend(send_ring_coefficients())
        rim_pending.extend(send_rim())
        take_coefficients(pending)

    def beside_fourth():
        take_ring_coefficients(ring_pending)
        take_rim(rim_pending)
        make_halo_inverse()

    nothing = lambda: None
    at = cycle(
        0,
        0,
        (
            beside_first,
            beside_second,
            beside_third,
            beside_fourth,
        ),
    )
    at = sweep(at, 3, residual)
    cycle(at, 1, (nothing,) * 4, last=True)


def local(counts, gradient, potential, coupling, region, contact, rates):
    nz = potential.shape[-1]
    tile = (ROWS, nz)
    f32 = jnp.float32
    scratch = []
    for parts in (18, 9, 3, 9):
        scratch += [pltpu.VMEM((n, parts) + tile, f32) for n in NX]
    scratch += [pltpu.VMEM((n, 3) + tile, f32) for n in NX[1:]]
    scratch += [pltpu.VMEM((3, n + 2, 3) + tile, f32) for n in NX]
    scratch += [
        pltpu.VMEM((4, 2, 3) + tile, f32),
        pltpu.VMEM((2,) + tile, f32),
        pltpu.VMEM((2, 3) + tile, f32),
        pltpu.SemaphoreType.DMA((4,)),
        pltpu.SemaphoreType.DMA((3, 4)),
        pltpu.VMEM((1, 18) + tile, f32),
        pltpu.VMEM((1, 9) + tile, f32),
        pltpu.VMEM((SLOTS, 18) + tile, f32),
        pltpu.VMEM((SLOTS, 9) + tile, f32),
        pltpu.VMEM((SLOTS, 3) + tile, f32),
        pltpu.VMEM((SLOTS, 9) + tile, f32),
        pltpu.VMEM((SLOTS, 3) + tile, f32),
        pltpu.VMEM((SLOTS, 3) + tile, f32),
        pltpu.VMEM((2, 4, 3) + tile, f32),
        pltpu.VMEM((27, 1, nz), f32),
        pltpu.VMEM((len(INNER), 27, 1, nz), f32),
        pltpu.VMEM((4, nz), f32),
        pltpu.VMEM((len(FOURTH), 4, nz), f32),
        pltpu.VMEM((2, 3, 1, nz), f32),
        pltpu.VMEM((2, len(INNER + OUTER), 3, 1, nz), f32),
        pltpu.VMEM((1, 1, nz), f32),
        pltpu.VMEM((2, len(THIRD), 1, nz), f32),
        pltpu.SemaphoreType.DMA,
        pltpu.SemaphoreType.DMA,
        pltpu.SemaphoreType.DMA,
        pltpu.SemaphoreType.DMA,
        pltpu.SemaphoreType.DMA,
        pltpu.SemaphoreType.DMA((2,)),
        pltpu.SemaphoreType.DMA,
        pltpu.SemaphoreType.DMA((2,)),
        pltpu.VMEM((8, 3) + tile, f32),
        pltpu.VMEM((6, 3) + tile, f32),
        pltpu.VMEM((6, 18) + tile, f32),
        pltpu.VMEM((6, 9) + tile, f32),
        pltpu.VMEM((6, 3) + tile, f32),
        pltpu.VMEM((6, 9) + tile, f32),
        pltpu.VMEM((6, 3) + tile, f32),
        pltpu.VMEM((4, 3) + tile, f32),
        pltpu.VMEM((2, 2, 2, 3) + tile, f32),
        pltpu.VMEM((2, 3) + tile, f32),
        pltpu.VMEM((2, 2, 3) + tile, f32),
        pltpu.VMEM((4, 2 * ROWS, nz), f32),
        pltpu.VMEM((2, 4, 2 * ROWS, nz), f32),
        pltpu.SemaphoreType.DMA((8,)),
        pltpu.SemaphoreType.DMA((2, 8)),
        pltpu.VMEM((4, 14) + tile, f32),
        pltpu.VMEM((2, 14) + tile, f32),
        pltpu.VMEM((2, 7) + tile, f32),
        pltpu.VMEM((2, 7) + tile, f32),
        pltpu.SemaphoreType.DMA((8,)),
        pltpu.SemaphoreType.DMA((8,)),
        pltpu.VMEM((NX[0], 3) + tile, f32),
        pltpu.VMEM((4, 2 * ROWS, nz), f32),
        pltpu.VMEM((4, 2 * ROWS, nz), f32),
        pltpu.VMEM((4, 18) + tile, f32),
        pltpu.VMEM((4, 9) + tile, f32),
        pltpu.VMEM((4, 3) + tile, f32),
        pltpu.VMEM((4, 9) + tile, f32),
        pltpu.VMEM((4, 3) + tile, f32),
        pltpu.VMEM((2,) + tile, f32),
        pltpu.VMEM((4, 1, nz), f32),
        pltpu.VMEM((4, 1, nz), f32),
        pltpu.VMEM((NX[0], 3) + tile, f32),
        pltpu.VMEM((2, 13) + tile, f32),
        pltpu.VMEM((2, 13) + tile, f32),
        pltpu.SemaphoreType.DMA((12,)),
        pltpu.SemaphoreType.DMA((12,)),
        pltpu.VMEM(gradient.shape, f32),
        pltpu.SemaphoreType.DMA((NX[0],)),
        pltpu.VMEM((4, 9) + tile, f32),
        pltpu.VMEM((4, 3) + tile, f32),
        pltpu.VMEM((4,) + tile, f32),
        pltpu.VMEM((4,) + tile, f32),
        pltpu.VMEM((4, 3) + tile, f32),
        pltpu.VMEM((2, 3) + tile, f32),
        pltpu.VMEM((2, 3) + tile, f32),
        pltpu.VMEM((2, 3) + tile, f32),
        pltpu.SemaphoreType.DMA((8,)),
        pltpu.SemaphoreType.DMA((8,)),
        pltpu.VMEM(gradient.shape, f32),
        pltpu.VMEM((10,) + tile, f32),
        pltpu.VMEM(coupling.shape, f32),
        pltpu.VMEM(region.shape, jnp.int32),
        pltpu.VMEM(contact.shape, jnp.int32),
        pltpu.SMEM(rates.shape, f32),
        pltpu.SemaphoreType.DMA((6,)),
    ]
    return pl.pallas_call(
        functools.partial(kernel, counts),
        out_shape=jax.ShapeDtypeStruct(gradient.shape, f32),
        in_specs=[pl.BlockSpec(memory_space=pltpu.HBM)] * 6,
        out_specs=pl.BlockSpec(memory_space=pltpu.HBM),
        scratch_shapes=scratch,
        compiler_params=pltpu.CompilerParams(
            collective_id=0, has_side_effects=True, vmem_limit_bytes=60 * 1024 * 1024
        ),
    )(gradient, potential, coupling, region, contact, rates)


def solution(mesh):
    placed = (
        P(None, "gx", "gy", None),
        P("gx", "gy", None),
        P(None, None, "gx", "gy", None),
        P("gx", "gy", None),
        P("gx", "gy", None),
        P(),
    )
    counts = (mesh.shape["gx"], mesh.shape["gy"])
    return jax.shard_map(
        functools.partial(local, counts),
        mesh=mesh,
        in_specs=placed,
        out_specs=P(None, "gx", "gy", None),
        check_vma=False,
    )
```

```python
import functools

import jax
import jax.numpy as jnp
from jax import lax
from jax.experimental import pallas as pl
from jax.experimental.pallas import tpu as pltpu
from jax.sharding import PartitionSpec as P

MESH = pl.DeviceIdType.MESH
LEVELS = 4
COARSE_SWEEPS = 6
REGIONS = 4
OMEGA = 0.8
STRENGTH = 8.0
ROWS = 8
NX = (8, 4, 2, 1)
RADIUS = 3
SLOTS = 8


def around(shape, far):
    reach = range(-6, 7)
    distance = lambda i, j: min(abs(i - a) + abs(j - b) for a, b in shape)
    found = [(i, j) for i in reach for j in reach if distance(i, j) <= far and (i, j) != (0, 0)]
    return sorted(found, key=lambda o: -abs(o[0]) - abs(o[1]))


OWN = [(0, 0)]
SQUARE = [(i, j) for i in (-1, 0, 1) for j in (-1, 0, 1)]
INNER = around(OWN, 2)
OUTER = [o for o in around(OWN, 3) if o not in INNER]
FOURTH = around(SQUARE, 2)
THIRD = around(SQUARE, 3)


def each(count, body):
    if count == 1:
        body(0)
        return

    def step(i, carry):
        body(i)
        return carry

    lax.fori_loop(0, count, step, 0, unroll=count)


def face_weights(difference):
    size = jnp.abs(difference)
    small = size < 0.5
    series = 1.0 / 362880.0
    for k in (40320.0, 5040.0, 720.0, 120.0, 24.0, 6.0, 2.0, 1.0):
        series = series * size + 1.0 / k
    below = jnp.where(small, series, jnp.exp(size) - 1.0)
    low = jnp.where(small, 1.0, size) / below
    low = jnp.where(size < 1e-4, 1.0 - 0.5 * size, low)
    high = low + size
    positive = difference > 0.0
    return jnp.where(positive, low, high), jnp.where(positive, high, low)


def kernel(counts, grad_in, pot_in, coup_in, region_in, contact_in, rates_in, out, *scratch):
    grad, pot, coup, region, contact, rates, in_sem = scratch[-7:]
    scratch = scratch[:-7]
    loads = {}
    for i, (name, source, target) in enumerate(
        (
            ("pot", pot_in, pot.at[pl.ds(1, 8)]),
            ("rates", rates_in, rates),
            ("region", region_in, region),
            ("contact", contact_in, contact),
            ("coup", coup_in, coup),
            ("grad", grad_in, grad),
        )
    ):
        loads[name] = pltpu.make_async_copy(source, target, in_sem.at[i])
        loads[name].start()
    weights, reaction, diag, inverse = (scratch[4 * i : 4 * i + 4] for i in range(4))
    sources = (None,) + tuple(scratch[16:19])
    fields = scratch[19:23]
    rows_halo, pot_y, send_y, send_sem, recv_sem = scratch[23:28]
    w_own, r_own, w_wide, r_wide, diag_wide, inverse_wide, u_wide, b_wide, e_rows = scratch[28:37]
    mid_send, mid_recv, low_send, low_recv, mid_cell, mid_cells, low_cell, low_cells = scratch[37:45]
    mid_send_sem, mid_recv_sem, low_send_sem, low_recv_sem, p_send, p_recv, q_send, q_recv = scratch[45:53]
    ring_u, ring_b, ring_w, ring_r, ring_diag, ring_inverse, ring_out = scratch[53:60]
    pair_own, pair_x, pair_y_send, pair_y, pair_corner_send, pair_corner, pair_send_sem, pair_recv_sem = scratch[60:68]
    coef_own, coef_x, coef_y_send, coef_y, coef_send_sem, coef_recv_sem, part, coef_corner_send, coef_corner = scratch[68:77]
    rim_w, rim_r, rim_diag, rim_inverse, rim_base, rim_pot, rim_pot_corner_send, rim_pot_corner = scratch[77:85]
    base, rim_y_send, rim_y, rim_send_sem, rim_recv_sem, result, out_sem = scratch[85:92]
    halo_inverse, cross, cross_send, cross_recv, lean, lean_x, lean_y_send, lean_y = scratch[92:100]
    lean_send_sem, lean_recv_sem, r_wide_2 = scratch[100:]
    n_x, n_y = counts
    lanes = out.shape[-1]
    gx, gy = lax.axis_index("gx"), lax.axis_index("gy")
    x_low, x_high = lax.rem(gx + n_x - 1, n_x), lax.rem(gx + 1, n_x)
    y_low, y_high = lax.rem(gy + n_y - 1, n_y), lax.rem(gy + 1, n_y)
    beside = ((x_high, gy), (x_low, gy), (gx, y_high), (gx, y_low))

    barrier = pltpu.get_barrier_semaphore()
    at_offset = lambda i, j: (lax.rem(gx + n_x + i, n_x), lax.rem(gy + n_y + j, n_y))
    devices = {o: at_offset(*o) for o in THIRD}
    for offset in INNER:
        pl.semaphore_signal(barrier, inc=1, device_id=devices[offset], device_id_type=MESH)
    pl.semaphore_wait(barrier, len(INNER))

    tile = (ROWS, lanes)
    row_at = lax.broadcasted_iota(jnp.int32, tile, 0)
    lane_at = lax.broadcasted_iota(jnp.int32, tile, 1)
    wide = lambda row: jnp.broadcast_to(row, tile)
    down = lambda v, by: pltpu.roll(v, by % ROWS, 0) if by % ROWS else v
    along = lambda v, by: pltpu.roll(v, by % lanes, 1)

    done = [0]

    def exchange(parts):
        slot = done[0] % 3
        done[0] += 1
        copies = []
        for i in (2, 3, 0, 1):
            source, target = parts[i]
            copy = pltpu.make_async_remote_copy(
                src_ref=source,
                dst_ref=target,
                send_sem=send_sem.at[i],
                recv_sem=recv_sem.at[slot, i],
                device_id=beside[i],
                device_id_type=MESH,
            )
            copy.start()
            copies.append(copy)

        def wait():
            for copy in copies:
                copy.wait()

        return wait

    def remote(source, target, send, recv, offset):
        copy = pltpu.make_async_remote_copy(
            src_ref=source,
            dst_ref=target,
            send_sem=send,
            recv_sem=recv,
            device_id=devices[offset],
            device_id_type=MESH,
        )
        copy.start()
        return copy

    def gather(offsets, source_of, target, send, recv):
        for n, (i, j) in enumerate(offsets):
            remote(source_of((i, j)), target.at[n], send, recv, (-i, -j))

        def wait():
            pltpu.make_async_copy(target, target, send).wait()
            pltpu.make_async_copy(target, target, recv).wait()

        return wait

    loads["pot"].wait()
    for side, at in ((0, ROWS - 1), (1, 0)):
        packed = wide(pot[1, at : at + 1, :])
        for x in range(1, 8):
            packed = jnp.where(row_at == x, wide(pot[x + 1, at : at + 1, :]), packed)
        send_y[side, 0] = packed
    wait = exchange(
        [
            (pot.at[8], pot.at[0]),
            (pot.at[1], pot.at[9]),
            (send_y.at[0, 0], pot_y.at[0]),
            (send_y.at[1, 0], pot_y.at[1]),
        ]
    )
    for name in ("rates", "region", "contact", "coup"):
        loads[name].wait()

    def put_faces(x, k, plus, minus):
        weights[0][x, 3 * k] = jnp.ones(tile, jnp.float32)
        weights[0][x, 3 * k + 1] = plus
        weights[0][x, 3 * k + 2] = minus

    def set_up(x):
        here = pot[x + 1]
        put_faces(x, 4, *face_weights(here - jnp.where(lane_at == lanes - 1, 0.0, along(here, -1))))
        put_faces(x, 5, *face_weights(here - jnp.where(lane_at == 0, 0.0, along(here, 1))))
        plus, minus = face_weights(here - down(here, -1))
        put_faces(x, 2, plus, minus)
        put_faces(x, 3, down(minus, 1), down(plus, 1))
        at_contact = STRENGTH * contact[x].astype(jnp.float32)
        regions = region[x]
        for c in range(3):
            extra = jnp.full(tile, rates[0, c])
            for pick in range(1, REGIONS):
                extra = jnp.where(regions == pick, rates[pick, c], extra)
            for d in range(3):
                value = coup[c, d, x]
                reaction[0][x, 3 * c + d] = value + (extra + at_contact) if c == d else value

    each(NX[0], set_up)
    for x in range(7):
        plus, minus = face_weights(pot[x + 1] - pot[x + 2])
        put_faces(x, 0, plus, minus)
        put_faces(x + 1, 1, minus, plus)
    wait()
    is_low_x, is_high_x = gx == 0, gx == n_x - 1
    is_low_y, is_high_y = gy == 0, gy == n_y - 1
    pot[0] = jnp.where(is_low_x, 0.0, pot[0])
    pot[9] = jnp.where(is_high_x, 0.0, pot[9])
    pot_y[0] = jnp.where(is_low_y, 0.0, pot_y[0])
    pot_y[1] = jnp.where(is_high_y, 0.0, pot_y[1])

    put_faces(0, 1, *face_weights(pot[1] - pot[0]))
    put_faces(7, 0, *face_weights(pot[8] - pot[9]))
    for side, k, row in ((0, 2, ROWS - 1), (1, 3, 0)):
        part[side, 0], part[side, 1] = face_weights(send_y[side, 0] - pot_y[1 - side])
        for x in range(8):
            for c in (1, 2):
                value = wide(part[side, c - 1, x : x + 1, :])
                weights[0][x, 3 * k + c] = jnp.where(row_at == row, value, weights[0][x, 3 * k + c])

    def finish(w, r, diagonal, inv, count):
        def body(x):
            m = [[r[x, 3 * col + row] for col in range(3)] for row in range(3)]
            for c in range(3):
                total = w[x, c]
                for k in range(1, 6):
                    total = total + w[x, 3 * k + c]
                m[c][c] = m[c][c] + total
                diagonal[x, c] = m[c][c]

            def cofactor(i, j):
                i1, i2, j1, j2 = (i + 1) % 3, (i + 2) % 3, (j + 1) % 3, (j + 2) % 3
                return m[i1][j1] * m[i2][j2] - m[i1][j2] * m[i2][j1]

            cof = [[cofactor(i, j) for j in range(3)] for i in range(3)]
            det = m[0][0] * cof[0][0] + m[0][1] * cof[0][1] + m[0][2] * cof[0][2]
            scale = OMEGA / det
            for i in range(3):
                for j in range(3):
                    inv[x, 3 * i + j] = cof[j][i] * scale

        each(count, body)

    def finish_level(level):
        finish(weights[level], reaction[level], diag[level], inverse[level], NX[level])

    def mask_level(level):
        w, span, last = weights[level], 1 << level, NX[level] - 1
        for c in range(3):
            w[last, c] = jnp.where(is_high_x, 0.0, w[last, c])
            w[0, 3 + c] = jnp.where(is_low_x, 0.0, w[0, 3 + c])
        off_high = jnp.logical_and(row_at >= ROWS - span, is_high_y)
        off_low = jnp.logical_and(row_at < span, is_low_y)
        off_up, off_down = lane_at >= lanes - span, lane_at < span

        def body(x):
            for k, off in ((2, off_high), (3, off_low), (4, off_up), (5, off_down)):
                for c in range(3):
                    w[x, 3 * k + c] = jnp.where(off, 0.0, w[x, 3 * k + c])

        each(NX[level], body)

    def pair_tools(level):
        span = 1 << level
        odd_row = (row_at & span) != 0
        odd_lane = (lane_at & span) != 0

        def high_row(v):
            return jnp.where(odd_row, v, down(v, -span))

        def low_row(v):
            return jnp.where(odd_row, down(v, span), v)

        def high_lane(v):
            return jnp.where(odd_lane, v, along(v, -span))

        def low_lane(v):
            return jnp.where(odd_lane, along(v, span), v)

        def rows(v):
            return v + jnp.where(odd_row, down(v, span), down(v, -span))

        def lanes_(v):
            return v + jnp.where(odd_lane, along(v, span), along(v, -span))

        return high_row, low_row, high_lane, low_lane, rows, lanes_

    def coarsen(level):
        high_row, low_row, high_lane, low_lane, rows, lanes_ = pair_tools(level)
        w, r = weights[level], reaction[level]
        w_next, r_next = (w_own, r_own) if level == LEVELS - 2 else (weights[level + 1], reaction[level + 1])

        def body(x):
            for c in range(3):
                w_next[x, c] = lanes_(rows(w[2 * x + 1, c]))
                w_next[x, 3 + c] = lanes_(rows(w[2 * x, 3 + c]))
                pair = lambda k: w[2 * x, 3 * k + c] + w[2 * x + 1, 3 * k + c]
                w_next[x, 6 + c] = lanes_(high_row(pair(2)))
                w_next[x, 9 + c] = lanes_(low_row(pair(3)))
                w_next[x, 12 + c] = high_lane(rows(pair(4)))
                w_next[x, 15 + c] = low_lane(rows(pair(5)))
            for i in range(9):
                r_next[x, i] = lanes_(rows(r[2 * x, i] + r[2 * x + 1, i]))

        each(NX[level + 1], body)

    slot_at = lane_at & (SLOTS - 1)
    x_at, y_at = row_at + (gx - RADIUS), slot_at + (gy - RADIUS)
    x_last = jnp.logical_or(x_at == n_x - 1, x_at == -1)
    x_first = jnp.logical_or(x_at == 0, x_at == n_x)
    y_last = jnp.logical_or(y_at == n_y - 1, y_at == -1)
    y_first = jnp.logical_or(y_at == 0, y_at == n_y)
    z_last, z_first = lane_at >= lanes - SLOTS, lane_at < SLOTS
    offs = (x_last, x_first, y_last, y_first, z_last, z_first)
    bits = (2, 2, 1, 1, 4, 4)

    def transposed(tiles):
        tiles = list(tiles)
        for bit in (1, 2, 4):
            clear = (slot_at & bit) == 0
            for p in range(SLOTS):
                if not p & bit:
                    one, two = tiles[p], tiles[p | bit]
                    tiles[p] = jnp.where(clear, one, along(two, bit))
                    tiles[p | bit] = jnp.where(clear, along(one, -bit), two)
        return tiles

    def unpacked(offsets, row_of, own, fill=0.0):
        tiles = [jnp.full(tile, fill) for _ in range(SLOTS)]
        for n, (i, j) in enumerate(list(offsets) + OWN):
            if min(i, j) >= -RADIUS:
                row = row_of(n) if n < len(offsets) else own
                tiles[j + RADIUS] = jnp.where(row_at == i + RADIUS, wide(row), tiles[j + RADIUS])
        return transposed(tiles)

    def child_row(f, x0, c):
        which = slot_at & 3
        rows = [wide(f[x0 + p // 2, c, 4 * (p % 2) : 4 * (p % 2) + 1, :]) for p in range(4)]
        packed = jnp.where(which == 0, rows[0], jnp.where(which == 1, rows[1], jnp.where(which == 2, rows[2], rows[3])))
        return packed[0:1, :]

    def slot_row(values):
        packed = values[0]
        for i in range(1, len(values)):
            packed = jnp.where(slot_at == i, values[i], packed)
        return packed

    def send_coefficients():
        for i in range(27):
            mid_send[i] = child_row(weights[2] if i < 18 else reaction[2], 0, i if i < 18 else i - 18)
        return gather(INNER, lambda o: mid_send, mid_recv, mid_send_sem, mid_recv_sem)

    def send_low_coefficients():
        fields_ = [w_own[0, i] for i in range(18)] + [r_own[0, i] for i in range(9)]
        for row in range(4):
            low_send[row : row + 1, :] = slot_row(fields_[SLOTS * row : SLOTS * row + SLOTS])[0:1, :]
        return gather(FOURTH, lambda o: low_send, low_recv, low_send_sem, low_recv_sem)

    def take_coefficients(waits):
        for wait in waits:
            wait()
        for i in range(27):
            made = unpacked(INNER, lambda n: mid_recv[n, i], mid_send[i], 1.0 if i in (18, 22, 26) else 0.0)
            for p in range(SLOTS):
                if i < 18:
                    w_wide[p, i] = made[p]
                else:
                    r_wide[p, i - 18] = made[p]
        finish(w_wide, r_wide, diag_wide, inverse_wide, SLOTS)
        for k in range(6):
            for p in range(SLOTS):
                if ((p & bits[k]) != 0) == (k % 2 == 0):
                    for c in range(3):
                        w_wide[p, 3 * k + c] = jnp.where(offs[k], 0.0, w_wide[p, 3 * k + c])
        top = LEVELS - 1
        w, r = weights[top], reaction[top]
        for row in range(4):
            here = slice(row, row + 1)
            made = unpacked(FOURTH, lambda n: low_recv[n, here, :], low_send[here, :])
            for p in range(SLOTS):
                i = SLOTS * row + p
                if i < 18:
                    w[0, i] = made[p]
                elif i < 27:
                    r[0, i - 18] = made[p]
        finish_level(top)
        for k in range(6):
            for c in range(3):
                w[0, 3 * k + c] = jnp.where(offs[k], 0.0, w[0, 3 * k + c])

    def turned(u, k):
        turn = -1 if k % 2 == 0 else 1
        return down(u, turn) if k < 2 else along(u, turn if k < 4 else turn * SLOTS)

    def wide_residual(p, u, b, near_of):
        left = []
        for c in range(3):
            value = -diag_wide[p, c] * u[p][c]
            if b is not None:
                value = b[p, c] + value
            for k in range(6):
                bit = bits[k]
                near = near_of(p ^ bit, c, k) if ((p & bit) != 0) == (k % 2 == 0) else u[p ^ bit][c]
                value = value + w_wide[p, 3 * k + c] * near
            for d in range(3):
                if d != c:
                    value = value - r_wide[p, 3 * d + c] * u[p][d]
            left.append(value)
        return left

    def apply_inverse(v, x, r):
        return [v[x, 3 * c] * r[0] + v[x, 3 * c + 1] * r[1] + v[x, 3 * c + 2] * r[2] for c in range(3)]

    def wide_fields():
        return [[u_wide[p, c] for c in range(3)] for p in range(SLOTS)]

    def window_sweep(b, u, patches=None):
        top = LEVELS - 1
        w, r = weights[top], reaction[top]
        left = []
        for c in range(3):
            value = b[c] - diag[top][0, c] * u[c]
            before_x, before_y = down(u[c], 1), along(u[c], 1)
            if patches is not None:
                before_x = jnp.where(row_at == 0, patches[0][c], before_x)
                before_y = jnp.where(slot_at == 0, patches[1][c], before_y)
            near = (down(u[c], -1), before_x, along(u[c], -1), before_y, along(u[c], -SLOTS), along(u[c], SLOTS))
            for k in range(6):
                value = value + w[0, 3 * k + c] * near[k]
            for d in range(3):
                if d != c:
                    value = value - r[0, 3 * d + c] * u[d]
            left.append(value)
        step = apply_inverse(inverse[top], 0, left)
        return [u[c] + step[c] for c in range(3)]

    def lower(turn, beside_p, beside_q):
        for c in range(3):
            mid_cell[0, c] = child_row(sources[2], 0, c)
            mid_cell[1, c] = child_row(fields[2].at[0], 1, c)
        near = INNER + OUTER
        wait = gather(
            near, lambda o: mid_cell.at[0 if o in INNER else 1], mid_cells.at[turn], p_send, p_recv.at[turn]
        )
        beside_p()
        wait()
        for c in range(3):
            made = unpacked(near, lambda n: mid_cells[turn, n, c], mid_cell[0, c])
            for p in range(SLOTS):
                b_wide[p, c] = made[p]
        inner = jnp.abs(row_at - RADIUS) + jnp.abs(slot_at - RADIUS) <= 2
        for p in range(SLOTS):
            b = [b_wide[p, c] for c in range(3)]
            first = apply_inverse(inverse_wide, p, b)
            for c in range(3):
                u_wide[p, c] = jnp.where(inner, first[c], b[c])
        u_mid = wide_fields()
        b = [jnp.zeros(tile, jnp.float32) for _ in range(3)]
        for p in range(SLOTS):
            left = wide_residual(p, u_mid, b_wide, lambda q, c, k: turned(u_mid[q][c], k))
            for c in range(3):
                b[c] = b[c] + left[c]
                r_wide_2[p, c] = left[c]
        u = apply_inverse(inverse[LEVELS - 1], 0, b)
        for _ in range(2):
            u = window_sweep(b, u)
        row = slot_row([along(value, i - RADIUS) for i, value in enumerate(u + b)])
        low_cell[0] = row[RADIUS : RADIUS + 1, :]
        wait = gather(THIRD, lambda o: low_cell.at[0], low_cells.at[turn], q_send, q_recv.at[turn])
        beside_q()
        for p in range(SLOTS):
            step = apply_inverse(inverse_wide, p, [r_wide_2[p, c] for c in range(3)])
            for c in range(3):
                u_wide[p, c] += step[c]
        wait()
        made = unpacked(THIRD, lambda n: low_cells[turn, n], low_cell[0])
        u, b = made[:3], made[3:6]
        before_x = [jnp.zeros(tile, jnp.float32) for _ in range(3)]
        last_y = jnp.zeros(tile, jnp.float32)
        for n, (i, j) in enumerate(THIRD):
            if i < -RADIUS:
                for c in range(3):
                    value = along(wide(low_cells[turn, n]), j + RADIUS - c)
                    before_x[c] = jnp.where(slot_at == j + RADIUS, value, before_x[c])
            if j < -RADIUS:
                last_y = jnp.where(row_at == i + RADIUS, wide(low_cells[turn, n]), last_y)
        before_y = [along(last_y, -c) for c in range(3)]
        u = window_sweep(b, u, (before_x, before_y))
        for _ in range(COARSE_SWEEPS - 4):
            u = window_sweep(b, u)
        around_e = [[turned(u[c], k) for k in range(6)] for c in range(3)]
        last = []
        for p in range(SLOTS):
            left = wide_residual(p, [u] * SLOTS, None, lambda q, c, k: around_e[c][k])
            step = apply_inverse(inverse_wide, p, left)
            last.append([u_wide[p, c] + u[c] + step[c] for c in range(3)])
        for c in range(3):
            for x in range(2):
                for at, (t, y) in enumerate(((RADIUS - 1, 1), (RADIUS, 0), (RADIUS, 1), (RADIUS + 1, 0))):
                    low, high = last[2 * x + y][c], last[4 + 2 * x + y][c]
                    if t & 4:
                        value = jnp.where(slot_at == t, high, 0.0) + along(jnp.where(slot_at == t, low, 0.0), -4)
                    else:
                        value = jnp.where(slot_at == t, low, 0.0) + along(jnp.where(slot_at == t, high, 0.0), 4)
                    for bit in (1, 2):
                        value = value + along(value, -bit if t & bit else bit)
                    e_rows[x, at, c] = value

    def mid_at(c, x, y):
        row = RADIUS + (x // 2)
        return wide(e_rows[x % 2, y + 1, c, row : row + 1, :])

    odd = (lane_at & 1) != 0

    def even_part(v):
        return jnp.where(odd, along(v, 1), v)

    def odd_part(v):
        return jnp.where(odd, v, along(v, -1))

    def rows_tile(rows):
        made = jnp.zeros(tile, jnp.float32)
        for at, value in rows:
            made = jnp.where(row_at == at, wide(value), made)
        return made

    def pair_up():
        for x in range(4):
            for j in range(14):
                part = [weights[1][x, i] if i < 18 else reaction[1][x, i - 18] for i in (2 * j, 2 * j + 1) if i < 27]
                coef_own[x, j] = jnp.where(odd, part[-1], part[0])
        for side, y in ((0, 6), (1, 0)):
            for j in range(0, 14, 2):
                rows = [(4 * i + x, coef_own[x, j + i, y : y + 1, :]) for i in range(2) for x in range(4)]
                coef_y_send[side, j // 2] = rows_tile(rows)

    def send_ring_coefficients():
        copies = []
        for side, turn in ((0, 1), (1, -1)):
            sems = lambda n: (coef_send_sem.at[n], coef_recv_sem.at[n])
            copies.append(remote(coef_y_send.at[side], coef_y.at[side], *sems(side), (0, turn)))
            copies.append(remote(coef_own.at[3 - 3 * side], coef_x.at[side], *sems(2 + side), (turn, 0)))
        for n in range(4):
            x, y = 3 - 3 * (n // 2), 6 - 6 * (n % 2)
            for j in range(14):
                coef_corner_send[n, j : j + 1, :] = coef_own[x, j, y : y + 1, :]
            to = (1 - 2 * (n // 2), 1 - 2 * (n % 2))
            copies.append(
                remote(coef_corner_send.at[n], coef_corner.at[n], coef_send_sem.at[4 + n], coef_recv_sem.at[4 + n], to)
            )
        return copies

    def take_ring_coefficients(copies):
        for copy in copies:
            copy.wait()
        for p in range(6):
            filled = jnp.logical_and(row_at >= 1, row_at < ROWS - 1)
            for j in range(14):
                if p in (0, 5):
                    rows = [(2 + k, coef_x[p // 5, j, 2 * k : 2 * k + 1, :]) for k in range(4)]
                    rows += [(1 + 5 * sy, coef_corner[2 * (p // 5) + sy, j : j + 1, :]) for sy in range(2)]
                else:
                    x = p - 1
                    rows = [(2 + k, coef_own[x, j, 2 * k : 2 * k + 1, :]) for k in range(4)]
                    at = 4 * (j % 2) + x
                    rows += [(1, coef_y[0, j // 2, at : at + 1, :]), (6, coef_y[1, j // 2, at : at + 1, :])]
                both = rows_tile(rows)
                for i, value in ((2 * j, even_part(both)), (2 * j + 1, odd_part(both))):
                    if i < 18:
                        ring_w[p, i] = value
                    elif i < 27:
                        ring_r[p, i - 18] = jnp.where(filled, value, 1.0) if i in (18, 22, 26) else value
        finish(ring_w, ring_r, ring_diag, ring_inverse, 6)
        off_high = jnp.logical_and(row_at == 5, is_high_y)
        off_low = jnp.logical_and(row_at == 2, is_low_y)
        for c in range(3):
            ring_w[4, c] = jnp.where(is_high_x, 0.0, ring_w[4, c])
            ring_w[1, 3 + c] = jnp.where(is_low_x, 0.0, ring_w[1, 3 + c])

        def body(p):
            for k, off in ((2, off_high), (3, off_low), (4, lane_at >= lanes - 2), (5, lane_at < 2)):
                for c in range(3):
                    ring_w[p, 3 * k + c] = jnp.where(off, 0.0, ring_w[p, 3 * k + c])

        each(6, body)

    def send_pairs(turn):
        for x in range(4):
            for c in range(3):
                pair_own[x, c] = jnp.where(odd, sources[1][x, c], fields[1][0, x + 1, c])
        for side, y in ((0, 4), (1, 0)):
            for c in range(3):
                rows = [(2 * x + k, pair_own[x, c, y + 2 * k : y + 2 * k + 1, :]) for x in range(4) for k in range(2)]
                pair_y_send[side, c] = rows_tile(rows)
        for sx in range(2):
            for sy in range(2):
                x, y = 3 - 3 * sx, 6 - 6 * sy
                for i, (at_x, at_y) in enumerate(((x, y), (2 - sx, y), (x, 4 - 2 * sy))):
                    for c in range(3):
                        n = 3 * i + c
                        pair_corner_send[2 * sx + sy, n : n + 1, :] = pair_own[at_x, c, at_y : at_y + 1, :]
        copies = []
        sems = lambda n: (pair_send_sem.at[n], pair_recv_sem.at[turn, n])
        for side, to in ((0, 1), (1, -1)):
            copies.append(remote(pair_y_send.at[side], pair_y.at[turn, side], *sems(side), (0, to)))
            source = pair_own.at[pl.ds(2 - 2 * side, 2)]
            copies.append(remote(source, pair_x.at[turn, side], *sems(2 + side), (to, 0)))
        for sx in range(2):
            for sy in range(2):
                n = 2 * sx + sy
                to = (1 - 2 * sx, 1 - 2 * sy)
                copies.append(remote(pair_corner_send.at[n], pair_corner.at[turn, n], *sems(4 + n), to))
        return copies

    def take_pairs(turn, copies):
        for copy in copies:
            copy.wait()
        for p in range(8):
            for c in range(3):
                if 2 <= p < 6:
                    x = p - 2
                    rows = [(2 + k, pair_own[x, c, 2 * k : 2 * k + 1, :]) for k in range(4)]
                    for side in range(2):
                        for k in range(2):
                            at = 2 * x + k
                            rows.append((6 * side + k, pair_y[turn, side, c, at : at + 1, :]))
                else:
                    side = p // 4
                    rows = [(2 + k, pair_x[turn, side, p - 6 * side, c, 2 * k : 2 * k + 1, :]) for k in range(4)]
                    for sy in range(2):
                        cells = ((0, 1 + 5 * sy), (2, 7 * sy)) if p in (1, 6) else ((1, 1 + 5 * sy),)
                        for i, row in cells:
                            n = 3 * i + c
                            rows.append((row, pair_corner[turn, 2 * side + sy, n : n + 1, :]))
                both = rows_tile(rows)
                ring_u[p, c] = even_part(both)
                if 1 <= p < 7:
                    ring_b[p - 1, c] = odd_part(both)

    def ring_sweep():
        def add(p):
            x = p // 2 - 1
            for c in range(3):
                e = jnp.where(row_at < 2, mid_at(c, x, -1), mid_at(c, x, 0))
                e = jnp.where(row_at < 4, e, jnp.where(row_at < 6, mid_at(c, x, 1), mid_at(c, x, 2)))
                ring_u[p, c] += e

        for p in range(8):
            add(p)
        for p in range(6):
            u = [ring_u[p + 1, c] for c in range(3)]
            left = []
            for c in range(3):
                value = ring_b[p, c] - ring_diag[p, c] * u[c]
                near = (ring_u[p + 2, c], ring_u[p, c], down(u[c], -1), down(u[c], 1), along(u[c], -2), along(u[c], 2))
                for k in range(6):
                    value = value + ring_w[p, 3 * k + c] * near[k]
                for d in range(3):
                    if d != c:
                        value = value - ring_r[p, 3 * d + c] * u[d]
                left.append(value)
            step = apply_inverse(ring_inverse, p, left)
            for c in range(3):
                ring_out[p, c] = u[c] + step[c]

    def packed_y(f, at):
        return rows_tile([(x, f(x)[at : at + 1, :]) for x in range(8)])

    def send_rim():
        copies = []
        sems = lambda n: (rim_send_sem.at[n], rim_recv_sem.at[n])
        for side, to in ((0, 1), (1, -1)):
            row, second = 7 - 7 * side, 6 - 5 * side
            for i in range(9):
                rim_y_send[side, i] = rows_tile([(x, reaction[0][x, i, row : row + 1, :]) for x in range(8)])
            rim_y_send[side, 9] = rows_tile([(x, pot[x + 1, second : second + 1, :]) for x in range(8)])
            for c in range(3):
                rim_y_send[side, 10 + c] = rows_tile([(x, base[x, c, row : row + 1, :]) for x in range(8)])
            copies.append(remote(rim_y_send.at[side], rim_y.at[side], *sems(side), (0, to)))
            copies.append(remote(reaction[0].at[row], rim_r.at[side], *sems(2 + side), (to, 0)))
            copies.append(remote(pot.at[second + 1], rim_pot.at[side], *sems(4 + side), (to, 0)))
            copies.append(remote(base.at[row], rim_base.at[side], *sems(6 + side), (to, 0)))
        for n in range(4):
            x, y = 7 - 7 * (n // 2), 7 - 7 * (n % 2)
            rim_pot_corner_send[n] = pot[x + 1, y : y + 1, :]
            to = (1 - 2 * (n // 2), 1 - 2 * (n % 2))
            copies.append(remote(rim_pot_corner_send.at[n], rim_pot_corner.at[n], *sems(8 + n), to))
        return copies

    def ordered(t, out_side, in_side, ahead, behind, above, below):
        across = (in_side, out_side) if t % 2 == 0 else (out_side, in_side)
        return (across + (ahead, behind) if t < 2 else (ahead, behind) + across) + (above, below)

    def take_rim(copies):
        for copy in copies:
            copy.wait()
        for side in range(2):
            for i in range(9):
                rim_r[2 + side, i] = rim_y[side, i]
            for c in range(3):
                rim_base[2 + side, c] = rim_y[side, 10 + c]
        for t in range(4):
            side = t % 2
            if t < 2:
                here, beyond, inside = pot[9 * side], rim_pot[side], pot[1 + 7 * side]
                first, last = 2 * side, 2 * side + 1
                edges = (is_low_y, is_high_y)
            else:
                here, beyond = pot_y[side], rim_y[side, 9]
                row = 7 * side
                inside = rows_tile([(x, pot[x + 1, row : row + 1, :]) for x in range(8)])
                first, last = side, 2 + side
                edges = (is_low_x, is_high_x)
            corner = lambda n, off: jnp.where(off, 0.0, wide(rim_pot_corner[n]))
            near = ordered(
                t,
                beyond,
                inside,
                jnp.where(row_at == ROWS - 1, corner(last, edges[1]), down(here, -1)),
                jnp.where(row_at == 0, corner(first, edges[0]), down(here, 1)),
                jnp.where(lane_at == lanes - 1, 0.0, along(here, -1)),
                jnp.where(lane_at == 0, 0.0, along(here, 1)),
            )
            for k in range(6):
                plus, minus = face_weights(here - near[k])
                rim_w[t, 3 * k] = jnp.ones(tile, jnp.float32)
                rim_w[t, 3 * k + 1] = plus
                rim_w[t, 3 * k + 2] = minus
        finish(rim_w, rim_r, rim_diag, rim_inverse, 4)
        for t in range(4):
            ahead, off_high, off_low = (2, is_high_y, is_low_y) if t < 2 else (0, is_high_x, is_low_x)
            masks = (
                (ahead, jnp.logical_and(row_at == ROWS - 1, off_high)),
                (ahead + 1, jnp.logical_and(row_at == 0, off_low)),
                (4, lane_at == lanes - 1),
                (5, lane_at == 0),
            )
            for k, off in masks:
                for c in range(3):
                    rim_w[t, 3 * k + c] = jnp.where(off, 0.0, rim_w[t, 3 * k + c])

    def doubled(rows):
        e = jnp.where(row_at < 2, wide(rows[0]), wide(rows[1]))
        return jnp.where(row_at < 4, e, jnp.where(row_at < 6, wide(rows[2]), wide(rows[3])))

    def rim_sweep(at):
        for t in range(4):
            side = t % 2
            e, near = [], []
            for c in range(3):
                cell = lambda p, row: ring_out[p, c, row : row + 1, :]
                if t < 2:
                    p, p_in = 5 * side, 1 + 3 * side
                    here = doubled([cell(p, 2 + k) for k in range(4)])
                    inside = doubled([cell(p_in, 2 + k) for k in range(4)])
                    first, last = cell(p, 1), cell(p, 6)
                else:
                    row, row_in = 1 + 5 * side, 2 + 3 * side
                    here = doubled([cell(1 + k, row) for k in range(4)])
                    inside = doubled([cell(1 + k, row_in) for k in range(4)])
                    first, last = cell(0, row), cell(5, row)
                e.append(here)
                near.append(
                    ordered(
                        t,
                        here,
                        inside,
                        jnp.where(row_at == ROWS - 1, wide(last), down(here, -1)),
                        jnp.where(row_at == 0, wide(first), down(here, 1)),
                        along(here, -1),
                        along(here, 1),
                    )
                )
            left = []
            for c in range(3):
                value = -rim_diag[t, c] * e[c]
                for k in range(6):
                    value = value + rim_w[t, 3 * k + c] * near[c][k]
                for d in range(3):
                    if d != c:
                        value = value - rim_r[t, 3 * d + c] * e[d]
                left.append(value)
            step = apply_inverse(rim_inverse, t, left)
            for c in range(3):
                value = rim_base[t, c] + e[c] + step[c]
                if t < 2:
                    fields[0][at, 9 * side, c] = value
                else:
                    rows_halo[3, side, c] = value

    def source(level, x):
        if level == 0:
            return [grad[c, x] for c in range(3)]
        return [sources[level][x, c] for c in range(3)]

    def solve(level, x, r):
        v = inverse[level]
        return [v[x, 3 * c] * r[0] + v[x, 3 * c + 1] * r[1] + v[x, 3 * c + 2] * r[2] for c in range(3)]

    def post(level, at):
        slot, f, count = done[0] % 3, fields[level], NX[level]
        for side, row in ((0, ROWS - 1), (1, 0)):
            for c in range(3):
                packed = wide(f[at, 1, c, row : row + 1, :])
                for x in range(1, count):
                    packed = jnp.where(row_at == x, wide(f[at, x + 1, c, row : row + 1, :]), packed)
                send_y[side, c] = packed
        wait = exchange(
            [
                (f.at[at, count], f.at[at, 0]),
                (f.at[at, 1], f.at[at, count + 1]),
                (send_y.at[0], rows_halo.at[slot, 0]),
                (send_y.at[1], rows_halo.at[slot, 1]),
            ]
        )
        return slot, wait

    def share(level, at, beside_it):
        slot, wait = post(level, at)
        beside_it()
        inner(level, at)
        wait()
        return slot

    def inner(level, at):
        f, w, r, span, count = fields[level], weights[level], reaction[level], 1 << level, NX[level]
        for x in range(count):
            u = [f[at, x + 1, c] for c in range(3)]
            b = source(level, x)
            for c in range(3):
                value = b[c] - diag[level][x, c] * u[c]
                value = value + w[x, 6 + c] * jnp.where(row_at >= ROWS - span, 0.0, down(u[c], -span))
                value = value + w[x, 9 + c] * jnp.where(row_at < span, 0.0, down(u[c], span))
                value = value + w[x, 12 + c] * along(u[c], -span) + w[x, 15 + c] * along(u[c], span)
                if x < count - 1:
                    value = value + w[x, c] * f[at, x + 2, c]
                if x > 0:
                    value = value + w[x, 3 + c] * f[at, x, c]
                for d in range(3):
                    if d != c:
                        value = value - r[x, 3 * d + c] * u[d]
                part[x, c] = value

    def rest(level, at, slot, x, stride=1, whole=True):
        f, w, span, count = fields[level], weights[level], 1 << level, NX[level]
        left = []
        for c in range(3):
            row = x * stride
            row_high, row_low = (rows_halo[slot, side, c, row : row + 1, :] for side in (1, 0))
            value = jnp.where(row_at >= ROWS - span, w[x, 6 + c] * wide(row_high), 0.0)
            value = jnp.where(row_at < span, w[x, 9 + c] * wide(row_low), value)
            if whole:
                value = part[x, c] + value
            if x == 0:
                value = value + w[x, 3 + c] * f[at, 0, c]
            if x == count - 1:
                value = value + w[x, c] * f[at, count + 1, c]
            left.append(value)
        return [f[at, x + 1, c] for c in range(3)], left

    def residual(level, at, slot, x):
        f, w, r, span = fields[level], weights[level], reaction[level], 1 << level
        u = [f[at, x + 1, c] for c in range(3)]
        b = source(level, x)
        left = []
        for c in range(3):
            near = (
                f[at, x + 2, c],
                f[at, x, c],
                jnp.where(row_at >= ROWS - span, wide(rows_halo[slot, 1, c, x : x + 1, :]), down(u[c], -span)),
                jnp.where(row_at < span, wide(rows_halo[slot, 0, c, x : x + 1, :]), down(u[c], span)),
                along(u[c], -span),
                along(u[c], span),
            )
            value = b[c] - diag[level][x, c] * u[c]
            for k in range(6):
                value = value + w[x, 3 * k + c] * near[k]
            for d in range(3):
                if d != c:
                    value = value - r[x, 3 * d + c] * u[d]
            left.append(value)
        return u, left

    def sweep(at, slot, left_of):
        for x in range(NX[0]):
            u, left = left_of(0, at, slot, x)
            step = solve(0, x, left)
            for c in range(3):
                fields[0][at + 1, x + 1, c] = u[c] + step[c]
        return at + 1

    def make_halo_inverse():
        for i in range(9):
            for side in range(2):
                row = 1 + 5 * side
                halo_inverse[side, i] = doubled([ring_inverse[5 * side, i, 2 + k : 3 + k, :] for k in range(4)])
                halo_inverse[2 + side, i] = doubled([ring_inverse[1 + k, i, row : row + 1, :] for k in range(4)])

    def restrict_with_halo(at):
        slot, wait = post(0, at)
        rows, lanes_ = pair_tools(0)[4:]
        outside = (is_low_x, is_high_x, is_low_y, is_high_y)
        for t in range(4):
            for c in range(3):
                edge = fields[0][at, 1 + 7 * t, c] if t < 2 else send_y[3 - t, c]
                value = jnp.where(outside[t], 0.0, rim_w[t, 3 * t + c] * edge)
                cross[t, c] = lanes_(rows(value))
        copies = []
        sems = lambda n: (lean_send_sem.at[n], lean_recv_sem.at[n])
        for n in range(4):
            sx, sy = n // 2, n % 2
            for c in range(3):
                row = 6 - 6 * sx
                cross_send[n, c : c + 1, :] = cross[3 - sy, c, row : row + 1, :]
                row = 6 - 6 * sy
                cross_send[n, 3 + c : 4 + c, :] = cross[1 - sx, c, row : row + 1, :]
            copies.append(remote(cross_send.at[n], cross_recv.at[n], *sems(4 + n), (1 - 2 * sx, 1 - 2 * sy)))
        inner(0, at)
        for x in range(4):
            for c in range(3):
                lean[x, c] = lanes_(rows(part[2 * x, c] + part[2 * x + 1, c]))
        for side, to in ((0, 1), (1, -1)):
            row = 6 - 6 * side
            for c in range(3):
                lean_y_send[side, c] = doubled([lean[k, c, row : row + 1, :] for k in range(4)])
            copies.append(remote(lean_y_send.at[side], lean_y.at[side], *sems(side), (0, to)))
            copies.append(remote(lean.at[3 - 3 * side], lean_x.at[side], *sems(2 + side), (to, 0)))
        wait()
        for x in range(4):
            more = [rest(0, at, slot, 2 * x + i, whole=False)[1] for i in range(2)]
            for i in range(2):
                for c in range(3):
                    base[2 * x + i, c] = part[2 * x + i, c] + more[i][c]
            total = [lean[x, c] + lanes_(rows(more[0][c] + more[1][c])) for c in range(3)]
            first = solve(1, x, total)
            for c in range(3):
                sources[1][x, c] = total[c]
                fields[1][0, x + 1, c] = first[c]
        for copy in copies:
            copy.wait()
        for t in range(4):
            side = t % 2
            total = []
            for c in range(3):
                if t < 2:
                    value, first, last, row = lean_x[side, c], 2 * side, 2 * side + 1, c
                else:
                    value, first, last, row = lean_y[side, c], side, 2 + side, 3 + c
                low, high = (wide(cross_recv[n, row : row + 1, :]) for n in (first, last))
                value = value + cross[t, c]
                total.append(value + jnp.where(row_at < 2, low, jnp.where(row_at >= 6, high, 0.0)))
            first = apply_inverse(halo_inverse, t, total)
            for c in range(3):
                if t < 2:
                    fields[1][0, 5 * side, c] = first[c]
                else:
                    rows_halo[3, side, c] = first[c]
        inner(1, 0)
        return slot

    def restrict(level, at, slot, keep=False, stride=1):
        rows, lanes_ = pair_tools(level)[4:]
        for x in range(NX[level + 1]):
            left = []
            for i in range(2):
                u, r = rest(level, at, slot, 2 * x + i, stride)
                left.append(r)
                if keep:
                    for c in range(3):
                        base[2 * x + i, c] = r[c]
            total = [lanes_(rows(left[0][c] + left[1][c])) for c in range(3)]
            first = solve(level + 1, x, total)
            for c in range(3):
                sources[level + 1][x, c] = total[c]
                fields[level + 1][0, x + 1, c] = first[c]

    def make_base(at):
        for x in range(NX[0]):
            step = solve(0, x, [base[x, c] for c in range(3)])
            for c in range(3):
                base[x, c] = fields[0][at, x + 1, c] + step[c]

    def correct_finest(at, last):
        copies = []
        planes = [[doubled([ring_out[p, c, 2 + k : 3 + k, :] for k in range(4)]) for c in range(3)] for p in range(6)]
        w, r, v = weights[0], reaction[0], inverse[0]
        for p in range(1, 5):
            e = planes[p]
            turned = []
            for c in range(3):
                after, before = wide(ring_out[p, c, 6:7, :]), wide(ring_out[p, c, 1:2, :])
                turned.append(
                    (
                        jnp.where(row_at == ROWS - 1, after, down(e[c], -1)),
                        jnp.where(row_at == 0, before, down(e[c], 1)),
                        along(e[c], -1),
                        along(e[c], 1),
                    )
                )
            for i in range(2):
                x = 2 * p - 2 + i
                left = []
                for c in range(3):
                    near = (e[c] if i == 0 else planes[p + 1][c], planes[p - 1][c] if i == 0 else e[c]) + turned[c]
                    value = -diag[0][x, c] * e[c]
                    for k in range(6):
                        value = value + w[x, 3 * k + c] * near[k]
                    for d in range(3):
                        if d != c:
                            value = value - r[x, 3 * d + c] * e[d]
                    left.append(value)
                step = apply_inverse(v, x, left)
                for c in range(3):
                    value = base[x, c] + e[c] + step[c]
                    if last:
                        result[c, x] = value
                    else:
                        fields[0][at + 1, x + 1, c] = value
                if last:
                    copies.append(pltpu.make_async_copy(result.at[:, x], out.at[:, x], out_sem.at[x]))
                    copies[-1].start()
        for copy in copies:
            copy.wait()
        return at + 1

    def cycle(at, turn, besides, last=False):
        pairs = []
        if last:
            slot = restrict_with_halo(at)
            restrict(1, 0, 3, stride=2)
        else:
            slot = share(0, at, besides[0])
            restrict(0, at, slot, keep=True)

            def beside():
                pairs.extend(send_pairs(turn))
                besides[1]()
                make_base(at)

            restrict(1, 0, share(1, 0, beside))

        def beside_p():
            if last:
                pairs.extend(send_pairs(turn))
                make_base(at)
            besides[2]()

        def beside_q():
            take_pairs(turn, pairs)
            besides[3]()

        lower(turn, beside_p, beside_q)
        ring_sweep()
        if not last:
            rim_sweep(at + 1)
        return correct_finest(at, last)

    def start(x):
        for c, value in enumerate(solve(0, x, source(0, x))):
            fields[0][0, x + 1, c] = value

    finish_level(0)
    loads["grad"].wait()
    each(NX[0], start)
    pending, ring_pending, rim_pending = [], [], []

    def beside_first():
        coarsen(0)
        mask_level(0)
        finish_level(1)
        coarsen(1)
        pending.append(send_coefficients())

    def beside_second():
        pair_up()
        mask_level(1)
        finish_level(2)
        coarsen(2)
        pending.append(send_low_coefficients())

    def beside_third():
        ring_pending.extend(send_ring_coefficients())
        rim_pending.extend(send_rim())
        take_coefficients(pending)

    def beside_fourth():
        take_ring_coefficients(ring_pending)
        take_rim(rim_pending)
        make_halo_inverse()

    nothing = lambda: None
    at = cycle(
        0,
        0,
        (
            beside_first,
            beside_second,
            beside_third,
            beside_fourth,
        ),
    )
    at = sweep(at, 3, residual)
    cycle(at, 1, (nothing,) * 4, last=True)


def local(counts, gradient, potential, coupling, region, contact, rates):
    nz = potential.shape[-1]
    tile = (ROWS, nz)
    f32 = jnp.float32
    scratch = []
    for parts in (18, 9, 3, 9):
        scratch += [pltpu.VMEM((n, parts) + tile, f32) for n in NX]
    scratch += [pltpu.VMEM((n, 3) + tile, f32) for n in NX[1:]]
    scratch += [pltpu.VMEM((3, n + 2, 3) + tile, f32) for n in NX]
    scratch += [
        pltpu.VMEM((4, 2, 3) + tile, f32),
        pltpu.VMEM((2,) + tile, f32),
        pltpu.VMEM((2, 3) + tile, f32),
        pltpu.SemaphoreType.DMA((4,)),
        pltpu.SemaphoreType.DMA((3, 4)),
        pltpu.VMEM((1, 18) + tile, f32),
        pltpu.VMEM((1, 9) + tile, f32),
        pltpu.VMEM((SLOTS, 18) + tile, f32),
        pltpu.VMEM((SLOTS, 9) + tile, f32),
        pltpu.VMEM((SLOTS, 3) + tile, f32),
        pltpu.VMEM((SLOTS, 9) + tile, f32),
        pltpu.VMEM((SLOTS, 3) + tile, f32),
        pltpu.VMEM((SLOTS, 3) + tile, f32),
        pltpu.VMEM((2, 4, 3) + tile, f32),
        pltpu.VMEM((27, 1, nz), f32),
        pltpu.VMEM((len(INNER), 27, 1, nz), f32),
        pltpu.VMEM((4, nz), f32),
        pltpu.VMEM((len(FOURTH), 4, nz), f32),
        pltpu.VMEM((2, 3, 1, nz), f32),
        pltpu.VMEM((2, len(INNER + OUTER), 3, 1, nz), f32),
        pltpu.VMEM((1, 1, nz), f32),
        pltpu.VMEM((2, len(THIRD), 1, nz), f32),
        pltpu.SemaphoreType.DMA,
        pltpu.SemaphoreType.DMA,
        pltpu.SemaphoreType.DMA,
        pltpu.SemaphoreType.DMA,
        pltpu.SemaphoreType.DMA,
        pltpu.SemaphoreType.DMA((2,)),
        pltpu.SemaphoreType.DMA,
        pltpu.SemaphoreType.DMA((2,)),
        pltpu.VMEM((8, 3) + tile, f32),
        pltpu.VMEM((6, 3) + tile, f32),
        pltpu.VMEM((6, 18) + tile, f32),
        pltpu.VMEM((6, 9) + tile, f32),
        pltpu.VMEM((6, 3) + tile, f32),
        pltpu.VMEM((6, 9) + tile, f32),
        pltpu.VMEM((6, 3) + tile, f32),
        pltpu.VMEM((4, 3) + tile, f32),
        pltpu.VMEM((2, 2, 2, 3) + tile, f32),
        pltpu.VMEM((2, 3) + tile, f32),
        pltpu.VMEM((2, 2, 3) + tile, f32),
        pltpu.VMEM((4, 2 * ROWS, nz), f32),
        pltpu.VMEM((2, 4, 2 * ROWS, nz), f32),
        pltpu.SemaphoreType.DMA((8,)),
        pltpu.SemaphoreType.DMA((2, 8)),
        pltpu.VMEM((4, 14) + tile, f32),
        pltpu.VMEM((2, 14) + tile, f32),
        pltpu.VMEM((2, 7) + tile, f32),
        pltpu.VMEM((2, 7) + tile, f32),
        pltpu.SemaphoreType.DMA((8,)),
        pltpu.SemaphoreType.DMA((8,)),
        pltpu.VMEM((NX[0], 3) + tile, f32),
        pltpu.VMEM((4, 2 * ROWS, nz), f32),
        pltpu.VMEM((4, 2 * ROWS, nz), f32),
        pltpu.VMEM((4, 18) + tile, f32),
        pltpu.VMEM((4, 9) + tile, f32),
        pltpu.VMEM((4, 3) + tile, f32),
        pltpu.VMEM((4, 9) + tile, f32),
        pltpu.VMEM((4, 3) + tile, f32),
        pltpu.VMEM((2,) + tile, f32),
        pltpu.VMEM((4, 1, nz), f32),
        pltpu.VMEM((4, 1, nz), f32),
        pltpu.VMEM((NX[0], 3) + tile, f32),
        pltpu.VMEM((2, 13) + tile, f32),
        pltpu.VMEM((2, 13) + tile, f32),
        pltpu.SemaphoreType.DMA((12,)),
        pltpu.SemaphoreType.DMA((12,)),
        pltpu.VMEM(gradient.shape, f32),
        pltpu.SemaphoreType.DMA((NX[0],)),
        pltpu.VMEM((4, 9) + tile, f32),
        pltpu.VMEM((4, 3) + tile, f32),
        pltpu.VMEM((4,) + tile, f32),
        pltpu.VMEM((4,) + tile, f32),
        pltpu.VMEM((4, 3) + tile, f32),
        pltpu.VMEM((2, 3) + tile, f32),
        pltpu.VMEM((2, 3) + tile, f32),
        pltpu.VMEM((2, 3) + tile, f32),
        pltpu.SemaphoreType.DMA((8,)),
        pltpu.SemaphoreType.DMA((8,)),
        pltpu.VMEM((SLOTS, 3) + tile, f32),
        pltpu.VMEM(gradient.shape, f32),
        pltpu.VMEM((10,) + tile, f32),
        pltpu.VMEM(coupling.shape, f32),
        pltpu.VMEM(region.shape, jnp.int32),
        pltpu.VMEM(contact.shape, jnp.int32),
        pltpu.SMEM(rates.shape, f32),
        pltpu.SemaphoreType.DMA((6,)),
    ]
    return pl.pallas_call(
        functools.partial(kernel, counts),
        out_shape=jax.ShapeDtypeStruct(gradient.shape, f32),
        in_specs=[pl.BlockSpec(memory_space=pltpu.HBM)] * 6,
        out_specs=pl.BlockSpec(memory_space=pltpu.HBM),
        scratch_shapes=scratch,
        compiler_params=pltpu.CompilerParams(
            collective_id=0, has_side_effects=True, vmem_limit_bytes=60 * 1024 * 1024
        ),
    )(gradient, potential, coupling, region, contact, rates)


def solution(mesh):
    placed = (
        P(None, "gx", "gy", None),
        P("gx", "gy", None),
        P(None, None, "gx", "gy", None),
        P("gx", "gy", None),
        P("gx", "gy", None),
        P(),
    )
    counts = (mesh.shape["gx"], mesh.shape["gy"])
    return jax.shard_map(
        functools.partial(local, counts),
        mesh=mesh,
        in_specs=placed,
        out_specs=P(None, "gx", "gy", None),
        check_vma=False,
    )
```

```python
import functools

import jax
import jax.numpy as jnp
from jax import lax
from jax.experimental import pallas as pl
from jax.experimental.pallas import tpu as pltpu
from jax.sharding import PartitionSpec as P

MESH = pl.DeviceIdType.MESH
LEVELS = 4
COARSE_SWEEPS = 6
REGIONS = 4
OMEGA = 0.8
STRENGTH = 8.0
ROWS = 8
NX = (8, 4, 2, 1)
RADIUS = 3
SLOTS = 8


def by_links(offsets):
    along_x, along_y = (0, 1, 1, 2, 2, 3, 3), (0, 2, 3, 2, 1, 2, 3)
    return sorted(offsets, key=lambda o: (-along_x[abs(o[0])] - along_y[abs(o[1])], o))


def around(shape, far):
    reach = range(-6, 7)
    distance = lambda i, j: min(abs(i - a) + abs(j - b) for a, b in shape)
    found = [(i, j) for i in reach for j in reach if distance(i, j) <= far and (i, j) != (0, 0)]
    return by_links(found)


OWN = [(0, 0)]
SQUARE = [(i, j) for i in (-1, 0, 1) for j in (-1, 0, 1)]
INNER = around(OWN, 2)
OUTER = [o for o in around(OWN, 3) if o not in INNER]
FOURTH = around(SQUARE, 2)
THIRD = around(SQUARE, 3)


def each(count, body):
    if count == 1:
        body(0)
        return

    def step(i, carry):
        body(i)
        return carry

    lax.fori_loop(0, count, step, 0, unroll=count)


def face_weights(difference):
    size = jnp.abs(difference)
    small = size < 0.5
    series = 1.0 / 362880.0
    for k in (40320.0, 5040.0, 720.0, 120.0, 24.0, 6.0, 2.0, 1.0):
        series = series * size + 1.0 / k
    below = jnp.where(small, series, jnp.exp(size) - 1.0)
    low = jnp.where(small, 1.0, size) / below
    low = jnp.where(size < 1e-4, 1.0 - 0.5 * size, low)
    high = low + size
    positive = difference > 0.0
    return jnp.where(positive, low, high), jnp.where(positive, high, low)


def kernel(counts, grad_in, pot_in, coup_in, region_in, contact_in, rates_in, out, *scratch):
    grad, pot, coup, region, contact, rates, in_sem = scratch[-7:]
    scratch = scratch[:-7]
    loads = {}
    for i, (name, source, target) in enumerate(
        (
            ("pot", pot_in, pot.at[pl.ds(1, 8)]),
            ("rates", rates_in, rates),
            ("region", region_in, region),
            ("contact", contact_in, contact),
            ("coup", coup_in, coup),
            ("grad", grad_in, grad),
        )
    ):
        loads[name] = pltpu.make_async_copy(source, target, in_sem.at[i])
        loads[name].start()
    weights, reaction, diag, inverse = (scratch[4 * i : 4 * i + 4] for i in range(4))
    sources = (None,) + tuple(scratch[16:19])
    fields = scratch[19:23]
    rows_halo, pot_y, send_y, send_sem, recv_sem = scratch[23:28]
    w_own, r_own, w_wide, r_wide, diag_wide, inverse_wide, u_wide, b_wide, e_rows = scratch[28:37]
    mid_send, mid_recv, low_send, low_recv, mid_cell, mid_cells, low_cell, low_cells = scratch[37:45]
    mid_send_sem, mid_recv_sem, low_send_sem, low_recv_sem, p_send, p_recv, q_send, q_recv = scratch[45:53]
    ring_u, ring_b, ring_w, ring_r, ring_diag, ring_inverse, ring_out = scratch[53:60]
    pair_own, pair_x, pair_y_send, pair_y, pair_corner_send, pair_corner, pair_send_sem, pair_recv_sem = scratch[60:68]
    coef_own, coef_x, coef_y_send, coef_y, coef_send_sem, coef_recv_sem, part, coef_corner_send, coef_corner = scratch[68:77]
    rim_w, rim_r, rim_diag, rim_inverse, rim_base, rim_pot, rim_pot_corner_send, rim_pot_corner = scratch[77:85]
    base, rim_y_send, rim_y, rim_send_sem, rim_recv_sem, result, out_sem = scratch[85:92]
    halo_inverse, cross, cross_send, cross_recv, lean, lean_x, lean_y_send, lean_y = scratch[92:100]
    lean_send_sem, lean_recv_sem, r_wide_2 = scratch[100:]
    n_x, n_y = counts
    lanes = out.shape[-1]
    gx, gy = lax.axis_index("gx"), lax.axis_index("gy")
    x_low, x_high = lax.rem(gx + n_x - 1, n_x), lax.rem(gx + 1, n_x)
    y_low, y_high = lax.rem(gy + n_y - 1, n_y), lax.rem(gy + 1, n_y)
    beside = ((x_high, gy), (x_low, gy), (gx, y_high), (gx, y_low))

    barrier = pltpu.get_barrier_semaphore()
    at_offset = lambda i, j: (lax.rem(gx + n_x + i, n_x), lax.rem(gy + n_y + j, n_y))
    devices = {o: at_offset(*o) for o in THIRD}
    for offset in INNER:
        pl.semaphore_signal(barrier, inc=1, device_id=devices[offset], device_id_type=MESH)
    pl.semaphore_wait(barrier, len(INNER))

    tile = (ROWS, lanes)
    row_at = lax.broadcasted_iota(jnp.int32, tile, 0)
    lane_at = lax.broadcasted_iota(jnp.int32, tile, 1)
    wide = lambda row: jnp.broadcast_to(row, tile)
    down = lambda v, by: pltpu.roll(v, by % ROWS, 0) if by % ROWS else v
    along = lambda v, by: pltpu.roll(v, by % lanes, 1)

    done = [0]

    def exchange(parts):
        slot = done[0] % 3
        done[0] += 1
        copies = []
        for i in (2, 3, 0, 1):
            source, target = parts[i]
            copy = pltpu.make_async_remote_copy(
                src_ref=source,
                dst_ref=target,
                send_sem=send_sem.at[i],
                recv_sem=recv_sem.at[slot, i],
                device_id=beside[i],
                device_id_type=MESH,
            )
            copy.start()
            copies.append(copy)

        def wait():
            for copy in copies:
                copy.wait()

        return wait

    def remote(source, target, send, recv, offset):
        copy = pltpu.make_async_remote_copy(
            src_ref=source,
            dst_ref=target,
            send_sem=send,
            recv_sem=recv,
            device_id=devices[offset],
            device_id_type=MESH,
        )
        copy.start()
        return copy

    def gather(offsets, source_of, target, send, recv):
        for n, (i, j) in enumerate(offsets):
            remote(source_of((i, j)), target.at[n], send, recv, (-i, -j))

        def wait():
            pltpu.make_async_copy(target, target, send).wait()
            pltpu.make_async_copy(target, target, recv).wait()

        return wait

    loads["pot"].wait()
    for side, at in ((0, ROWS - 1), (1, 0)):
        packed = wide(pot[1, at : at + 1, :])
        for x in range(1, 8):
            packed = jnp.where(row_at == x, wide(pot[x + 1, at : at + 1, :]), packed)
        send_y[side, 0] = packed
    wait = exchange(
        [
            (pot.at[8], pot.at[0]),
            (pot.at[1], pot.at[9]),
            (send_y.at[0, 0], pot_y.at[0]),
            (send_y.at[1, 0], pot_y.at[1]),
        ]
    )
    for name in ("rates", "region", "contact", "coup"):
        loads[name].wait()

    def put_faces(x, k, plus, minus):
        weights[0][x, 3 * k] = jnp.ones(tile, jnp.float32)
        weights[0][x, 3 * k + 1] = plus
        weights[0][x, 3 * k + 2] = minus

    def set_up(x):
        here = pot[x + 1]
        put_faces(x, 4, *face_weights(here - jnp.where(lane_at == lanes - 1, 0.0, along(here, -1))))
        put_faces(x, 5, *face_weights(here - jnp.where(lane_at == 0, 0.0, along(here, 1))))
        plus, minus = face_weights(here - down(here, -1))
        put_faces(x, 2, plus, minus)
        put_faces(x, 3, down(minus, 1), down(plus, 1))
        at_contact = STRENGTH * contact[x].astype(jnp.float32)
        regions = region[x]
        for c in range(3):
            extra = jnp.full(tile, rates[0, c])
            for pick in range(1, REGIONS):
                extra = jnp.where(regions == pick, rates[pick, c], extra)
            for d in range(3):
                value = coup[c, d, x]
                reaction[0][x, 3 * c + d] = value + (extra + at_contact) if c == d else value

    each(NX[0], set_up)
    for x in range(7):
        plus, minus = face_weights(pot[x + 1] - pot[x + 2])
        put_faces(x, 0, plus, minus)
        put_faces(x + 1, 1, minus, plus)
    wait()
    is_low_x, is_high_x = gx == 0, gx == n_x - 1
    is_low_y, is_high_y = gy == 0, gy == n_y - 1
    pot[0] = jnp.where(is_low_x, 0.0, pot[0])
    pot[9] = jnp.where(is_high_x, 0.0, pot[9])
    pot_y[0] = jnp.where(is_low_y, 0.0, pot_y[0])
    pot_y[1] = jnp.where(is_high_y, 0.0, pot_y[1])

    put_faces(0, 1, *face_weights(pot[1] - pot[0]))
    put_faces(7, 0, *face_weights(pot[8] - pot[9]))
    for side, k, row in ((0, 2, ROWS - 1), (1, 3, 0)):
        part[side, 0], part[side, 1] = face_weights(send_y[side, 0] - pot_y[1 - side])
        for x in range(8):
            for c in (1, 2):
                value = wide(part[side, c - 1, x : x + 1, :])
                weights[0][x, 3 * k + c] = jnp.where(row_at == row, value, weights[0][x, 3 * k + c])

    def finish(w, r, diagonal, inv, count):
        def body(x):
            m = [[r[x, 3 * col + row] for col in range(3)] for row in range(3)]
            for c in range(3):
                total = w[x, c]
                for k in range(1, 6):
                    total = total + w[x, 3 * k + c]
                m[c][c] = m[c][c] + total
                diagonal[x, c] = m[c][c]

            def cofactor(i, j):
                i1, i2, j1, j2 = (i + 1) % 3, (i + 2) % 3, (j + 1) % 3, (j + 2) % 3
                return m[i1][j1] * m[i2][j2] - m[i1][j2] * m[i2][j1]

            cof = [[cofactor(i, j) for j in range(3)] for i in range(3)]
            det = m[0][0] * cof[0][0] + m[0][1] * cof[0][1] + m[0][2] * cof[0][2]
            scale = OMEGA / det
            for i in range(3):
                for j in range(3):
                    inv[x, 3 * i + j] = cof[j][i] * scale

        each(count, body)

    def finish_level(level):
        finish(weights[level], reaction[level], diag[level], inverse[level], NX[level])

    def mask_level(level):
        w, span, last = weights[level], 1 << level, NX[level] - 1
        for c in range(3):
            w[last, c] = jnp.where(is_high_x, 0.0, w[last, c])
            w[0, 3 + c] = jnp.where(is_low_x, 0.0, w[0, 3 + c])
        off_high = jnp.logical_and(row_at >= ROWS - span, is_high_y)
        off_low = jnp.logical_and(row_at < span, is_low_y)
        off_up, off_down = lane_at >= lanes - span, lane_at < span

        def body(x):
            for k, off in ((2, off_high), (3, off_low), (4, off_up), (5, off_down)):
                for c in range(3):
                    w[x, 3 * k + c] = jnp.where(off, 0.0, w[x, 3 * k + c])

        each(NX[level], body)

    def pair_tools(level):
        span = 1 << level
        odd_row = (row_at & span) != 0
        odd_lane = (lane_at & span) != 0

        def high_row(v):
            return jnp.where(odd_row, v, down(v, -span))

        def low_row(v):
            return jnp.where(odd_row, down(v, span), v)

        def high_lane(v):
            return jnp.where(odd_lane, v, along(v, -span))

        def low_lane(v):
            return jnp.where(odd_lane, along(v, span), v)

        def rows(v):
            return v + jnp.where(odd_row, down(v, span), down(v, -span))

        def lanes_(v):
            return v + jnp.where(odd_lane, along(v, span), along(v, -span))

        return high_row, low_row, high_lane, low_lane, rows, lanes_

    def coarsen(level):
        high_row, low_row, high_lane, low_lane, rows, lanes_ = pair_tools(level)
        w, r = weights[level], reaction[level]
        w_next, r_next = (w_own, r_own) if level == LEVELS - 2 else (weights[level + 1], reaction[level + 1])

        def body(x):
            for c in range(3):
                w_next[x, c] = lanes_(rows(w[2 * x + 1, c]))
                w_next[x, 3 + c] = lanes_(rows(w[2 * x, 3 + c]))
                pair = lambda k: w[2 * x, 3 * k + c] + w[2 * x + 1, 3 * k + c]
                w_next[x, 6 + c] = lanes_(high_row(pair(2)))
                w_next[x, 9 + c] = lanes_(low_row(pair(3)))
                w_next[x, 12 + c] = high_lane(rows(pair(4)))
                w_next[x, 15 + c] = low_lane(rows(pair(5)))
            for i in range(9):
                r_next[x, i] = lanes_(rows(r[2 * x, i] + r[2 * x + 1, i]))

        each(NX[level + 1], body)

    slot_at = lane_at & (SLOTS - 1)
    x_at, y_at = row_at + (gx - RADIUS), slot_at + (gy - RADIUS)
    x_last = jnp.logical_or(x_at == n_x - 1, x_at == -1)
    x_first = jnp.logical_or(x_at == 0, x_at == n_x)
    y_last = jnp.logical_or(y_at == n_y - 1, y_at == -1)
    y_first = jnp.logical_or(y_at == 0, y_at == n_y)
    z_last, z_first = lane_at >= lanes - SLOTS, lane_at < SLOTS
    offs = (x_last, x_first, y_last, y_first, z_last, z_first)
    bits = (2, 2, 1, 1, 4, 4)

    def transposed(tiles):
        tiles = list(tiles)
        for bit in (1, 2, 4):
            clear = (slot_at & bit) == 0
            for p in range(SLOTS):
                if not p & bit:
                    one, two = tiles[p], tiles[p | bit]
                    tiles[p] = jnp.where(clear, one, along(two, bit))
                    tiles[p | bit] = jnp.where(clear, along(one, -bit), two)
        return tiles

    def unpacked(offsets, row_of, own, fill=0.0):
        tiles = [jnp.full(tile, fill) for _ in range(SLOTS)]
        for n, (i, j) in enumerate(list(offsets) + OWN):
            if min(i, j) >= -RADIUS:
                row = row_of(n) if n < len(offsets) else own
                tiles[j + RADIUS] = jnp.where(row_at == i + RADIUS, wide(row), tiles[j + RADIUS])
        return transposed(tiles)

    def child_row(f, x0, c):
        which = slot_at & 3
        rows = [wide(f[x0 + p // 2, c, 4 * (p % 2) : 4 * (p % 2) + 1, :]) for p in range(4)]
        packed = jnp.where(which == 0, rows[0], jnp.where(which == 1, rows[1], jnp.where(which == 2, rows[2], rows[3])))
        return packed[0:1, :]

    def slot_row(values):
        packed = values[0]
        for i in range(1, len(values)):
            packed = jnp.where(slot_at == i, values[i], packed)
        return packed

    def send_coefficients():
        for i in range(27):
            mid_send[i] = child_row(weights[2] if i < 18 else reaction[2], 0, i if i < 18 else i - 18)
        return gather(INNER, lambda o: mid_send, mid_recv, mid_send_sem, mid_recv_sem)

    def send_low_coefficients():
        fields_ = [w_own[0, i] for i in range(18)] + [r_own[0, i] for i in range(9)]
        for row in range(4):
            low_send[row : row + 1, :] = slot_row(fields_[SLOTS * row : SLOTS * row + SLOTS])[0:1, :]
        return gather(FOURTH, lambda o: low_send, low_recv, low_send_sem, low_recv_sem)

    def take_coefficients(waits):
        for wait in waits:
            wait()
        for i in range(27):
            made = unpacked(INNER, lambda n: mid_recv[n, i], mid_send[i], 1.0 if i in (18, 22, 26) else 0.0)
            for p in range(SLOTS):
                if i < 18:
                    w_wide[p, i] = made[p]
                else:
                    r_wide[p, i - 18] = made[p]
        finish(w_wide, r_wide, diag_wide, inverse_wide, SLOTS)
        for k in range(6):
            for p in range(SLOTS):
                if ((p & bits[k]) != 0) == (k % 2 == 0):
                    for c in range(3):
                        w_wide[p, 3 * k + c] = jnp.where(offs[k], 0.0, w_wide[p, 3 * k + c])
        top = LEVELS - 1
        w, r = weights[top], reaction[top]
        for row in range(4):
            here = slice(row, row + 1)
            made = unpacked(FOURTH, lambda n: low_recv[n, here, :], low_send[here, :])
            for p in range(SLOTS):
                i = SLOTS * row + p
                if i < 18:
                    w[0, i] = made[p]
                elif i < 27:
                    r[0, i - 18] = made[p]
        finish_level(top)
        for k in range(6):
            for c in range(3):
                w[0, 3 * k + c] = jnp.where(offs[k], 0.0, w[0, 3 * k + c])

    def turned(u, k):
        turn = -1 if k % 2 == 0 else 1
        return down(u, turn) if k < 2 else along(u, turn if k < 4 else turn * SLOTS)

    def wide_residual(p, u, b, near_of):
        left = []
        for c in range(3):
            value = -diag_wide[p, c] * u[p][c]
            if b is not None:
                value = b[p, c] + value
            for k in range(6):
                bit = bits[k]
                near = near_of(p ^ bit, c, k) if ((p & bit) != 0) == (k % 2 == 0) else u[p ^ bit][c]
                value = value + w_wide[p, 3 * k + c] * near
            for d in range(3):
                if d != c:
                    value = value - r_wide[p, 3 * d + c] * u[p][d]
            left.append(value)
        return left

    def apply_inverse(v, x, r):
        return [v[x, 3 * c] * r[0] + v[x, 3 * c + 1] * r[1] + v[x, 3 * c + 2] * r[2] for c in range(3)]

    def wide_fields():
        return [[u_wide[p, c] for c in range(3)] for p in range(SLOTS)]

    def window_sweep(b, u, patches=None):
        top = LEVELS - 1
        w, r = weights[top], reaction[top]
        left = []
        for c in range(3):
            value = b[c] - diag[top][0, c] * u[c]
            before_x, before_y = down(u[c], 1), along(u[c], 1)
            if patches is not None:
                before_x = jnp.where(row_at == 0, patches[0][c], before_x)
                before_y = jnp.where(slot_at == 0, patches[1][c], before_y)
            near = (down(u[c], -1), before_x, along(u[c], -1), before_y, along(u[c], -SLOTS), along(u[c], SLOTS))
            for k in range(6):
                value = value + w[0, 3 * k + c] * near[k]
            for d in range(3):
                if d != c:
                    value = value - r[0, 3 * d + c] * u[d]
            left.append(value)
        step = apply_inverse(inverse[top], 0, left)
        return [u[c] + step[c] for c in range(3)]

    def lower(turn, beside_p, beside_q):
        for c in range(3):
            mid_cell[0, c] = child_row(sources[2], 0, c)
            mid_cell[1, c] = child_row(fields[2].at[0], 1, c)
        near = by_links(INNER + OUTER)
        wait = gather(
            near, lambda o: mid_cell.at[0 if o in INNER else 1], mid_cells.at[turn], p_send, p_recv.at[turn]
        )
        beside_p()
        wait()
        for c in range(3):
            made = unpacked(near, lambda n: mid_cells[turn, n, c], mid_cell[0, c])
            for p in range(SLOTS):
                b_wide[p, c] = made[p]
        inner = jnp.abs(row_at - RADIUS) + jnp.abs(slot_at - RADIUS) <= 2
        for p in range(SLOTS):
            b = [b_wide[p, c] for c in range(3)]
            first = apply_inverse(inverse_wide, p, b)
            for c in range(3):
                u_wide[p, c] = jnp.where(inner, first[c], b[c])
        u_mid = wide_fields()
        b = [jnp.zeros(tile, jnp.float32) for _ in range(3)]
        for p in range(SLOTS):
            left = wide_residual(p, u_mid, b_wide, lambda q, c, k: turned(u_mid[q][c], k))
            for c in range(3):
                b[c] = b[c] + left[c]
                r_wide_2[p, c] = left[c]
        u = apply_inverse(inverse[LEVELS - 1], 0, b)
        for _ in range(2):
            u = window_sweep(b, u)
        row = slot_row([along(value, i - RADIUS) for i, value in enumerate(u + b)])
        low_cell[0] = row[RADIUS : RADIUS + 1, :]
        wait = gather(THIRD, lambda o: low_cell.at[0], low_cells.at[turn], q_send, q_recv.at[turn])
        beside_q()
        for p in range(SLOTS):
            step = apply_inverse(inverse_wide, p, [r_wide_2[p, c] for c in range(3)])
            for c in range(3):
                u_wide[p, c] += step[c]
        wait()
        made = unpacked(THIRD, lambda n: low_cells[turn, n], low_cell[0])
        u, b = made[:3], made[3:6]
        before_x = [jnp.zeros(tile, jnp.float32) for _ in range(3)]
        last_y = jnp.zeros(tile, jnp.float32)
        for n, (i, j) in enumerate(THIRD):
            if i < -RADIUS:
                for c in range(3):
                    value = along(wide(low_cells[turn, n]), j + RADIUS - c)
                    before_x[c] = jnp.where(slot_at == j + RADIUS, value, before_x[c])
            if j < -RADIUS:
                last_y = jnp.where(row_at == i + RADIUS, wide(low_cells[turn, n]), last_y)
        before_y = [along(last_y, -c) for c in range(3)]
        u = window_sweep(b, u, (before_x, before_y))
        for _ in range(COARSE_SWEEPS - 4):
            u = window_sweep(b, u)
        around_e = [[turned(u[c], k) for k in range(6)] for c in range(3)]
        last = []
        for p in range(SLOTS):
            left = wide_residual(p, [u] * SLOTS, None, lambda q, c, k: around_e[c][k])
            step = apply_inverse(inverse_wide, p, left)
            last.append([u_wide[p, c] + u[c] + step[c] for c in range(3)])
        for c in range(3):
            for x in range(2):
                for at, (t, y) in enumerate(((RADIUS - 1, 1), (RADIUS, 0), (RADIUS, 1), (RADIUS + 1, 0))):
                    low, high = last[2 * x + y][c], last[4 + 2 * x + y][c]
                    if t & 4:
                        value = jnp.where(slot_at == t, high, 0.0) + along(jnp.where(slot_at == t, low, 0.0), -4)
                    else:
                        value = jnp.where(slot_at == t, low, 0.0) + along(jnp.where(slot_at == t, high, 0.0), 4)
                    for bit in (1, 2):
                        value = value + along(value, -bit if t & bit else bit)
                    e_rows[x, at, c] = value

    def mid_at(c, x, y):
        row = RADIUS + (x // 2)
        return wide(e_rows[x % 2, y + 1, c, row : row + 1, :])

    odd = (lane_at & 1) != 0

    def even_part(v):
        return jnp.where(odd, along(v, 1), v)

    def odd_part(v):
        return jnp.where(odd, v, along(v, -1))

    def rows_tile(rows):
        made = jnp.zeros(tile, jnp.float32)
        for at, value in rows:
            made = jnp.where(row_at == at, wide(value), made)
        return made

    def pair_up():
        for x in range(4):
            for j in range(14):
                part = [weights[1][x, i] if i < 18 else reaction[1][x, i - 18] for i in (2 * j, 2 * j + 1) if i < 27]
                coef_own[x, j] = jnp.where(odd, part[-1], part[0])
        for side, y in ((0, 6), (1, 0)):
            for j in range(0, 14, 2):
                rows = [(4 * i + x, coef_own[x, j + i, y : y + 1, :]) for i in range(2) for x in range(4)]
                coef_y_send[side, j // 2] = rows_tile(rows)

    def send_ring_coefficients():
        copies = []
        for side, turn in ((0, 1), (1, -1)):
            sems = lambda n: (coef_send_sem.at[n], coef_recv_sem.at[n])
            copies.append(remote(coef_y_send.at[side], coef_y.at[side], *sems(side), (0, turn)))
            copies.append(remote(coef_own.at[3 - 3 * side], coef_x.at[side], *sems(2 + side), (turn, 0)))
        for n in range(4):
            x, y = 3 - 3 * (n // 2), 6 - 6 * (n % 2)
            for j in range(14):
                coef_corner_send[n, j : j + 1, :] = coef_own[x, j, y : y + 1, :]
            to = (1 - 2 * (n // 2), 1 - 2 * (n % 2))
            copies.append(
                remote(coef_corner_send.at[n], coef_corner.at[n], coef_send_sem.at[4 + n], coef_recv_sem.at[4 + n], to)
            )
        return copies

    def take_ring_coefficients(copies):
        for copy in copies:
            copy.wait()
        for p in range(6):
            filled = jnp.logical_and(row_at >= 1, row_at < ROWS - 1)
            for j in range(14):
                if p in (0, 5):
                    rows = [(2 + k, coef_x[p // 5, j, 2 * k : 2 * k + 1, :]) for k in range(4)]
                    rows += [(1 + 5 * sy, coef_corner[2 * (p // 5) + sy, j : j + 1, :]) for sy in range(2)]
                else:
                    x = p - 1
                    rows = [(2 + k, coef_own[x, j, 2 * k : 2 * k + 1, :]) for k in range(4)]
                    at = 4 * (j % 2) + x
                    rows += [(1, coef_y[0, j // 2, at : at + 1, :]), (6, coef_y[1, j // 2, at : at + 1, :])]
                both = rows_tile(rows)
                for i, value in ((2 * j, even_part(both)), (2 * j + 1, odd_part(both))):
                    if i < 18:
                        ring_w[p, i] = value
                    elif i < 27:
                        ring_r[p, i - 18] = jnp.where(filled, value, 1.0) if i in (18, 22, 26) else value
        finish(ring_w, ring_r, ring_diag, ring_inverse, 6)
        off_high = jnp.logical_and(row_at == 5, is_high_y)
        off_low = jnp.logical_and(row_at == 2, is_low_y)
        for c in range(3):
            ring_w[4, c] = jnp.where(is_high_x, 0.0, ring_w[4, c])
            ring_w[1, 3 + c] = jnp.where(is_low_x, 0.0, ring_w[1, 3 + c])

        def body(p):
            for k, off in ((2, off_high), (3, off_low), (4, lane_at >= lanes - 2), (5, lane_at < 2)):
                for c in range(3):
                    ring_w[p, 3 * k + c] = jnp.where(off, 0.0, ring_w[p, 3 * k + c])

        each(6, body)

    def send_pairs(turn):
        for x in range(4):
            for c in range(3):
                pair_own[x, c] = jnp.where(odd, sources[1][x, c], fields[1][0, x + 1, c])
        for side, y in ((0, 4), (1, 0)):
            for c in range(3):
                rows = [(2 * x + k, pair_own[x, c, y + 2 * k : y + 2 * k + 1, :]) for x in range(4) for k in range(2)]
                pair_y_send[side, c] = rows_tile(rows)
        for sx in range(2):
            for sy in range(2):
                x, y = 3 - 3 * sx, 6 - 6 * sy
                for i, (at_x, at_y) in enumerate(((x, y), (2 - sx, y), (x, 4 - 2 * sy))):
                    for c in range(3):
                        n = 3 * i + c
                        pair_corner_send[2 * sx + sy, n : n + 1, :] = pair_own[at_x, c, at_y : at_y + 1, :]
        copies = []
        sems = lambda n: (pair_send_sem.at[n], pair_recv_sem.at[turn, n])
        for side, to in ((0, 1), (1, -1)):
            copies.append(remote(pair_y_send.at[side], pair_y.at[turn, side], *sems(side), (0, to)))
            source = pair_own.at[pl.ds(2 - 2 * side, 2)]
            copies.append(remote(source, pair_x.at[turn, side], *sems(2 + side), (to, 0)))
        for sx in range(2):
            for sy in range(2):
                n = 2 * sx + sy
                to = (1 - 2 * sx, 1 - 2 * sy)
                copies.append(remote(pair_corner_send.at[n], pair_corner.at[turn, n], *sems(4 + n), to))
        return copies

    def take_pairs(turn, copies):
        for copy in copies:
            copy.wait()
        for p in range(8):
            for c in range(3):
                if 2 <= p < 6:
                    x = p - 2
                    rows = [(2 + k, pair_own[x, c, 2 * k : 2 * k + 1, :]) for k in range(4)]
                    for side in range(2):
                        for k in range(2):
                            at = 2 * x + k
                            rows.append((6 * side + k, pair_y[turn, side, c, at : at + 1, :]))
                else:
                    side = p // 4
                    rows = [(2 + k, pair_x[turn, side, p - 6 * side, c, 2 * k : 2 * k + 1, :]) for k in range(4)]
                    for sy in range(2):
                        cells = ((0, 1 + 5 * sy), (2, 7 * sy)) if p in (1, 6) else ((1, 1 + 5 * sy),)
                        for i, row in cells:
                            n = 3 * i + c
                            rows.append((row, pair_corner[turn, 2 * side + sy, n : n + 1, :]))
                both = rows_tile(rows)
                ring_u[p, c] = even_part(both)
                if 1 <= p < 7:
                    ring_b[p - 1, c] = odd_part(both)

    def ring_sweep():
        def add(p):
            x = p // 2 - 1
            for c in range(3):
                e = jnp.where(row_at < 2, mid_at(c, x, -1), mid_at(c, x, 0))
                e = jnp.where(row_at < 4, e, jnp.where(row_at < 6, mid_at(c, x, 1), mid_at(c, x, 2)))
                ring_u[p, c] += e

        for p in range(8):
            add(p)
        for p in range(6):
            u = [ring_u[p + 1, c] for c in range(3)]
            left = []
            for c in range(3):
                value = ring_b[p, c] - ring_diag[p, c] * u[c]
                near = (ring_u[p + 2, c], ring_u[p, c], down(u[c], -1), down(u[c], 1), along(u[c], -2), along(u[c], 2))
                for k in range(6):
                    value = value + ring_w[p, 3 * k + c] * near[k]
                for d in range(3):
                    if d != c:
                        value = value - ring_r[p, 3 * d + c] * u[d]
                left.append(value)
            step = apply_inverse(ring_inverse, p, left)
            for c in range(3):
                ring_out[p, c] = u[c] + step[c]

    def packed_y(f, at):
        return rows_tile([(x, f(x)[at : at + 1, :]) for x in range(8)])

    def send_rim():
        copies = []
        sems = lambda n: (rim_send_sem.at[n], rim_recv_sem.at[n])
        for side, to in ((0, 1), (1, -1)):
            row, second = 7 - 7 * side, 6 - 5 * side
            for i in range(9):
                rim_y_send[side, i] = rows_tile([(x, reaction[0][x, i, row : row + 1, :]) for x in range(8)])
            rim_y_send[side, 9] = rows_tile([(x, pot[x + 1, second : second + 1, :]) for x in range(8)])
            for c in range(3):
                rim_y_send[side, 10 + c] = rows_tile([(x, base[x, c, row : row + 1, :]) for x in range(8)])
            copies.append(remote(rim_y_send.at[side], rim_y.at[side], *sems(side), (0, to)))
            copies.append(remote(reaction[0].at[row], rim_r.at[side], *sems(2 + side), (to, 0)))
            copies.append(remote(pot.at[second + 1], rim_pot.at[side], *sems(4 + side), (to, 0)))
            copies.append(remote(base.at[row], rim_base.at[side], *sems(6 + side), (to, 0)))
        for n in range(4):
            x, y = 7 - 7 * (n // 2), 7 - 7 * (n % 2)
            rim_pot_corner_send[n] = pot[x + 1, y : y + 1, :]
            to = (1 - 2 * (n // 2), 1 - 2 * (n % 2))
            copies.append(remote(rim_pot_corner_send.at[n], rim_pot_corner.at[n], *sems(8 + n), to))
        return copies

    def ordered(t, out_side, in_side, ahead, behind, above, below):
        across = (in_side, out_side) if t % 2 == 0 else (out_side, in_side)
        return (across + (ahead, behind) if t < 2 else (ahead, behind) + across) + (above, below)

    def take_rim(copies):
        for copy in copies:
            copy.wait()
        for side in range(2):
            for i in range(9):
                rim_r[2 + side, i] = rim_y[side, i]
            for c in range(3):
                rim_base[2 + side, c] = rim_y[side, 10 + c]
        for t in range(4):
            side = t % 2
            if t < 2:
                here, beyond, inside = pot[9 * side], rim_pot[side], pot[1 + 7 * side]
                first, last = 2 * side, 2 * side + 1
                edges = (is_low_y, is_high_y)
            else:
                here, beyond = pot_y[side], rim_y[side, 9]
                row = 7 * side
                inside = rows_tile([(x, pot[x + 1, row : row + 1, :]) for x in range(8)])
                first, last = side, 2 + side
                edges = (is_low_x, is_high_x)
            corner = lambda n, off: jnp.where(off, 0.0, wide(rim_pot_corner[n]))
            near = ordered(
                t,
                beyond,
                inside,
                jnp.where(row_at == ROWS - 1, corner(last, edges[1]), down(here, -1)),
                jnp.where(row_at == 0, corner(first, edges[0]), down(here, 1)),
                jnp.where(lane_at == lanes - 1, 0.0, along(here, -1)),
                jnp.where(lane_at == 0, 0.0, along(here, 1)),
            )
            for k in range(6):
                plus, minus = face_weights(here - near[k])
                rim_w[t, 3 * k] = jnp.ones(tile, jnp.float32)
                rim_w[t, 3 * k + 1] = plus
                rim_w[t, 3 * k + 2] = minus
        finish(rim_w, rim_r, rim_diag, rim_inverse, 4)
        for t in range(4):
            ahead, off_high, off_low = (2, is_high_y, is_low_y) if t < 2 else (0, is_high_x, is_low_x)
            masks = (
                (ahead, jnp.logical_and(row_at == ROWS - 1, off_high)),
                (ahead + 1, jnp.logical_and(row_at == 0, off_low)),
                (4, lane_at == lanes - 1),
                (5, lane_at == 0),
            )
            for k, off in masks:
                for c in range(3):
                    rim_w[t, 3 * k + c] = jnp.where(off, 0.0, rim_w[t, 3 * k + c])

    def doubled(rows):
        e = jnp.where(row_at < 2, wide(rows[0]), wide(rows[1]))
        return jnp.where(row_at < 4, e, jnp.where(row_at < 6, wide(rows[2]), wide(rows[3])))

    def rim_sweep(at):
        for t in range(4):
            side = t % 2
            e, near = [], []
            for c in range(3):
                cell = lambda p, row: ring_out[p, c, row : row + 1, :]
                if t < 2:
                    p, p_in = 5 * side, 1 + 3 * side
                    here = doubled([cell(p, 2 + k) for k in range(4)])
                    inside = doubled([cell(p_in, 2 + k) for k in range(4)])
                    first, last = cell(p, 1), cell(p, 6)
                else:
                    row, row_in = 1 + 5 * side, 2 + 3 * side
                    here = doubled([cell(1 + k, row) for k in range(4)])
                    inside = doubled([cell(1 + k, row_in) for k in range(4)])
                    first, last = cell(0, row), cell(5, row)
                e.append(here)
                near.append(
                    ordered(
                        t,
                        here,
                        inside,
                        jnp.where(row_at == ROWS - 1, wide(last), down(here, -1)),
                        jnp.where(row_at == 0, wide(first), down(here, 1)),
                        along(here, -1),
                        along(here, 1),
                    )
                )
            left = []
            for c in range(3):
                value = -rim_diag[t, c] * e[c]
                for k in range(6):
                    value = value + rim_w[t, 3 * k + c] * near[c][k]
                for d in range(3):
                    if d != c:
                        value = value - rim_r[t, 3 * d + c] * e[d]
                left.append(value)
            step = apply_inverse(rim_inverse, t, left)
            for c in range(3):
                value = rim_base[t, c] + e[c] + step[c]
                if t < 2:
                    fields[0][at, 9 * side, c] = value
                else:
                    rows_halo[3, side, c] = value

    def source(level, x):
        if level == 0:
            return [grad[c, x] for c in range(3)]
        return [sources[level][x, c] for c in range(3)]

    def solve(level, x, r):
        v = inverse[level]
        return [v[x, 3 * c] * r[0] + v[x, 3 * c + 1] * r[1] + v[x, 3 * c + 2] * r[2] for c in range(3)]

    def post(level, at):
        slot, f, count = done[0] % 3, fields[level], NX[level]
        for side, row in ((0, ROWS - 1), (1, 0)):
            for c in range(3):
                packed = wide(f[at, 1, c, row : row + 1, :])
                for x in range(1, count):
                    packed = jnp.where(row_at == x, wide(f[at, x + 1, c, row : row + 1, :]), packed)
                send_y[side, c] = packed
        wait = exchange(
            [
                (f.at[at, count], f.at[at, 0]),
                (f.at[at, 1], f.at[at, count + 1]),
                (send_y.at[0], rows_halo.at[slot, 0]),
                (send_y.at[1], rows_halo.at[slot, 1]),
            ]
        )
        return slot, wait

    def share(level, at, beside_it):
        slot, wait = post(level, at)
        beside_it()
        inner(level, at)
        wait()
        return slot

    def inner(level, at):
        f, w, r, span, count = fields[level], weights[level], reaction[level], 1 << level, NX[level]
        for x in range(count):
            u = [f[at, x + 1, c] for c in range(3)]
            b = source(level, x)
            for c in range(3):
                value = b[c] - diag[level][x, c] * u[c]
                value = value + w[x, 6 + c] * jnp.where(row_at >= ROWS - span, 0.0, down(u[c], -span))
                value = value + w[x, 9 + c] * jnp.where(row_at < span, 0.0, down(u[c], span))
                value = value + w[x, 12 + c] * along(u[c], -span) + w[x, 15 + c] * along(u[c], span)
                if x < count - 1:
                    value = value + w[x, c] * f[at, x + 2, c]
                if x > 0:
                    value = value + w[x, 3 + c] * f[at, x, c]
                for d in range(3):
                    if d != c:
                        value = value - r[x, 3 * d + c] * u[d]
                part[x, c] = value

    def rest(level, at, slot, x, stride=1, whole=True):
        f, w, span, count = fields[level], weights[level], 1 << level, NX[level]
        left = []
        for c in range(3):
            row = x * stride
            row_high, row_low = (rows_halo[slot, side, c, row : row + 1, :] for side in (1, 0))
            value = jnp.where(row_at >= ROWS - span, w[x, 6 + c] * wide(row_high), 0.0)
            value = jnp.where(row_at < span, w[x, 9 + c] * wide(row_low), value)
            if whole:
                value = part[x, c] + value
            if x == 0:
                value = value + w[x, 3 + c] * f[at, 0, c]
            if x == count - 1:
                value = value + w[x, c] * f[at, count + 1, c]
            left.append(value)
        return [f[at, x + 1, c] for c in range(3)], left

    def residual(level, at, slot, x):
        f, w, r, span = fields[level], weights[level], reaction[level], 1 << level
        u = [f[at, x + 1, c] for c in range(3)]
        b = source(level, x)
        left = []
        for c in range(3):
            near = (
                f[at, x + 2, c],
                f[at, x, c],
                jnp.where(row_at >= ROWS - span, wide(rows_halo[slot, 1, c, x : x + 1, :]), down(u[c], -span)),
                jnp.where(row_at < span, wide(rows_halo[slot, 0, c, x : x + 1, :]), down(u[c], span)),
                along(u[c], -span),
                along(u[c], span),
            )
            value = b[c] - diag[level][x, c] * u[c]
            for k in range(6):
                value = value + w[x, 3 * k + c] * near[k]
            for d in range(3):
                if d != c:
                    value = value - r[x, 3 * d + c] * u[d]
            left.append(value)
        return u, left

    def sweep(at, slot, left_of):
        for x in range(NX[0]):
            u, left = left_of(0, at, slot, x)
            step = solve(0, x, left)
            for c in range(3):
                fields[0][at + 1, x + 1, c] = u[c] + step[c]
        return at + 1

    def make_halo_inverse():
        for i in range(9):
            for side in range(2):
                row = 1 + 5 * side
                halo_inverse[side, i] = doubled([ring_inverse[5 * side, i, 2 + k : 3 + k, :] for k in range(4)])
                halo_inverse[2 + side, i] = doubled([ring_inverse[1 + k, i, row : row + 1, :] for k in range(4)])

    def restrict_with_halo(at):
        slot, wait = post(0, at)
        rows, lanes_ = pair_tools(0)[4:]
        outside = (is_low_x, is_high_x, is_low_y, is_high_y)
        for t in range(4):
            for c in range(3):
                edge = fields[0][at, 1 + 7 * t, c] if t < 2 else send_y[3 - t, c]
                value = jnp.where(outside[t], 0.0, rim_w[t, 3 * t + c] * edge)
                cross[t, c] = lanes_(rows(value))
        copies = []
        sems = lambda n: (lean_send_sem.at[n], lean_recv_sem.at[n])
        for n in range(4):
            sx, sy = n // 2, n % 2
            for c in range(3):
                row = 6 - 6 * sx
                cross_send[n, c : c + 1, :] = cross[3 - sy, c, row : row + 1, :]
                row = 6 - 6 * sy
                cross_send[n, 3 + c : 4 + c, :] = cross[1 - sx, c, row : row + 1, :]
            copies.append(remote(cross_send.at[n], cross_recv.at[n], *sems(4 + n), (1 - 2 * sx, 1 - 2 * sy)))
        inner(0, at)
        for x in range(4):
            for c in range(3):
                lean[x, c] = lanes_(rows(part[2 * x, c] + part[2 * x + 1, c]))
        for side, to in ((0, 1), (1, -1)):
            row = 6 - 6 * side
            for c in range(3):
                lean_y_send[side, c] = doubled([lean[k, c, row : row + 1, :] for k in range(4)])
            copies.append(remote(lean_y_send.at[side], lean_y.at[side], *sems(side), (0, to)))
            copies.append(remote(lean.at[3 - 3 * side], lean_x.at[side], *sems(2 + side), (to, 0)))
        wait()
        for x in range(4):
            more = [rest(0, at, slot, 2 * x + i, whole=False)[1] for i in range(2)]
            for i in range(2):
                for c in range(3):
                    base[2 * x + i, c] = part[2 * x + i, c] + more[i][c]
            total = [lean[x, c] + lanes_(rows(more[0][c] + more[1][c])) for c in range(3)]
            first = solve(1, x, total)
            for c in range(3):
                sources[1][x, c] = total[c]
                fields[1][0, x + 1, c] = first[c]
        for copy in copies:
            copy.wait()
        for t in range(4):
            side = t % 2
            total = []
            for c in range(3):
                if t < 2:
                    value, first, last, row = lean_x[side, c], 2 * side, 2 * side + 1, c
                else:
                    value, first, last, row = lean_y[side, c], side, 2 + side, 3 + c
                low, high = (wide(cross_recv[n, row : row + 1, :]) for n in (first, last))
                value = value + cross[t, c]
                total.append(value + jnp.where(row_at < 2, low, jnp.where(row_at >= 6, high, 0.0)))
            first = apply_inverse(halo_inverse, t, total)
            for c in range(3):
                if t < 2:
                    fields[1][0, 5 * side, c] = first[c]
                else:
                    rows_halo[3, side, c] = first[c]
        inner(1, 0)
        return slot

    def restrict(level, at, slot, keep=False, stride=1):
        rows, lanes_ = pair_tools(level)[4:]
        for x in range(NX[level + 1]):
            left = []
            for i in range(2):
                u, r = rest(level, at, slot, 2 * x + i, stride)
                left.append(r)
                if keep:
                    for c in range(3):
                        base[2 * x + i, c] = r[c]
            total = [lanes_(rows(left[0][c] + left[1][c])) for c in range(3)]
            first = solve(level + 1, x, total)
            for c in range(3):
                sources[level + 1][x, c] = total[c]
                fields[level + 1][0, x + 1, c] = first[c]

    def make_base(at):
        for x in range(NX[0]):
            step = solve(0, x, [base[x, c] for c in range(3)])
            for c in range(3):
                base[x, c] = fields[0][at, x + 1, c] + step[c]

    def correct_finest(at, last):
        copies = []
        planes = [[doubled([ring_out[p, c, 2 + k : 3 + k, :] for k in range(4)]) for c in range(3)] for p in range(6)]
        w, r, v = weights[0], reaction[0], inverse[0]
        for p in range(1, 5):
            e = planes[p]
            turned = []
            for c in range(3):
                after, before = wide(ring_out[p, c, 6:7, :]), wide(ring_out[p, c, 1:2, :])
                turned.append(
                    (
                        jnp.where(row_at == ROWS - 1, after, down(e[c], -1)),
                        jnp.where(row_at == 0, before, down(e[c], 1)),
                        along(e[c], -1),
                        along(e[c], 1),
                    )
                )
            for i in range(2):
                x = 2 * p - 2 + i
                left = []
                for c in range(3):
                    near = (e[c] if i == 0 else planes[p + 1][c], planes[p - 1][c] if i == 0 else e[c]) + turned[c]
                    value = -diag[0][x, c] * e[c]
                    for k in range(6):
                        value = value + w[x, 3 * k + c] * near[k]
                    for d in range(3):
                        if d != c:
                            value = value - r[x, 3 * d + c] * e[d]
                    left.append(value)
                step = apply_inverse(v, x, left)
                for c in range(3):
                    value = base[x, c] + e[c] + step[c]
                    if last:
                        result[c, x] = value
                    else:
                        fields[0][at + 1, x + 1, c] = value
                if last:
                    copies.append(pltpu.make_async_copy(result.at[:, x], out.at[:, x], out_sem.at[x]))
                    copies[-1].start()
        for copy in copies:
            copy.wait()
        return at + 1

    def cycle(at, turn, besides, last=False):
        pairs = []
        if last:
            slot = restrict_with_halo(at)
            restrict(1, 0, 3, stride=2)
        else:
            slot = share(0, at, besides[0])
            restrict(0, at, slot, keep=True)

            def beside():
                pairs.extend(send_pairs(turn))
                besides[1]()
                make_base(at)

            restrict(1, 0, share(1, 0, beside))

        def beside_p():
            if last:
                pairs.extend(send_pairs(turn))
                make_base(at)
            besides[2]()

        def beside_q():
            take_pairs(turn, pairs)
            besides[3]()

        lower(turn, beside_p, beside_q)
        ring_sweep()
        if not last:
            rim_sweep(at + 1)
        return correct_finest(at, last)

    def start(x):
        for c, value in enumerate(solve(0, x, source(0, x))):
            fields[0][0, x + 1, c] = value

    finish_level(0)
    loads["grad"].wait()
    each(NX[0], start)
    pending, ring_pending, rim_pending = [], [], []

    def beside_first():
        coarsen(0)
        mask_level(0)
        finish_level(1)
        coarsen(1)
        pending.append(send_coefficients())

    def beside_second():
        pair_up()
        mask_level(1)
        finish_level(2)
        coarsen(2)
        pending.append(send_low_coefficients())

    def beside_third():
        ring_pending.extend(send_ring_coefficients())
        rim_pending.extend(send_rim())
        take_coefficients(pending)

    def beside_fourth():
        take_ring_coefficients(ring_pending)
        take_rim(rim_pending)
        make_halo_inverse()

    nothing = lambda: None
    at = cycle(
        0,
        0,
        (
            beside_first,
            beside_second,
            beside_third,
            beside_fourth,
        ),
    )
    at = sweep(at, 3, residual)
    cycle(at, 1, (nothing,) * 4, last=True)


def local(counts, gradient, potential, coupling, region, contact, rates):
    nz = potential.shape[-1]
    tile = (ROWS, nz)
    f32 = jnp.float32
    scratch = []
    for parts in (18, 9, 3, 9):
        scratch += [pltpu.VMEM((n, parts) + tile, f32) for n in NX]
    scratch += [pltpu.VMEM((n, 3) + tile, f32) for n in NX[1:]]
    scratch += [pltpu.VMEM((3, n + 2, 3) + tile, f32) for n in NX]
    scratch += [
        pltpu.VMEM((4, 2, 3) + tile, f32),
        pltpu.VMEM((2,) + tile, f32),
        pltpu.VMEM((2, 3) + tile, f32),
        pltpu.SemaphoreType.DMA((4,)),
        pltpu.SemaphoreType.DMA((3, 4)),
        pltpu.VMEM((1, 18) + tile, f32),
        pltpu.VMEM((1, 9) + tile, f32),
        pltpu.VMEM((SLOTS, 18) + tile, f32),
        pltpu.VMEM((SLOTS, 9) + tile, f32),
        pltpu.VMEM((SLOTS, 3) + tile, f32),
        pltpu.VMEM((SLOTS, 9) + tile, f32),
        pltpu.VMEM((SLOTS, 3) + tile, f32),
        pltpu.VMEM((SLOTS, 3) + tile, f32),
        pltpu.VMEM((2, 4, 3) + tile, f32),
        pltpu.VMEM((27, 1, nz), f32),
        pltpu.VMEM((len(INNER), 27, 1, nz), f32),
        pltpu.VMEM((4, nz), f32),
        pltpu.VMEM((len(FOURTH), 4, nz), f32),
        pltpu.VMEM((2, 3, 1, nz), f32),
        pltpu.VMEM((2, len(INNER + OUTER), 3, 1, nz), f32),
        pltpu.VMEM((1, 1, nz), f32),
        pltpu.VMEM((2, len(THIRD), 1, nz), f32),
        pltpu.SemaphoreType.DMA,
        pltpu.SemaphoreType.DMA,
        pltpu.SemaphoreType.DMA,
        pltpu.SemaphoreType.DMA,
        pltpu.SemaphoreType.DMA,
        pltpu.SemaphoreType.DMA((2,)),
        pltpu.SemaphoreType.DMA,
        pltpu.SemaphoreType.DMA((2,)),
        pltpu.VMEM((8, 3) + tile, f32),
        pltpu.VMEM((6, 3) + tile, f32),
        pltpu.VMEM((6, 18) + tile, f32),
        pltpu.VMEM((6, 9) + tile, f32),
        pltpu.VMEM((6, 3) + tile, f32),
        pltpu.VMEM((6, 9) + tile, f32),
        pltpu.VMEM((6, 3) + tile, f32),
        pltpu.VMEM((4, 3) + tile, f32),
        pltpu.VMEM((2, 2, 2, 3) + tile, f32),
        pltpu.VMEM((2, 3) + tile, f32),
        pltpu.VMEM((2, 2, 3) + tile, f32),
        pltpu.VMEM((4, 2 * ROWS, nz), f32),
        pltpu.VMEM((2, 4, 2 * ROWS, nz), f32),
        pltpu.SemaphoreType.DMA((8,)),
        pltpu.SemaphoreType.DMA((2, 8)),
        pltpu.VMEM((4, 14) + tile, f32),
        pltpu.VMEM((2, 14) + tile, f32),
        pltpu.VMEM((2, 7) + tile, f32),
        pltpu.VMEM((2, 7) + tile, f32),
        pltpu.SemaphoreType.DMA((8,)),
        pltpu.SemaphoreType.DMA((8,)),
        pltpu.VMEM((NX[0], 3) + tile, f32),
        pltpu.VMEM((4, 2 * ROWS, nz), f32),
        pltpu.VMEM((4, 2 * ROWS, nz), f32),
        pltpu.VMEM((4, 18) + tile, f32),
        pltpu.VMEM((4, 9) + tile, f32),
        pltpu.VMEM((4, 3) + tile, f32),
        pltpu.VMEM((4, 9) + tile, f32),
        pltpu.VMEM((4, 3) + tile, f32),
        pltpu.VMEM((2,) + tile, f32),
        pltpu.VMEM((4, 1, nz), f32),
        pltpu.VMEM((4, 1, nz), f32),
        pltpu.VMEM((NX[0], 3) + tile, f32),
        pltpu.VMEM((2, 13) + tile, f32),
        pltpu.VMEM((2, 13) + tile, f32),
        pltpu.SemaphoreType.DMA((12,)),
        pltpu.SemaphoreType.DMA((12,)),
        pltpu.VMEM(gradient.shape, f32),
        pltpu.SemaphoreType.DMA((NX[0],)),
        pltpu.VMEM((4, 9) + tile, f32),
        pltpu.VMEM((4, 3) + tile, f32),
        pltpu.VMEM((4,) + tile, f32),
        pltpu.VMEM((4,) + tile, f32),
        pltpu.VMEM((4, 3) + tile, f32),
        pltpu.VMEM((2, 3) + tile, f32),
        pltpu.VMEM((2, 3) + tile, f32),
        pltpu.VMEM((2, 3) + tile, f32),
        pltpu.SemaphoreType.DMA((8,)),
        pltpu.SemaphoreType.DMA((8,)),
        pltpu.VMEM((SLOTS, 3) + tile, f32),
        pltpu.VMEM(gradient.shape, f32),
        pltpu.VMEM((10,) + tile, f32),
        pltpu.VMEM(coupling.shape, f32),
        pltpu.VMEM(region.shape, jnp.int32),
        pltpu.VMEM(contact.shape, jnp.int32),
        pltpu.SMEM(rates.shape, f32),
        pltpu.SemaphoreType.DMA((6,)),
    ]
    return pl.pallas_call(
        functools.partial(kernel, counts),
        out_shape=jax.ShapeDtypeStruct(gradient.shape, f32),
        in_specs=[pl.BlockSpec(memory_space=pltpu.HBM)] * 6,
        out_specs=pl.BlockSpec(memory_space=pltpu.HBM),
        scratch_shapes=scratch,
        compiler_params=pltpu.CompilerParams(
            collective_id=0, has_side_effects=True, vmem_limit_bytes=60 * 1024 * 1024
        ),
    )(gradient, potential, coupling, region, contact, rates)


def solution(mesh):
    placed = (
        P(None, "gx", "gy", None),
        P("gx", "gy", None),
        P(None, None, "gx", "gy", None),
        P("gx", "gy", None),
        P("gx", "gy", None),
        P(),
    )
    counts = (mesh.shape["gx"], mesh.shape["gy"])
    return jax.shard_map(
        functools.partial(local, counts),
        mesh=mesh,
        in_specs=placed,
        out_specs=P(None, "gx", "gy", None),
        check_vma=False,
    )
```
